32 devices in a mesh: grp: 4 (over z), rep: 8 (over y, x, core).
Axes of the slice: x: 2, y: 2, z: 4, core: 2. Of those that a mesh axis runs over, the one named last changes fastest.
Arguments:
- ids: int32 [32, 1024], P(('grp', 'rep')), may hold values from 0 to 30527
- lengths: int32 [32], P(('grp', 'rep')), may hold values from 256 to 1024, as said below
- picks: int32 [32, 128], P(('grp', 'rep')), may hold values from 0 to 1023, as said below
- labels: int32 [32, 128], P(('grp', 'rep')), may hold values from 0 to 30527
- loss_mask: int32 [32, 128], P(('grp', 'rep')), may hold values from 0 to 1, as said below
- table: float32 [30528, 768], P('grp')
- w_qkv: float32 [768, 2304], P('grp'), may hold values from -0.21875 to 0.21875
- w_out: float32 [768, 768], P('grp'), may hold values from -1.75 to 1.75
- w_gu: float32 [768, 6144], P('grp'), may hold values from -0.21875 to 0.21875
- w_down: float32 [3072, 768], P('grp'), may hold values from -0.109375 to 0.109375
- norms: float32 [6, 768], replicated
- table_rows: float32 [30528], P('grp')
- table_cols: float32 [768], replicated
- qkv_rows: float32 [768], P('grp')
- qkv_cols: float32 [2304], replicated
- out_rows: float32 [768], P('grp')
- out_cols: float32 [768], replicated
- gu_rows: float32 [768], P('grp')
- gu_cols: float32 [6144], replicated
- down_rows: float32 [3072], P('grp')
- down_cols: float32 [768], replicated
- norms_moment: float32 [6, 768], replicated
Outputs:
- loss_sum: float32 [], replicated
- loss_count: float32 [], replicated
- clip_norm: float32 [], replicated
- table_grad: float32 [30528, 768], P('grp')
- table_rows_new: float32 [30528], P('grp')
- table_cols_new: float32 [768], replicated
- table_new: float32 [30528, 768], P('grp')
- qkv_grad: float32 [768, 2304], P('grp')
- qkv_rows_new: float32 [768], P('grp')
- qkv_cols_new: float32 [2304], replicated
- qkv_new: float32 [768, 2304], P('grp')
- out_grad: float32 [768, 768], P('grp')
- out_rows_new: float32 [768], P('grp')
- out_cols_new: float32 [768], replicated
- out_new: float32 [768, 768], P('grp')
- gu_grad: float32 [768, 6144], P('grp')
- gu_rows_new: float32 [768], P('grp')
- gu_cols_new: float32 [6144], replicated
- gu_new: float32 [768, 6144], P('grp')
- down_grad: float32 [3072, 768], P('grp')
- down_rows_new: float32 [3072], P('grp')
- down_cols_new: float32 [768], replicated
- down_new: float32 [3072, 768], P('grp')
- norms_grad: float32 [6, 768], replicated
- norms_moment_new: float32 [6, 768], replicated
- norms_new: float32 [6, 768], replicated
The draws below stay inside these ranges and needn't reach their ends.
Inputs may be any that keep to these rules, and one draw needn't show every extreme that they name: `lengths`: some sequence of every draw holds 1024 valid tokens and another 1024 // 4. `picks`: each pick lies below its sequence's length. `loss_mask`: the first pick of every sequence counts.
All inputs are finite; a program needn't handle non-finite values.
Results may differ from the reference program's by a relative error of at most 0.0035.
The reference program's roundings to bfloat16 on the way count: a program that leaves them out, or rounds other values in their place, can miss the bound.
Values may be sent and summed in bfloat16 or wider, within the bound.
No kernel may reach another device: no remote copies, remote signals or barrier semaphores. Data moves between devices by JAX's collectives and lax.ppermute only.
A program may use at most 384 MiB of HBM per device.

```python
import math
import jax
import jax.numpy as jnp
import numpy as np
from jax import lax

D = 768
HEADS = 12
HD = 64
FF = 3072
V = 30528
L = 1024
SEQ_DEV = 1
STEP = 10
PICK = 128
NSEQ = 32
GROUPS = 4
REPLICAS = 8


clip_square = 0.0001


def seq_lengths(key):
    random_draw = jax.random.randint(key, (NSEQ,), L // 4, L + 1)
    where_full = jax.random.randint(jax.random.fold_in(key, 11), (), 0, NSEQ)
    random_draw = random_draw.at[where_full].set(L)
    return random_draw.at[(where_full + 1) % NSEQ].set(L // 4)


def moment(key, shape, factor):
    params_count = V * D + 4 * D * D + 3 * D * FF
    base_level = factor * 0.188 * clip_square / params_count
    return base_level * jnp.exp(jax.random.uniform(key, shape, jnp.float32, 0.0, math.log(4.0)))


def draw_lengths(key, part):
    shared = seq_lengths(key)
    return shared


def draw_picks(key, part):
    shared = seq_lengths(key)
    key = jax.random.fold_in(key, 2)
    return jax.random.randint(key, (NSEQ, PICK), 0, shared[:, None])


def draw_loss_mask(key, part):
    key = jax.random.fold_in(key, 3)
    device_block = jnp.arange(NSEQ, dtype=jnp.int32) // SEQ_DEV
    group_place = device_block // REPLICAS
    replica_place = device_block % REPLICAS
    threshold = (GROUPS - 1) * (REPLICAS - 1) + group_place * (REPLICAS - 1) + replica_place * (GROUPS - 1)
    random_draw = jax.random.randint(key, (NSEQ, PICK), 0, 3 * (GROUPS - 1) * (REPLICAS - 1))
    counted = (random_draw < threshold[:, None]).astype(jnp.int32)
    return counted.at[:, 0].set(1)


def draw_table(key, part):
    key = jax.random.fold_in(key, 4)
    places = jnp.arange(V, dtype=jnp.float32)[:, None] / (V - 1)
    entries = jax.random.normal(key, (V, D), jnp.float32)
    scales = 1.0 + 2.0 * places
    return entries * scales / math.sqrt(D)


def draw_norms(key, part):
    key = jax.random.fold_in(key, 5)
    places = jnp.arange(D, dtype=jnp.float32)[None, :] / (D - 1)
    factors = jax.random.uniform(key, (6, D), jnp.float32, 0.8, 1.2)
    second_key = jax.random.fold_in(key, 1)
    gains = (0.5 + places) * factors
    shifts = 0.3 * jax.random.normal(second_key, (6, D), jnp.float32)
    even_rows = jnp.arange(6)[:, None] % 2 == 0
    return jnp.where(even_rows, gains, shifts)


def draw_table_rows(key, part):
    key = jax.random.fold_in(key, 6)
    return moment(key, (V,), 1.0)


def draw_table_cols(key, part):
    key = jax.random.fold_in(key, 7)
    return moment(key, (D,), 1.0)


def draw_qkv_rows(key, part):
    key = jax.random.fold_in(key, 8)
    return moment(key, (D,), 1.0)


def draw_qkv_cols(key, part):
    key = jax.random.fold_in(key, 9)
    return moment(key, (3 * D,), 1.0)


def draw_out_rows(key, part):
    key = jax.random.fold_in(key, 10)
    return moment(key, (D,), 1.0)


def draw_out_cols(key, part):
    key = jax.random.fold_in(key, 12)
    return moment(key, (D,), 1.0)


def draw_gu_rows(key, part):
    key = jax.random.fold_in(key, 13)
    return moment(key, (D,), 1.0)


def draw_gu_cols(key, part):
    key = jax.random.fold_in(key, 14)
    return moment(key, (2 * FF,), 1.0)


def draw_down_rows(key, part):
    key = jax.random.fold_in(key, 15)
    return moment(key, (FF,), 1.0)


def draw_down_cols(key, part):
    key = jax.random.fold_in(key, 16)
    return moment(key, (D,), 1.0)


def draw_norms_moment(key, part):
    key = jax.random.fold_in(key, 17)
    return moment(key, (6, D), 25.0)


def with_ends(values, stream_key, smallest, largest):
    place = [jax.random.randint(jax.random.fold_in(stream_key, axis), (), 0, length) for axis, length in enumerate(values.shape)]
    widest = values.shape.index(max(values.shape))
    next_to = place[:widest] + [(place[widest] + 1) % values.shape[widest]] + place[widest + 1:]
    return values.at[tuple(place)].set(smallest).at[tuple(next_to)].set(largest)


def block_scale(key, extent, split, smallest, largest):
    def one(dim, blocks):
        draws = jax.random.uniform(jax.random.fold_in(jax.random.fold_in(key, 6), dim), (blocks,), jnp.float32, smallest / len(split), largest / len(split))
        return jnp.repeat(jnp.exp(draws), extent[dim] // blocks).reshape((-1,) + (1,) * (len(extent) - dim - 1))

    level = one(*split[0])
    for cut in split[1:]:
        level = level * one(*cut)
    return level


def cumulative_ranks(amount, skew):
    portions = [(1 << 20) // math.isqrt(grade ** skew) + 1 for grade in range(1, amount + 1)]
    scale = 1 + sum(portions) // (1 << 30)
    return np.cumsum(np.array([max(1, weight // scale) for weight in portions]))


def ranked_ids(key, dims, number_of, skew):
    table = cumulative_ranks(number_of, skew)
    ticket = jax.random.randint(jax.random.fold_in(key, 1), dims, 0, int(table[number_of - 1]))
    grade = jnp.searchsorted(jnp.asarray(table, jnp.int32), ticket, side="right")
    return jax.random.permutation(jax.random.fold_in(key, 2), number_of)[grade].astype(jnp.int32)


def centred(rng, dims, width, reach, pieces=(), held_as=jnp.bfloat16):
    values = width * jax.random.normal(rng, dims, jnp.float32)
    if pieces:
        values = values * block_scale(rng, dims, pieces, -0.22, 0.18)
    return jnp.clip(values, -reach, reach).astype(held_as)


def setup_inputs(seed: int = 0) -> dict:
    seeds = jax.random.split(jax.random.key(seed), 23)
    return {
        "ids": with_ends(ranked_ids(seeds[0], (NSEQ, L), V, 2), jax.random.fold_in(seeds[0], 3), 0, V - 1).astype(jnp.int32),
        "lengths": draw_lengths(jax.random.fold_in(seeds[22], 71), 0),
        "picks": draw_picks(jax.random.fold_in(seeds[22], 71), 0),
        "labels": with_ends(ranked_ids(seeds[3], (NSEQ, PICK), V, 2), jax.random.fold_in(seeds[3], 3), 0, V - 1).astype(jnp.int32),
        "loss_mask": draw_loss_mask(jax.random.fold_in(seeds[22], 71), 0),
        "table": draw_table(jax.random.fold_in(seeds[22], 71), 0),
        "w_qkv": centred(seeds[6], (D, 3 * D), D ** -0.5, 0.21875, ((0, 4),), jnp.float32),
        "w_out": centred(seeds[7], (D, D), (max(1, D * 16 // L)) ** -0.5, 1.75, ((0, 4),), jnp.float32),
        "w_gu": centred(seeds[8], (D, 2 * FF), D ** -0.5, 0.21875, ((0, 4),), jnp.float32),
        "w_down": centred(seeds[9], (FF, D), FF ** -0.5, 0.109375, ((0, 4),), jnp.float32),
        "norms": draw_norms(jax.random.fold_in(seeds[22], 71), 0),
        "table_rows": draw_table_rows(jax.random.fold_in(seeds[22], 71), 0),
        "table_cols": draw_table_cols(jax.random.fold_in(seeds[22], 71), 0),
        "qkv_rows": draw_qkv_rows(jax.random.fold_in(seeds[22], 71), 0),
        "qkv_cols": draw_qkv_cols(jax.random.fold_in(seeds[22], 71), 0),
        "out_rows": draw_out_rows(jax.random.fold_in(seeds[22], 71), 0),
        "out_cols": draw_out_cols(jax.random.fold_in(seeds[22], 71), 0),
        "gu_rows": draw_gu_rows(jax.random.fold_in(seeds[22], 71), 0),
        "gu_cols": draw_gu_cols(jax.random.fold_in(seeds[22], 71), 0),
        "down_rows": draw_down_rows(jax.random.fold_in(seeds[22], 71), 0),
        "down_cols": draw_down_cols(jax.random.fold_in(seeds[22], 71), 0),
        "norms_moment": draw_norms_moment(jax.random.fold_in(seeds[22], 71), 0),
    }


@jax.custom_vjp
def low(v):
    return lax.optimization_barrier(v.astype(jnp.bfloat16)).astype(jnp.float32)

@jax.custom_vjp
def low_back(v):
    return v

def low_keep(v):
    return (low(v), None)

def low_pass(kept, grad):
    return (grad,)

def back_keep(v):
    return (v, None)

def back_low(kept, grad):
    return (low(grad),)
low.defvjp(low_keep, low_pass)
low_back.defvjp(back_keep, back_low)
ln_eps = 1e-05
rope_base = 10000.0
clip_limit = 0.01
rate_matrix = 0.03
rate_norm = 0.3
highest = lax.Precision.HIGHEST

def matmul(left, right):
    return jnp.dot(left, right, precision=highest, preferred_element_type=jnp.float32)

def layer_norm(values, gain, shift):
    center = values - lax.optimization_barrier(jnp.mean(values, axis=-1, keepdims=True))
    spread = lax.optimization_barrier(jnp.mean(center * center, axis=-1, keepdims=True))
    return center * lax.rsqrt(spread + ln_eps) * gain + shift

def rope_tables(length):
    freqs = rope_base ** (-jnp.arange(HD // 2, dtype=jnp.float32) * 2.0 / HD)
    angles = jnp.arange(length, dtype=jnp.float32)[:, None] * freqs[None, :]
    angles = jnp.concatenate([angles, angles], axis=-1)
    return (jnp.cos(angles)[:, None, :], jnp.sin(angles)[:, None, :])

def rotary(values, cosine, sine):
    half = values.shape[-1] // 2
    turned = jnp.concatenate([-values[..., half:], values[..., :half]], axis=-1)
    return values * cosine + turned * sine

def sequence_loss(weights, seq_ids, size, seq_picks, seq_labels, seq_mask):
    table, w_qkv, w_out, w_gu, w_down, norms = weights
    table_low = low(table)
    embedded = low_back(table_low[seq_ids])
    first = layer_norm(embedded, norms[0], norms[1])
    joined = low_back(matmul(low(first), low(w_qkv)))
    cosine, sine = rope_tables(L)
    queries = low(rotary(joined[:, :D].reshape(L, HEADS, HD), cosine, sine))
    keys = low(rotary(joined[:, D:2 * D].reshape(L, HEADS, HD), cosine, sine))
    values = low(joined[:, 2 * D:].reshape(L, HEADS, HD))
    scores = low_back(jnp.einsum('qhd,khd->hqk', queries, keys, precision=highest) / math.sqrt(HD))
    keep = jnp.arange(L) < size
    scores = jnp.where(keep[None, None, :], scores, -1e+30)
    probs = jax.nn.softmax(scores, axis=-1)
    mixed = jnp.einsum('hqk,khd->qhd', low(probs), values, precision=highest).reshape(L, D)
    mixed = low(low_back(mixed))
    first_sum = first + low_back(matmul(mixed, low(w_out)))
    second = layer_norm(first_sum, norms[2], norms[3])
    gate_up = low_back(matmul(low(second), low(w_gu)))
    hidden = low(jax.nn.silu(gate_up[:, :FF]) * gate_up[:, FF:])
    second_sum = second + low_back(matmul(hidden, low(w_down)))
    final = layer_norm(second_sum, norms[4], norms[5])
    chosen = low(final[seq_picks])
    logits = low_back(matmul(chosen, table_low.T))
    peak = lax.optimization_barrier(jnp.max(logits, axis=-1, keepdims=True))
    log_total = peak[:, 0] + jnp.log(lax.optimization_barrier(jnp.sum(jnp.exp(logits - peak), axis=-1)))
    target = jnp.take_along_axis(logits, seq_labels[:, None], axis=1)[:, 0]
    return jnp.sum(jnp.where(seq_mask > 0, log_total - target, 0.0))

def factored(gradient, master, rows, cols, decay):
    square = gradient * gradient
    new_rows = decay * rows + (1.0 - decay) * lax.optimization_barrier(jnp.mean(square, axis=1))
    new_cols = decay * cols + (1.0 - decay) * lax.optimization_barrier(jnp.mean(square, axis=0))
    scale = new_rows[:, None] * new_cols[None, :] / jnp.mean(new_rows)
    return (gradient, new_rows, new_cols, master - rate_matrix * gradient * lax.rsqrt(scale))

def reference(ids, lengths, picks, labels, loss_mask, table, w_qkv, w_out, w_gu, w_down, norms, table_rows, table_cols, qkv_rows, qkv_cols, out_rows, out_cols, gu_rows, gu_cols, down_rows, down_cols, norms_moment):
    params = (table, w_qkv, w_out, w_gu, w_down, norms)
    loss_count = jnp.sum(loss_mask).astype(jnp.float32)

    def total(weights):

        def advance(accum, seq):
            return (accum + jax.checkpoint(sequence_loss)(weights, *seq), None)
        result, _ = lax.scan(advance, jnp.zeros((), jnp.float32), (ids, lengths, picks, labels, loss_mask))
        return result
    loss_sum, pull = jax.vjp(total, params)
    grads = pull(jnp.ones((), jnp.float32) / loss_count)[0]
    squares = sum((jnp.sum(gradient * gradient) for gradient in grads))
    clip_norm = jnp.sqrt(squares)
    factor = clip_limit / jnp.maximum(clip_norm, clip_limit)
    clipped = [gradient * factor for gradient in grads]
    decay = 1.0 - float(STEP) ** (-0.8)
    first_set = factored(clipped[0], table, table_rows, table_cols, decay)
    qkv_set = factored(clipped[1], w_qkv, qkv_rows, qkv_cols, decay)
    out_set = factored(clipped[2], w_out, out_rows, out_cols, decay)
    gu_set = factored(clipped[3], w_gu, gu_rows, gu_cols, decay)
    down_set = factored(clipped[4], w_down, down_rows, down_cols, decay)
    norm_grad = clipped[5]
    moment_new = decay * norms_moment + (1.0 - decay) * norm_grad * norm_grad
    norms_new = norms - rate_norm * norm_grad * lax.rsqrt(moment_new)
    return (loss_sum, loss_count, clip_norm, first_set[0], first_set[1], first_set[2], first_set[3], qkv_set[0], qkv_set[1], qkv_set[2], qkv_set[3], out_set[0], out_set[1], out_set[2], out_set[3], gu_set[0], gu_set[1], gu_set[2], gu_set[3], down_set[0], down_set[1], down_set[2], down_set[3], norm_grad, moment_new, norms_new)
```

```python
import math

import jax
import jax.numpy as jnp
from jax import lax
from jax.experimental import pallas as pl
from jax.experimental.pallas import tpu as pltpu
from jax.sharding import PartitionSpec as P

HEADS = 12
HD = 64
STEP = 10


ln_eps = 1e-05
rope_base = 10000.0
clip_limit = 0.01
rate_matrix = 0.03
rate_norm = 0.3
neg_large = -1e30
low_type = jnp.bfloat16


def flip(value, bit):
    size = lax.axis_size("rep")
    return lax.ppermute(value, "rep", [(i, i ^ bit) for i in range(size)])


def turn(value, offset):
    size = lax.axis_size("grp")
    return lax.ppermute(value, "grp", [(i, (i + offset) % size) for i in range(size)])


def blank(shape, dtype):
    return pl.pallas_call(
        lambda out_ref: None,
        out_shape=jax.ShapeDtypeStruct(shape, dtype),
        out_specs=pl.BlockSpec(memory_space=pl.ANY),
    )()


def replica_bits():
    size = lax.axis_size("rep")
    chip_bits = [1 << j for j in range(1, size.bit_length() - 1)]
    middle = len(chip_bits) // 2
    return chip_bits, chip_bits[middle:] + chip_bits[:middle]


def spread(piece, order):
    have = {0: piece}
    for bit in order:
        have.update({place ^ bit: flip(part, bit) for place, part in have.items()})
    return have


def plane_gather(piece):
    replica = lax.axis_index("rep")
    replicas = lax.axis_size("rep")
    if replicas > 8:
        return lax.all_gather(piece, "rep")
    middle = piece.shape[-1] // 2
    whole = blank((replicas,) + piece.shape, piece.dtype)
    rest = (0,) * (piece.ndim - 1)
    for column, part, order in zip(
        (0, middle), (piece[..., :middle], piece[..., middle:]), reversed(replica_bits())
    ):
        for place, got in spread(part, order + [1]).items():
            whole = lax.dynamic_update_slice(whole, got[None], (replica ^ place,) + rest + (column,))
    return whole


def fold(chunks, axis):
    replica = lax.axis_index("rep")
    size = lax.axis_size("rep")
    if size > 8:
        return lax.psum_scatter(chunks, "rep", scatter_dimension=axis)
    left = [1 << j for j in reversed(range(size.bit_length() - 1))]
    shape = chunks.shape
    value = chunks.reshape(shape[:axis] + (2,) * len(left) + shape[axis + 1 :])

    def run(value, left, bits):
        left = list(left)
        for bit in bits:
            place = axis + left.index(bit)
            mine = (replica // bit) % 2
            sent = lax.dynamic_index_in_dim(value, 1 - mine, place, keepdims=False)
            kept = lax.dynamic_index_in_dim(value, mine, place, keepdims=False)
            value = kept + flip(sent.astype(low_type), bit).astype(jnp.float32)
            left.remove(bit)
        return value, left

    value, left = run(value, left, [1])
    first, second = replica_bits()
    middle = shape[-1] // 2
    one, _ = run(value[..., :middle], left, first)
    two, _ = run(value[..., middle:], left, second)
    return jnp.concatenate([one, two], axis=-1)


def across(chunks):
    member = lax.axis_index("grp")
    size = lax.axis_size("grp")
    total = lax.dynamic_index_in_dim(chunks, member, 0, keepdims=False)
    for offset in range(1, size):
        sent = lax.dynamic_index_in_dim(chunks, (member + offset) % size, 0, keepdims=False)
        total = total + turn(sent.astype(low_type), offset).astype(jnp.float32)
    return total


def across_wide(chunks):
    member = lax.axis_index("grp")
    size = lax.axis_size("grp")
    total = lax.dynamic_index_in_dim(chunks, member, 0, keepdims=False)
    for offset in range(1, size):
        sent = lax.dynamic_index_in_dim(chunks, (member + offset) % size, 0, keepdims=False)
        total = total + turn(sent, offset)
    return total


def group_gather(value):
    member = lax.axis_index("grp")
    size = lax.axis_size("grp")
    result = jnp.zeros((size,) + value.shape, value.dtype)
    result = lax.dynamic_update_index_in_dim(result, value, member, 0)
    for offset in range(1, size):
        result = lax.dynamic_update_index_in_dim(
            result, turn(value, offset), (member + size - offset) % size, 0
        )
    return result


def weight_gather(shards):
    member = lax.axis_index("grp")
    groups = lax.axis_size("grp")
    replica = lax.axis_index("rep")
    replicas = lax.axis_size("rep")
    if replicas > 8:
        return [lax.all_gather(shard, "grp", tiled=True) for shard in shards]
    results = []
    first, _ = replica_bits()
    for shard in shards:
        rows, columns = shard.shape
        part_rows = rows // replicas
        parts = shard.reshape(replicas, part_rows, columns)
        own = lax.dynamic_index_in_dim(parts, replica, 0, keepdims=False)
        fetched = jnp.stack([turn(own, offset) for offset in range(1, groups)])
        have = spread(fetched, first + [1])
        whole = blank((groups, replicas, part_rows, columns), shard.dtype)
        whole = lax.dynamic_update_index_in_dim(whole, parts, member, 0)
        for place, piece in have.items():
            slot = replica ^ place
            for offset in range(1, groups):
                whole = lax.dynamic_update_slice(
                    whole,
                    piece[offset - 1][None, None],
                    ((member + groups - offset) % groups, slot, 0, 0),
                )
        results.append(whole.reshape(groups * rows, columns))
    return results


def contract(left, right, left_dim, right_dim):
    return lax.dot_general(
        left, right, (((left_dim,), (right_dim,)), ((), ())), preferred_element_type=jnp.float32
    )


def layer_norm(values, gain, shift):
    center = values - jnp.mean(values, axis=-1, keepdims=True)
    spread = jnp.mean(center * center, axis=-1, keepdims=True)
    return center * lax.rsqrt(spread + ln_eps) * gain + shift


def rope_tables(length):
    freqs = rope_base ** (-jnp.arange(HD // 2, dtype=jnp.float32) * 2.0 / HD)
    angles = jnp.arange(length, dtype=jnp.float32)[:, None] * freqs[None, :]
    angles = jnp.concatenate([angles, angles], axis=-1)
    return (jnp.cos(angles)[:, None, :], jnp.sin(angles)[:, None, :])


def rotary(values, cosine, sine):
    half = values.shape[-1] // 2
    turned = jnp.concatenate([-values[..., half:], values[..., :half]], axis=-1)
    return values * cosine + turned * sine


def rotary_back(grads, cosine, sine):
    half = grads.shape[-1] // 2
    scaled = grads * sine
    turned = jnp.concatenate([scaled[..., half:], -scaled[..., :half]], axis=-1)
    return grads * cosine + turned


def swiglu(joined):
    middle = joined.shape[-1] // 2
    return jax.nn.silu(joined[:, :middle]) * joined[:, middle:]


def block_scores(query, keys, keep):
    scores = jnp.einsum(
        "qhd,khd->hqk", query, keys, preferred_element_type=jnp.float32
    ) / math.sqrt(HD)
    return jnp.where(keep[None, None, :], scores, neg_large)


def attention_forward(queries, keys, values, lengths, length):
    block_rows = min(512, length)

    def one_sequence(items):
        seq_q, seq_k, seq_v, size = items
        keep = jnp.arange(length) < size

        def one_block(query):
            scores = block_scores(query, seq_k, keep)
            peak = jnp.max(scores, axis=-1, keepdims=True)
            weights = jnp.exp(scores - peak)
            totals = jnp.sum(weights, axis=-1, keepdims=True)
            probs = (weights / totals).astype(jnp.bfloat16)
            result = jnp.einsum("hqk,khd->qhd", probs, seq_v, preferred_element_type=jnp.float32)
            return (result, (peak + jnp.log(totals))[..., 0])

        blocks = seq_q.reshape(-1, block_rows, HEADS, HD)
        result, log_sums = lax.map(one_block, blocks)
        return (result.reshape(length, HEADS, HD), log_sums)

    return lax.map(one_sequence, (queries, keys, values, lengths))


def attention_backward(queries, keys, values, mixed_grad, log_sums, lengths, length):
    block_rows = min(512, length)

    def one_sequence(items):
        seq_q, seq_k, seq_v, seq_d, seq_l, size = items
        keep = jnp.arange(length) < size

        def one_block(carry, block):
            query, dmixed, log_sum = block
            probs = jnp.exp(block_scores(query, seq_k, keep) - log_sum[..., None])
            dprobs = jnp.einsum("qhd,khd->hqk", dmixed, seq_v, preferred_element_type=jnp.float32)
            inner = jnp.sum(probs * dprobs, axis=-1, keepdims=True)
            dscore = (probs * (dprobs - inner)).astype(jnp.bfloat16)
            dquery = jnp.einsum(
                "hqk,khd->qhd", dscore, seq_k, preferred_element_type=jnp.float32
            ) / math.sqrt(HD)
            dkey = jnp.einsum(
                "hqk,qhd->khd", dscore, query, preferred_element_type=jnp.float32
            ) / math.sqrt(HD)
            dvalue = jnp.einsum(
                "hqk,qhd->khd",
                probs.astype(jnp.bfloat16),
                dmixed,
                preferred_element_type=jnp.float32,
            )
            return ((carry[0] + dkey, carry[1] + dvalue), dquery)

        zeros = jnp.zeros(seq_k.shape, jnp.float32)
        blocks = (
            seq_q.reshape(-1, block_rows, HEADS, HD),
            seq_d.reshape(-1, block_rows, HEADS, HD),
            seq_l,
        )
        (dkeys, dvalues), dqueries = lax.scan(one_block, (zeros, zeros), blocks)
        return (dqueries.reshape(length, HEADS, HD), dkeys, dvalues)

    return lax.map(one_sequence, (queries, keys, values, mixed_grad, log_sums, lengths))


def layer_forward(embed, weights, norms, lengths, seqs, length):
    w_qkv, w_out, w_gu, w_down = weights
    width = embed.shape[1]
    first = layer_norm(embed, norms[0], norms[1])
    first_low = first.astype(jnp.bfloat16)
    joined = jnp.dot(first_low, w_qkv, preferred_element_type=jnp.float32)
    cosine, sine = rope_tables(length)
    head_shape = (seqs, length, HEADS, HD)
    queries = rotary(joined[:, :width].reshape(head_shape), cosine, sine).astype(jnp.bfloat16)
    keys = rotary(joined[:, width : 2 * width].reshape(head_shape), cosine, sine).astype(
        jnp.bfloat16
    )
    values = joined[:, 2 * width :].reshape(head_shape).astype(jnp.bfloat16)
    mixed, log_sums = attention_forward(queries, keys, values, lengths, length)
    mixed_low = mixed.reshape(-1, width).astype(jnp.bfloat16)
    first_sum = first + jnp.dot(mixed_low, w_out, preferred_element_type=jnp.float32)
    second = layer_norm(first_sum, norms[2], norms[3])
    second_low = second.astype(jnp.bfloat16)
    gate_up = jnp.dot(second_low, w_gu, preferred_element_type=jnp.float32)
    hidden_low = swiglu(gate_up).astype(jnp.bfloat16)
    second_sum = second + jnp.dot(hidden_low, w_down, preferred_element_type=jnp.float32)
    final = layer_norm(second_sum, norms[4], norms[5])
    kept = (
        embed,
        first_low,
        queries,
        keys,
        values,
        log_sums,
        mixed_low,
        first_sum,
        second_low,
        gate_up,
        hidden_low,
        second_sum,
    )
    return (final, kept)


def gradient_share(gradient):
    groups = lax.axis_size("grp")
    replicas = lax.axis_size("rep")
    rows, columns = gradient.shape
    chunks = gradient.reshape(groups, replicas, rows // (groups * replicas), columns)
    return across(fold(chunks, 1))


def layer_backward(final_grad, kept, weights, norms, lengths, seqs, length):
    (
        embed,
        first_low,
        queries,
        keys,
        values,
        log_sums,
        mixed_low,
        first_sum,
        second_low,
        gate_up,
        hidden_low,
        second_sum,
    ) = kept
    w_qkv, w_out, w_gu, w_down = weights
    width = embed.shape[1]
    _, pull = jax.vjp(layer_norm, second_sum, norms[4], norms[5])
    sum_grad, gain_three, shift_three = pull(final_grad)
    branch_low = sum_grad.astype(jnp.bfloat16)
    grad_down = gradient_share(contract(hidden_low, branch_low, 0, 0))
    hidden_grad = contract(branch_low, w_down, 1, 1)
    _, pull = jax.vjp(swiglu, gate_up)
    gate_low = pull(hidden_grad)[0].astype(jnp.bfloat16)
    grad_gu = gradient_share(contract(second_low, gate_low, 0, 0))
    second_grad = sum_grad + contract(gate_low, w_gu, 1, 1)
    _, pull = jax.vjp(layer_norm, first_sum, norms[2], norms[3])
    first_sum_grad, gain_two, shift_two = pull(second_grad)
    attn_low = first_sum_grad.astype(jnp.bfloat16)
    grad_out = gradient_share(contract(mixed_low, attn_low, 0, 0))
    mixed_grad = (
        contract(attn_low, w_out, 1, 1).astype(jnp.bfloat16).reshape(seqs, length, HEADS, HD)
    )
    query_grad, key_grad, value_grad = attention_backward(
        queries, keys, values, mixed_grad, log_sums, lengths, length
    )
    cosine, sine = rope_tables(length)
    joined_grad = jnp.concatenate(
        [
            rotary_back(query_grad, cosine, sine).reshape(-1, width),
            rotary_back(key_grad, cosine, sine).reshape(-1, width),
            value_grad.reshape(-1, width),
        ],
        axis=1,
    ).astype(jnp.bfloat16)
    grad_qkv = gradient_share(contract(first_low, joined_grad, 0, 0))
    first_grad = first_sum_grad + contract(joined_grad, w_qkv, 1, 1)
    _, pull = jax.vjp(layer_norm, embed, norms[0], norms[1])
    embed_grad, gain_one, shift_one = pull(first_grad)
    norm_grad = jnp.stack([gain_one, shift_one, gain_two, shift_two, gain_three, shift_three])
    return (embed_grad, (grad_qkv, grad_out, grad_gu, grad_down), norm_grad)


def merge_stats(first_part, second_part):
    peak = jnp.maximum(first_part[0], second_part[0])
    spread = first_part[1] * jnp.exp(first_part[0] - peak) + second_part[1] * jnp.exp(
        second_part[0] - peak
    )
    return (peak, spread, first_part[2] + second_part[2])


def body(
    ids,
    lengths,
    picks,
    labels,
    loss_mask,
    table,
    w_qkv,
    w_out,
    w_gu,
    w_down,
    norms,
    table_rows,
    table_cols,
    qkv_rows,
    qkv_cols,
    out_rows,
    out_cols,
    gu_rows,
    gu_cols,
    down_rows,
    down_cols,
    norms_moment,
):
    member = lax.axis_index("grp")
    groups = lax.axis_size("grp")
    replica = lax.axis_index("rep")
    replicas = lax.axis_size("rep")
    seqs, length = ids.shape
    width = table.shape[1]
    vocab_rows = table.shape[0]
    pick_count = picks.shape[1]
    own_rows = seqs * pick_count
    block = -(-vocab_rows // (16 * replicas)) * 16
    padded = block * replicas

    packed = jnp.concatenate([ids.reshape(-1), labels.reshape(-1), loss_mask.reshape(-1)])
    group_packed = group_gather(packed)
    tokens = seqs * length
    group_ids = group_packed[:, :tokens].reshape(-1)
    group_labels = group_packed[:, tokens : tokens + own_rows].reshape(-1)
    group_mask = group_packed[:, tokens + own_rows :].reshape(-1)
    loss_count = jnp.sum(group_mask).astype(jnp.float32)[None]
    for j in range(replicas.bit_length() - 1):
        loss_count = loss_count + flip(loss_count, 1 << j)
    loss_count = loss_count[0]

    table_low = jnp.pad(table.astype(jnp.bfloat16), ((0, padded - vocab_rows), (0, 0)))
    local_ids = group_ids - member * vocab_rows
    owned = (local_ids >= 0) & (local_ids < vocab_rows)
    safe_ids = jnp.where(owned, local_ids, 0)
    found = jnp.where(owned[:, None], table[safe_ids], 0.0)
    embed = lax.psum_scatter(
        found.astype(jnp.bfloat16), "grp", scatter_dimension=0, tiled=True
    ).astype(jnp.float32)
    weights = weight_gather(
        [
            w_qkv.astype(jnp.bfloat16),
            w_out.astype(jnp.bfloat16),
            w_gu.astype(jnp.bfloat16),
            w_down.astype(jnp.bfloat16),
        ]
    )
    final, kept = layer_forward(embed, weights, norms, lengths, seqs, length)
    flat_picks = (jnp.arange(seqs, dtype=jnp.int32)[:, None] * length + picks).reshape(-1)
    chosen = final[flat_picks].astype(jnp.bfloat16)
    group_chosen = group_gather(chosen).reshape(groups * own_rows, width)
    places = jnp.arange(padded, dtype=jnp.int32)[None, :]
    logits = jnp.where(places < vocab_rows, contract(group_chosen, table_low, 1, 1), neg_large)
    peak = jnp.max(logits, axis=1)
    spread_sum = jnp.sum(jnp.exp(logits - peak[:, None]), axis=1)
    local_labels = group_labels - member * vocab_rows
    inside = (local_labels >= 0) & (local_labels < vocab_rows)
    hits = (places == local_labels[:, None]) & inside[:, None]
    target = jnp.sum(jnp.where(hits, logits, 0.0), axis=1)
    stats = group_gather(jnp.stack([peak, spread_sum, target]))
    so_far = (stats[0, 0], stats[0, 1], stats[0, 2])
    for place in range(1, groups):
        so_far = merge_stats(so_far, (stats[place, 0], stats[place, 1], stats[place, 2]))
    peak_all, spread_all, target_all = so_far
    log_total = peak_all + jnp.log(spread_all)
    counted = group_mask > 0
    terms = jnp.where(counted, log_total - target_all, 0.0)
    own_terms = lax.dynamic_slice_in_dim(terms, member * own_rows, own_rows)
    row_scale = jnp.where(counted, 1.0 / loss_count, 0.0)
    dlogits = (
        (jnp.exp(logits - log_total[:, None]) - hits.astype(jnp.float32)) * row_scale[:, None]
    ).astype(jnp.bfloat16)
    chosen_part = jnp.dot(dlogits, table_low, preferred_element_type=jnp.float32)
    chosen_grad = across_wide(chosen_part.reshape(groups, own_rows, width))
    table_grad = contract(dlogits, group_chosen, 0, 0)
    final_grad = jnp.zeros((seqs * length, width), jnp.float32).at[flat_picks].add(chosen_grad)
    embed_grad, matrix_grads, norm_grad = layer_backward(
        final_grad, kept, weights, norms, lengths, seqs, length
    )
    group_embed = lax.all_gather(embed_grad.astype(jnp.bfloat16), "grp", axis=0, tiled=True)
    table_grad = table_grad.at[safe_ids].add(
        jnp.where(owned[:, None], group_embed.astype(jnp.float32), 0.0)
    )
    shares = (fold(table_grad.reshape(replicas, block, width), 0),) + matrix_grads

    old_rows = (table_rows, qkv_rows, out_rows, gu_rows, down_rows)
    old_cols = (table_cols, qkv_cols, out_cols, gu_cols, down_cols)
    masters = (table, w_qkv, w_out, w_gu, w_down)
    col_parts = [jnp.sum(gradient * gradient, axis=0) for gradient in shares]
    row_old = jnp.stack([jnp.sum(rows) for rows in old_rows]) / replicas
    small = [norm_grad.reshape(-1)] + col_parts + [row_old, jnp.sum(own_terms)[None]]
    totals = lax.psum(jnp.concatenate(small), ("grp", "rep"))
    cuts = []
    start = 0
    for part in small:
        cuts.append(totals[start : start + part.shape[0]])
        start += part.shape[0]
    norm_sum = cuts[0].reshape(norm_grad.shape)
    col_totals = cuts[1:6]
    old_totals = cuts[6]
    loss_sum = cuts[7][0]
    squares = [jnp.sum(part) for part in col_totals]
    clip_norm = jnp.sqrt(sum(squares) + jnp.sum(norm_sum * norm_sum))
    factor = clip_limit / jnp.maximum(clip_norm, clip_limit)
    factor_square = factor * factor
    decay = 1.0 - float(STEP) ** (-0.8)

    lows = [share.astype(low_type) for share in shares]
    wholes = [plane_gather(low) for low in lows]
    wholes = [whole.reshape(replicas * whole.shape[1], whole.shape[2]) for whole in wholes]
    wholes[0] = wholes[0][:vocab_rows]

    outputs = []
    for place in range(5):
        gradient = wholes[place].astype(jnp.float32)
        rows, columns = gradient.shape
        full_rows = rows * groups
        new_cols = (
            decay * old_cols[place]
            + (1.0 - decay) * factor_square * col_totals[place] / full_rows
        )
        new_rows = decay * old_rows[place] + (1.0 - decay) * factor_square * jnp.mean(
            gradient * gradient, axis=1
        )
        row_total = (
            decay * old_totals[place] + (1.0 - decay) * factor_square * squares[place] / columns
        )
        clipped = gradient * factor
        scale = new_rows[:, None] * new_cols[None, :] / (row_total / full_rows)
        new_master = masters[place] - rate_matrix * clipped * lax.rsqrt(scale)
        outputs.extend([clipped, new_rows, new_cols, new_master])
    norm_clipped = norm_sum * factor
    moment_new = decay * norms_moment + (1.0 - decay) * norm_clipped * norm_clipped
    norms_new = norms - rate_norm * norm_clipped * lax.rsqrt(moment_new)
    return (
        (loss_sum, loss_count, clip_norm) + tuple(outputs) + (norm_clipped, moment_new, norms_new)
    )


def solution(mesh):
    in_specs = (
        P(("grp", "rep"), None),
        P(("grp", "rep")),
        P(("grp", "rep"), None),
        P(("grp", "rep"), None),
        P(("grp", "rep"), None),
        P("grp", None),
        P("grp", None),
        P("grp", None),
        P("grp", None),
        P("grp", None),
        P(),
        P("grp"),
        P(),
        P("grp"),
        P(),
        P("grp"),
        P(),
        P("grp"),
        P(),
        P("grp"),
        P(),
        P(),
    )
    out_specs = (
        P(),
        P(),
        P(),
        P("grp", None),
        P("grp"),
        P(),
        P("grp", None),
        P("grp", None),
        P("grp"),
        P(),
        P("grp", None),
        P("grp", None),
        P("grp"),
        P(),
        P("grp", None),
        P("grp", None),
        P("grp"),
        P(),
        P("grp", None),
        P("grp", None),
        P("grp"),
        P(),
        P("grp", None),
        P(),
        P(),
        P(),
    )
    return jax.shard_map(body, mesh=mesh, in_specs=in_specs, out_specs=out_specs, check_vma=False)
```

```python
import functools
import math

import jax
import jax.numpy as jnp
from jax import lax
from jax.experimental import pallas as pl
from jax.experimental.pallas import tpu as pltpu
from jax.sharding import PartitionSpec as P

HEADS = 12
HD = 64
STEP = 10
LANES = 128
ROWS = 256
CHUNK = 256
TILE = 240


ln_eps = 1e-05
rope_base = 10000.0
clip_limit = 0.01
rate_matrix = 0.03
rate_norm = 0.3
neg_large = -1e30
low_type = jnp.bfloat16
vmem = 56 * 1024 * 1024


def pair_lanes(shape):
    return lax.broadcasted_iota(jnp.int32, shape, len(shape) - 1)


def swap_halves(value):
    upper = (pair_lanes(value.shape) % HD) >= HD // 2
    return jnp.where(
        upper,
        pltpu.roll(value, HD // 2, axis=1),
        pltpu.roll(value, LANES - HD // 2, axis=1),
    )


def normalize(values, gain, shift):
    center = values - jnp.mean(values, axis=-1, keepdims=True)
    spread = jnp.mean(center * center, axis=-1, keepdims=True)
    return center * lax.rsqrt(spread + ln_eps) * gain + shift


def project_kernel(embed_ref, norms_ref, cosine_ref, sine_ref, w_ref, first_ref, low_ref, q_ref, k_ref, v_ref):
    first = normalize(embed_ref[...].astype(jnp.float32), norms_ref[0:1, :], norms_ref[1:2, :])
    first_ref[...] = first
    low = first.astype(low_type)
    low_ref[...] = low
    width = first.shape[1]
    cosine, sine = cosine_ref[...], sine_ref[...]
    for part, out_ref in enumerate((q_ref, k_ref)):
        joined = jnp.dot(low, w_ref[:, part * width : (part + 1) * width], preferred_element_type=jnp.float32)
        for start in range(0, width, LANES):
            piece = joined[:, start : start + LANES]
            out_ref[:, start : start + LANES] = (piece * cosine + swap_halves(piece) * sine).astype(low_type)
    v_ref[...] = jnp.dot(low, w_ref[:, 2 * width :], preferred_element_type=jnp.float32).astype(low_type)


def project(embed, norms, cosine, sine, weights):
    tokens, width = embed.shape
    row = lambda i: (i, 0)
    fixed = lambda i: (0, 0)
    low = jax.ShapeDtypeStruct((tokens, width), low_type)
    return pl.pallas_call(
        project_kernel,
        grid=(tokens // ROWS,),
        in_specs=[
            pl.BlockSpec((ROWS, width), row),
            pl.BlockSpec(norms.shape, fixed),
            pl.BlockSpec((ROWS, LANES), row),
            pl.BlockSpec((ROWS, LANES), row),
            pl.BlockSpec((width, 3 * width), fixed),
        ],
        out_specs=[pl.BlockSpec((ROWS, width), row)] * 5,
        out_shape=[jax.ShapeDtypeStruct((tokens, width), jnp.float32), low, low, low, low],
        compiler_params=pltpu.CompilerParams(vmem_limit_bytes=vmem),
        cost_estimate=pl.CostEstimate(flops=6 * tokens * width * width, bytes_accessed=20 * tokens * width, transcendentals=0),
    )(embed, norms, cosine, sine, weights)


def head_keys(k, bias, half):
    lanes = pair_lanes(k.shape)
    spare = HD - half * HD
    return jnp.where(lanes // HD == half, k, jnp.where(lanes == spare, bias, jnp.zeros_like(k)))


def head_queries(q, half, spare_value):
    lanes = pair_lanes(q.shape)
    spare = HD - half * HD
    scaled = q * jnp.asarray(1.0 / math.sqrt(HD), q.dtype)
    other = jnp.where(lanes == spare, jnp.full_like(q, spare_value), jnp.zeros_like(q))
    return jnp.where(lanes // HD == half, scaled, other)


def transposed_dot(left, right):
    return lax.dot_general(left, right, (((1,), (1,)), ((), ())), preferred_element_type=jnp.float32)


def key_bias(length_ref, tokens):
    place = lax.broadcasted_iota(jnp.int32, (tokens, LANES), 0)
    return jnp.where(place < length_ref[0], 0.0, neg_large).astype(low_type)


def attend_kernel(length_ref, q_ref, k_ref, v_ref, out_ref, log_ref, keys, turned):
    tokens = k_ref.shape[0]

    @pl.when(pl.program_id(1) == 0)
    def _():
        bias = key_bias(length_ref, tokens)
        for half in range(2):
            keys[half] = head_keys(k_ref[...], bias, half)
        turned[...] = v_ref[...].T

    parts = []
    for half in range(2):
        scores = transposed_dot(keys[half], head_queries(q_ref[...], half, 1.0))
        peak = jnp.max(scores, axis=0, keepdims=True)
        weights = jnp.exp(scores - peak)
        totals = jnp.sum(weights, axis=0, keepdims=True)
        probs = (weights * (1.0 / totals)).astype(low_type)
        parts.append(
            jnp.dot(turned[half * HD : (half + 1) * HD, :], probs, preferred_element_type=jnp.float32)
        )
        log_ref[0, half : half + 1, :] = peak + jnp.log(totals)
    out_ref[...] = jnp.concatenate(parts, axis=0).T.astype(low_type)


def attend(length, q, k, v):
    tokens, width = q.shape
    pairs = width // LANES
    own = lambda p, i, *_: (i, p)
    whole = lambda p, i, *_: (0, p)
    return pl.pallas_call(
        attend_kernel,
        grid_spec=pltpu.PrefetchScalarGridSpec(
            num_scalar_prefetch=1,
            grid=(pairs, tokens // ROWS),
            in_specs=[
                pl.BlockSpec((ROWS, LANES), own),
                pl.BlockSpec((tokens, LANES), whole),
                pl.BlockSpec((tokens, LANES), whole),
            ],
            out_specs=[
                pl.BlockSpec((ROWS, LANES), own),
                pl.BlockSpec((1, 2, ROWS), lambda p, i, *_: (p, 0, i)),
            ],
            scratch_shapes=[
                pltpu.VMEM((2, tokens, LANES), low_type),
                pltpu.VMEM((LANES, tokens), low_type),
            ],
        ),
        out_shape=[
            jax.ShapeDtypeStruct((tokens, width), low_type),
            jax.ShapeDtypeStruct((pairs, 2, tokens), jnp.float32),
        ],
        compiler_params=pltpu.CompilerParams(vmem_limit_bytes=vmem),
        cost_estimate=pl.CostEstimate(
            flops=16 * tokens * tokens * width, bytes_accessed=8 * tokens * width, transcendentals=tokens * tokens * width // HD
        ),
    )(length, q, k, v)


def rotate_back(grads, cosine, sine):
    return grads * cosine + swap_halves(grads * sine)


def attend_back_kernel(first_pair, length_ref, q_ref, k_ref, v_ref, d_ref, log_ref, cosq_ref, sinq_ref, cos_ref, sin_ref, *rest):
    dq_ref, dk_ref, dv_ref, keys, values, turned, dk_total, dv_total = rest[-8:]
    tokens = k_ref.shape[0]
    step = pl.program_id(1)

    @pl.when(step == 0)
    def _():
        bias = key_bias(length_ref, tokens)
        lanes = pair_lanes((tokens, LANES))
        for half in range(2):
            keys[half] = head_keys(k_ref[...], bias, half)
            values[half] = jnp.where(lanes // HD == half, v_ref[...], jnp.zeros_like(v_ref[...]))
        turned[...] = k_ref[...].T
        dk_total[...] = jnp.zeros_like(dk_total)
        dv_total[...] = jnp.zeros_like(dv_total)

    d = d_ref[...]
    lanes = pair_lanes(d.shape)
    parts = []
    dk = dv = None
    for half in range(2):
        scores = transposed_dot(keys[half], head_queries(q_ref[...], half, 1.0))
        probs = jnp.exp(scores - log_ref[0, half : half + 1, :])
        dprobs = transposed_dot(values[half], d)
        inner = jnp.sum(probs * dprobs, axis=0, keepdims=True)
        dscore = (probs * (dprobs - inner)).astype(low_type)
        parts.append(jnp.dot(turned[half * HD : (half + 1) * HD, :], dscore, preferred_element_type=jnp.float32))
        one_k = jnp.dot(dscore, head_queries(q_ref[...], half, 0.0), preferred_element_type=jnp.float32)
        one_v = jnp.dot(
            probs.astype(low_type), jnp.where(lanes // HD == half, d, jnp.zeros_like(d)), preferred_element_type=jnp.float32
        )
        dk = one_k if dk is None else dk + one_k
        dv = one_v if dv is None else dv + one_v
    dk_total[...] += dk
    dv_total[...] += dv
    dq = jnp.concatenate(parts, axis=0).T * (1.0 / math.sqrt(HD))
    dq_ref[...] = rotate_back(dq, cosq_ref[...], sinq_ref[...]).astype(low_type)

    @pl.when(step == pl.num_programs(1) - 1)
    def _():
        dk_ref[...] = rotate_back(dk_total[...], cos_ref[...], sin_ref[...]).astype(low_type)
        dv_ref[...] = dv_total[...].astype(low_type)


def attend_back(length, q, k, v, d, logs, cosine, sine, first_pair, pairs, after=()):
    tokens, width = q.shape
    own = lambda p, i, *_: (i, first_pair + p)
    whole = lambda p, i, *_: (0, first_pair + p)
    low = jax.ShapeDtypeStruct((tokens, pairs * LANES), low_type)
    fixed = pl.BlockSpec((tokens, LANES), lambda p, i, *_: (0, 0))
    row = pl.BlockSpec((ROWS, LANES), lambda p, i, *_: (i, 0))
    return pl.pallas_call(
        functools.partial(attend_back_kernel, first_pair),
        grid_spec=pltpu.PrefetchScalarGridSpec(
            num_scalar_prefetch=1,
            grid=(pairs, tokens // ROWS),
            in_specs=[
                pl.BlockSpec((ROWS, LANES), own),
                pl.BlockSpec((tokens, LANES), whole),
                pl.BlockSpec((tokens, LANES), whole),
                pl.BlockSpec((ROWS, LANES), own),
                pl.BlockSpec((1, 2, ROWS), lambda p, i, *_: (first_pair + p, 0, i)),
                row,
                row,
                fixed,
                fixed,
            ]
            + [pl.BlockSpec(memory_space=pl.ANY)] * len(after),
            out_specs=[
                pl.BlockSpec((ROWS, LANES), lambda p, i, *_: (i, p)),
                pl.BlockSpec((tokens, LANES), lambda p, i, *_: (0, p)),
                pl.BlockSpec((tokens, LANES), lambda p, i, *_: (0, p)),
            ],
            scratch_shapes=[
                pltpu.VMEM((2, tokens, LANES), low_type),
                pltpu.VMEM((2, tokens, LANES), low_type),
                pltpu.VMEM((LANES, tokens), low_type),
                pltpu.VMEM((tokens, LANES), jnp.float32),
                pltpu.VMEM((tokens, LANES), jnp.float32),
            ],
        ),
        out_shape=[low, low, low],
        compiler_params=pltpu.CompilerParams(vmem_limit_bytes=vmem),
        cost_estimate=pl.CostEstimate(
            flops=40 * tokens * tokens * pairs * LANES,
            bytes_accessed=16 * tokens * pairs * LANES,
            transcendentals=tokens * tokens * pairs * 2,
        ),
    )(length, q, k, v, d, logs, cosine, sine, cosine, sine, *after)


def blank(shape, dtype):
    return pl.pallas_call(
        lambda out_ref: None,
        out_shape=jax.ShapeDtypeStruct(shape, dtype),
        out_specs=pl.BlockSpec(memory_space=pl.ANY),
    )()


def lookup_kernel(places_ref, table_ref, out_ref, rows):
    base = pl.program_id(0) * CHUNK
    rows[...] = jnp.zeros_like(rows)

    def one(i, carry):
        place = places_ref[base + i]

        @pl.when(place >= 0)
        def _():
            rows[pl.ds(i, 1), :] = table_ref[pl.ds(place, 1), :]

        return carry

    lax.fori_loop(0, CHUNK, one, 0, unroll=8)
    out_ref[...] = rows[...].astype(low_type)


def lookup(places, table):
    count = places.shape[0]
    width = table.shape[1]
    return pl.pallas_call(
        lookup_kernel,
        grid_spec=pltpu.PrefetchScalarGridSpec(
            num_scalar_prefetch=1,
            grid=(count // CHUNK,),
            in_specs=[pl.BlockSpec(table.shape, lambda i, *_: (0, 0), pipeline_mode=pl.Buffered(1))],
            out_specs=pl.BlockSpec((CHUNK, width), lambda i, *_: (i, 0)),
            scratch_shapes=[pltpu.VMEM((CHUNK, width), jnp.float32)],
        ),
        out_shape=jax.ShapeDtypeStruct((count, width), low_type),
        compiler_params=pltpu.CompilerParams(vmem_limit_bytes=vmem),
        cost_estimate=pl.CostEstimate(flops=0, bytes_accessed=table.size * 8, transcendentals=0),
    )(places, table)


def table_grad_kernel(core_ref, starts_ref, places_ref, order_ref, dlogits_ref, chosen_ref, embed_ref, out_ref, rows, total):
    step = pl.program_id(0)
    count = embed_ref.shape[0]
    block = total.shape[0]

    @pl.when(step == 0)
    def _():
        for start in range(0, count, CHUNK):
            rows[start : start + CHUNK, :] = embed_ref[start : start + CHUNK, :].astype(jnp.float32)

    total[...] = jnp.dot(dlogits_ref[...], chosen_ref[...], preferred_element_type=jnp.float32)
    chunk = 2 * step + core_ref[0]
    base = chunk * block

    def one(i, carry):
        place = places_ref[i] - base
        total[pl.ds(place, 1), :] += rows[pl.ds(order_ref[i], 1), :]
        return carry

    lax.fori_loop(starts_ref[chunk], starts_ref[chunk + 1], one, 0)
    out_ref[0] = total[...].astype(out_ref.dtype)


def table_grad_half(core, starts, places, order, dlogits, chosen, embed, block, dtype):
    count, width = embed.shape
    picked = chosen.shape[0]
    chunks = dlogits.shape[0] // block // 2
    fixed = lambda i, *_: (0, 0)
    return pl.pallas_call(
        table_grad_kernel,
        grid_spec=pltpu.PrefetchScalarGridSpec(
            num_scalar_prefetch=4,
            grid=(chunks,),
            in_specs=[
                pl.BlockSpec((block, picked), lambda i, core, *_: (2 * i + core[0], 0)),
                pl.BlockSpec((picked, width), fixed),
                pl.BlockSpec((count, width), fixed, pipeline_mode=pl.Buffered(1)),
            ],
            out_specs=pl.BlockSpec((1, block, width), lambda i, *_: (i, 0, 0)),
            scratch_shapes=[pltpu.VMEM((count, width), jnp.float32), pltpu.VMEM((block, width), jnp.float32)],
        ),
        out_shape=jax.ShapeDtypeStruct((chunks, block, width), dtype),
        compiler_params=pltpu.CompilerParams(vmem_limit_bytes=vmem),
        cost_estimate=pl.CostEstimate(
            flops=2 * chunks * block * picked * width, bytes_accessed=8 * chunks * block * width, transcendentals=0
        ),
    )(core, starts, places, order, dlogits, chosen, embed)


TILE = 240

def update_kernel(slot_ref, scalars_ref, one_ref, two_ref, table_ref, rows_ref, cols_ref, *rest):
    grad_ref, new_ref, rows_new_ref = rest[-3:]
    gradient = jnp.concatenate([one_ref[...], two_ref[...]], axis=1).astype(jnp.float32)
    factor, row_mean = scalars_ref[0], scalars_ref[1]
    decay = 1.0 - float(STEP) ** (-0.8)
    old = jnp.broadcast_to(rows_ref[0], (LANES, TILE)).T[:, 0:1]
    means = jnp.mean(gradient * gradient, axis=1, keepdims=True)
    rows_new = decay * old + (1.0 - decay) * (means * factor * factor)
    clipped = gradient * factor
    grad_ref[...] = clipped
    scale = rows_new * cols_ref[...] / row_mean
    new_ref[...] = table_ref[...] - rate_matrix * clipped * lax.rsqrt(scale)
    rows_new_ref[0] = jnp.broadcast_to(rows_new, (TILE, LANES)).T[0:1, :]


def update(slot, scalars, one, two, table, rows, cols, so_far):
    block, half = one.shape
    width = 2 * half
    steps = block // TILE
    place = lambda i, slot: (slot[0] * steps + i, 0)
    place3 = lambda i, slot: (slot[0] * steps + i, 0, 0)
    own = lambda i, slot: (i, 0)
    fixed = lambda i, slot: (0, 0)
    any_space = pl.BlockSpec(memory_space=pl.ANY)
    return pl.pallas_call(
        update_kernel,
        grid_spec=pltpu.PrefetchScalarGridSpec(
            num_scalar_prefetch=1,
            grid=(steps,),
            in_specs=[
                pl.BlockSpec(memory_space=pltpu.SMEM),
                pl.BlockSpec((TILE, half), own),
                pl.BlockSpec((TILE, half), own),
                pl.BlockSpec((TILE, width), place),
                pl.BlockSpec((1, 1, TILE), place3),
                pl.BlockSpec((1, width), fixed),
                any_space,
                any_space,
                any_space,
            ],
            out_specs=[
                pl.BlockSpec((TILE, width), place),
                pl.BlockSpec((TILE, width), place),
                pl.BlockSpec((1, 1, TILE), place3),
            ],
        ),
        out_shape=[jax.ShapeDtypeStruct(part.shape, part.dtype) for part in so_far],
        input_output_aliases={7: 0, 8: 1, 9: 2},
        compiler_params=pltpu.CompilerParams(vmem_limit_bytes=vmem),
        cost_estimate=pl.CostEstimate(flops=10 * block * width, bytes_accessed=14 * block * width, transcendentals=block * width),
    )(slot, scalars, one, two, table, rows, cols, *so_far)


def assemble_kernel(members_ref, slots_ref, own_ref, *rest):
    pieces, out_ref, marks = rest[:-2], rest[-2], rest[-1]
    copies = [pltpu.make_async_copy(own_ref, out_ref.at[members_ref[0]], marks.at[0])]
    for place, piece in enumerate(pieces):
        for offset in range(piece.shape[0]):
            copies.append(
                pltpu.make_async_copy(
                    piece.at[offset],
                    out_ref.at[members_ref[offset + 1], slots_ref[place]],
                    marks.at[len(copies)],
                )
            )
    for copy in copies:
        copy.start()
    for copy in copies:
        copy.wait()


def assemble(members, slots, own, pieces):
    groups, replicas = members.shape[0], slots.shape[0]
    any_space = pl.BlockSpec(memory_space=pl.ANY)
    return pl.pallas_call(
        assemble_kernel,
        grid_spec=pltpu.PrefetchScalarGridSpec(
            num_scalar_prefetch=2,
            grid=(1,),
            in_specs=[any_space] * (1 + len(pieces)),
            out_specs=any_space,
            scratch_shapes=[pltpu.SemaphoreType.DMA((1 + replicas * (groups - 1),))],
        ),
        out_shape=jax.ShapeDtypeStruct((groups,) + own.shape, own.dtype),
        cost_estimate=pl.CostEstimate(flops=0, bytes_accessed=4 * groups * own.size, transcendentals=0),
    )(members, slots, own, *pieces)


def place_kernel(slots_ref, *rest):
    pieces, out_ref, marks = rest[:-2], rest[-2], rest[-1]
    copies = [
        pltpu.make_async_copy(piece, out_ref.at[slots_ref[place]], marks.at[place])
        for place, piece in enumerate(pieces)
    ]
    for copy in copies:
        copy.start()
    for copy in copies:
        copy.wait()


def lay_out(slots, pieces):
    any_space = pl.BlockSpec(memory_space=pl.ANY)
    return pl.pallas_call(
        place_kernel,
        grid_spec=pltpu.PrefetchScalarGridSpec(
            num_scalar_prefetch=1,
            grid=(1,),
            in_specs=[any_space] * len(pieces),
            out_specs=any_space,
            scratch_shapes=[pltpu.SemaphoreType.DMA((len(pieces),))],
        ),
        out_shape=jax.ShapeDtypeStruct((len(pieces),) + pieces[0].shape, pieces[0].dtype),
        cost_estimate=pl.CostEstimate(flops=0, bytes_accessed=4 * len(pieces) * pieces[0].size, transcendentals=0),
    )(slots, *pieces)


def flip(value, bit):
    size = lax.axis_size("rep")
    return lax.ppermute(value, "rep", [(i, i ^ bit) for i in range(size)])


def turn(value, offset):
    size = lax.axis_size("grp")
    return lax.ppermute(value, "grp", [(i, (i + offset) % size) for i in range(size)])


def spread(piece, order):
    have = {0: piece}
    for bit in order:
        have.update({place ^ bit: flip(part, bit) for place, part in have.items()})
    return have


def slots_of():
    return lax.axis_index("rep") ^ jnp.arange(lax.axis_size("rep"), dtype=jnp.int32)


def plane_gather(piece):
    if lax.axis_size("rep") != 8:
        return lax.all_gather(piece, "rep")
    have = spread(piece, [2, 4, 1])
    return lay_out(slots_of(), [have[place] for place in range(8)])


def halve(value, axis, bit):
    mine = (lax.axis_index("rep") // bit) % 2
    kept = lax.dynamic_index_in_dim(value, mine, axis, keepdims=False)
    sent = lax.dynamic_index_in_dim(value, 1 - mine, axis, keepdims=False)
    return kept, sent.astype(low_type)


class Fold:
    def __init__(self, axis):
        self.axis = axis
        self.quick = lax.axis_size("rep") == 8

    def cores(self, chunks):
        axis = self.axis
        if not self.quick:
            self.value = lax.psum_scatter(chunks, "rep", scatter_dimension=axis)
            return []
        shape = chunks.shape
        kept, sent = halve(chunks.reshape(shape[:axis] + (4, 2) + shape[axis + 1 :]), axis + 1, 1)
        return self.from_cores(kept, sent)

    def from_cores(self, kept, sent):
        self.kept, self.got = [kept], [flip(sent, 1)]
        return [sent]

    def planes(self):
        if not self.quick:
            return []
        axis = self.axis
        value = self.kept[0] + self.got[0].astype(jnp.float32)
        shape = value.shape
        value = value.reshape(shape[:axis] + (2, 2) + shape[axis + 1 :])
        middle = shape[-1] // 2
        one = halve(value[..., :middle], axis + 1, 2)
        two = halve(value[..., middle:], axis, 4)
        self.kept = [one[0], two[0]]
        self.got = [flip(one[1], 2), flip(two[1], 4)]
        return [one[1], two[1]]

    def crossed(self):
        if not self.quick:
            return []
        one, two = (kept + got.astype(jnp.float32) for kept, got in zip(self.kept, self.got))
        one, two = halve(one, self.axis, 4), halve(two, self.axis, 2)
        self.kept = [one[0], two[0]]
        self.got = [flip(one[1], 4), flip(two[1], 2)]
        return [one[1], two[1]]

    def halves(self):
        if not self.quick:
            middle = self.value.shape[-1] // 2
            return self.value[..., :middle], self.value[..., middle:]
        return tuple(kept + got.astype(jnp.float32) for kept, got in zip(self.kept, self.got))

    def members(self):
        value = jnp.concatenate(self.halves(), axis=-1)
        member = lax.axis_index("grp")
        size = lax.axis_size("grp")
        self.own = lax.dynamic_index_in_dim(value, member, 0, keepdims=False)
        sent = [
            lax.dynamic_index_in_dim(value, (member + offset) % size, 0, keepdims=False).astype(low_type)
            for offset in range(1, size)
        ]
        self.got = [turn(part, offset + 1) for offset, part in enumerate(sent)]
        return sent

    def total(self):
        return sum((got.astype(jnp.float32) for got in self.got), self.own)


def gradient_chunks(gradient):
    groups = lax.axis_size("grp")
    replicas = lax.axis_size("rep")
    rows, columns = gradient.shape
    return gradient.reshape(groups, replicas, rows // (groups * replicas), columns)


def across_wide(chunks):
    member = lax.axis_index("grp")
    size = lax.axis_size("grp")
    total = lax.dynamic_index_in_dim(chunks, member, 0, keepdims=False)
    for offset in range(1, size):
        sent = lax.dynamic_index_in_dim(chunks, (member + offset) % size, 0, keepdims=False)
        total = total + turn(sent, offset)
    return total


def group_gather(value):
    member = lax.axis_index("grp")
    size = lax.axis_size("grp")
    result = jnp.zeros((size,) + value.shape, value.dtype)
    result = lax.dynamic_update_index_in_dim(result, value, member, 0)
    for offset in range(1, size):
        result = lax.dynamic_update_index_in_dim(
            result, turn(value, offset), (member + size - offset) % size, 0
        )
    return result


def total_sum(value):
    for j in range(lax.axis_size("rep").bit_length() - 1):
        value = value + flip(value, 1 << j)
    return jnp.sum(group_gather(value), axis=0)


def weight_gather(shard):
    member = lax.axis_index("grp")
    groups = lax.axis_size("grp")
    replicas = lax.axis_size("rep")
    rows, columns = shard.shape
    if replicas != 8:
        return lax.all_gather(shard, "grp", tiled=True)
    parts = shard.reshape(replicas, rows // replicas, columns)
    own = lax.dynamic_index_in_dim(parts, lax.axis_index("rep"), 0, keepdims=False)
    fetched = jnp.stack([turn(own, offset) for offset in range(1, groups)])
    have = spread(fetched, [2, 4, 1])
    members = (member + groups - jnp.arange(groups, dtype=jnp.int32)) % groups
    whole = assemble(members, slots_of(), parts, [have[place] for place in range(replicas)])
    return whole.reshape(groups * rows, columns)


def contract(left, right, left_dim, right_dim):
    return lax.dot_general(
        left, right, (((left_dim,), (right_dim,)), ((), ())), preferred_element_type=jnp.float32
    )


def layer_norm(values, gain, shift):
    center = values - jnp.mean(values, axis=-1, keepdims=True)
    spread = jnp.mean(center * center, axis=-1, keepdims=True)
    return center * lax.rsqrt(spread + ln_eps) * gain + shift


def rope_tables(length):
    freqs = rope_base ** (-jnp.arange(HD // 2, dtype=jnp.float32) * 2.0 / HD)
    angles = jnp.arange(length, dtype=jnp.float32)[:, None] * freqs[None, :]
    cosine, sine = jnp.cos(angles), jnp.sin(angles)
    return (
        jnp.concatenate([cosine] * 4, axis=-1),
        jnp.concatenate([-sine, sine, -sine, sine], axis=-1),
    )


def swiglu(joined):
    middle = joined.shape[-1] // 2
    return jax.nn.silu(joined[:, :middle]) * joined[:, middle:]


def merge_stats(first_part, second_part):
    peak = jnp.maximum(first_part[0], second_part[0])
    spread = first_part[1] * jnp.exp(first_part[0] - peak) + second_part[1] * jnp.exp(
        second_part[0] - peak
    )
    return (peak, spread, first_part[2] + second_part[2])


def body(
    ids,
    lengths,
    picks,
    labels,
    loss_mask,
    table,
    w_qkv,
    w_out,
    w_gu,
    w_down,
    norms,
    table_rows,
    table_cols,
    qkv_rows,
    qkv_cols,
    out_rows,
    out_cols,
    gu_rows,
    gu_cols,
    down_rows,
    down_cols,
    norms_moment,
):
    member = lax.axis_index("grp")
    groups = lax.axis_size("grp")
    replica = lax.axis_index("rep")
    replicas = lax.axis_size("rep")
    seqs, length = ids.shape
    width = table.shape[1]
    vocab_rows = table.shape[0]
    own_rows = seqs * picks.shape[1]
    tokens = seqs * length
    block = -(-vocab_rows // (16 * replicas)) * 16
    padded = block * replicas

    packed = jnp.concatenate([ids.reshape(-1), labels.reshape(-1), loss_mask.reshape(-1)])
    group_packed = group_gather(packed)
    group_ids = group_packed[:, :tokens].reshape(-1)
    group_labels = group_packed[:, tokens : tokens + own_rows].reshape(-1)
    group_mask = group_packed[:, tokens + own_rows :].reshape(-1)
    shard_rows = w_qkv.shape[0]
    near = weight_gather(jnp.concatenate([w_qkv, w_out], axis=1).astype(low_type))
    far = weight_gather(
        jnp.concatenate([w_gu.astype(low_type), w_down.astype(low_type).reshape(shard_rows, -1)], axis=1)
    )
    loss_count = jnp.sum(group_mask).astype(jnp.float32)[None]
    for j in range(replicas.bit_length() - 1):
        loss_count = loss_count + flip(loss_count, 1 << j)
    loss_count = loss_count[0]

    local_ids = group_ids - member * vocab_rows
    owned = (local_ids >= 0) & (local_ids < vocab_rows)
    found = lookup(jnp.where(owned, local_ids, -1), table)
    embed = lax.psum_scatter(found, "grp", scatter_dimension=0, tiled=True)
    late_table, _ = lax.optimization_barrier((table, found))
    table_low = jnp.pad(late_table.astype(low_type), ((0, padded - vocab_rows), (0, 0)))
    places, order = lax.sort(
        (jnp.where(owned, local_ids, padded), jnp.arange(local_ids.shape[0], dtype=jnp.int32)), num_keys=1
    )
    bounds = jnp.arange(replicas + 1, dtype=jnp.int32) * block
    starts = jnp.sum((places[None, :] < bounds[:, None]).astype(jnp.int32), axis=1)

    w_out_low = near[:, 3 * width :]
    w_gu_low = far[:, : w_gu.shape[1]]
    w_down_low = far[:, w_gu.shape[1] :].reshape(-1, width)
    cosine, sine = rope_tables(length)
    first, first_low, queries, keys, values = project(embed, norms, cosine, sine, near)
    mixed_low, log_sums = attend(lengths, queries, keys, values)
    first_sum = first + jnp.dot(mixed_low, w_out_low, preferred_element_type=jnp.float32)
    second = layer_norm(first_sum, norms[2], norms[3])
    second_low = second.astype(low_type)
    gate_up = jnp.dot(second_low, w_gu_low, preferred_element_type=jnp.float32)
    hidden_low = swiglu(gate_up).astype(low_type)
    second_sum = second + jnp.dot(hidden_low, w_down_low, preferred_element_type=jnp.float32)
    final = layer_norm(second_sum, norms[4], norms[5])

    flat_picks = (jnp.arange(seqs, dtype=jnp.int32)[:, None] * length + picks).reshape(-1)
    chosen = final[flat_picks].astype(low_type)
    group_chosen = group_gather(chosen).reshape(groups * own_rows, width)
    rows_at = jnp.arange(padded, dtype=jnp.int32)[:, None]
    logits = jnp.where(rows_at < vocab_rows, contract(table_low, group_chosen, 1, 1), neg_large)
    peak = jnp.max(logits, axis=0)
    spread_sum = jnp.sum(jnp.exp(logits - peak[None, :]), axis=0)
    local_labels = group_labels - member * vocab_rows
    inside = (local_labels >= 0) & (local_labels < vocab_rows)
    hits = (rows_at == local_labels[None, :]) & inside[None, :]
    target = jnp.sum(jnp.where(hits, logits, 0.0), axis=0)
    stats = group_gather(jnp.stack([peak, spread_sum, target]))
    so_far = (stats[0, 0], stats[0, 1], stats[0, 2])
    for place in range(1, groups):
        so_far = merge_stats(so_far, (stats[place, 0], stats[place, 1], stats[place, 2]))
    peak_all, spread_all, target_all = so_far
    log_total = peak_all + jnp.log(spread_all)
    counted = group_mask > 0
    terms = jnp.where(counted, log_total - target_all, 0.0)
    own_terms = lax.dynamic_slice_in_dim(terms, member * own_rows, own_rows)
    row_scale = jnp.where(counted, 1.0 / loss_count, 0.0)
    dlogits = (
        (jnp.exp(logits - log_total[None, :]) - hits.astype(jnp.float32)) * row_scale[None, :]
    ).astype(low_type)
    chosen_part = contract(dlogits, table_low, 0, 0)
    chosen_grad = across_wide(chosen_part.reshape(groups, own_rows, width))
    final_grad = jnp.zeros((tokens, width), jnp.float32).at[flat_picks].add(chosen_grad)

    _, pull = jax.vjp(layer_norm, second_sum, norms[4], norms[5])
    sum_grad, gain_three, shift_three = pull(final_grad)
    branch_low = sum_grad.astype(low_type)
    down = Fold(1)
    down.cores(gradient_chunks(contract(hidden_low, branch_low, 0, 0)))
    hidden_grad = contract(branch_low, w_down_low, 1, 1)
    _, pull = jax.vjp(swiglu, gate_up)
    gate_low = pull(hidden_grad)[0].astype(low_type)
    gate = Fold(1)
    gate.cores(gradient_chunks(contract(second_low, gate_low, 0, 0)))
    second_grad = sum_grad + contract(gate_low, w_gu_low, 1, 1)
    _, pull = jax.vjp(layer_norm, first_sum, norms[2], norms[3])
    first_sum_grad, gain_two, shift_two = pull(second_grad)
    attn_low = first_sum_grad.astype(low_type)
    mixed_grad = contract(attn_low, w_out_low, 1, 1).astype(low_type)
    after = down.planes() + gate.planes()
    pairs = width // LANES
    one_part = attend_back(
        lengths, queries, keys, values, mixed_grad, log_sums, cosine, sine, 0, pairs // 2, after
    )
    after = down.crossed() + gate.crossed()
    two_part = attend_back(
        lengths, queries, keys, values, mixed_grad, log_sums, cosine, sine, pairs // 2, pairs // 2, after + list(one_part[:1])
    )
    joined_grad = jnp.concatenate(
        [side for parts in zip(one_part, two_part) for side in parts], axis=1
    )
    after = down.members() + gate.members()
    joined_grad, after = lax.optimization_barrier((joined_grad, after))
    first_grad = first_sum_grad + contract(joined_grad, near[:, : 3 * width], 1, 1)
    _, pull = jax.vjp(layer_norm, embed.astype(jnp.float32), norms[0], norms[1])
    embed_grad, gain_one, shift_one = pull(first_grad)
    norm_grad = jnp.stack([gain_one, shift_one, gain_two, shift_two, gain_three, shift_three])
    group_embed = lax.all_gather(embed_grad.astype(low_type), "grp", axis=0, tiled=True)
    join = Fold(1)
    join.cores(
        gradient_chunks(
            jnp.concatenate(
                [contract(first_low, joined_grad, 0, 0), contract(mixed_low, attn_low, 0, 0)], axis=1
            )
        )
    )
    join.planes()
    join.crossed()
    join.members()
    gu_share, down_share, join_share = gate.total(), down.total(), join.total()
    part_rows = join_share.shape[0]

    core = replica % 2
    half_args = (starts, places, order, dlogits, group_chosen, group_embed, block)
    head = Fold(0)
    if head.quick:
        sent = table_grad_half((1 - core)[None], *half_args, low_type)
        kept = table_grad_half(core[None], *half_args, jnp.float32)
        head.from_cores(kept, sent)
    else:
        sides = [table_grad_half(jnp.full((1,), j, jnp.int32), *half_args, jnp.float32) for j in range(2)]
        head.cores(jnp.stack(sides, axis=1).reshape(replicas, block, width))
    head.planes()
    head.crossed()
    table_one, table_two = head.halves()
    table_share = jnp.concatenate([table_one, table_two], axis=1)

    shares = (
        table_share,
        join_share[:, : 3 * width],
        join_share[:, 3 * width :],
        gu_share,
        down_share,
    )
    old_rows = (table_rows, qkv_rows, out_rows, gu_rows, down_rows)
    old_cols = (table_cols, qkv_cols, out_cols, gu_cols, down_cols)
    masters = (table, w_qkv, w_out, w_gu, w_down)
    col_parts = [jnp.sum(gradient * gradient, axis=0) for gradient in shares]
    row_old = jnp.stack([jnp.sum(rows) for rows in old_rows]) / replicas
    small = [norm_grad.reshape(-1)] + col_parts + [row_old, jnp.sum(own_terms)[None]]
    totals = total_sum(jnp.concatenate(small))
    cuts = []
    start = 0
    for part in small:
        cuts.append(totals[start : start + part.shape[0]])
        start += part.shape[0]
    norm_sum = cuts[0].reshape(norm_grad.shape)
    col_totals = cuts[1:6]
    old_totals = cuts[6]
    loss_sum = cuts[7][0]
    squares = [jnp.sum(part) for part in col_totals]
    clip_norm = jnp.sqrt(sum(squares) + jnp.sum(norm_sum * norm_sum))
    factor = clip_limit / jnp.maximum(clip_norm, clip_limit)
    decay = 1.0 - float(STEP) ** (-0.8)

    far_whole = plane_gather(
        jnp.concatenate(
            [gu_share.astype(low_type), down_share.astype(low_type).reshape(part_rows, -1)], axis=1
        )
    ).reshape(shard_rows, -1)
    near_whole = plane_gather(join_share.astype(low_type)).reshape(shard_rows, -1)
    wholes = [
        None,
        near_whole[:, : 3 * width],
        near_whole[:, 3 * width :],
        far_whole[:, : w_gu.shape[1]],
        far_whole[:, w_gu.shape[1] :].reshape(w_down.shape),
    ]
    table_one, table_two = table_one.astype(low_type), table_two.astype(low_type)

    outputs = []
    for place in range(5):
        rows, columns = masters[place].shape
        full_rows = rows * groups
        new_cols = (
            decay * old_cols[place] + (1.0 - decay) * (col_totals[place] * factor * factor) / full_rows
        )
        row_total = decay * old_totals[place] + (1.0 - decay) * (squares[place] * factor * factor) / columns
        row_mean = row_total / full_rows
        if place == 0 and head.quick:
            ones = spread(table_one, [4, 2, 1])
            twos = spread(table_two, [2, 4, 1])
            tiles = padded // TILE
            row_tiles = jnp.pad(table_rows, (0, padded - vocab_rows), constant_values=1.0).reshape(tiles, 1, TILE)
            scalars = jnp.stack([factor, row_mean])
            so_far = (
                blank(table.shape, jnp.float32),
                blank(table.shape, jnp.float32),
                blank((tiles, 1, TILE), jnp.float32),
            )
            slots = slots_of()
            for part in (0, 4, 2, 6, 1, 5, 3, 7):
                so_far = update(
                    slots[part][None], scalars, ones[part], twos[part], table, row_tiles, new_cols[None, :], so_far
                )
            outputs.extend([so_far[0], so_far[2].reshape(-1)[:vocab_rows], new_cols, so_far[1]])
            continue
        if place == 0:
            whole = plane_gather(jnp.concatenate([table_one, table_two], axis=1))
            gradient = whole.reshape(padded, width)[:vocab_rows].astype(jnp.float32)
        else:
            gradient = wholes[place].astype(jnp.float32)
        row_means = jnp.mean(gradient * gradient, axis=1)
        new_rows = decay * old_rows[place] + (1.0 - decay) * (row_means * factor * factor)
        clipped = gradient * factor
        scale = new_rows[:, None] * new_cols[None, :] / row_mean
        new_master = masters[place] - rate_matrix * clipped * lax.rsqrt(scale)
        outputs.extend([clipped, new_rows, new_cols, new_master])
    norm_clipped = norm_sum * factor
    moment_new = decay * norms_moment + (1.0 - decay) * norm_clipped * norm_clipped
    norms_new = norms - rate_norm * norm_clipped * lax.rsqrt(moment_new)
    return (
        (loss_sum, loss_count, clip_norm) + tuple(outputs) + (norm_clipped, moment_new, norms_new)
    )


def solution(mesh):
    in_specs = (
        P(("grp", "rep"), None),
        P(("grp", "rep")),
        P(("grp", "rep"), None),
        P(("grp", "rep"), None),
        P(("grp", "rep"), None),
        P("grp", None),
        P("grp", None),
        P("grp", None),
        P("grp", None),
        P("grp", None),
        P(),
        P("grp"),
        P(),
        P("grp"),
        P(),
        P("grp"),
        P(),
        P("grp"),
        P(),
        P("grp"),
        P(),
        P(),
    )
    out_specs = (
        P(),
        P(),
        P(),
        P("grp", None),
        P("grp"),
        P(),
        P("grp", None),
        P("grp", None),
        P("grp"),
        P(),
        P("grp", None),
        P("grp", None),
        P("grp"),
        P(),
        P("grp", None),
        P("grp", None),
        P("grp"),
        P(),
        P("grp", None),
        P("grp", None),
        P("grp"),
        P(),
        P("grp", None),
        P(),
        P(),
        P(),
    )
    return jax.shard_map(body, mesh=mesh, in_specs=in_specs, out_specs=out_specs, check_vma=False)
```

```python
import functools
import math

import jax
import jax.numpy as jnp
from jax import lax
from jax.experimental import pallas as pl
from jax.experimental.pallas import tpu as pltpu
from jax.sharding import PartitionSpec as P

HEADS = 12
HD = 64
STEP = 10
LANES = 128
ROWS = 256
CHUNK = 256
TILE = 240


ln_eps = 1e-05
rope_base = 10000.0
clip_limit = 0.01
rate_matrix = 0.03
rate_norm = 0.3
neg_large = -1e30
low_type = jnp.bfloat16
vmem = 56 * 1024 * 1024


def pair_lanes(shape):
    return lax.broadcasted_iota(jnp.int32, shape, len(shape) - 1)


def swap_halves(value):
    upper = (pair_lanes(value.shape) % HD) >= HD // 2
    return jnp.where(
        upper,
        pltpu.roll(value, HD // 2, axis=1),
        pltpu.roll(value, LANES - HD // 2, axis=1),
    )


def normalize(values, gain, shift):
    center = values - jnp.mean(values, axis=-1, keepdims=True)
    spread = jnp.mean(center * center, axis=-1, keepdims=True)
    return center * lax.rsqrt(spread + ln_eps) * gain + shift


def project_kernel(embed_ref, norms_ref, cosine_ref, sine_ref, w_ref, first_ref, low_ref, q_ref, k_ref, v_ref):
    first = normalize(embed_ref[...].astype(jnp.float32), norms_ref[0:1, :], norms_ref[1:2, :])
    first_ref[...] = first
    low = first.astype(low_type)
    low_ref[...] = low
    width = first.shape[1]
    cosine, sine = cosine_ref[...], sine_ref[...]
    for part, out_ref in enumerate((q_ref, k_ref)):
        joined = jnp.dot(low, w_ref[:, part * width : (part + 1) * width], preferred_element_type=jnp.float32)
        for start in range(0, width, LANES):
            piece = joined[:, start : start + LANES]
            out_ref[:, start : start + LANES] = (piece * cosine + swap_halves(piece) * sine).astype(low_type)
    v_ref[...] = jnp.dot(low, w_ref[:, 2 * width :], preferred_element_type=jnp.float32).astype(low_type)


def project(embed, norms, cosine, sine, weights):
    tokens, width = embed.shape
    row = lambda i: (i, 0)
    fixed = lambda i: (0, 0)
    low = jax.ShapeDtypeStruct((tokens, width), low_type)
    return pl.pallas_call(
        project_kernel,
        grid=(tokens // ROWS,),
        in_specs=[
            pl.BlockSpec((ROWS, width), row),
            pl.BlockSpec(norms.shape, fixed),
            pl.BlockSpec((ROWS, LANES), row),
            pl.BlockSpec((ROWS, LANES), row),
            pl.BlockSpec((width, 3 * width), fixed),
        ],
        out_specs=[pl.BlockSpec((ROWS, width), row)] * 5,
        out_shape=[jax.ShapeDtypeStruct((tokens, width), jnp.float32), low, low, low, low],
        compiler_params=pltpu.CompilerParams(vmem_limit_bytes=vmem),
        cost_estimate=pl.CostEstimate(flops=6 * tokens * width * width, bytes_accessed=20 * tokens * width, transcendentals=0),
    )(embed, norms, cosine, sine, weights)


def head_keys(k, bias, half):
    lanes = pair_lanes(k.shape)
    spare = HD - half * HD
    return jnp.where(lanes // HD == half, k, jnp.where(lanes == spare, bias, jnp.zeros_like(k)))


def head_queries(q, half, spare_value):
    lanes = pair_lanes(q.shape)
    spare = HD - half * HD
    scaled = q * jnp.asarray(1.0 / math.sqrt(HD), q.dtype)
    other = jnp.where(lanes == spare, jnp.full_like(q, spare_value), jnp.zeros_like(q))
    return jnp.where(lanes // HD == half, scaled, other)


def transposed_dot(left, right):
    return lax.dot_general(left, right, (((1,), (1,)), ((), ())), preferred_element_type=jnp.float32)


def key_bias(length_ref, tokens):
    place = lax.broadcasted_iota(jnp.int32, (tokens, LANES), 0)
    return jnp.where(place < length_ref[0], 0.0, neg_large).astype(low_type)


def attend_kernel(length_ref, q_ref, k_ref, v_ref, out_ref, log_ref, keys, turned):
    tokens = k_ref.shape[0]

    @pl.when(pl.program_id(1) == 0)
    def _():
        bias = key_bias(length_ref, tokens)
        for half in range(2):
            keys[half] = head_keys(k_ref[...], bias, half)
        turned[...] = v_ref[...].T

    parts = []
    for half in range(2):
        scores = transposed_dot(keys[half], head_queries(q_ref[...], half, 1.0))
        peak = jnp.max(scores, axis=0, keepdims=True)
        weights = jnp.exp(scores - peak)
        totals = jnp.sum(weights, axis=0, keepdims=True)
        probs = (weights * (1.0 / totals)).astype(low_type)
        parts.append(
            jnp.dot(turned[half * HD : (half + 1) * HD, :], probs, preferred_element_type=jnp.float32)
        )
        log_ref[0, half : half + 1, :] = peak + jnp.log(totals)
    out_ref[...] = jnp.concatenate(parts, axis=0).T.astype(low_type)


def attend(length, q, k, v):
    tokens, width = q.shape
    pairs = width // LANES
    own = lambda p, i, *_: (i, p)
    whole = lambda p, i, *_: (0, p)
    return pl.pallas_call(
        attend_kernel,
        grid_spec=pltpu.PrefetchScalarGridSpec(
            num_scalar_prefetch=1,
            grid=(pairs, tokens // ROWS),
            in_specs=[
                pl.BlockSpec((ROWS, LANES), own),
                pl.BlockSpec((tokens, LANES), whole),
                pl.BlockSpec((tokens, LANES), whole),
            ],
            out_specs=[
                pl.BlockSpec((ROWS, LANES), own),
                pl.BlockSpec((1, 2, ROWS), lambda p, i, *_: (p, 0, i)),
            ],
            scratch_shapes=[
                pltpu.VMEM((2, tokens, LANES), low_type),
                pltpu.VMEM((LANES, tokens), low_type),
            ],
        ),
        out_shape=[
            jax.ShapeDtypeStruct((tokens, width), low_type),
            jax.ShapeDtypeStruct((pairs, 2, tokens), jnp.float32),
        ],
        compiler_params=pltpu.CompilerParams(vmem_limit_bytes=vmem),
        cost_estimate=pl.CostEstimate(
            flops=16 * tokens * tokens * width, bytes_accessed=8 * tokens * width, transcendentals=tokens * tokens * width // HD
        ),
    )(length, q, k, v)


def rotate_back(grads, cosine, sine):
    return grads * cosine + swap_halves(grads * sine)


def attend_back_kernel(first_pair, length_ref, q_ref, k_ref, v_ref, d_ref, log_ref, cosq_ref, sinq_ref, cos_ref, sin_ref, *rest):
    dq_ref, dk_ref, dv_ref, keys, values, turned, dk_total, dv_total = rest[-8:]
    tokens = k_ref.shape[0]
    step = pl.program_id(1)

    @pl.when(step == 0)
    def _():
        bias = key_bias(length_ref, tokens)
        lanes = pair_lanes((tokens, LANES))
        for half in range(2):
            keys[half] = head_keys(k_ref[...], bias, half)
            values[half] = jnp.where(lanes // HD == half, v_ref[...], jnp.zeros_like(v_ref[...]))
        turned[...] = k_ref[...].T
        dk_total[...] = jnp.zeros_like(dk_total)
        dv_total[...] = jnp.zeros_like(dv_total)

    d = d_ref[...]
    lanes = pair_lanes(d.shape)
    parts = []
    dk = dv = None
    for half in range(2):
        scores = transposed_dot(keys[half], head_queries(q_ref[...], half, 1.0))
        probs = jnp.exp(scores - log_ref[0, half : half + 1, :])
        dprobs = transposed_dot(values[half], d)
        inner = jnp.sum(probs * dprobs, axis=0, keepdims=True)
        dscore = (probs * (dprobs - inner)).astype(low_type)
        parts.append(jnp.dot(turned[half * HD : (half + 1) * HD, :], dscore, preferred_element_type=jnp.float32))
        one_k = jnp.dot(dscore, head_queries(q_ref[...], half, 0.0), preferred_element_type=jnp.float32)
        one_v = jnp.dot(
            probs.astype(low_type), jnp.where(lanes // HD == half, d, jnp.zeros_like(d)), preferred_element_type=jnp.float32
        )
        dk = one_k if dk is None else dk + one_k
        dv = one_v if dv is None else dv + one_v
    dk_total[...] += dk
    dv_total[...] += dv
    dq = jnp.concatenate(parts, axis=0).T * (1.0 / math.sqrt(HD))
    dq_ref[...] = rotate_back(dq, cosq_ref[...], sinq_ref[...]).astype(low_type)

    @pl.when(step == pl.num_programs(1) - 1)
    def _():
        dk_ref[...] = rotate_back(dk_total[...], cos_ref[...], sin_ref[...]).astype(low_type)
        dv_ref[...] = dv_total[...].astype(low_type)


def attend_back(length, q, k, v, d, logs, cosine, sine, first_pair, pairs, after=()):
    tokens, width = q.shape
    own = lambda p, i, *_: (i, first_pair + p)
    whole = lambda p, i, *_: (0, first_pair + p)
    low = jax.ShapeDtypeStruct((tokens, pairs * LANES), low_type)
    fixed = pl.BlockSpec((tokens, LANES), lambda p, i, *_: (0, 0))
    row = pl.BlockSpec((ROWS, LANES), lambda p, i, *_: (i, 0))
    return pl.pallas_call(
        functools.partial(attend_back_kernel, first_pair),
        grid_spec=pltpu.PrefetchScalarGridSpec(
            num_scalar_prefetch=1,
            grid=(pairs, tokens // ROWS),
            in_specs=[
                pl.BlockSpec((ROWS, LANES), own),
                pl.BlockSpec((tokens, LANES), whole),
                pl.BlockSpec((tokens, LANES), whole),
                pl.BlockSpec((ROWS, LANES), own),
                pl.BlockSpec((1, 2, ROWS), lambda p, i, *_: (first_pair + p, 0, i)),
                row,
                row,
                fixed,
                fixed,
            ]
            + [pl.BlockSpec(memory_space=pl.ANY)] * len(after),
            out_specs=[
                pl.BlockSpec((ROWS, LANES), lambda p, i, *_: (i, p)),
                pl.BlockSpec((tokens, LANES), lambda p, i, *_: (0, p)),
                pl.BlockSpec((tokens, LANES), lambda p, i, *_: (0, p)),
            ],
            scratch_shapes=[
                pltpu.VMEM((2, tokens, LANES), low_type),
                pltpu.VMEM((2, tokens, LANES), low_type),
                pltpu.VMEM((LANES, tokens), low_type),
                pltpu.VMEM((tokens, LANES), jnp.float32),
                pltpu.VMEM((tokens, LANES), jnp.float32),
            ],
        ),
        out_shape=[low, low, low],
        compiler_params=pltpu.CompilerParams(vmem_limit_bytes=vmem),
        cost_estimate=pl.CostEstimate(
            flops=40 * tokens * tokens * pairs * LANES,
            bytes_accessed=16 * tokens * pairs * LANES,
            transcendentals=tokens * tokens * pairs * 2,
        ),
    )(length, q, k, v, d, logs, cosine, sine, cosine, sine, *after)


def blank(shape, dtype):
    return pl.pallas_call(
        lambda out_ref: None,
        out_shape=jax.ShapeDtypeStruct(shape, dtype),
        out_specs=pl.BlockSpec(memory_space=pl.ANY),
    )()


def lookup_kernel(starts_ref, places_ref, order_ref, table_ref, out_ref, rows):
    count = out_ref.shape[0]
    owned = starts_ref[starts_ref.shape[0] - 1]
    for start in range(0, count, CHUNK):
        rows[start : start + CHUNK, :] = jnp.zeros((CHUNK, rows.shape[1]), jnp.float32)

    def eight(step, carry):
        for j in range(8):
            i = step * 8 + j
            valid = i < owned
            source = jnp.where(valid, places_ref[i], 0)
            target = jnp.where(valid, order_ref[i], count)
            rows[pl.ds(target, 1), :] = table_ref[pl.ds(source, 1), :]
        return carry

    lax.fori_loop(0, (owned + 7) // 8, eight, 0)
    for start in range(0, count, CHUNK):
        out_ref[start : start + CHUNK, :] = rows[start : start + CHUNK, :].astype(low_type)


def lookup(starts, places, order, table):
    count = places.shape[0]
    width = table.shape[1]
    return pl.pallas_call(
        lookup_kernel,
        grid_spec=pltpu.PrefetchScalarGridSpec(
            num_scalar_prefetch=3,
            grid=(1,),
            in_specs=[pl.BlockSpec(table.shape, lambda i, *_: (0, 0), pipeline_mode=pl.Buffered(1))],
            out_specs=pl.BlockSpec((count, width), lambda i, *_: (0, 0), pipeline_mode=pl.Buffered(1)),
            scratch_shapes=[pltpu.VMEM((count + 8, width), jnp.float32)],
        ),
        out_shape=jax.ShapeDtypeStruct((count, width), low_type),
        compiler_params=pltpu.CompilerParams(vmem_limit_bytes=vmem),
        cost_estimate=pl.CostEstimate(flops=0, bytes_accessed=table.size * 12, transcendentals=0),
    )(starts, places, order, table)


def table_grad_kernel(core_ref, starts_ref, places_ref, order_ref, dlogits_ref, chosen_ref, embed_ref, out_ref, rows, total):
    step = pl.program_id(0)
    count = embed_ref.shape[0]
    block = total.shape[0]

    @pl.when(step == 0)
    def _():
        for start in range(0, count, CHUNK):
            rows[start : start + CHUNK, :] = embed_ref[start : start + CHUNK, :].astype(jnp.float32)

    total[...] = jnp.dot(dlogits_ref[...], chosen_ref[...], preferred_element_type=jnp.float32)
    chunk = 2 * step + core_ref[0]
    base = chunk * block

    def one(i, carry):
        place = places_ref[i] - base
        total[pl.ds(place, 1), :] += rows[pl.ds(order_ref[i], 1), :]
        return carry

    lax.fori_loop(starts_ref[chunk], starts_ref[chunk + 1], one, 0)
    out_ref[0] = total[...].astype(out_ref.dtype)


def table_grad_half(core, starts, places, order, dlogits, chosen, embed, block, dtype):
    count, width = embed.shape
    picked = chosen.shape[0]
    chunks = dlogits.shape[0] // block // 2
    fixed = lambda i, *_: (0, 0)
    return pl.pallas_call(
        table_grad_kernel,
        grid_spec=pltpu.PrefetchScalarGridSpec(
            num_scalar_prefetch=4,
            grid=(chunks,),
            in_specs=[
                pl.BlockSpec((block, picked), lambda i, core, *_: (2 * i + core[0], 0)),
                pl.BlockSpec((picked, width), fixed),
                pl.BlockSpec((count, width), fixed, pipeline_mode=pl.Buffered(1)),
            ],
            out_specs=pl.BlockSpec((1, block, width), lambda i, *_: (i, 0, 0)),
            scratch_shapes=[pltpu.VMEM((count, width), jnp.float32), pltpu.VMEM((block, width), jnp.float32)],
        ),
        out_shape=jax.ShapeDtypeStruct((chunks, block, width), dtype),
        compiler_params=pltpu.CompilerParams(vmem_limit_bytes=vmem),
        cost_estimate=pl.CostEstimate(
            flops=2 * chunks * block * picked * width, bytes_accessed=8 * chunks * block * width, transcendentals=0
        ),
    )(core, starts, places, order, dlogits, chosen, embed)


TILE = 240

def update_kernel(parts, slots_ref, scalars_ref, *rest):
    pieces = rest[: 4 * parts]
    table_ref, rows_ref, cols_ref = rest[4 * parts : 4 * parts + 3]
    grad_ref, new_ref, rows_new_ref = rest[-3:]
    factor, rate = scalars_ref[0], scalars_ref[1]
    decay = 1.0 - float(STEP) ** (-0.8)
    old = jnp.broadcast_to(rows_ref[0], (LANES, TILE)).T[:, 0:1]
    for part in range(4):

        @pl.when(pl.program_id(0) == part)
        def _(part=part):
            own = pieces[part * parts : (part + 1) * parts]
            gradient = jnp.concatenate([piece[...] for piece in own], axis=1).astype(jnp.float32)
            means = jnp.mean(gradient * gradient, axis=1, keepdims=True)
            rows_new = decay * old + (1.0 - decay) * (means * factor * factor)
            grad_ref[...] = gradient * factor
            new_ref[...] = table_ref[...] - rate * gradient * lax.rsqrt(rows_new * cols_ref[...])
            rows_new_ref[0] = jnp.broadcast_to(rows_new, (TILE, LANES)).T[0:1, :]


def update(slots, scalars, pieces, table, rows, cols, so_far):
    parts = len(pieces[0])
    block = pieces[0][0].shape[0]
    width = table.shape[1]
    steps = block // TILE
    place = lambda p, i, slots: (slots[p] * steps + i, 0)
    place3 = lambda p, i, slots: (slots[p] * steps + i, 0, 0)

    def own(part):
        return lambda p, i, slots: (jnp.where(p < part, 0, jnp.where(p > part, steps - 1, i)), 0)

    fixed = lambda p, i, slots: (0, 0)
    any_space = pl.BlockSpec(memory_space=pl.ANY)
    given = 5 + 4 * parts
    return pl.pallas_call(
        functools.partial(update_kernel, parts),
        grid_spec=pltpu.PrefetchScalarGridSpec(
            num_scalar_prefetch=1,
            grid=(4, steps),
            in_specs=[pl.BlockSpec(memory_space=pltpu.SMEM)]
            + [pl.BlockSpec((TILE, piece.shape[1]), own(part)) for part in range(4) for piece in pieces[part]]
            + [
                pl.BlockSpec((TILE, width), place),
                pl.BlockSpec((1, 1, TILE), place3),
                pl.BlockSpec((1, width), fixed),
                any_space,
                any_space,
                any_space,
            ],
            out_specs=[
                pl.BlockSpec((TILE, width), place),
                pl.BlockSpec((TILE, width), place),
                pl.BlockSpec((1, 1, TILE), place3),
            ],
        ),
        out_shape=[jax.ShapeDtypeStruct(part.shape, part.dtype) for part in so_far],
        input_output_aliases={given: 0, given + 1: 1, given + 2: 2},
        compiler_params=pltpu.CompilerParams(vmem_limit_bytes=vmem),
        cost_estimate=pl.CostEstimate(
            flops=40 * block * width, bytes_accessed=56 * block * width, transcendentals=4 * block * width
        ),
    )(slots, scalars, *[piece for four in pieces for piece in four], table, rows, cols, *so_far)


def stack_kernel(slots_ref, *refs):
    pieces, out_ref = refs[:-1], refs[-1]
    for place, piece in enumerate(pieces):

        @pl.when(pl.program_id(0) == place)
        def _(piece=piece):
            out_ref[0] = piece[...]


def lay_out(slots, pieces):
    shape = pieces[0].shape
    return pl.pallas_call(
        stack_kernel,
        grid_spec=pltpu.PrefetchScalarGridSpec(
            num_scalar_prefetch=1,
            grid=(len(pieces),),
            in_specs=[pl.BlockSpec(shape, lambda i, slots: (0, 0), pipeline_mode=pl.Buffered(1))] * len(pieces),
            out_specs=pl.BlockSpec((1,) + shape, lambda i, slots: (slots[i], 0, 0)),
        ),
        out_shape=jax.ShapeDtypeStruct((len(pieces),) + shape, pieces[0].dtype),
        compiler_params=pltpu.CompilerParams(vmem_limit_bytes=vmem),
        cost_estimate=pl.CostEstimate(flops=0, bytes_accessed=4 * len(pieces) * pieces[0].size, transcendentals=0),
    )(slots, *pieces)


def columns_kernel(main, members_ref, slots_ref, *refs):
    replicas = slots_ref.shape[0]
    pieces, outs = refs[:replicas], refs[replicas + (len(refs) - replicas - (1 if main is None else 2)) :]
    groups, rows = pieces[0].shape[0], pieces[0].shape[1]
    for place, piece in enumerate(pieces):

        @pl.when(pl.program_id(0) == place)
        def _(piece=piece):
            for offset in range(groups):
                member = members_ref[offset]
                at = pl.ds(pl.multiple_of(member * rows, rows), rows)
                if main is None:
                    outs[0][at, :] = piece[offset]
                else:
                    outs[0][at, :] = piece[offset, :, :main]
                    half = piece.shape[2] - main
                    outs[1][member, 0, :, :half] = piece[offset, : rows // 2, main:]
                    outs[1][member, 0, :, half:] = piece[offset, rows // 2 :, main:]


def lay_columns(members, slots, pieces, main=None, after=()):
    groups, rows, columns = pieces[0].shape
    replicas = len(pieces)
    wide = columns if main is None else main
    out_shape = [jax.ShapeDtypeStruct((groups * rows, replicas * wide), low_type)]
    out_specs = [pl.BlockSpec((groups * rows, wide), lambda i, members, slots: (0, slots[i]))]
    if main is not None:
        out_shape.append(jax.ShapeDtypeStruct((groups, replicas, rows // 2, 2 * (columns - main)), low_type))
        out_specs.append(
            pl.BlockSpec((groups, 1, rows // 2, 2 * (columns - main)), lambda i, members, slots: (0, slots[i], 0, 0))
        )
    return pl.pallas_call(
        functools.partial(columns_kernel, main),
        grid_spec=pltpu.PrefetchScalarGridSpec(
            num_scalar_prefetch=2,
            grid=(replicas,),
            in_specs=[pl.BlockSpec(pieces[0].shape, lambda i, *_: (0, 0, 0), pipeline_mode=pl.Buffered(1))] * replicas
            + [pl.BlockSpec(memory_space=pl.ANY)] * len(after),
            out_specs=out_specs,
        ),
        out_shape=out_shape,
        compiler_params=pltpu.CompilerParams(vmem_limit_bytes=vmem),
        cost_estimate=pl.CostEstimate(flops=0, bytes_accessed=4 * replicas * pieces[0].size, transcendentals=0),
    )(members, slots, *pieces, *after)


def flip(value, bit):
    size = lax.axis_size("rep")
    return lax.ppermute(value, "rep", [(i, i ^ bit) for i in range(size)])


def turn(value, offset):
    size = lax.axis_size("grp")
    return lax.ppermute(value, "grp", [(i, (i + offset) % size) for i in range(size)])


def spread(piece, order):
    have = {0: piece}
    for bit in order:
        have.update({place ^ bit: flip(part, bit) for place, part in have.items()})
    return have


def slots_of():
    return lax.axis_index("rep") ^ jnp.arange(lax.axis_size("rep"), dtype=jnp.int32)


def plane_gather(piece):
    if lax.axis_size("rep") != 8:
        return lax.all_gather(piece, "rep")
    have = spread(piece, [2, 4, 1])
    return lay_out(slots_of(), [have[place] for place in range(8)])


def halve(value, axis, bit):
    mine = (lax.axis_index("rep") // bit) % 2
    kept = lax.dynamic_index_in_dim(value, mine, axis, keepdims=False)
    sent = lax.dynamic_index_in_dim(value, 1 - mine, axis, keepdims=False)
    return kept, sent.astype(low_type)


class Fold:
    def __init__(self, axis, order):
        self.axis = axis
        self.order = order
        self.quick = lax.axis_size("rep") == 8

    def cores(self, chunks):
        axis = self.axis
        if not self.quick:
            self.value = lax.psum_scatter(chunks, "rep", scatter_dimension=axis)
            return []
        shape = chunks.shape
        kept, sent = halve(chunks.reshape(shape[:axis] + (4, 2) + shape[axis + 1 :]), axis + 1, 1)
        return self.from_cores(kept, sent)

    def from_cores(self, kept, sent):
        self.kept, self.got = kept, flip(sent, 1)
        return [sent]

    def sum(self):
        return self.kept + self.got.astype(jnp.float32) if self.quick else self.value

    def plane(self, first):
        if not self.quick:
            return []
        value = self.sum()
        axis = self.axis
        bit = self.order[0 if first else 1]
        if first:
            shape = value.shape
            value = value.reshape(shape[:axis] + (2, 2) + shape[axis + 1 :])
            axis = axis + (1 if bit == 2 else 0)
        self.kept, sent = halve(value, axis, bit)
        self.got = flip(sent, bit)
        return [sent]

    def members(self):
        value = self.sum()
        member = lax.axis_index("grp")
        size = lax.axis_size("grp")
        self.own = lax.dynamic_index_in_dim(value, member, 0, keepdims=False)
        sent = [
            lax.dynamic_index_in_dim(value, (member + offset) % size, 0, keepdims=False).astype(low_type)
            for offset in range(1, size)
        ]
        self.came = [turn(part, offset + 1) for offset, part in enumerate(sent)]
        return sent

    def total(self):
        return sum((came.astype(jnp.float32) for came in self.came), self.own)


def gradient_chunks(gradient):
    groups = lax.axis_size("grp")
    replicas = lax.axis_size("rep")
    rows, columns = gradient.shape
    return gradient.reshape(groups, replicas, rows // (groups * replicas), columns)


def across_wide(chunks):
    member = lax.axis_index("grp")
    size = lax.axis_size("grp")
    total = lax.dynamic_index_in_dim(chunks, member, 0, keepdims=False)
    for offset in range(1, size):
        sent = lax.dynamic_index_in_dim(chunks, (member + offset) % size, 0, keepdims=False)
        total = total + turn(sent, offset)
    return total


def group_gather(value):
    member = lax.axis_index("grp")
    size = lax.axis_size("grp")
    result = jnp.zeros((size,) + value.shape, value.dtype)
    result = lax.dynamic_update_index_in_dim(result, value, member, 0)
    for offset in range(1, size):
        result = lax.dynamic_update_index_in_dim(
            result, turn(value, offset), (member + size - offset) % size, 0
        )
    return result


def total_sum(value):
    for j in range(lax.axis_size("rep").bit_length() - 1):
        value = value + flip(value, 1 << j)
    size = lax.axis_size("grp")
    for j in range(size.bit_length() - 1):
        value = value + lax.ppermute(value, "grp", [(i, i ^ (1 << j)) for i in range(size)])
    return value


def fetch(own):
    groups = lax.axis_size("grp")
    return jnp.stack([own] + [turn(own, offset) for offset in range(1, groups)])


def cut(value, axis):
    replicas = lax.axis_size("rep")
    size = value.shape[axis] // replicas
    return lax.dynamic_slice_in_dim(value, lax.axis_index("rep") * size, size, axis)


def members_of():
    groups = lax.axis_size("grp")
    return (lax.axis_index("grp") + groups - jnp.arange(groups, dtype=jnp.int32)) % groups


def contract(left, right, left_dim, right_dim):
    return lax.dot_general(
        left, right, (((left_dim,), (right_dim,)), ((), ())), preferred_element_type=jnp.float32
    )


def layer_norm(values, gain, shift):
    center = values - jnp.mean(values, axis=-1, keepdims=True)
    spread = jnp.mean(center * center, axis=-1, keepdims=True)
    return center * lax.rsqrt(spread + ln_eps) * gain + shift


def rope_tables(length):
    freqs = rope_base ** (-jnp.arange(HD // 2, dtype=jnp.float32) * 2.0 / HD)
    angles = jnp.arange(length, dtype=jnp.float32)[:, None] * freqs[None, :]
    cosine, sine = jnp.cos(angles), jnp.sin(angles)
    return (
        jnp.concatenate([cosine] * 4, axis=-1),
        jnp.concatenate([-sine, sine, -sine, sine], axis=-1),
    )


def swiglu(joined):
    middle = joined.shape[-1] // 2
    return jax.nn.silu(joined[:, :middle]) * joined[:, middle:]


def merge_stats(first_part, second_part):
    peak = jnp.maximum(first_part[0], second_part[0])
    spread = first_part[1] * jnp.exp(first_part[0] - peak) + second_part[1] * jnp.exp(
        second_part[0] - peak
    )
    return (peak, spread, first_part[2] + second_part[2])


def body(
    ids,
    lengths,
    picks,
    labels,
    loss_mask,
    table,
    w_qkv,
    w_out,
    w_gu,
    w_down,
    norms,
    table_rows,
    table_cols,
    qkv_rows,
    qkv_cols,
    out_rows,
    out_cols,
    gu_rows,
    gu_cols,
    down_rows,
    down_cols,
    norms_moment,
):
    member = lax.axis_index("grp")
    groups = lax.axis_size("grp")
    replica = lax.axis_index("rep")
    replicas = lax.axis_size("rep")
    seqs, length = ids.shape
    width = table.shape[1]
    vocab_rows = table.shape[0]
    own_rows = seqs * picks.shape[1]
    tokens = seqs * length
    block = -(-vocab_rows // (16 * replicas)) * 16
    padded = block * replicas

    packed = jnp.concatenate([ids.reshape(-1), labels.reshape(-1), loss_mask.reshape(-1)])
    group_packed = group_gather(packed)
    group_ids = group_packed[:, :tokens].reshape(-1)
    group_labels = group_packed[:, tokens : tokens + own_rows].reshape(-1)
    group_mask = group_packed[:, tokens + own_rows :].reshape(-1)
    shard_rows = w_qkv.shape[0]
    quick = replicas == 8
    near_shard = jnp.concatenate([w_qkv, w_out], axis=1)
    if quick:
        near_part = fetch(cut(near_shard, 1).astype(low_type))
        down_part = cut(w_down, 0)
        down_part = jnp.concatenate([down_part[:, : width // 2], down_part[:, width // 2 :]], axis=0)
        far_part = fetch(jnp.concatenate([cut(w_gu, 1), down_part], axis=1).astype(low_type))
    loss_count = jnp.sum(group_mask).astype(jnp.float32)[None]
    for j in range(replicas.bit_length() - 1):
        loss_count = loss_count + flip(loss_count, 1 << j)
    loss_count = loss_count[0]

    local_ids = group_ids - member * vocab_rows
    owned = (local_ids >= 0) & (local_ids < vocab_rows)
    places, order = lax.sort(
        (jnp.where(owned, local_ids, padded), jnp.arange(local_ids.shape[0], dtype=jnp.int32)), num_keys=1
    )
    bounds = jnp.arange(replicas + 1, dtype=jnp.int32) * block
    starts = jnp.sum((places[None, :] < bounds[:, None]).astype(jnp.int32), axis=1)
    found = lookup(starts, places, order, table)
    if quick:
        found, near_part, far_part = lax.optimization_barrier((found, near_part, far_part))
    embed = lax.psum_scatter(found, "grp", scatter_dimension=0, tiled=True)
    late_table, _ = lax.optimization_barrier((table, found))
    table_low = jnp.pad(late_table.astype(low_type), ((0, padded - vocab_rows), (0, 0)))

    if quick:
        near_have = spread(near_part, [2, 4, 1])
        far_have = spread(far_part, [4, 2, 1])
        (near,) = lay_columns(members_of(), slots_of(), [near_have[place] for place in range(replicas)])
    else:
        near = lax.all_gather(near_shard.astype(low_type), "grp", tiled=True)
    cosine, sine = rope_tables(length)
    first, first_low, queries, keys, values = project(embed, norms, cosine, sine, near)
    mixed_low, log_sums = attend(lengths, queries, keys, values)
    if quick:
        w_gu_low, w_down_low = lay_columns(
            members_of(),
            slots_of(),
            [far_have[place] for place in range(replicas)],
            w_gu.shape[1] // replicas,
            (mixed_low,),
        )
        w_down_low = w_down_low.reshape(-1, width)
    else:
        w_gu_low = lax.all_gather(w_gu.astype(low_type), "grp", tiled=True)
        w_down_low = lax.all_gather(w_down.astype(low_type), "grp", tiled=True)
    w_out_low = near[:, 3 * width :]
    first_sum = first + jnp.dot(mixed_low, w_out_low, preferred_element_type=jnp.float32)
    second = layer_norm(first_sum, norms[2], norms[3])
    second_low = second.astype(low_type)
    gate_up = jnp.dot(second_low, w_gu_low, preferred_element_type=jnp.float32)
    hidden_low = swiglu(gate_up).astype(low_type)
    second_sum = second + jnp.dot(hidden_low, w_down_low, preferred_element_type=jnp.float32)
    final = layer_norm(second_sum, norms[4], norms[5])

    flat_picks = (jnp.arange(seqs, dtype=jnp.int32)[:, None] * length + picks).reshape(-1)
    chosen = final[flat_picks].astype(low_type)
    group_chosen = group_gather(chosen).reshape(groups * own_rows, width)
    rows_at = jnp.arange(padded, dtype=jnp.int32)[:, None]
    logits = jnp.where(rows_at < vocab_rows, contract(table_low, group_chosen, 1, 1), neg_large)
    peak = jnp.max(logits, axis=0)
    spread_sum = jnp.sum(jnp.exp(logits - peak[None, :]), axis=0)
    local_labels = group_labels - member * vocab_rows
    inside = (local_labels >= 0) & (local_labels < vocab_rows)
    hits = (rows_at == local_labels[None, :]) & inside[None, :]
    target = jnp.sum(jnp.where(hits, logits, 0.0), axis=0)
    stats = group_gather(jnp.stack([peak, spread_sum, target]))
    so_far = (stats[0, 0], stats[0, 1], stats[0, 2])
    for place in range(1, groups):
        so_far = merge_stats(so_far, (stats[place, 0], stats[place, 1], stats[place, 2]))
    peak_all, spread_all, target_all = so_far
    log_total = peak_all + jnp.log(spread_all)
    counted = group_mask > 0
    terms = jnp.where(counted, log_total - target_all, 0.0)
    own_terms = lax.dynamic_slice_in_dim(terms, member * own_rows, own_rows)
    row_scale = jnp.where(counted, 1.0 / loss_count, 0.0)
    dlogits = (
        (jnp.exp(logits - log_total[None, :]) - hits.astype(jnp.float32)) * row_scale[None, :]
    ).astype(low_type)
    chosen_part = contract(dlogits, table_low, 0, 0)
    chosen_grad = across_wide(chosen_part.reshape(groups, own_rows, width))
    final_grad = jnp.zeros((tokens, width), jnp.float32).at[flat_picks].add(chosen_grad)

    _, pull = jax.vjp(layer_norm, second_sum, norms[4], norms[5])
    sum_grad, gain_three, shift_three = pull(final_grad)
    branch_low = sum_grad.astype(low_type)
    down = Fold(1, (2, 4))
    down.cores(gradient_chunks(contract(hidden_low, branch_low, 0, 0)))
    hidden_grad = contract(branch_low, w_down_low, 1, 1)
    _, pull = jax.vjp(swiglu, gate_up)
    gate_low = pull(hidden_grad)[0].astype(low_type)
    gate = Fold(1, (4, 2))
    gate.cores(gradient_chunks(contract(second_low, gate_low, 0, 0)))
    second_grad = sum_grad + contract(gate_low, w_gu_low, 1, 1)
    _, pull = jax.vjp(layer_norm, first_sum, norms[2], norms[3])
    first_sum_grad, gain_two, shift_two = pull(second_grad)
    attn_low = first_sum_grad.astype(low_type)
    mixed_grad = contract(attn_low, w_out_low, 1, 1).astype(low_type)
    pairs = width // LANES
    third = pairs // 3
    sides = []
    for stage in range(3):
        if stage < 2:
            after = down.plane(stage == 0) + gate.plane(stage == 0)
        else:
            after = down.members() + gate.members()
        after = after + [side[0] for side in sides[-1:]]
        sides.append(
            attend_back(
                lengths, queries, keys, values, mixed_grad, log_sums, cosine, sine, stage * third, third, after
            )
        )
    joined_grad = jnp.concatenate([side for parts in zip(*sides) for side in parts], axis=1)
    first_grad = first_sum_grad + contract(joined_grad, near[:, : 3 * width], 1, 1)
    _, pull = jax.vjp(layer_norm, embed.astype(jnp.float32), norms[0], norms[1])
    embed_grad, gain_one, shift_one = pull(first_grad)
    norm_grad = jnp.stack([gain_one, shift_one, gain_two, shift_two, gain_three, shift_three])
    parts = 3
    wide = width // parts
    embed_low = embed_grad.astype(low_type)
    group_embeds = [
        lax.all_gather(embed_low[:, part * wide : (part + 1) * wide], "grp", axis=0, tiled=True)
        for part in range(parts)
    ]
    join = Fold(1, (2, 4))
    join.cores(
        gradient_chunks(
            jnp.concatenate(
                [contract(first_low, joined_grad, 0, 0), contract(mixed_low, attn_low, 0, 0)], axis=1
            )
        )
    )
    join.plane(True)
    join.plane(False)
    join.members()
    gu_share, down_share, join_share = gate.total(), down.total(), join.total()
    part_rows = join_share.shape[0]
    core = replica % 2
    table_parts = []
    for part in range(parts):
        half_args = (
            starts,
            places,
            order,
            dlogits,
            group_chosen[:, part * wide : (part + 1) * wide],
            group_embeds[part],
            block,
        )
        head = Fold(0, (4, 2) if part % 2 else (2, 4))
        if quick:
            sent = table_grad_half((1 - core)[None], *half_args, low_type)
            kept = table_grad_half(core[None], *half_args, jnp.float32)
            head.from_cores(kept, sent)
        else:
            both = [table_grad_half(jnp.full((1,), j, jnp.int32), *half_args, jnp.float32) for j in range(2)]
            head.cores(jnp.stack(both, axis=1).reshape(replicas, block, wide))
        head.plane(True)
        head.plane(False)
        table_parts.append(head.sum())

    shares = (
        join_share[:, : 3 * width],
        join_share[:, 3 * width :],
        gu_share,
        down_share,
    )
    old_rows = (table_rows, qkv_rows, out_rows, gu_rows, down_rows)
    old_cols = (table_cols, qkv_cols, out_cols, gu_cols, down_cols)
    masters = (table, w_qkv, w_out, w_gu, w_down)
    col_parts = [
        jnp.concatenate([jnp.sum(gradient * gradient, axis=0) for gradient in table_parts])
    ] + [jnp.sum(gradient * gradient, axis=0) for gradient in shares]
    row_old = jnp.stack([jnp.sum(rows) for rows in old_rows]) / replicas
    small = [norm_grad.reshape(-1)] + col_parts + [row_old, jnp.sum(own_terms)[None]]
    totals = total_sum(jnp.concatenate(small))
    cuts = []
    start = 0
    for part in small:
        cuts.append(totals[start : start + part.shape[0]])
        start += part.shape[0]
    norm_sum = cuts[0].reshape(norm_grad.shape)
    col_totals = cuts[1:6]
    old_totals = cuts[6]
    loss_sum = cuts[7][0]
    squares = [jnp.sum(part) for part in col_totals]
    clip_norm = jnp.sqrt(sum(squares) + jnp.sum(norm_sum * norm_sum))
    factor = clip_limit / jnp.maximum(clip_norm, clip_limit)
    decay = 1.0 - float(STEP) ** (-0.8)

    far_whole = plane_gather(
        jnp.concatenate(
            [gu_share.astype(low_type), down_share.astype(low_type).reshape(part_rows, -1)], axis=1
        )
    ).reshape(shard_rows, -1)
    near_whole = plane_gather(join_share.astype(low_type)).reshape(shard_rows, -1)
    wholes = [
        None,
        near_whole[:, : 3 * width],
        near_whole[:, 3 * width :],
        far_whole[:, : w_gu.shape[1]],
        far_whole[:, w_gu.shape[1] :].reshape(w_down.shape),
    ]
    table_lows = [part.astype(low_type) for part in table_parts]

    outputs = []
    for place in range(5):
        rows, columns = masters[place].shape
        full_rows = rows * groups
        new_cols = (
            decay * old_cols[place] + (1.0 - decay) * (col_totals[place] * factor * factor) / full_rows
        )
        row_total = decay * old_totals[place] + (1.0 - decay) * (squares[place] * factor * factor) / columns
        row_mean = row_total / full_rows
        if place == 0 and quick:
            have = [
                spread(low, [2, 4, 1] if part % 2 else [4, 2, 1]) for part, low in enumerate(table_lows)
            ]
            tiles = padded // TILE
            row_tiles = jnp.pad(table_rows, (0, padded - vocab_rows), constant_values=1.0).reshape(tiles, 1, TILE)
            scalars = jnp.stack([factor, rate_matrix * factor * jnp.sqrt(row_mean)])
            so_far = (
                blank(table.shape, jnp.float32),
                blank(table.shape, jnp.float32),
                blank((tiles, 1, TILE), jnp.float32),
            )
            slots = slots_of()
            for four in ((0, 2, 4, 6), (1, 3, 5, 7)):
                so_far = update(
                    jnp.stack([slots[part] for part in four]),
                    scalars,
                    [[got[part] for got in have] for part in four],
                    table,
                    row_tiles,
                    new_cols[None, :],
                    so_far,
                )
            outputs.extend([so_far[0], so_far[2].reshape(-1)[:vocab_rows], new_cols, so_far[1]])
            continue
        if place == 0:
            whole = plane_gather(jnp.concatenate(table_lows, axis=1))
            gradient = whole.reshape(padded, width)[:vocab_rows].astype(jnp.float32)
        else:
            gradient = wholes[place].astype(jnp.float32)
        row_means = jnp.mean(gradient * gradient, axis=1)
        new_rows = decay * old_rows[place] + (1.0 - decay) * (row_means * factor * factor)
        clipped = gradient * factor
        scale = new_rows[:, None] * new_cols[None, :] / row_mean
        new_master = masters[place] - rate_matrix * clipped * lax.rsqrt(scale)
        outputs.extend([clipped, new_rows, new_cols, new_master])
    norm_clipped = norm_sum * factor
    moment_new = decay * norms_moment + (1.0 - decay) * norm_clipped * norm_clipped
    norms_new = norms - rate_norm * norm_clipped * lax.rsqrt(moment_new)
    return (
        (loss_sum, loss_count, clip_norm) + tuple(outputs) + (norm_clipped, moment_new, norms_new)
    )


def solution(mesh):
    in_specs = (
        P(("grp", "rep"), None),
        P(("grp", "rep")),
        P(("grp", "rep"), None),
        P(("grp", "rep"), None),
        P(("grp", "rep"), None),
        P("grp", None),
        P("grp", None),
        P("grp", None),
        P("grp", None),
        P("grp", None),
        P(),
        P("grp"),
        P(),
        P("grp"),
        P(),
        P("grp"),
        P(),
        P("grp"),
        P(),
        P("grp"),
        P(),
        P(),
    )
    out_specs = (
        P(),
        P(),
        P(),
        P("grp", None),
        P("grp"),
        P(),
        P("grp", None),
        P("grp", None),
        P("grp"),
        P(),
        P("grp", None),
        P("grp", None),
        P("grp"),
        P(),
        P("grp", None),
        P("grp", None),
        P("grp"),
        P(),
        P("grp", None),
        P("grp", None),
        P("grp"),
        P(),
        P("grp", None),
        P(),
        P(),
        P(),
    )
    return jax.shard_map(body, mesh=mesh, in_specs=in_specs, out_specs=out_specs, check_vma=False)
```

```python
import functools
import math

import jax
import jax.numpy as jnp
from jax import lax
from jax.experimental import pallas as pl
from jax.experimental.pallas import tpu as pltpu
from jax.sharding import PartitionSpec as P

HEADS = 12
HD = 64
STEP = 10
LANES = 128
ROWS = 256
CHUNK = 256
TILE = 240


ln_eps = 1e-05
rope_base = 10000.0
clip_limit = 0.01
rate_matrix = 0.03
rate_norm = 0.3
neg_large = -1e30
low_type = jnp.bfloat16
vmem = 56 * 1024 * 1024


def pair_lanes(shape):
    return lax.broadcasted_iota(jnp.int32, shape, len(shape) - 1)


def swap_halves(value):
    upper = (pair_lanes(value.shape) % HD) >= HD // 2
    return jnp.where(
        upper,
        pltpu.roll(value, HD // 2, axis=1),
        pltpu.roll(value, LANES - HD // 2, axis=1),
    )


def normalize(values, gain, shift):
    center = values - jnp.mean(values, axis=-1, keepdims=True)
    spread = jnp.mean(center * center, axis=-1, keepdims=True)
    return center * lax.rsqrt(spread + ln_eps) * gain + shift


def project_kernel(embed_ref, norms_ref, cosine_ref, sine_ref, w_ref, first_ref, low_ref, q_ref, k_ref, v_ref):
    first = normalize(embed_ref[...].astype(jnp.float32), norms_ref[0:1, :], norms_ref[1:2, :])
    first_ref[...] = first
    low = first.astype(low_type)
    low_ref[...] = low
    width = first.shape[1]
    cosine, sine = cosine_ref[...], sine_ref[...]
    for part, out_ref in enumerate((q_ref, k_ref)):
        joined = jnp.dot(low, w_ref[:, part * width : (part + 1) * width], preferred_element_type=jnp.float32)
        for start in range(0, width, LANES):
            piece = joined[:, start : start + LANES]
            out_ref[:, start : start + LANES] = (piece * cosine + swap_halves(piece) * sine).astype(low_type)
    v_ref[...] = jnp.dot(low, w_ref[:, 2 * width :], preferred_element_type=jnp.float32).astype(low_type)


def project(embed, norms, cosine, sine, weights):
    tokens, width = embed.shape
    row = lambda i: (i, 0)
    fixed = lambda i: (0, 0)
    low = jax.ShapeDtypeStruct((tokens, width), low_type)
    return pl.pallas_call(
        project_kernel,
        grid=(tokens // ROWS,),
        in_specs=[
            pl.BlockSpec((ROWS, width), row),
            pl.BlockSpec(norms.shape, fixed),
            pl.BlockSpec((ROWS, LANES), row),
            pl.BlockSpec((ROWS, LANES), row),
            pl.BlockSpec((width, 3 * width), fixed),
        ],
        out_specs=[pl.BlockSpec((ROWS, width), row)] * 5,
        out_shape=[jax.ShapeDtypeStruct((tokens, width), jnp.float32), low, low, low, low],
        compiler_params=pltpu.CompilerParams(vmem_limit_bytes=vmem),
        cost_estimate=pl.CostEstimate(flops=6 * tokens * width * width, bytes_accessed=20 * tokens * width, transcendentals=0),
    )(embed, norms, cosine, sine, weights)


def head_keys(k, bias, half):
    lanes = pair_lanes(k.shape)
    spare = HD - half * HD
    return jnp.where(lanes // HD == half, k, jnp.where(lanes == spare, bias, jnp.zeros_like(k)))


def head_queries(q, half, spare_value):
    lanes = pair_lanes(q.shape)
    spare = HD - half * HD
    scaled = q * jnp.asarray(1.0 / math.sqrt(HD), q.dtype)
    other = jnp.where(lanes == spare, jnp.full_like(q, spare_value), jnp.zeros_like(q))
    return jnp.where(lanes // HD == half, scaled, other)


def transposed_dot(left, right):
    return lax.dot_general(left, right, (((1,), (1,)), ((), ())), preferred_element_type=jnp.float32)


def key_bias(length_ref, tokens):
    place = lax.broadcasted_iota(jnp.int32, (tokens, LANES), 0)
    return jnp.where(place < length_ref[0], 0.0, neg_large).astype(low_type)


def attend_kernel(length_ref, q_ref, k_ref, v_ref, out_ref, log_ref, keys, turned):
    tokens = k_ref.shape[0]

    @pl.when(pl.program_id(1) == 0)
    def _():
        bias = key_bias(length_ref, tokens)
        for half in range(2):
            keys[half] = head_keys(k_ref[...], bias, half)
        turned[...] = v_ref[...].T

    parts = []
    for half in range(2):
        scores = transposed_dot(keys[half], head_queries(q_ref[...], half, 1.0))
        peak = jnp.max(scores, axis=0, keepdims=True)
        weights = jnp.exp(scores - peak)
        totals = jnp.sum(weights, axis=0, keepdims=True)
        probs = (weights * (1.0 / totals)).astype(low_type)
        parts.append(
            jnp.dot(turned[half * HD : (half + 1) * HD, :], probs, preferred_element_type=jnp.float32)
        )
        log_ref[0, half : half + 1, :] = peak + jnp.log(totals)
    out_ref[...] = jnp.concatenate(parts, axis=0).T.astype(low_type)


def attend(length, q, k, v):
    tokens, width = q.shape
    pairs = width // LANES
    own = lambda p, i, *_: (i, p)
    whole = lambda p, i, *_: (0, p)
    return pl.pallas_call(
        attend_kernel,
        grid_spec=pltpu.PrefetchScalarGridSpec(
            num_scalar_prefetch=1,
            grid=(pairs, tokens // ROWS),
            in_specs=[
                pl.BlockSpec((ROWS, LANES), own),
                pl.BlockSpec((tokens, LANES), whole),
                pl.BlockSpec((tokens, LANES), whole),
            ],
            out_specs=[
                pl.BlockSpec((ROWS, LANES), own),
                pl.BlockSpec((1, 2, ROWS), lambda p, i, *_: (p, 0, i)),
            ],
            scratch_shapes=[
                pltpu.VMEM((2, tokens, LANES), low_type),
                pltpu.VMEM((LANES, tokens), low_type),
            ],
        ),
        out_shape=[
            jax.ShapeDtypeStruct((tokens, width), low_type),
            jax.ShapeDtypeStruct((pairs, 2, tokens), jnp.float32),
        ],
        compiler_params=pltpu.CompilerParams(vmem_limit_bytes=vmem),
        cost_estimate=pl.CostEstimate(
            flops=16 * tokens * tokens * width, bytes_accessed=8 * tokens * width, transcendentals=tokens * tokens * width // HD
        ),
    )(length, q, k, v)


def rotate_back(grads, cosine, sine):
    return grads * cosine + swap_halves(grads * sine)


def attend_back_kernel(first_pair, length_ref, q_ref, k_ref, v_ref, d_ref, log_ref, cosq_ref, sinq_ref, cos_ref, sin_ref, *rest):
    dq_ref, dk_ref, dv_ref, keys, values, turned, dk_total, dv_total = rest[-8:]
    tokens = k_ref.shape[0]
    step = pl.program_id(1)

    @pl.when(step == 0)
    def _():
        bias = key_bias(length_ref, tokens)
        lanes = pair_lanes((tokens, LANES))
        for half in range(2):
            keys[half] = head_keys(k_ref[...], bias, half)
            values[half] = jnp.where(lanes // HD == half, v_ref[...], jnp.zeros_like(v_ref[...]))
        turned[...] = k_ref[...].T
        dk_total[...] = jnp.zeros_like(dk_total)
        dv_total[...] = jnp.zeros_like(dv_total)

    d = d_ref[...]
    lanes = pair_lanes(d.shape)
    parts = []
    dk = dv = None
    for half in range(2):
        scores = transposed_dot(keys[half], head_queries(q_ref[...], half, 1.0))
        probs = jnp.exp(scores - log_ref[0, half : half + 1, :])
        dprobs = transposed_dot(values[half], d)
        inner = jnp.sum(probs * dprobs, axis=0, keepdims=True)
        dscore = (probs * (dprobs - inner)).astype(low_type)
        parts.append(jnp.dot(turned[half * HD : (half + 1) * HD, :], dscore, preferred_element_type=jnp.float32))
        one_k = jnp.dot(dscore, head_queries(q_ref[...], half, 0.0), preferred_element_type=jnp.float32)
        one_v = jnp.dot(
            probs.astype(low_type), jnp.where(lanes // HD == half, d, jnp.zeros_like(d)), preferred_element_type=jnp.float32
        )
        dk = one_k if dk is None else dk + one_k
        dv = one_v if dv is None else dv + one_v
    dk_total[...] += dk
    dv_total[...] += dv
    dq = jnp.concatenate(parts, axis=0).T * (1.0 / math.sqrt(HD))
    dq_ref[...] = rotate_back(dq, cosq_ref[...], sinq_ref[...]).astype(low_type)

    @pl.when(step == pl.num_programs(1) - 1)
    def _():
        dk_ref[...] = rotate_back(dk_total[...], cos_ref[...], sin_ref[...]).astype(low_type)
        dv_ref[...] = dv_total[...].astype(low_type)


def attend_back(length, q, k, v, d, logs, cosine, sine, first_pair, pairs, after=()):
    tokens, width = q.shape
    own = lambda p, i, *_: (i, first_pair + p)
    whole = lambda p, i, *_: (0, first_pair + p)
    low = jax.ShapeDtypeStruct((tokens, pairs * LANES), low_type)
    fixed = pl.BlockSpec((tokens, LANES), lambda p, i, *_: (0, 0))
    row = pl.BlockSpec((ROWS, LANES), lambda p, i, *_: (i, 0))
    return pl.pallas_call(
        functools.partial(attend_back_kernel, first_pair),
        grid_spec=pltpu.PrefetchScalarGridSpec(
            num_scalar_prefetch=1,
            grid=(pairs, tokens // ROWS),
            in_specs=[
                pl.BlockSpec((ROWS, LANES), own),
                pl.BlockSpec((tokens, LANES), whole),
                pl.BlockSpec((tokens, LANES), whole),
                pl.BlockSpec((ROWS, LANES), own),
                pl.BlockSpec((1, 2, ROWS), lambda p, i, *_: (first_pair + p, 0, i)),
                row,
                row,
                fixed,
                fixed,
            ]
            + [pl.BlockSpec(memory_space=pl.ANY)] * len(after),
            out_specs=[
                pl.BlockSpec((ROWS, LANES), lambda p, i, *_: (i, p)),
                pl.BlockSpec((tokens, LANES), lambda p, i, *_: (0, p)),
                pl.BlockSpec((tokens, LANES), lambda p, i, *_: (0, p)),
            ],
            scratch_shapes=[
                pltpu.VMEM((2, tokens, LANES), low_type),
                pltpu.VMEM((2, tokens, LANES), low_type),
                pltpu.VMEM((LANES, tokens), low_type),
                pltpu.VMEM((tokens, LANES), jnp.float32),
                pltpu.VMEM((tokens, LANES), jnp.float32),
            ],
        ),
        out_shape=[low, low, low],
        compiler_params=pltpu.CompilerParams(vmem_limit_bytes=vmem),
        cost_estimate=pl.CostEstimate(
            flops=40 * tokens * tokens * pairs * LANES,
            bytes_accessed=16 * tokens * pairs * LANES,
            transcendentals=tokens * tokens * pairs * 2,
        ),
    )(length, q, k, v, d, logs, cosine, sine, cosine, sine, *after)


def blank(shape, dtype):
    return pl.pallas_call(
        lambda out_ref: None,
        out_shape=jax.ShapeDtypeStruct(shape, dtype),
        out_specs=pl.BlockSpec(memory_space=pl.ANY),
    )()


def lookup_kernel(starts_ref, places_ref, order_ref, table_ref, out_ref, rows):
    count = out_ref.shape[0]
    owned = starts_ref[starts_ref.shape[0] - 1]
    for start in range(0, count, CHUNK):
        rows[start : start + CHUNK, :] = jnp.zeros((CHUNK, rows.shape[1]), jnp.float32)

    def eight(step, carry):
        for j in range(8):
            i = step * 8 + j
            valid = i < owned
            source = jnp.where(valid, places_ref[i], 0)
            target = jnp.where(valid, order_ref[i], count)
            rows[pl.ds(target, 1), :] = table_ref[pl.ds(source, 1), :]
        return carry

    lax.fori_loop(0, (owned + 7) // 8, eight, 0)
    for start in range(0, count, CHUNK):
        out_ref[start : start + CHUNK, :] = rows[start : start + CHUNK, :].astype(low_type)


def lookup(starts, places, order, table):
    count = places.shape[0]
    width = table.shape[1]
    return pl.pallas_call(
        lookup_kernel,
        grid_spec=pltpu.PrefetchScalarGridSpec(
            num_scalar_prefetch=3,
            grid=(1,),
            in_specs=[pl.BlockSpec(table.shape, lambda i, *_: (0, 0), pipeline_mode=pl.Buffered(1))],
            out_specs=pl.BlockSpec((count, width), lambda i, *_: (0, 0), pipeline_mode=pl.Buffered(1)),
            scratch_shapes=[pltpu.VMEM((count + 8, width), jnp.float32)],
        ),
        out_shape=jax.ShapeDtypeStruct((count, width), low_type),
        compiler_params=pltpu.CompilerParams(vmem_limit_bytes=vmem),
        cost_estimate=pl.CostEstimate(flops=0, bytes_accessed=table.size * 12, transcendentals=0),
    )(starts, places, order, table)


def table_grad_kernel(core_ref, starts_ref, places_ref, order_ref, dlogits_ref, chosen_ref, embed_ref, out_ref, rows, total):
    step = pl.program_id(0)
    count = embed_ref.shape[0]
    block = total.shape[0] - 8

    @pl.when(step == 0)
    def _():
        for start in range(0, count, CHUNK):
            rows[start : start + CHUNK, :] = embed_ref[start : start + CHUNK, :].astype(jnp.float32)

    total[:block, :] = jnp.dot(dlogits_ref[...], chosen_ref[...], preferred_element_type=jnp.float32)
    chunk = 2 * step + core_ref[0]
    base = chunk * block
    first, last = starts_ref[chunk], starts_ref[chunk + 1]

    def eight(turn, carry):
        for j in range(8):
            i = first + turn * 8 + j
            at = jnp.minimum(i, count - 1)
            place = jnp.where(i < last, places_ref[at] - base, block)
            total[pl.ds(place, 1), :] += rows[pl.ds(order_ref[at], 1), :]
        return carry

    lax.fori_loop(0, (last - first + 7) // 8, eight, 0)
    out_ref[0] = total[:block, :].astype(out_ref.dtype)


def table_grad_half(core, starts, places, order, dlogits, chosen, embed, block, dtype):
    count, width = embed.shape
    picked = chosen.shape[0]
    chunks = dlogits.shape[0] // block // 2
    fixed = lambda i, *_: (0, 0)
    return pl.pallas_call(
        table_grad_kernel,
        grid_spec=pltpu.PrefetchScalarGridSpec(
            num_scalar_prefetch=4,
            grid=(chunks,),
            in_specs=[
                pl.BlockSpec((block, picked), lambda i, core, *_: (2 * i + core[0], 0)),
                pl.BlockSpec((picked, width), fixed),
                pl.BlockSpec((count, width), fixed, pipeline_mode=pl.Buffered(1)),
            ],
            out_specs=pl.BlockSpec((1, block, width), lambda i, *_: (i, 0, 0)),
            scratch_shapes=[pltpu.VMEM((count, width), jnp.float32), pltpu.VMEM((block + 8, width), jnp.float32)],
        ),
        out_shape=jax.ShapeDtypeStruct((chunks, block, width), dtype),
        compiler_params=pltpu.CompilerParams(vmem_limit_bytes=vmem),
        cost_estimate=pl.CostEstimate(
            flops=2 * chunks * block * picked * width, bytes_accessed=8 * chunks * block * width, transcendentals=0
        ),
    )(core, starts, places, order, dlogits, chosen, embed)


TILE = 240

def update_kernel(parts, slots_ref, scalars_ref, *rest):
    pieces = rest[: 4 * parts]
    table_ref, rows_ref, cols_ref = rest[4 * parts : 4 * parts + 3]
    grad_ref, new_ref, rows_new_ref = rest[-3:]
    factor, rate = scalars_ref[0], scalars_ref[1]
    decay = 1.0 - float(STEP) ** (-0.8)
    old = jnp.broadcast_to(rows_ref[0], (LANES, TILE)).T[:, 0:1]
    for part in range(4):

        @pl.when(pl.program_id(0) == part)
        def _(part=part):
            own = pieces[part * parts : (part + 1) * parts]
            gradient = jnp.concatenate([piece[...] for piece in own], axis=1).astype(jnp.float32)
            means = jnp.mean(gradient * gradient, axis=1, keepdims=True)
            rows_new = decay * old + (1.0 - decay) * (means * factor * factor)
            grad_ref[...] = gradient * factor
            new_ref[...] = table_ref[...] - gradient * (rate * lax.rsqrt(rows_new)) * cols_ref[...]
            rows_new_ref[0] = jnp.broadcast_to(rows_new, (TILE, LANES)).T[0:1, :]


def update(slots, scalars, pieces, table, rows, cols, so_far):
    parts = len(pieces[0])
    block = pieces[0][0].shape[0]
    width = table.shape[1]
    steps = block // TILE
    place = lambda p, i, slots: (slots[p] * steps + i, 0)
    place3 = lambda p, i, slots: (slots[p] * steps + i, 0, 0)

    def own(part):
        return lambda p, i, slots: (jnp.where(p < part, 0, jnp.where(p > part, steps - 1, i)), 0)

    fixed = lambda p, i, slots: (0, 0)
    any_space = pl.BlockSpec(memory_space=pl.ANY)
    given = 5 + 4 * parts
    return pl.pallas_call(
        functools.partial(update_kernel, parts),
        grid_spec=pltpu.PrefetchScalarGridSpec(
            num_scalar_prefetch=1,
            grid=(4, steps),
            in_specs=[pl.BlockSpec(memory_space=pltpu.SMEM)]
            + [pl.BlockSpec((TILE, piece.shape[1]), own(part)) for part in range(4) for piece in pieces[part]]
            + [
                pl.BlockSpec((TILE, width), place),
                pl.BlockSpec((1, 1, TILE), place3),
                pl.BlockSpec((1, width), fixed),
                any_space,
                any_space,
                any_space,
            ],
            out_specs=[
                pl.BlockSpec((TILE, width), place),
                pl.BlockSpec((TILE, width), place),
                pl.BlockSpec((1, 1, TILE), place3),
            ],
        ),
        out_shape=[jax.ShapeDtypeStruct(part.shape, part.dtype) for part in so_far],
        input_output_aliases={given: 0, given + 1: 1, given + 2: 2},
        compiler_params=pltpu.CompilerParams(vmem_limit_bytes=vmem),
        cost_estimate=pl.CostEstimate(
            flops=40 * block * width, bytes_accessed=56 * block * width, transcendentals=4 * block * width
        ),
    )(slots, scalars, *[piece for four in pieces for piece in four], table, rows, cols, *so_far)


def stack_kernel(slots_ref, *refs):
    pieces, out_ref = refs[:-1], refs[-1]
    for place, piece in enumerate(pieces):

        @pl.when(pl.program_id(0) == place)
        def _(piece=piece):
            out_ref[0] = piece[...]


def lay_out(slots, pieces):
    shape = pieces[0].shape
    return pl.pallas_call(
        stack_kernel,
        grid_spec=pltpu.PrefetchScalarGridSpec(
            num_scalar_prefetch=1,
            grid=(len(pieces),),
            in_specs=[pl.BlockSpec(shape, lambda i, slots: (0, 0), pipeline_mode=pl.Buffered(1))] * len(pieces),
            out_specs=pl.BlockSpec((1,) + shape, lambda i, slots: (slots[i], 0, 0)),
        ),
        out_shape=jax.ShapeDtypeStruct((len(pieces),) + shape, pieces[0].dtype),
        compiler_params=pltpu.CompilerParams(vmem_limit_bytes=vmem),
        cost_estimate=pl.CostEstimate(flops=0, bytes_accessed=4 * len(pieces) * pieces[0].size, transcendentals=0),
    )(slots, *pieces)


def columns_kernel(main, members_ref, slots_ref, *refs):
    replicas = slots_ref.shape[0]
    pieces, outs = refs[:replicas], refs[replicas + (len(refs) - replicas - (1 if main is None else 2)) :]
    groups, rows = pieces[0].shape[0], pieces[0].shape[1]
    for place, piece in enumerate(pieces):

        @pl.when(pl.program_id(0) == place)
        def _(piece=piece):
            for offset in range(groups):
                member = members_ref[offset]
                at = pl.ds(pl.multiple_of(member * rows, rows), rows)
                if main is None:
                    outs[0][at, :] = piece[offset]
                else:
                    outs[0][at, :] = piece[offset, :, :main]
                    half = piece.shape[2] - main
                    outs[1][member, 0, :, :half] = piece[offset, : rows // 2, main:]
                    outs[1][member, 0, :, half:] = piece[offset, rows // 2 :, main:]


def lay_columns(members, slots, pieces, main=None, after=()):
    groups, rows, columns = pieces[0].shape
    replicas = len(pieces)
    wide = columns if main is None else main
    out_shape = [jax.ShapeDtypeStruct((groups * rows, replicas * wide), low_type)]
    out_specs = [pl.BlockSpec((groups * rows, wide), lambda i, members, slots: (0, slots[i]))]
    if main is not None:
        out_shape.append(jax.ShapeDtypeStruct((groups, replicas, rows // 2, 2 * (columns - main)), low_type))
        out_specs.append(
            pl.BlockSpec((groups, 1, rows // 2, 2 * (columns - main)), lambda i, members, slots: (0, slots[i], 0, 0))
        )
    return pl.pallas_call(
        functools.partial(columns_kernel, main),
        grid_spec=pltpu.PrefetchScalarGridSpec(
            num_scalar_prefetch=2,
            grid=(replicas,),
            in_specs=[pl.BlockSpec(pieces[0].shape, lambda i, *_: (0, 0, 0), pipeline_mode=pl.Buffered(1))] * replicas
            + [pl.BlockSpec(memory_space=pl.ANY)] * len(after),
            out_specs=out_specs,
        ),
        out_shape=out_shape,
        compiler_params=pltpu.CompilerParams(vmem_limit_bytes=vmem),
        cost_estimate=pl.CostEstimate(flops=0, bytes_accessed=4 * replicas * pieces[0].size, transcendentals=0),
    )(members, slots, *pieces, *after)


tie = lax.optimization_barrier


def flip(value, bit):
    size = lax.axis_size("rep")
    return lax.ppermute(value, "rep", [(i, i ^ bit) for i in range(size)])


def turn(value, offset):
    size = lax.axis_size("grp")
    return lax.ppermute(value, "grp", [(i, (i + offset) % size) for i in range(size)])


def spread(piece, order):
    have = {0: piece}
    for bit in order:
        have.update({place ^ bit: flip(part, bit) for place, part in have.items()})
    return have


def slots_of():
    return lax.axis_index("rep") ^ jnp.arange(lax.axis_size("rep"), dtype=jnp.int32)


def plane_gather(piece):
    if lax.axis_size("rep") != 8:
        return lax.all_gather(piece, "rep")
    have = spread(piece, [2, 4, 1])
    return lay_out(slots_of(), [have[place] for place in range(8)])


def halve(value, axis, bit):
    mine = (lax.axis_index("rep") // bit) % 2
    kept = lax.dynamic_index_in_dim(value, mine, axis, keepdims=False)
    sent = lax.dynamic_index_in_dim(value, 1 - mine, axis, keepdims=False)
    return kept, sent.astype(low_type)


class Fold:
    def __init__(self, axis, order):
        self.axis = axis
        self.order = order
        self.quick = lax.axis_size("rep") == 8

    def cores(self, chunks):
        axis = self.axis
        if not self.quick:
            self.value = lax.psum_scatter(chunks, "rep", scatter_dimension=axis)
            return []
        shape = chunks.shape
        kept, sent = halve(chunks.reshape(shape[:axis] + (4, 2) + shape[axis + 1 :]), axis + 1, 1)
        return self.from_cores(kept, sent)

    def from_cores(self, kept, sent):
        self.kept, self.got = kept, flip(sent, 1)
        return [sent]

    def sum(self):
        return self.kept + self.got.astype(jnp.float32) if self.quick else self.value

    def plane(self, first):
        if not self.quick:
            return []
        value = self.sum()
        axis = self.axis
        bit = self.order[0 if first else 1]
        if first:
            shape = value.shape
            value = value.reshape(shape[:axis] + (2, 2) + shape[axis + 1 :])
            axis = axis + (1 if bit == 2 else 0)
        self.kept, sent = halve(value, axis, bit)
        self.got = flip(sent, bit)
        return [sent]

    def members(self):
        value = self.sum()
        member = lax.axis_index("grp")
        size = lax.axis_size("grp")
        self.own = lax.dynamic_index_in_dim(value, member, 0, keepdims=False)
        sent = [
            lax.dynamic_index_in_dim(value, (member + offset) % size, 0, keepdims=False).astype(low_type)
            for offset in range(1, size)
        ]
        self.came = [turn(part, offset + 1) for offset, part in enumerate(sent)]
        return sent

    def total(self):
        return sum((came.astype(jnp.float32) for came in self.came), self.own)


def gradient_chunks(gradient):
    groups = lax.axis_size("grp")
    replicas = lax.axis_size("rep")
    rows, columns = gradient.shape
    return gradient.reshape(groups, replicas, rows // (groups * replicas), columns)


def across_wide(chunks):
    member = lax.axis_index("grp")
    size = lax.axis_size("grp")
    total = lax.dynamic_index_in_dim(chunks, member, 0, keepdims=False)
    for offset in range(1, size):
        sent = lax.dynamic_index_in_dim(chunks, (member + offset) % size, 0, keepdims=False)
        total = total + turn(sent, offset)
    return total


def group_gather(value):
    member = lax.axis_index("grp")
    size = lax.axis_size("grp")
    result = jnp.zeros((size,) + value.shape, value.dtype)
    result = lax.dynamic_update_index_in_dim(result, value, member, 0)
    for offset in range(1, size):
        result = lax.dynamic_update_index_in_dim(
            result, turn(value, offset), (member + size - offset) % size, 0
        )
    return result


def plane_sum(value):
    for j in range(1, lax.axis_size("rep").bit_length() - 1):
        value = value + flip(value, 1 << j)
    return value


def rest_sum(value):
    value = value + flip(value, 1)
    size = lax.axis_size("grp")
    for j in range(size.bit_length() - 1):
        value = value + lax.ppermute(value, "grp", [(i, i ^ (1 << j)) for i in range(size)])
    return value


def fetch(own):
    groups = lax.axis_size("grp")
    return jnp.stack([own] + [turn(own, offset) for offset in range(1, groups)])


def cut(value, axis):
    replicas = lax.axis_size("rep")
    size = value.shape[axis] // replicas
    return lax.dynamic_slice_in_dim(value, lax.axis_index("rep") * size, size, axis)


def members_of():
    groups = lax.axis_size("grp")
    return (lax.axis_index("grp") + groups - jnp.arange(groups, dtype=jnp.int32)) % groups


def contract(left, right, left_dim, right_dim):
    return lax.dot_general(
        left, right, (((left_dim,), (right_dim,)), ((), ())), preferred_element_type=jnp.float32
    )


def layer_norm(values, gain, shift):
    center = values - jnp.mean(values, axis=-1, keepdims=True)
    spread = jnp.mean(center * center, axis=-1, keepdims=True)
    return center * lax.rsqrt(spread + ln_eps) * gain + shift


def rope_tables(length):
    freqs = rope_base ** (-jnp.arange(HD // 2, dtype=jnp.float32) * 2.0 / HD)
    angles = jnp.arange(length, dtype=jnp.float32)[:, None] * freqs[None, :]
    cosine, sine = jnp.cos(angles), jnp.sin(angles)
    return (
        jnp.concatenate([cosine] * 4, axis=-1),
        jnp.concatenate([-sine, sine, -sine, sine], axis=-1),
    )


def swiglu(joined):
    middle = joined.shape[-1] // 2
    return jax.nn.silu(joined[:, :middle]) * joined[:, middle:]


def merge_stats(first_part, second_part):
    peak = jnp.maximum(first_part[0], second_part[0])
    spread = first_part[1] * jnp.exp(first_part[0] - peak) + second_part[1] * jnp.exp(
        second_part[0] - peak
    )
    return (peak, spread, first_part[2] + second_part[2])


def body(
    ids,
    lengths,
    picks,
    labels,
    loss_mask,
    table,
    w_qkv,
    w_out,
    w_gu,
    w_down,
    norms,
    table_rows,
    table_cols,
    qkv_rows,
    qkv_cols,
    out_rows,
    out_cols,
    gu_rows,
    gu_cols,
    down_rows,
    down_cols,
    norms_moment,
):
    member = lax.axis_index("grp")
    groups = lax.axis_size("grp")
    replica = lax.axis_index("rep")
    replicas = lax.axis_size("rep")
    seqs, length = ids.shape
    width = table.shape[1]
    vocab_rows = table.shape[0]
    own_rows = seqs * picks.shape[1]
    tokens = seqs * length
    block = -(-vocab_rows // (16 * replicas)) * 16
    padded = block * replicas

    packed = jnp.concatenate([ids.reshape(-1), labels.reshape(-1), loss_mask.reshape(-1)])
    group_packed = group_gather(packed)
    group_ids = group_packed[:, :tokens].reshape(-1)
    group_labels = group_packed[:, tokens : tokens + own_rows].reshape(-1)
    group_mask = group_packed[:, tokens + own_rows :].reshape(-1)
    shard_rows = w_qkv.shape[0]
    quick = replicas == 8
    near_shard = jnp.concatenate([w_qkv, w_out], axis=1)
    if quick:
        near_part = fetch(cut(near_shard, 1).astype(low_type))
        down_part = cut(w_down, 0)
        down_part = jnp.concatenate([down_part[:, : width // 2], down_part[:, width // 2 :]], axis=0)
        far_part = fetch(jnp.concatenate([cut(w_gu, 1), down_part], axis=1).astype(low_type))

    local_ids = group_ids - member * vocab_rows
    owned = (local_ids >= 0) & (local_ids < vocab_rows)
    places, order = lax.sort(
        (jnp.where(owned, local_ids, padded), jnp.arange(local_ids.shape[0], dtype=jnp.int32)), num_keys=1
    )
    bounds = jnp.arange(replicas + 1, dtype=jnp.int32) * block
    starts = jnp.sum((places[None, :] < bounds[:, None]).astype(jnp.int32), axis=1)
    found = lookup(starts, places, order, table)
    if quick:
        found, near_part, far_part = lax.optimization_barrier((found, near_part, far_part))
    embed = lax.psum_scatter(found, "grp", scatter_dimension=0, tiled=True)
    late_table, _ = lax.optimization_barrier((table, found))
    table_low = jnp.pad(late_table.astype(low_type), ((0, padded - vocab_rows), (0, 0)))

    if quick:
        near_have = spread(near_part, [2, 4, 1])
        far_have = spread(far_part, [4, 2, 1])
        (near,) = lay_columns(members_of(), slots_of(), [near_have[place] for place in range(replicas)])
        w_gu_low, w_down_low = lay_columns(
            members_of(),
            slots_of(),
            [far_have[place] for place in range(replicas)],
            w_gu.shape[1] // replicas,
        )
        w_down_low = w_down_low.reshape(-1, width)
        embed, near, w_gu_low, w_down_low, table_low = tie((embed, near, w_gu_low, w_down_low, table_low))
    else:
        near = lax.all_gather(near_shard.astype(low_type), "grp", tiled=True)
        w_gu_low = lax.all_gather(w_gu.astype(low_type), "grp", tiled=True)
        w_down_low = lax.all_gather(w_down.astype(low_type), "grp", tiled=True)
    w_out_low = near[:, 3 * width :]
    cosine, sine = rope_tables(length)
    first, first_low, queries, keys, values = project(embed, norms, cosine, sine, near)
    queries, group_mask = tie((queries, group_mask))
    loss_count = jnp.sum(group_mask).astype(jnp.float32)[None]
    for j in range(replicas.bit_length() - 1):
        loss_count = loss_count + flip(loss_count, 1 << j)
    loss_count = loss_count[0]
    mixed_low, log_sums = attend(lengths, queries, keys, values)
    first_sum = first + jnp.dot(mixed_low, w_out_low, preferred_element_type=jnp.float32)
    second = layer_norm(first_sum, norms[2], norms[3])
    second_low = second.astype(low_type)
    gate_up = jnp.dot(second_low, w_gu_low, preferred_element_type=jnp.float32)
    hidden_low = swiglu(gate_up).astype(low_type)
    second_sum = second + jnp.dot(hidden_low, w_down_low, preferred_element_type=jnp.float32)
    final = layer_norm(second_sum, norms[4], norms[5])

    flat_picks = (jnp.arange(seqs, dtype=jnp.int32)[:, None] * length + picks).reshape(-1)
    chosen = final[flat_picks].astype(low_type)
    group_chosen = group_gather(chosen).reshape(groups * own_rows, width)
    rows_at = jnp.arange(padded, dtype=jnp.int32)[:, None]
    logits = jnp.where(rows_at < vocab_rows, contract(table_low, group_chosen, 1, 1), neg_large)
    peak = jnp.max(logits, axis=0)
    spread_sum = jnp.sum(jnp.exp(logits - peak[None, :]), axis=0)
    local_labels = group_labels - member * vocab_rows
    inside = (local_labels >= 0) & (local_labels < vocab_rows)
    hits = (rows_at == local_labels[None, :]) & inside[None, :]
    target = jnp.sum(jnp.where(hits, logits, 0.0), axis=0)
    stats = group_gather(jnp.stack([peak, spread_sum, target]))
    so_far = (stats[0, 0], stats[0, 1], stats[0, 2])
    for place in range(1, groups):
        so_far = merge_stats(so_far, (stats[place, 0], stats[place, 1], stats[place, 2]))
    peak_all, spread_all, target_all = so_far
    log_total = peak_all + jnp.log(spread_all)
    counted = group_mask > 0
    terms = jnp.where(counted, log_total - target_all, 0.0)
    own_terms = lax.dynamic_slice_in_dim(terms, member * own_rows, own_rows)
    row_scale = jnp.where(counted, 1.0 / loss_count, 0.0)
    dlogits = (
        (jnp.exp(logits - log_total[None, :]) - hits.astype(jnp.float32)) * row_scale[None, :]
    ).astype(low_type)
    chosen_part = contract(dlogits, table_low, 0, 0)
    chosen_grad = across_wide(chosen_part.reshape(groups, own_rows, width))
    final_grad = jnp.zeros((tokens, width), jnp.float32).at[flat_picks].add(chosen_grad)

    _, pull = jax.vjp(layer_norm, second_sum, norms[4], norms[5])
    sum_grad, gain_three, shift_three = pull(final_grad)
    branch_low = sum_grad.astype(low_type)
    down = Fold(1, (2, 4))
    down.cores(gradient_chunks(contract(hidden_low, branch_low, 0, 0)))
    hidden_grad = contract(branch_low, w_down_low, 1, 1)
    _, pull = jax.vjp(swiglu, gate_up)
    gate_low = pull(hidden_grad)[0].astype(low_type)
    gate_low, _ = tie((gate_low, down.plane(True)))
    gate, up = Fold(1, (4, 2)), Fold(1, (2, 4))
    middle = gate_up.shape[1] // 2
    sent = gate.cores(gradient_chunks(contract(second_low, gate_low[:, :middle], 0, 0)))
    sent += up.cores(gradient_chunks(contract(second_low, gate_low[:, middle:], 0, 0)))
    gate_low, _ = tie((gate_low, sent))
    second_grad = sum_grad + contract(gate_low, w_gu_low, 1, 1)
    second_grad, _ = tie((second_grad, gate.plane(True) + up.plane(True) + down.plane(False)))
    _, pull = jax.vjp(layer_norm, first_sum, norms[2], norms[3])
    first_sum_grad, gain_two, shift_two = pull(second_grad)
    attn_low = first_sum_grad.astype(low_type)
    mixed_grad = contract(attn_low, w_out_low, 1, 1).astype(low_type)
    pairs = width // LANES
    third = pairs // 3
    sides = []
    for stage in range(3):
        if stage:
            sent = gate.plane(False) + up.plane(False) + down.members() if stage == 1 else gate.members() + up.members()
            mixed_grad, sides[-1], _ = tie((mixed_grad, sides[-1], sent))
        sides.append(
            attend_back(lengths, queries, keys, values, mixed_grad, log_sums, cosine, sine, stage * third, third)
        )
    joined_grad = jnp.concatenate([side for parts in zip(*sides) for side in parts], axis=1)
    first_grad = first_sum_grad + contract(joined_grad, near[:, : 3 * width], 1, 1)
    _, pull = jax.vjp(layer_norm, embed.astype(jnp.float32), norms[0], norms[1])
    embed_grad, gain_one, shift_one = pull(first_grad)
    norm_grad = jnp.stack([gain_one, shift_one, gain_two, shift_two, gain_three, shift_three])
    cuts_at = (0, width // 2, width // 6 * 5, width)
    spans = list(zip(cuts_at[:-1], cuts_at[1:]))
    embed_low = embed_grad.astype(low_type)
    group_embeds = []
    for begin, end in spans:
        piece, _ = tie((embed_low[:, begin:end], group_embeds[-1:]))
        group_embeds.append(lax.all_gather(piece, "grp", axis=0, tiled=True))
    join = Fold(1, (2, 4))
    join.cores(
        gradient_chunks(
            jnp.concatenate(
                [contract(first_low, joined_grad, 0, 0), contract(mixed_low, attn_low, 0, 0)], axis=1
            )
        )
    )
    sent = join.plane(True)
    gu_share = jnp.concatenate([gate.total(), up.total()], axis=1)
    down_share = down.total()
    part_rows = gu_share.shape[0]
    far_low = jnp.concatenate(
        [gu_share.astype(low_type), down_share.astype(low_type).reshape(part_rows, -1)], axis=1
    )
    if quick:
        far_got = spread(far_low, [2, 4, 1])
        group_embeds[0], _, _ = tie((group_embeds[0], sent, list(far_got.values())))
    core = replica % 2
    heads = [Fold(0, (4, 2) if part % 2 else (2, 4)) for part in range(3)]
    for part, (begin, end) in enumerate(spans):
        head = heads[part]
        if part == 1:
            group_embeds[1], _ = tie((group_embeds[1], heads[0].plane(True) + join.plane(False)))
        if part == 2:
            sent = heads[1].plane(True) + heads[0].plane(False) + join.members()
            group_embeds[2], _ = tie((group_embeds[2], sent))
        half_args = (
            starts,
            places,
            order,
            dlogits,
            group_chosen[:, begin:end],
            group_embeds[part],
            block,
        )
        if quick:
            sent = table_grad_half((1 - core)[None], *half_args, low_type)
            kept = table_grad_half(core[None], *half_args, jnp.float32)
            head.from_cores(kept, sent)
        else:
            both = [table_grad_half(jnp.full((1,), j, jnp.int32), *half_args, jnp.float32) for j in range(2)]
            head.cores(jnp.stack(both, axis=1).reshape(replicas, block, end - begin))
    heads[2].plane(True)
    heads[1].plane(False)
    heads[2].plane(False)
    table_parts = [head.sum() for head in heads]
    join_share = join.total()

    shares = (
        join_share[:, : 3 * width],
        join_share[:, 3 * width :],
        gu_share,
        down_share,
    )
    old_rows = (table_rows, qkv_rows, out_rows, gu_rows, down_rows)
    old_cols = (table_cols, qkv_cols, out_cols, gu_cols, down_cols)
    masters = (table, w_qkv, w_out, w_gu, w_down)
    col_parts = [
        jnp.concatenate([jnp.sum(gradient * gradient, axis=0) for gradient in table_parts])
    ] + [jnp.sum(gradient * gradient, axis=0) for gradient in shares]
    row_old = jnp.stack([jnp.sum(rows) for rows in old_rows]) / replicas
    small = [norm_grad.reshape(-1)] + col_parts + [row_old, jnp.sum(own_terms)[None]]
    plane_totals = plane_sum(jnp.concatenate(small))
    table_lows = [table_parts[0].astype(low_type), jnp.concatenate(table_parts[1:], axis=1).astype(low_type)]
    plane_totals, table_lows = tie((plane_totals, table_lows))
    totals = rest_sum(plane_totals)
    cuts = []
    start = 0
    for part in small:
        cuts.append(totals[start : start + part.shape[0]])
        start += part.shape[0]
    norm_sum = cuts[0].reshape(norm_grad.shape)
    col_totals = cuts[1:6]
    old_totals = cuts[6]
    loss_sum = cuts[7][0]
    squares = [jnp.sum(part) for part in col_totals]
    clip_norm = jnp.sqrt(sum(squares) + jnp.sum(norm_sum * norm_sum))
    factor = clip_limit / jnp.maximum(clip_norm, clip_limit)
    decay = 1.0 - float(STEP) ** (-0.8)

    if quick:
        far_whole = lay_out(slots_of(), [far_got[place] for place in range(replicas)])
    else:
        far_whole = plane_gather(far_low)
    far_whole = far_whole.reshape(shard_rows, -1)
    near_whole = plane_gather(join_share.astype(low_type)).reshape(shard_rows, -1)
    wholes = [
        None,
        near_whole[:, : 3 * width],
        near_whole[:, 3 * width :],
        far_whole[:, : w_gu.shape[1]],
        far_whole[:, w_gu.shape[1] :].reshape(w_down.shape),
    ]

    outputs = []
    for place in range(5):
        rows, columns = masters[place].shape
        full_rows = rows * groups
        new_cols = (
            decay * old_cols[place] + (1.0 - decay) * (col_totals[place] * factor * factor) / full_rows
        )
        row_total = decay * old_totals[place] + (1.0 - decay) * (squares[place] * factor * factor) / columns
        row_mean = row_total / full_rows
        if place == 0 and quick:
            have = [
                spread(low, [2, 4, 1] if part % 2 else [4, 2, 1]) for part, low in enumerate(table_lows)
            ]
            tiles = padded // TILE
            row_tiles = jnp.pad(table_rows, (0, padded - vocab_rows), constant_values=1.0).reshape(tiles, 1, TILE)
            scalars = jnp.stack([factor, rate_matrix * factor * jnp.sqrt(row_mean)])
            so_far = (
                blank(table.shape, jnp.float32),
                blank(table.shape, jnp.float32),
                blank((tiles, 1, TILE), jnp.float32),
            )
            slots = slots_of()
            for four in ((0, 2, 4, 6), (1, 3, 5, 7)):
                so_far = update(
                    jnp.stack([slots[part] for part in four]),
                    scalars,
                    [[got[part] for got in have] for part in four],
                    table,
                    row_tiles,
                    lax.rsqrt(new_cols)[None, :],
                    so_far,
                )
            outputs.extend([so_far[0], so_far[2].reshape(-1)[:vocab_rows], new_cols, so_far[1]])
            continue
        if place == 0:
            whole = plane_gather(jnp.concatenate(table_lows, axis=1))
            gradient = whole.reshape(padded, width)[:vocab_rows].astype(jnp.float32)
        else:
            gradient = wholes[place].astype(jnp.float32)
        row_means = jnp.mean(gradient * gradient, axis=1)
        new_rows = decay * old_rows[place] + (1.0 - decay) * (row_means * factor * factor)
        clipped = gradient * factor
        scale = new_rows[:, None] * new_cols[None, :] / row_mean
        new_master = masters[place] - rate_matrix * clipped * lax.rsqrt(scale)
        outputs.extend([clipped, new_rows, new_cols, new_master])
    norm_clipped = norm_sum * factor
    moment_new = decay * norms_moment + (1.0 - decay) * norm_clipped * norm_clipped
    norms_new = norms - rate_norm * norm_clipped * lax.rsqrt(moment_new)
    return (
        (loss_sum, loss_count, clip_norm) + tuple(outputs) + (norm_clipped, moment_new, norms_new)
    )


def solution(mesh):
    in_specs = (
        P(("grp", "rep"), None),
        P(("grp", "rep")),
        P(("grp", "rep"), None),
        P(("grp", "rep"), None),
        P(("grp", "rep"), None),
        P("grp", None),
        P("grp", None),
        P("grp", None),
        P("grp", None),
        P("grp", None),
        P(),
        P("grp"),
        P(),
        P("grp"),
        P(),
        P("grp"),
        P(),
        P("grp"),
        P(),
        P("grp"),
        P(),
        P(),
    )
    out_specs = (
        P(),
        P(),
        P(),
        P("grp", None),
        P("grp"),
        P(),
        P("grp", None),
        P("grp", None),
        P("grp"),
        P(),
        P("grp", None),
        P("grp", None),
        P("grp"),
        P(),
        P("grp", None),
        P("grp", None),
        P("grp"),
        P(),
        P("grp", None),
        P("grp", None),
        P("grp"),
        P(),
        P("grp", None),
        P(),
        P(),
        P(),
    )
    return jax.shard_map(body, mesh=mesh, in_specs=in_specs, out_specs=out_specs, check_vma=False)
```

```python
import functools
import math

import jax
import jax.numpy as jnp
from jax import lax
from jax.experimental import pallas as pl
from jax.experimental.pallas import tpu as pltpu
from jax.sharding import PartitionSpec as P

HEADS = 12
HD = 64
STEP = 10
LANES = 128
ROWS = 256
CHUNK = 256
TILE = 480


ln_eps = 1e-05
rope_base = 10000.0
clip_limit = 0.01
rate_matrix = 0.03
rate_norm = 0.3
neg_large = -1e30
low_type = jnp.bfloat16
vmem = 56 * 1024 * 1024


def pair_lanes(shape):
    return lax.broadcasted_iota(jnp.int32, shape, len(shape) - 1)


def swap_halves(value):
    upper = (pair_lanes(value.shape) % HD) >= HD // 2
    return jnp.where(
        upper,
        pltpu.roll(value, HD // 2, axis=1),
        pltpu.roll(value, LANES - HD // 2, axis=1),
    )


def normalize(values, gain, shift):
    center = values - jnp.mean(values, axis=-1, keepdims=True)
    spread = jnp.mean(center * center, axis=-1, keepdims=True)
    return center * lax.rsqrt(spread + ln_eps) * gain + shift


def project_kernel(embed_ref, norms_ref, cosine_ref, sine_ref, w_ref, first_ref, low_ref, q_ref, k_ref, v_ref):
    first = normalize(embed_ref[...].astype(jnp.float32), norms_ref[0:1, :], norms_ref[1:2, :])
    first_ref[...] = first
    low = first.astype(low_type)
    low_ref[...] = low
    width = first.shape[1]
    cosine, sine = cosine_ref[...], sine_ref[...]
    for part, out_ref in enumerate((q_ref, k_ref)):
        joined = jnp.dot(low, w_ref[:, part * width : (part + 1) * width], preferred_element_type=jnp.float32)
        for start in range(0, width, LANES):
            piece = joined[:, start : start + LANES]
            out_ref[:, start : start + LANES] = (piece * cosine + swap_halves(piece) * sine).astype(low_type)
    v_ref[...] = jnp.dot(low, w_ref[:, 2 * width :], preferred_element_type=jnp.float32).astype(low_type)


def project(embed, norms, cosine, sine, weights):
    tokens, width = embed.shape
    row = lambda i: (i, 0)
    fixed = lambda i: (0, 0)
    low = jax.ShapeDtypeStruct((tokens, width), low_type)
    return pl.pallas_call(
        project_kernel,
        grid=(tokens // ROWS,),
        in_specs=[
            pl.BlockSpec((ROWS, width), row),
            pl.BlockSpec(norms.shape, fixed),
            pl.BlockSpec((ROWS, LANES), row),
            pl.BlockSpec((ROWS, LANES), row),
            pl.BlockSpec((width, 3 * width), fixed),
        ],
        out_specs=[pl.BlockSpec((ROWS, width), row)] * 5,
        out_shape=[jax.ShapeDtypeStruct((tokens, width), jnp.float32), low, low, low, low],
        compiler_params=pltpu.CompilerParams(vmem_limit_bytes=vmem),
        cost_estimate=pl.CostEstimate(flops=6 * tokens * width * width, bytes_accessed=20 * tokens * width, transcendentals=0),
    )(embed, norms, cosine, sine, weights)


def head_keys(k, bias, half):
    lanes = pair_lanes(k.shape)
    spare = HD - half * HD
    return jnp.where(lanes // HD == half, k, jnp.where(lanes == spare, bias, jnp.zeros_like(k)))


def head_queries(q, half, spare_value):
    lanes = pair_lanes(q.shape)
    spare = HD - half * HD
    scaled = q * jnp.asarray(1.0 / math.sqrt(HD), q.dtype)
    other = jnp.where(lanes == spare, jnp.full_like(q, spare_value), jnp.zeros_like(q))
    return jnp.where(lanes // HD == half, scaled, other)


def transposed_dot(left, right):
    return lax.dot_general(left, right, (((1,), (1,)), ((), ())), preferred_element_type=jnp.float32)


def key_bias(length_ref, tokens):
    place = lax.broadcasted_iota(jnp.int32, (tokens, LANES), 0)
    return jnp.where(place < length_ref[0], 0.0, neg_large).astype(low_type)


def attend_kernel(length_ref, q_ref, k_ref, v_ref, out_ref, log_ref, keys, turned):
    tokens = k_ref.shape[0]

    @pl.when(pl.program_id(1) == 0)
    def _():
        bias = key_bias(length_ref, tokens)
        for half in range(2):
            keys[half] = head_keys(k_ref[...], bias, half)
        turned[...] = v_ref[...].T

    parts = []
    for half in range(2):
        scores = transposed_dot(keys[half], head_queries(q_ref[...], half, 1.0))
        peak = jnp.max(scores, axis=0, keepdims=True)
        weights = jnp.exp(scores - peak)
        totals = jnp.sum(weights, axis=0, keepdims=True)
        probs = (weights * (1.0 / totals)).astype(low_type)
        parts.append(
            jnp.dot(turned[half * HD : (half + 1) * HD, :], probs, preferred_element_type=jnp.float32)
        )
        log_ref[0, half : half + 1, :] = peak + jnp.log(totals)
    out_ref[...] = jnp.concatenate(parts, axis=0).T.astype(low_type)


def attend(length, q, k, v):
    tokens, width = q.shape
    pairs = width // LANES
    own = lambda p, i, *_: (i, p)
    whole = lambda p, i, *_: (0, p)
    return pl.pallas_call(
        attend_kernel,
        grid_spec=pltpu.PrefetchScalarGridSpec(
            num_scalar_prefetch=1,
            grid=(pairs, tokens // ROWS),
            in_specs=[
                pl.BlockSpec((ROWS, LANES), own),
                pl.BlockSpec((tokens, LANES), whole),
                pl.BlockSpec((tokens, LANES), whole),
            ],
            out_specs=[
                pl.BlockSpec((ROWS, LANES), own),
                pl.BlockSpec((1, 2, ROWS), lambda p, i, *_: (p, 0, i)),
            ],
            scratch_shapes=[
                pltpu.VMEM((2, tokens, LANES), low_type),
                pltpu.VMEM((LANES, tokens), low_type),
            ],
        ),
        out_shape=[
            jax.ShapeDtypeStruct((tokens, width), low_type),
            jax.ShapeDtypeStruct((pairs, 2, tokens), jnp.float32),
        ],
        compiler_params=pltpu.CompilerParams(vmem_limit_bytes=vmem),
        cost_estimate=pl.CostEstimate(
            flops=16 * tokens * tokens * width, bytes_accessed=8 * tokens * width, transcendentals=tokens * tokens * width // HD
        ),
    )(length, q, k, v)


def rotate_back(grads, cosine, sine):
    return grads * cosine + swap_halves(grads * sine)


def attend_back_kernel(first_pair, length_ref, q_ref, k_ref, v_ref, d_ref, log_ref, cosq_ref, sinq_ref, cos_ref, sin_ref, *rest):
    dq_ref, dk_ref, dv_ref, keys, values, turned, dk_total, dv_total = rest[-8:]
    tokens = k_ref.shape[0]
    step = pl.program_id(1)

    @pl.when(step == 0)
    def _():
        bias = key_bias(length_ref, tokens)
        lanes = pair_lanes((tokens, LANES))
        for half in range(2):
            keys[half] = head_keys(k_ref[...], bias, half)
            values[half] = jnp.where(lanes // HD == half, v_ref[...], jnp.zeros_like(v_ref[...]))
        turned[...] = k_ref[...].T
        dk_total[...] = jnp.zeros_like(dk_total)
        dv_total[...] = jnp.zeros_like(dv_total)

    d = d_ref[...]
    lanes = pair_lanes(d.shape)
    parts = []
    dk = dv = None
    for half in range(2):
        scores = transposed_dot(keys[half], head_queries(q_ref[...], half, 1.0))
        probs = jnp.exp(scores - log_ref[0, half : half + 1, :])
        dprobs = transposed_dot(values[half], d)
        inner = jnp.sum(probs * dprobs, axis=0, keepdims=True)
        dscore = (probs * (dprobs - inner)).astype(low_type)
        parts.append(jnp.dot(turned[half * HD : (half + 1) * HD, :], dscore, preferred_element_type=jnp.float32))
        one_k = jnp.dot(dscore, head_queries(q_ref[...], half, 0.0), preferred_element_type=jnp.float32)
        one_v = jnp.dot(
            probs.astype(low_type), jnp.where(lanes // HD == half, d, jnp.zeros_like(d)), preferred_element_type=jnp.float32
        )
        dk = one_k if dk is None else dk + one_k
        dv = one_v if dv is None else dv + one_v
    dk_total[...] += dk
    dv_total[...] += dv
    dq = jnp.concatenate(parts, axis=0).T * (1.0 / math.sqrt(HD))
    dq_ref[...] = rotate_back(dq, cosq_ref[...], sinq_ref[...]).astype(low_type)

    @pl.when(step == pl.num_programs(1) - 1)
    def _():
        dk_ref[...] = rotate_back(dk_total[...], cos_ref[...], sin_ref[...]).astype(low_type)
        dv_ref[...] = dv_total[...].astype(low_type)


def attend_back(length, q, k, v, d, logs, cosine, sine, first_pair, pairs, after=()):
    tokens, width = q.shape
    own = lambda p, i, *_: (i, first_pair + p)
    whole = lambda p, i, *_: (0, first_pair + p)
    low = jax.ShapeDtypeStruct((tokens, pairs * LANES), low_type)
    fixed = pl.BlockSpec((tokens, LANES), lambda p, i, *_: (0, 0))
    row = pl.BlockSpec((ROWS, LANES), lambda p, i, *_: (i, 0))
    return pl.pallas_call(
        functools.partial(attend_back_kernel, first_pair),
        grid_spec=pltpu.PrefetchScalarGridSpec(
            num_scalar_prefetch=1,
            grid=(pairs, tokens // ROWS),
            in_specs=[
                pl.BlockSpec((ROWS, LANES), own),
                pl.BlockSpec((tokens, LANES), whole),
                pl.BlockSpec((tokens, LANES), whole),
                pl.BlockSpec((ROWS, LANES), own),
                pl.BlockSpec((1, 2, ROWS), lambda p, i, *_: (first_pair + p, 0, i)),
                row,
                row,
                fixed,
                fixed,
            ]
            + [pl.BlockSpec(memory_space=pl.ANY)] * len(after),
            out_specs=[
                pl.BlockSpec((ROWS, LANES), lambda p, i, *_: (i, p)),
                pl.BlockSpec((tokens, LANES), lambda p, i, *_: (0, p)),
                pl.BlockSpec((tokens, LANES), lambda p, i, *_: (0, p)),
            ],
            scratch_shapes=[
                pltpu.VMEM((2, tokens, LANES), low_type),
                pltpu.VMEM((2, tokens, LANES), low_type),
                pltpu.VMEM((LANES, tokens), low_type),
                pltpu.VMEM((tokens, LANES), jnp.float32),
                pltpu.VMEM((tokens, LANES), jnp.float32),
            ],
        ),
        out_shape=[low, low, low],
        compiler_params=pltpu.CompilerParams(vmem_limit_bytes=vmem),
        cost_estimate=pl.CostEstimate(
            flops=40 * tokens * tokens * pairs * LANES,
            bytes_accessed=16 * tokens * pairs * LANES,
            transcendentals=tokens * tokens * pairs * 2,
        ),
    )(length, q, k, v, d, logs, cosine, sine, cosine, sine, *after)


def blank(shape, dtype):
    return pl.pallas_call(
        lambda out_ref: None,
        out_shape=jax.ShapeDtypeStruct(shape, dtype),
        out_specs=pl.BlockSpec(memory_space=pl.ANY),
    )()


def lookup_kernel(starts_ref, places_ref, order_ref, table_ref, out_ref, rows):
    count = out_ref.shape[0]
    owned = starts_ref[starts_ref.shape[0] - 1]
    for start in range(0, count, CHUNK):
        rows[start : start + CHUNK, :] = jnp.zeros((CHUNK, rows.shape[1]), jnp.float32)

    def eight(step, carry):
        for j in range(8):
            i = step * 8 + j
            valid = i < owned
            source = jnp.where(valid, places_ref[i], 0)
            target = jnp.where(valid, order_ref[i], count)
            rows[pl.ds(target, 1), :] = table_ref[pl.ds(source, 1), :]
        return carry

    lax.fori_loop(0, (owned + 7) // 8, eight, 0)
    for start in range(0, count, CHUNK):
        out_ref[start : start + CHUNK, :] = rows[start : start + CHUNK, :].astype(low_type)


def lookup(starts, places, order, table):
    count = places.shape[0]
    width = table.shape[1]
    return pl.pallas_call(
        lookup_kernel,
        grid_spec=pltpu.PrefetchScalarGridSpec(
            num_scalar_prefetch=3,
            grid=(1,),
            in_specs=[pl.BlockSpec(table.shape, lambda i, *_: (0, 0), pipeline_mode=pl.Buffered(1))],
            out_specs=pl.BlockSpec((count, width), lambda i, *_: (0, 0), pipeline_mode=pl.Buffered(1)),
            scratch_shapes=[pltpu.VMEM((count + 8, width), jnp.float32)],
        ),
        out_shape=jax.ShapeDtypeStruct((count, width), low_type),
        compiler_params=pltpu.CompilerParams(vmem_limit_bytes=vmem),
        cost_estimate=pl.CostEstimate(flops=0, bytes_accessed=table.size * 12, transcendentals=0),
    )(starts, places, order, table)


def table_grad_kernel(core_ref, starts_ref, places_ref, order_ref, dlogits_ref, chosen_ref, embed_ref, sent_ref, kept_ref, rows, total):
    step = pl.program_id(0)
    half = pl.num_programs(0) // 2
    count, width = embed_ref.shape
    block = kept_ref.shape[1]
    tiles = width // LANES

    @pl.when(step == 0)
    def _():
        for start in range(0, count, CHUNK):
            some = embed_ref[start : start + CHUNK, :].astype(jnp.float32)
            for j in range(tiles):
                rows[pl.ds(start * 8 + j, CHUNK, stride=8), :] = some[:, j * LANES : (j + 1) * LANES]

    product = jnp.dot(dlogits_ref[...], chosen_ref[...], preferred_element_type=jnp.float32)
    for j in range(tiles):
        total[pl.ds(j, block, stride=8), :] = product[:, j * LANES : (j + 1) * LANES]
    side = jnp.where(step < half, 1 - core_ref[0], core_ref[0])
    chunk = 2 * (step % half) + side
    base = chunk * block
    first, last = starts_ref[chunk], starts_ref[chunk + 1]

    def eight(turn, carry):
        for j in range(8):
            i = first + turn * 8 + j
            at = jnp.minimum(i, count - 1)
            place = jnp.where(i < last, places_ref[at] - base, block)
            to = pl.ds(pl.multiple_of(place * 8, 8), 8)
            total[to, :] += rows[pl.ds(pl.multiple_of(order_ref[at] * 8, 8), 8), :]
        return carry

    lax.fori_loop(0, (last - first + 7) // 8, eight, 0)
    result = [total[pl.ds(j, block, stride=8), :] for j in range(tiles)]

    @pl.when(step < half)
    def _():
        for j in range(tiles):
            sent_ref[0, :, j * LANES : (j + 1) * LANES] = result[j].astype(sent_ref.dtype)

    @pl.when(step >= half)
    def _():
        for j in range(tiles):
            kept_ref[0, :, j * LANES : (j + 1) * LANES] = result[j]


def table_grad_halves(core, starts, places, order, dlogits, chosen, embed, block, dtype):
    count, width = embed.shape
    picked = chosen.shape[0]
    half = dlogits.shape[0] // block // 2
    fixed = lambda i, *_: (0, 0)

    def chunk_at(i, core, *_):
        return (2 * (i % half) + jnp.where(i < half, 1 - core[0], core[0]), 0)

    return pl.pallas_call(
        table_grad_kernel,
        grid_spec=pltpu.PrefetchScalarGridSpec(
            num_scalar_prefetch=4,
            grid=(2 * half,),
            in_specs=[
                pl.BlockSpec((block, picked), chunk_at),
                pl.BlockSpec((picked, width), fixed),
                pl.BlockSpec((count, width), fixed, pipeline_mode=pl.Buffered(1)),
            ],
            out_specs=[
                pl.BlockSpec((1, block, width), lambda i, *_: (jnp.minimum(i, half - 1), 0, 0)),
                pl.BlockSpec((1, block, width), lambda i, *_: (jnp.maximum(i - half, 0), 0, 0)),
            ],
            scratch_shapes=[
                pltpu.VMEM((count * 8, LANES), jnp.float32),
                pltpu.VMEM((block * 8 + 8, LANES), jnp.float32),
            ],
        ),
        out_shape=[
            jax.ShapeDtypeStruct((half, block, width), dtype),
            jax.ShapeDtypeStruct((half, block, width), jnp.float32),
        ],
        compiler_params=pltpu.CompilerParams(vmem_limit_bytes=vmem),
        cost_estimate=pl.CostEstimate(
            flops=4 * half * block * picked * width, bytes_accessed=16 * half * block * width, transcendentals=0
        ),
    )(core, starts, places, order, dlogits, chosen, embed)


def update_kernel(parts, slots_ref, scalars_ref, *rest):
    pieces = rest[: 4 * parts]
    table_ref, rows_ref, cols_ref = rest[4 * parts : 4 * parts + 3]
    grad_ref, new_ref, rows_new_ref = rest[-3:]
    factor, rate = scalars_ref[0], scalars_ref[1]
    decay = 1.0 - float(STEP) ** (-0.8)
    old = jnp.broadcast_to(rows_ref[0], (LANES, TILE)).T[:, 0:1]
    for part in range(4):

        @pl.when(pl.program_id(0) == part)
        def _(part=part):
            own = pieces[part * parts : (part + 1) * parts]
            gradient = jnp.concatenate([piece[...] for piece in own], axis=1).astype(jnp.float32)
            means = jnp.mean(gradient * gradient, axis=1, keepdims=True)
            rows_new = decay * old + (1.0 - decay) * (means * factor * factor)
            grad_ref[...] = gradient * factor
            new_ref[...] = table_ref[...] - gradient * (rate * lax.rsqrt(rows_new)) * cols_ref[...]
            rows_new_ref[0] = jnp.broadcast_to(rows_new, (TILE, LANES)).T[0:1, :]


def update(slots, scalars, pieces, table, rows, cols, so_far):
    parts = len(pieces[0])
    block = pieces[0][0].shape[0]
    width = table.shape[1]
    steps = block // TILE
    place = lambda p, i, slots: (slots[p] * steps + i, 0)
    place3 = lambda p, i, slots: (slots[p] * steps + i, 0, 0)

    def own(part):
        return lambda p, i, slots: (jnp.where(p < part, 0, jnp.where(p > part, steps - 1, i)), 0)

    fixed = lambda p, i, slots: (0, 0)
    any_space = pl.BlockSpec(memory_space=pl.ANY)
    given = 5 + 4 * parts
    return pl.pallas_call(
        functools.partial(update_kernel, parts),
        grid_spec=pltpu.PrefetchScalarGridSpec(
            num_scalar_prefetch=1,
            grid=(4, steps),
            in_specs=[pl.BlockSpec(memory_space=pltpu.SMEM)]
            + [pl.BlockSpec((TILE, piece.shape[1]), own(part)) for part in range(4) for piece in pieces[part]]
            + [
                pl.BlockSpec((TILE, width), place),
                pl.BlockSpec((1, 1, TILE), place3),
                pl.BlockSpec((1, width), fixed),
                any_space,
                any_space,
                any_space,
            ],
            out_specs=[
                pl.BlockSpec((TILE, width), place),
                pl.BlockSpec((TILE, width), place),
                pl.BlockSpec((1, 1, TILE), place3),
            ],
        ),
        out_shape=[jax.ShapeDtypeStruct(part.shape, part.dtype) for part in so_far],
        input_output_aliases={given: 0, given + 1: 1, given + 2: 2},
        compiler_params=pltpu.CompilerParams(vmem_limit_bytes=vmem),
        cost_estimate=pl.CostEstimate(
            flops=40 * block * width, bytes_accessed=56 * block * width, transcendentals=4 * block * width
        ),
    )(slots, scalars, *[piece for four in pieces for piece in four], table, rows, cols, *so_far)


def stack_kernel(slots_ref, *refs):
    pieces, out_ref = refs[:-1], refs[-1]
    for place, piece in enumerate(pieces):

        @pl.when(pl.program_id(0) == place)
        def _(piece=piece):
            out_ref[0] = piece[...]


def lay_out(slots, pieces):
    shape = pieces[0].shape
    return pl.pallas_call(
        stack_kernel,
        grid_spec=pltpu.PrefetchScalarGridSpec(
            num_scalar_prefetch=1,
            grid=(len(pieces),),
            in_specs=[pl.BlockSpec(shape, lambda i, slots: (0, 0), pipeline_mode=pl.Buffered(1))] * len(pieces),
            out_specs=pl.BlockSpec((1,) + shape, lambda i, slots: (slots[i], 0, 0)),
        ),
        out_shape=jax.ShapeDtypeStruct((len(pieces),) + shape, pieces[0].dtype),
        compiler_params=pltpu.CompilerParams(vmem_limit_bytes=vmem),
        cost_estimate=pl.CostEstimate(flops=0, bytes_accessed=4 * len(pieces) * pieces[0].size, transcendentals=0),
    )(slots, *pieces)


def columns_kernel(members_ref, slots_ref, own_ref, *refs):
    pieces, out_ref = refs[:-1], refs[-1]
    rows = own_ref.shape[0]

    def at(offset):
        return pl.ds(pl.multiple_of(members_ref[offset] * rows, rows), rows)

    out_ref[at(0), :] = own_ref[...].astype(low_type)
    for place, piece in enumerate(pieces):

        @pl.when(pl.program_id(0) == place)
        def _(piece=piece):
            for offset in range(piece.shape[0]):
                out_ref[at(offset + 1), :] = piece[offset]


def lay_columns(members, slots, own, pieces):
    others, rows, columns = pieces[0].shape
    replicas = len(pieces)
    whole = jax.ShapeDtypeStruct(((others + 1) * rows, replicas * columns), low_type)
    return pl.pallas_call(
        columns_kernel,
        grid_spec=pltpu.PrefetchScalarGridSpec(
            num_scalar_prefetch=2,
            grid=(replicas,),
            in_specs=[pl.BlockSpec((rows, columns), lambda i, members, slots: (0, slots[i]))]
            + [pl.BlockSpec(pieces[0].shape, lambda i, *_: (0, 0, 0), pipeline_mode=pl.Buffered(1))] * replicas,
            out_specs=pl.BlockSpec(((others + 1) * rows, columns), lambda i, members, slots: (0, slots[i])),
        ),
        out_shape=whole,
        compiler_params=pltpu.CompilerParams(vmem_limit_bytes=vmem),
        cost_estimate=pl.CostEstimate(flops=0, bytes_accessed=4 * whole.size, transcendentals=0),
    )(members, slots, own, *pieces)


def rows_kernel(members_ref, slots_ref, own_ref, *refs):
    pieces, out_ref = refs[:-1], refs[-1]
    out_ref[members_ref[0], 0] = own_ref[0].astype(low_type)
    for place, piece in enumerate(pieces):

        @pl.when(pl.program_id(0) == place)
        def _(piece=piece):
            for offset in range(piece.shape[0]):
                out_ref[members_ref[offset + 1], 0] = piece[offset]


def lay_rows(members, slots, own, pieces):
    others, rows, columns = pieces[0].shape
    replicas = len(pieces)
    whole = jax.ShapeDtypeStruct((others + 1, replicas, rows, columns), low_type)
    return pl.pallas_call(
        rows_kernel,
        grid_spec=pltpu.PrefetchScalarGridSpec(
            num_scalar_prefetch=2,
            grid=(replicas,),
            in_specs=[pl.BlockSpec((1, rows, columns), lambda i, members, slots: (slots[i], 0, 0))]
            + [pl.BlockSpec(pieces[0].shape, lambda i, *_: (0, 0, 0), pipeline_mode=pl.Buffered(1))] * replicas,
            out_specs=pl.BlockSpec((others + 1, 1, rows, columns), lambda i, members, slots: (0, slots[i], 0, 0)),
        ),
        out_shape=whole,
        compiler_params=pltpu.CompilerParams(vmem_limit_bytes=vmem),
        cost_estimate=pl.CostEstimate(flops=0, bytes_accessed=4 * whole.size, transcendentals=0),
    )(members, slots, own.reshape(replicas, rows, columns), *pieces).reshape(-1, columns)


tie = lax.optimization_barrier


def flip(value, bit):
    size = lax.axis_size("rep")
    return lax.ppermute(value, "rep", [(i, i ^ bit) for i in range(size)])


def turn(value, offset):
    size = lax.axis_size("grp")
    return lax.ppermute(value, "grp", [(i, (i + offset) % size) for i in range(size)])


def spread(piece, order):
    have = {0: piece}
    for bit in order:
        have.update({place ^ bit: flip(part, bit) for place, part in have.items()})
    return have


def slots_of():
    return lax.axis_index("rep") ^ jnp.arange(lax.axis_size("rep"), dtype=jnp.int32)


def plane_gather(piece):
    if lax.axis_size("rep") != 8:
        return lax.all_gather(piece, "rep")
    have = spread(piece, [2, 4, 1])
    return lay_out(slots_of(), [have[place] for place in range(8)])


def halve(value, axis, bit):
    mine = (lax.axis_index("rep") // bit) % 2
    kept = lax.dynamic_index_in_dim(value, mine, axis, keepdims=False)
    sent = lax.dynamic_index_in_dim(value, 1 - mine, axis, keepdims=False)
    return kept, sent.astype(low_type)


class Fold:
    def __init__(self, axis, order):
        self.axis = axis
        self.order = order
        self.quick = lax.axis_size("rep") == 8

    def cores(self, chunks):
        axis = self.axis
        if not self.quick:
            self.value = lax.psum_scatter(chunks, "rep", scatter_dimension=axis)
            return []
        shape = chunks.shape
        kept, sent = halve(chunks.reshape(shape[:axis] + (4, 2) + shape[axis + 1 :]), axis + 1, 1)
        return self.from_cores(kept, sent)

    def from_cores(self, kept, sent):
        self.kept, self.got = kept, flip(sent, 1)
        return [sent]

    def sum(self):
        return self.kept + self.got.astype(jnp.float32) if self.quick else self.value

    def plane(self, first):
        if not self.quick:
            return []
        value = self.sum()
        axis = self.axis
        bit = self.order[0 if first else 1]
        if first:
            shape = value.shape
            value = value.reshape(shape[:axis] + (2, 2) + shape[axis + 1 :])
            axis = axis + (1 if bit == 2 else 0)
        self.kept, sent = halve(value, axis, bit)
        self.got = flip(sent, bit)
        return [sent]

    def members(self):
        value = self.sum()
        member = lax.axis_index("grp")
        size = lax.axis_size("grp")
        self.own = lax.dynamic_index_in_dim(value, member, 0, keepdims=False)
        sent = [
            lax.dynamic_index_in_dim(value, (member + offset) % size, 0, keepdims=False).astype(low_type)
            for offset in range(1, size)
        ]
        self.came = [turn(part, offset + 1) for offset, part in enumerate(sent)]
        return sent

    def total(self):
        return sum((came.astype(jnp.float32) for came in self.came), self.own)


def gradient_chunks(gradient):
    groups = lax.axis_size("grp")
    replicas = lax.axis_size("rep")
    rows, columns = gradient.shape
    return gradient.reshape(groups, replicas, rows // (groups * replicas), columns)


def across_wide(chunks):
    member = lax.axis_index("grp")
    size = lax.axis_size("grp")
    total = lax.dynamic_index_in_dim(chunks, member, 0, keepdims=False)
    for offset in range(1, size):
        sent = lax.dynamic_index_in_dim(chunks, (member + offset) % size, 0, keepdims=False)
        total = total + turn(sent, offset)
    return total


def group_gather(value):
    member = lax.axis_index("grp")
    size = lax.axis_size("grp")
    result = jnp.zeros((size,) + value.shape, value.dtype)
    result = lax.dynamic_update_index_in_dim(result, value, member, 0)
    for offset in range(1, size):
        result = lax.dynamic_update_index_in_dim(
            result, turn(value, offset), (member + size - offset) % size, 0
        )
    return result


def plane_sum(value):
    for j in range(1, lax.axis_size("rep").bit_length() - 1):
        value = value + flip(value, 1 << j)
    return value


def rest_sum(value):
    value = value + flip(value, 1)
    size = lax.axis_size("grp")
    for j in range(size.bit_length() - 1):
        value = value + lax.ppermute(value, "grp", [(i, i ^ (1 << j)) for i in range(size)])
    return value


def fetch(own):
    return jnp.stack([turn(own, offset) for offset in range(1, lax.axis_size("grp"))])


def cut(value, axis):
    replicas = lax.axis_size("rep")
    size = value.shape[axis] // replicas
    return lax.dynamic_slice_in_dim(value, lax.axis_index("rep") * size, size, axis)


def members_of():
    groups = lax.axis_size("grp")
    return (lax.axis_index("grp") + groups - jnp.arange(groups, dtype=jnp.int32)) % groups


def contract(left, right, left_dim, right_dim):
    return lax.dot_general(
        left, right, (((left_dim,), (right_dim,)), ((), ())), preferred_element_type=jnp.float32
    )


def layer_norm(values, gain, shift):
    center = values - jnp.mean(values, axis=-1, keepdims=True)
    spread = jnp.mean(center * center, axis=-1, keepdims=True)
    return center * lax.rsqrt(spread + ln_eps) * gain + shift


def rope_tables(length):
    freqs = rope_base ** (-jnp.arange(HD // 2, dtype=jnp.float32) * 2.0 / HD)
    angles = jnp.arange(length, dtype=jnp.float32)[:, None] * freqs[None, :]
    cosine, sine = jnp.cos(angles), jnp.sin(angles)
    return (
        jnp.concatenate([cosine] * 4, axis=-1),
        jnp.concatenate([-sine, sine, -sine, sine], axis=-1),
    )


def swiglu(joined):
    middle = joined.shape[-1] // 2
    return jax.nn.silu(joined[:, :middle]) * joined[:, middle:]


def merge_stats(first_part, second_part):
    peak = jnp.maximum(first_part[0], second_part[0])
    spread = first_part[1] * jnp.exp(first_part[0] - peak) + second_part[1] * jnp.exp(
        second_part[0] - peak
    )
    return (peak, spread, first_part[2] + second_part[2])


def body(
    ids,
    lengths,
    picks,
    labels,
    loss_mask,
    table,
    w_qkv,
    w_out,
    w_gu,
    w_down,
    norms,
    table_rows,
    table_cols,
    qkv_rows,
    qkv_cols,
    out_rows,
    out_cols,
    gu_rows,
    gu_cols,
    down_rows,
    down_cols,
    norms_moment,
):
    member = lax.axis_index("grp")
    groups = lax.axis_size("grp")
    replica = lax.axis_index("rep")
    replicas = lax.axis_size("rep")
    seqs, length = ids.shape
    width = table.shape[1]
    vocab_rows = table.shape[0]
    own_rows = seqs * picks.shape[1]
    tokens = seqs * length
    block = -(-vocab_rows // (16 * replicas)) * 16
    padded = block * replicas

    packed = jnp.concatenate([ids.reshape(-1), labels.reshape(-1), loss_mask.reshape(-1)])
    group_packed = group_gather(packed)
    group_ids = group_packed[:, :tokens].reshape(-1)
    group_labels = group_packed[:, tokens : tokens + own_rows].reshape(-1)
    group_mask = group_packed[:, tokens + own_rows :].reshape(-1)
    shard_rows = w_qkv.shape[0]
    quick = replicas == 8
    near_shard = jnp.concatenate([w_qkv, w_out], axis=1)
    if quick:
        near_part = fetch(cut(near_shard, 1).astype(low_type))
        gu_part = fetch(cut(w_gu, 1).astype(low_type))
        down_part = fetch(cut(w_down, 0).astype(low_type))

    local_ids = group_ids - member * vocab_rows
    owned = (local_ids >= 0) & (local_ids < vocab_rows)
    places, order = lax.sort(
        (jnp.where(owned, local_ids, padded), jnp.arange(local_ids.shape[0], dtype=jnp.int32)), num_keys=1
    )
    bounds = jnp.arange(replicas + 1, dtype=jnp.int32) * block
    starts = jnp.sum((places[None, :] < bounds[:, None]).astype(jnp.int32), axis=1)
    if quick:
        places, near_part = tie((places, near_part))
    found = lookup(starts, places, order, table)
    if quick:
        found, gu_part, down_part = tie((found, gu_part, down_part))
    embed = lax.psum_scatter(found, "grp", scatter_dimension=0, tiled=True)
    late_table, _ = lax.optimization_barrier((table, found))
    table_low = jnp.pad(late_table.astype(low_type), ((0, padded - vocab_rows), (0, 0)))

    if quick:
        members, slots = members_of(), slots_of()

        def shared(part, order):
            have = spread(part, order)
            return [have[place] for place in range(replicas)]

        near = lay_columns(members, slots, near_shard, shared(near_part, [4, 2, 1]))
        w_gu_low = lay_columns(members, slots, w_gu, shared(gu_part, [2, 4, 1]))
        w_down_low = lay_rows(members, slots, w_down, shared(down_part, [4, 2, 1]))
        embed, near, w_gu_low, w_down_low, table_low = tie((embed, near, w_gu_low, w_down_low, table_low))
    else:
        near = lax.all_gather(near_shard.astype(low_type), "grp", tiled=True)
        w_gu_low = lax.all_gather(w_gu.astype(low_type), "grp", tiled=True)
        w_down_low = lax.all_gather(w_down.astype(low_type), "grp", tiled=True)
    w_out_low = near[:, 3 * width :]
    cosine, sine = rope_tables(length)
    first, first_low, queries, keys, values = project(embed, norms, cosine, sine, near)
    queries, group_mask = tie((queries, group_mask))
    loss_count = jnp.sum(group_mask).astype(jnp.float32)[None]
    for j in range(replicas.bit_length() - 1):
        loss_count = loss_count + flip(loss_count, 1 << j)
    loss_count = loss_count[0]
    mixed_low, log_sums = attend(lengths, queries, keys, values)
    first_sum = first + jnp.dot(mixed_low, w_out_low, preferred_element_type=jnp.float32)
    second = layer_norm(first_sum, norms[2], norms[3])
    second_low = second.astype(low_type)
    gate_up = jnp.dot(second_low, w_gu_low, preferred_element_type=jnp.float32)
    hidden_low = swiglu(gate_up).astype(low_type)
    second_sum = second + jnp.dot(hidden_low, w_down_low, preferred_element_type=jnp.float32)
    final = layer_norm(second_sum, norms[4], norms[5])

    flat_picks = (jnp.arange(seqs, dtype=jnp.int32)[:, None] * length + picks).reshape(-1)
    chosen = final[flat_picks].astype(low_type)
    group_chosen = group_gather(chosen).reshape(groups * own_rows, width)
    rows_at = jnp.arange(padded, dtype=jnp.int32)[:, None]
    logits = jnp.where(rows_at < vocab_rows, contract(table_low, group_chosen, 1, 1), neg_large)
    peak = jnp.max(logits, axis=0)
    spread_sum = jnp.sum(jnp.exp(logits - peak[None, :]), axis=0)
    local_labels = group_labels - member * vocab_rows
    inside = (local_labels >= 0) & (local_labels < vocab_rows)
    hits = (rows_at == local_labels[None, :]) & inside[None, :]
    target = jnp.sum(jnp.where(hits, logits, 0.0), axis=0)
    stats = group_gather(jnp.stack([peak, spread_sum, target]))
    so_far = (stats[0, 0], stats[0, 1], stats[0, 2])
    for place in range(1, groups):
        so_far = merge_stats(so_far, (stats[place, 0], stats[place, 1], stats[place, 2]))
    peak_all, spread_all, target_all = so_far
    log_total = peak_all + jnp.log(spread_all)
    counted = group_mask > 0
    terms = jnp.where(counted, log_total - target_all, 0.0)
    own_terms = lax.dynamic_slice_in_dim(terms, member * own_rows, own_rows)
    row_scale = jnp.where(counted, 1.0 / loss_count, 0.0)
    dlogits = (
        (jnp.exp(logits - log_total[None, :]) - hits.astype(jnp.float32)) * row_scale[None, :]
    ).astype(low_type)
    chosen_part = contract(dlogits, table_low, 0, 0)
    chosen_grad = across_wide(chosen_part.reshape(groups, own_rows, width))
    final_grad = jnp.zeros((tokens, width), jnp.float32).at[flat_picks].add(chosen_grad)

    _, pull = jax.vjp(layer_norm, second_sum, norms[4], norms[5])
    sum_grad, gain_three, shift_three = pull(final_grad)
    branch_low = sum_grad.astype(low_type)
    down = Fold(1, (2, 4))
    down.cores(gradient_chunks(contract(hidden_low, branch_low, 0, 0)))
    hidden_grad = contract(branch_low, w_down_low, 1, 1)
    _, pull = jax.vjp(swiglu, gate_up)
    gate_low = pull(hidden_grad)[0].astype(low_type)
    gate_low, _ = tie((gate_low, down.plane(True)))
    gate, up = Fold(1, (4, 2)), Fold(1, (2, 4))
    middle = gate_up.shape[1] // 2
    sent = gate.cores(gradient_chunks(contract(second_low, gate_low[:, :middle], 0, 0)))
    sent += up.cores(gradient_chunks(contract(second_low, gate_low[:, middle:], 0, 0)))
    gate_low, _ = tie((gate_low, sent))
    second_grad = sum_grad + contract(gate_low, w_gu_low, 1, 1)
    second_grad, _ = tie((second_grad, gate.plane(True) + up.plane(True) + down.plane(False)))
    _, pull = jax.vjp(layer_norm, first_sum, norms[2], norms[3])
    first_sum_grad, gain_two, shift_two = pull(second_grad)
    attn_low = first_sum_grad.astype(low_type)
    mixed_grad = contract(attn_low, w_out_low, 1, 1).astype(low_type)
    pairs = width // LANES
    third = pairs // 3
    sides = []
    for stage in range(3):
        if stage:
            sent = gate.plane(False) + up.plane(False) + down.members() if stage == 1 else gate.members() + up.members()
            mixed_grad, sides[-1], _ = tie((mixed_grad, sides[-1], sent))
        sides.append(
            attend_back(lengths, queries, keys, values, mixed_grad, log_sums, cosine, sine, stage * third, third)
        )
    joined_grad = jnp.concatenate([side for parts in zip(*sides) for side in parts], axis=1)
    first_grad = first_sum_grad + contract(joined_grad, near[:, : 3 * width], 1, 1)
    _, pull = jax.vjp(layer_norm, embed.astype(jnp.float32), norms[0], norms[1])
    embed_grad, gain_one, shift_one = pull(first_grad)
    norm_grad = jnp.stack([gain_one, shift_one, gain_two, shift_two, gain_three, shift_three])
    wide = width // 3
    spans = [(part * wide, (part + 1) * wide) for part in range(3)]
    embed_low = embed_grad.astype(low_type)
    join_grad = contract(first_low, joined_grad, 0, 0)
    late_embed, join_grad = tie((embed_low, join_grad))
    join_grad = jnp.concatenate([join_grad, contract(mixed_low, attn_low, 0, 0)], axis=1)
    last_embed, join_grad = tie((late_embed, join_grad))
    group_embeds = [
        lax.all_gather(piece[:, begin:end], "grp", axis=0, tiled=True)
        for piece, (begin, end) in zip((embed_low, late_embed, last_embed), spans)
    ]
    join = Fold(1, (2, 4))
    join.cores(gradient_chunks(join_grad))
    sent = join.plane(True)
    gu_share = jnp.concatenate([gate.total(), up.total()], axis=1)
    down_share = down.total()
    part_rows = gu_share.shape[0]
    far_low = jnp.concatenate(
        [gu_share.astype(low_type), down_share.astype(low_type).reshape(part_rows, -1)], axis=1
    )
    if quick:
        far_got = spread(far_low, [2, 4, 1])
        group_embeds[0], _, _ = tie((group_embeds[0], sent, list(far_got.values())))
    core = replica % 2
    heads = [Fold(0, (4, 2) if part % 2 else (2, 4)) for part in range(3)]
    for part, (begin, end) in enumerate(spans):
        head = heads[part]
        if part == 1:
            group_embeds[1], _ = tie((group_embeds[1], heads[0].plane(True)))
        if part == 2:
            sent = heads[1].plane(True) + heads[0].plane(False) + join.plane(False)
            group_embeds[2], _ = tie((group_embeds[2], sent))
        half_args = (
            starts,
            places,
            order,
            dlogits,
            group_chosen[:, begin:end],
            group_embeds[part],
            block,
        )
        sent, kept = table_grad_halves(core[None], *half_args, low_type if quick else jnp.float32)
        if quick:
            head.from_cores(kept, sent)
        else:
            both = [jnp.where(core == j, kept, sent) for j in range(2)]
            head.cores(jnp.stack(both, axis=1).reshape(replicas, block, end - begin))
    heads[2].plane(True)
    heads[1].plane(False)
    heads[2].plane(False)
    join.members()
    table_parts = [head.sum() for head in heads]
    join_share = join.total()

    shares = (
        join_share[:, : 3 * width],
        join_share[:, 3 * width :],
        gu_share,
        down_share,
    )
    old_rows = (table_rows, qkv_rows, out_rows, gu_rows, down_rows)
    old_cols = (table_cols, qkv_cols, out_cols, gu_cols, down_cols)
    masters = (table, w_qkv, w_out, w_gu, w_down)
    col_parts = [
        jnp.concatenate([jnp.sum(gradient * gradient, axis=0) for gradient in table_parts])
    ] + [jnp.sum(gradient * gradient, axis=0) for gradient in shares]
    row_old = jnp.stack([jnp.sum(rows) for rows in old_rows]) / replicas
    small = [norm_grad.reshape(-1)] + col_parts + [row_old, jnp.sum(own_terms)[None]]
    plane_totals = plane_sum(jnp.concatenate(small))
    table_lows = [table_parts[0].astype(low_type), jnp.concatenate(table_parts[1:], axis=1).astype(low_type)]
    plane_totals, table_lows = tie((plane_totals, table_lows))
    totals = rest_sum(plane_totals)
    cuts = []
    start = 0
    for part in small:
        cuts.append(totals[start : start + part.shape[0]])
        start += part.shape[0]
    norm_sum = cuts[0].reshape(norm_grad.shape)
    col_totals = cuts[1:6]
    old_totals = cuts[6]
    loss_sum = cuts[7][0]
    squares = [jnp.sum(part) for part in col_totals]
    clip_norm = jnp.sqrt(sum(squares) + jnp.sum(norm_sum * norm_sum))
    factor = clip_limit / jnp.maximum(clip_norm, clip_limit)
    decay = 1.0 - float(STEP) ** (-0.8)

    if quick:
        far_whole = lay_out(slots_of(), [far_got[place] for place in range(replicas)])
    else:
        far_whole = plane_gather(far_low)
    far_whole = far_whole.reshape(shard_rows, -1)
    near_whole = plane_gather(join_share.astype(low_type)).reshape(shard_rows, -1)
    wholes = [
        None,
        near_whole[:, : 3 * width],
        near_whole[:, 3 * width :],
        far_whole[:, : w_gu.shape[1]],
        far_whole[:, w_gu.shape[1] :].reshape(w_down.shape),
    ]

    outputs = []
    for place in range(5):
        rows, columns = masters[place].shape
        full_rows = rows * groups
        new_cols = (
            decay * old_cols[place] + (1.0 - decay) * (col_totals[place] * factor * factor) / full_rows
        )
        row_total = decay * old_totals[place] + (1.0 - decay) * (squares[place] * factor * factor) / columns
        row_mean = row_total / full_rows
        if place == 0 and quick:
            have = [
                spread(low, [2, 4, 1] if part % 2 else [4, 2, 1]) for part, low in enumerate(table_lows)
            ]
            tiles = padded // TILE
            row_tiles = jnp.pad(table_rows, (0, padded - vocab_rows), constant_values=1.0).reshape(tiles, 1, TILE)
            scalars = jnp.stack([factor, rate_matrix * factor * jnp.sqrt(row_mean)])
            so_far = (
                blank(table.shape, jnp.float32),
                blank(table.shape, jnp.float32),
                blank((tiles, 1, TILE), jnp.float32),
            )
            slots = slots_of()
            for four in ((0, 2, 4, 6), (1, 3, 5, 7)):
                so_far = update(
                    jnp.stack([slots[part] for part in four]),
                    scalars,
                    [[got[part] for got in have] for part in four],
                    table,
                    row_tiles,
                    lax.rsqrt(new_cols)[None, :],
                    so_far,
                )
            outputs.extend([so_far[0], so_far[2].reshape(-1)[:vocab_rows], new_cols, so_far[1]])
            continue
        if place == 0:
            whole = plane_gather(jnp.concatenate(table_lows, axis=1))
            gradient = whole.reshape(padded, width)[:vocab_rows].astype(jnp.float32)
        else:
            gradient = wholes[place].astype(jnp.float32)
        row_means = jnp.mean(gradient * gradient, axis=1)
        new_rows = decay * old_rows[place] + (1.0 - decay) * (row_means * factor * factor)
        clipped = gradient * factor
        scale = new_rows[:, None] * new_cols[None, :] / row_mean
        new_master = masters[place] - rate_matrix * clipped * lax.rsqrt(scale)
        outputs.extend([clipped, new_rows, new_cols, new_master])
    norm_clipped = norm_sum * factor
    moment_new = decay * norms_moment + (1.0 - decay) * norm_clipped * norm_clipped
    norms_new = norms - rate_norm * norm_clipped * lax.rsqrt(moment_new)
    return (
        (loss_sum, loss_count, clip_norm) + tuple(outputs) + (norm_clipped, moment_new, norms_new)
    )


def solution(mesh):
    in_specs = (
        P(("grp", "rep"), None),
        P(("grp", "rep")),
        P(("grp", "rep"), None),
        P(("grp", "rep"), None),
        P(("grp", "rep"), None),
        P("grp", None),
        P("grp", None),
        P("grp", None),
        P("grp", None),
        P("grp", None),
        P(),
        P("grp"),
        P(),
        P("grp"),
        P(),
        P("grp"),
        P(),
        P("grp"),
        P(),
        P("grp"),
        P(),
        P(),
    )
    out_specs = (
        P(),
        P(),
        P(),
        P("grp", None),
        P("grp"),
        P(),
        P("grp", None),
        P("grp", None),
        P("grp"),
        P(),
        P("grp", None),
        P("grp", None),
        P("grp"),
        P(),
        P("grp", None),
        P("grp", None),
        P("grp"),
        P(),
        P("grp", None),
        P("grp", None),
        P("grp"),
        P(),
        P("grp", None),
        P(),
        P(),
        P(),
    )
    return jax.shard_map(body, mesh=mesh, in_specs=in_specs, out_specs=out_specs, check_vma=False)
```

```python
import functools
import math

import jax
import jax.numpy as jnp
from jax import lax
from jax.experimental import pallas as pl
from jax.experimental.pallas import tpu as pltpu
from jax.sharding import PartitionSpec as P

HEADS = 12
HD = 64
STEP = 10
LANES = 128
ROWS = 256
CHUNK = 256
TILE = 480


ln_eps = 1e-05
rope_base = 10000.0
clip_limit = 0.01
rate_matrix = 0.03
rate_norm = 0.3
neg_large = -1e30
low_type = jnp.bfloat16
vmem = 56 * 1024 * 1024


def pair_lanes(shape):
    return lax.broadcasted_iota(jnp.int32, shape, len(shape) - 1)


def swap_halves(value):
    upper = (pair_lanes(value.shape) % HD) >= HD // 2
    return jnp.where(
        upper,
        pltpu.roll(value, HD // 2, axis=1),
        pltpu.roll(value, LANES - HD // 2, axis=1),
    )


def normalize(values, gain, shift):
    center = values - jnp.mean(values, axis=-1, keepdims=True)
    spread = jnp.mean(center * center, axis=-1, keepdims=True)
    return center * lax.rsqrt(spread + ln_eps) * gain + shift


def project_kernel(embed_ref, norms_ref, cosine_ref, sine_ref, w_ref, first_ref, low_ref, q_ref, k_ref, v_ref):
    first = normalize(embed_ref[...].astype(jnp.float32), norms_ref[0:1, :], norms_ref[1:2, :])
    first_ref[...] = first
    low = first.astype(low_type)
    low_ref[...] = low
    width = first.shape[1]
    cosine, sine = cosine_ref[...], sine_ref[...]
    for part, out_ref in enumerate((q_ref, k_ref)):
        joined = jnp.dot(low, w_ref[:, part * width : (part + 1) * width], preferred_element_type=jnp.float32)
        for start in range(0, width, LANES):
            piece = joined[:, start : start + LANES]
            out_ref[:, start : start + LANES] = (piece * cosine + swap_halves(piece) * sine).astype(low_type)
    v_ref[...] = jnp.dot(low, w_ref[:, 2 * width :], preferred_element_type=jnp.float32).astype(low_type)


def project(embed, norms, cosine, sine, weights):
    tokens, width = embed.shape
    row = lambda i: (i, 0)
    fixed = lambda i: (0, 0)
    low = jax.ShapeDtypeStruct((tokens, width), low_type)
    return pl.pallas_call(
        project_kernel,
        grid=(tokens // ROWS,),
        in_specs=[
            pl.BlockSpec((ROWS, width), row),
            pl.BlockSpec(norms.shape, fixed),
            pl.BlockSpec((ROWS, LANES), row),
            pl.BlockSpec((ROWS, LANES), row),
            pl.BlockSpec((width, 3 * width), fixed),
        ],
        out_specs=[pl.BlockSpec((ROWS, width), row)] * 5,
        out_shape=[jax.ShapeDtypeStruct((tokens, width), jnp.float32), low, low, low, low],
        compiler_params=pltpu.CompilerParams(vmem_limit_bytes=vmem),
        cost_estimate=pl.CostEstimate(flops=6 * tokens * width * width, bytes_accessed=20 * tokens * width, transcendentals=0),
    )(embed, norms, cosine, sine, weights)


def head_keys(k, bias, half):
    lanes = pair_lanes(k.shape)
    spare = HD - half * HD
    return jnp.where(lanes // HD == half, k, jnp.where(lanes == spare, bias, jnp.zeros_like(k)))


def head_queries(q, half, spare_value):
    lanes = pair_lanes(q.shape)
    spare = HD - half * HD
    scaled = q * jnp.asarray(1.0 / math.sqrt(HD), q.dtype)
    other = jnp.where(lanes == spare, jnp.full_like(q, spare_value), jnp.zeros_like(q))
    return jnp.where(lanes // HD == half, scaled, other)


def transposed_dot(left, right):
    return lax.dot_general(left, right, (((1,), (1,)), ((), ())), preferred_element_type=jnp.float32)


def key_bias(length_ref, tokens):
    place = lax.broadcasted_iota(jnp.int32, (tokens, LANES), 0)
    return jnp.where(place < length_ref[0], 0.0, neg_large).astype(low_type)


def attend_kernel(length_ref, q_ref, k_ref, v_ref, out_ref, log_ref, keys, turned):
    tokens = k_ref.shape[0]

    @pl.when(pl.program_id(1) == 0)
    def _():
        bias = key_bias(length_ref, tokens)
        for half in range(2):
            keys[half] = head_keys(k_ref[...], bias, half)
        turned[...] = v_ref[...].T

    parts = []
    for half in range(2):
        scores = transposed_dot(keys[half], head_queries(q_ref[...], half, 1.0))
        peak = jnp.max(scores, axis=0, keepdims=True)
        weights = jnp.exp(scores - peak)
        totals = jnp.sum(weights, axis=0, keepdims=True)
        probs = (weights * (1.0 / totals)).astype(low_type)
        parts.append(
            jnp.dot(turned[half * HD : (half + 1) * HD, :], probs, preferred_element_type=jnp.float32)
        )
        log_ref[0, half : half + 1, :] = peak + jnp.log(totals)
    out_ref[...] = jnp.concatenate(parts, axis=0).T.astype(low_type)


def attend(length, q, k, v):
    tokens, width = q.shape
    pairs = width // LANES
    own = lambda p, i, *_: (i, p)
    whole = lambda p, i, *_: (0, p)
    return pl.pallas_call(
        attend_kernel,
        grid_spec=pltpu.PrefetchScalarGridSpec(
            num_scalar_prefetch=1,
            grid=(pairs, tokens // ROWS),
            in_specs=[
                pl.BlockSpec((ROWS, LANES), own),
                pl.BlockSpec((tokens, LANES), whole),
                pl.BlockSpec((tokens, LANES), whole),
            ],
            out_specs=[
                pl.BlockSpec((ROWS, LANES), own),
                pl.BlockSpec((1, 2, ROWS), lambda p, i, *_: (p, 0, i)),
            ],
            scratch_shapes=[
                pltpu.VMEM((2, tokens, LANES), low_type),
                pltpu.VMEM((LANES, tokens), low_type),
            ],
        ),
        out_shape=[
            jax.ShapeDtypeStruct((tokens, width), low_type),
            jax.ShapeDtypeStruct((pairs, 2, tokens), jnp.float32),
        ],
        compiler_params=pltpu.CompilerParams(vmem_limit_bytes=vmem),
        cost_estimate=pl.CostEstimate(
            flops=16 * tokens * tokens * width, bytes_accessed=8 * tokens * width, transcendentals=tokens * tokens * width // HD
        ),
    )(length, q, k, v)


def rotate_back(grads, cosine, sine):
    return grads * cosine + swap_halves(grads * sine)


def attend_back_kernel(first_pair, length_ref, q_ref, k_ref, v_ref, d_ref, log_ref, cosq_ref, sinq_ref, cos_ref, sin_ref, *rest):
    dq_ref, dk_ref, dv_ref, keys, values, turned, dk_total, dv_total = rest[-8:]
    tokens = k_ref.shape[0]
    step = pl.program_id(1)

    @pl.when(step == 0)
    def _():
        bias = key_bias(length_ref, tokens)
        lanes = pair_lanes((tokens, LANES))
        for half in range(2):
            keys[half] = head_keys(k_ref[...], bias, half)
            values[half] = jnp.where(lanes // HD == half, v_ref[...], jnp.zeros_like(v_ref[...]))
        turned[...] = k_ref[...].T
        dk_total[...] = jnp.zeros_like(dk_total)
        dv_total[...] = jnp.zeros_like(dv_total)

    d = d_ref[...]
    lanes = pair_lanes(d.shape)
    parts = []
    dk = dv = None
    for half in range(2):
        scores = transposed_dot(keys[half], head_queries(q_ref[...], half, 1.0))
        probs = jnp.exp(scores - log_ref[0, half : half + 1, :])
        dprobs = transposed_dot(values[half], d)
        inner = jnp.sum(probs * dprobs, axis=0, keepdims=True)
        dscore = (probs * (dprobs - inner)).astype(low_type)
        parts.append(jnp.dot(turned[half * HD : (half + 1) * HD, :], dscore, preferred_element_type=jnp.float32))
        one_k = jnp.dot(dscore, head_queries(q_ref[...], half, 0.0), preferred_element_type=jnp.float32)
        one_v = jnp.dot(
            probs.astype(low_type), jnp.where(lanes // HD == half, d, jnp.zeros_like(d)), preferred_element_type=jnp.float32
        )
        dk = one_k if dk is None else dk + one_k
        dv = one_v if dv is None else dv + one_v
    dk_total[...] += dk
    dv_total[...] += dv
    dq = jnp.concatenate(parts, axis=0).T * (1.0 / math.sqrt(HD))
    dq_ref[...] = rotate_back(dq, cosq_ref[...], sinq_ref[...]).astype(low_type)

    @pl.when(step == pl.num_programs(1) - 1)
    def _():
        dk_ref[...] = rotate_back(dk_total[...], cos_ref[...], sin_ref[...]).astype(low_type)
        dv_ref[...] = dv_total[...].astype(low_type)


def attend_back(length, q, k, v, d, logs, cosine, sine, first_pair, pairs, after=()):
    tokens, width = q.shape
    own = lambda p, i, *_: (i, first_pair + p)
    whole = lambda p, i, *_: (0, first_pair + p)
    low = jax.ShapeDtypeStruct((tokens, pairs * LANES), low_type)
    fixed = pl.BlockSpec((tokens, LANES), lambda p, i, *_: (0, 0))
    row = pl.BlockSpec((ROWS, LANES), lambda p, i, *_: (i, 0))
    return pl.pallas_call(
        functools.partial(attend_back_kernel, first_pair),
        grid_spec=pltpu.PrefetchScalarGridSpec(
            num_scalar_prefetch=1,
            grid=(pairs, tokens // ROWS),
            in_specs=[
                pl.BlockSpec((ROWS, LANES), own),
                pl.BlockSpec((tokens, LANES), whole),
                pl.BlockSpec((tokens, LANES), whole),
                pl.BlockSpec((ROWS, LANES), own),
                pl.BlockSpec((1, 2, ROWS), lambda p, i, *_: (first_pair + p, 0, i)),
                row,
                row,
                fixed,
                fixed,
            ]
            + [pl.BlockSpec(memory_space=pl.ANY)] * len(after),
            out_specs=[
                pl.BlockSpec((ROWS, LANES), lambda p, i, *_: (i, p)),
                pl.BlockSpec((tokens, LANES), lambda p, i, *_: (0, p)),
                pl.BlockSpec((tokens, LANES), lambda p, i, *_: (0, p)),
            ],
            scratch_shapes=[
                pltpu.VMEM((2, tokens, LANES), low_type),
                pltpu.VMEM((2, tokens, LANES), low_type),
                pltpu.VMEM((LANES, tokens), low_type),
                pltpu.VMEM((tokens, LANES), jnp.float32),
                pltpu.VMEM((tokens, LANES), jnp.float32),
            ],
        ),
        out_shape=[low, low, low],
        compiler_params=pltpu.CompilerParams(vmem_limit_bytes=vmem),
        cost_estimate=pl.CostEstimate(
            flops=40 * tokens * tokens * pairs * LANES,
            bytes_accessed=16 * tokens * pairs * LANES,
            transcendentals=tokens * tokens * pairs * 2,
        ),
    )(length, q, k, v, d, logs, cosine, sine, cosine, sine, *after)


def blank(shape, dtype):
    return pl.pallas_call(
        lambda out_ref: None,
        out_shape=jax.ShapeDtypeStruct(shape, dtype),
        out_specs=pl.BlockSpec(memory_space=pl.ANY),
    )()


def lookup_kernel(starts_ref, places_ref, order_ref, table_ref, out_ref, rows):
    count = out_ref.shape[0]
    owned = starts_ref[starts_ref.shape[0] - 1]
    for start in range(0, count, CHUNK):
        rows[start : start + CHUNK, :] = jnp.zeros((CHUNK, rows.shape[1]), jnp.float32)

    def eight(step, carry):
        for j in range(8):
            i = step * 8 + j
            valid = i < owned
            source = jnp.where(valid, places_ref[i], 0)
            target = jnp.where(valid, order_ref[i], count)
            rows[pl.ds(target, 1), :] = table_ref[pl.ds(source, 1), :]
        return carry

    lax.fori_loop(0, (owned + 7) // 8, eight, 0)
    for start in range(0, count, CHUNK):
        out_ref[start : start + CHUNK, :] = rows[start : start + CHUNK, :].astype(low_type)


def lookup(starts, places, order, table):
    count = places.shape[0]
    width = table.shape[1]
    return pl.pallas_call(
        lookup_kernel,
        grid_spec=pltpu.PrefetchScalarGridSpec(
            num_scalar_prefetch=3,
            grid=(1,),
            in_specs=[pl.BlockSpec(table.shape, lambda i, *_: (0, 0), pipeline_mode=pl.Buffered(1))],
            out_specs=pl.BlockSpec((count, width), lambda i, *_: (0, 0), pipeline_mode=pl.Buffered(1)),
            scratch_shapes=[pltpu.VMEM((count + 8, width), jnp.float32)],
        ),
        out_shape=jax.ShapeDtypeStruct((count, width), low_type),
        compiler_params=pltpu.CompilerParams(vmem_limit_bytes=vmem),
        cost_estimate=pl.CostEstimate(flops=0, bytes_accessed=table.size * 12, transcendentals=0),
    )(starts, places, order, table)


def table_grad_kernel(core_ref, starts_ref, codes_ref, order_ref, dlogits_ref, chosen_ref, embed_ref, out_ref, rows, sums):
    step = pl.program_id(0)
    count, width = embed_ref.shape
    block = out_ref.shape[1]

    @pl.when(step == 0)
    def _():
        for start in range(0, count, CHUNK):
            rows[start : start + CHUNK, :] = embed_ref[start : start + CHUNK, :].astype(jnp.float32)

    sums[...] = jnp.zeros_like(sums)
    chunk = 2 * step + core_ref[0]
    first, last = starts_ref[chunk], starts_ref[chunk + 1]

    def eight(turn, running):
        for j in range(8):
            i = first + turn * 8 + j
            code = codes_ref[i]
            place = jnp.where(i < last, code >> 1, block)
            running = jnp.where(code & 1, running, 0.0) + rows[pl.ds(order_ref[i], 1), :]
            sums[pl.ds(place, 1), :] = running
        return running

    lax.fori_loop(0, (last - first + 7) // 8, eight, jnp.zeros((1, width), jnp.float32))
    product = jnp.dot(dlogits_ref[...], chosen_ref[...], preferred_element_type=jnp.float32)
    out_ref[0] = (product + sums[:block, :]).astype(out_ref.dtype)


def table_grad_half(core, starts, codes, order, dlogits, chosen, embed, block, dtype):
    count, width = embed.shape
    picked = chosen.shape[0]
    chunks = dlogits.shape[0] // block // 2
    fixed = lambda i, *_: (0, 0)
    return pl.pallas_call(
        table_grad_kernel,
        grid_spec=pltpu.PrefetchScalarGridSpec(
            num_scalar_prefetch=4,
            grid=(chunks,),
            in_specs=[
                pl.BlockSpec((block, picked), lambda i, core, *_: (2 * i + core[0], 0)),
                pl.BlockSpec((picked, width), fixed),
                pl.BlockSpec((count, width), fixed, pipeline_mode=pl.Buffered(1)),
            ],
            out_specs=pl.BlockSpec((1, block, width), lambda i, *_: (i, 0, 0)),
            scratch_shapes=[
                pltpu.VMEM((count, width), jnp.float32),
                pltpu.VMEM((block + 8, width), jnp.float32),
            ],
        ),
        out_shape=jax.ShapeDtypeStruct((chunks, block, width), dtype),
        compiler_params=pltpu.CompilerParams(vmem_limit_bytes=vmem),
        cost_estimate=pl.CostEstimate(
            flops=2 * chunks * block * picked * width, bytes_accessed=8 * chunks * block * width, transcendentals=0
        ),
    )(core, starts, codes, order, dlogits, chosen, embed)


def update_kernel(parts, slots_ref, scalars_ref, *rest):
    pieces = rest[: 4 * parts]
    table_ref, rows_ref, cols_ref = rest[4 * parts : 4 * parts + 3]
    grad_ref, new_ref, rows_new_ref = rest[-3:]
    factor, rate = scalars_ref[0], scalars_ref[1]
    decay = 1.0 - float(STEP) ** (-0.8)
    old = jnp.broadcast_to(rows_ref[0], (LANES, TILE)).T[:, 0:1]
    for part in range(4):

        @pl.when(pl.program_id(0) == part)
        def _(part=part):
            own = pieces[part * parts : (part + 1) * parts]
            gradient = jnp.concatenate([piece[...] for piece in own], axis=1).astype(jnp.float32)
            means = jnp.mean(gradient * gradient, axis=1, keepdims=True)
            rows_new = decay * old + (1.0 - decay) * (means * factor * factor)
            grad_ref[...] = gradient * factor
            new_ref[...] = table_ref[...] - gradient * (rate * lax.rsqrt(rows_new)) * cols_ref[...]
            rows_new_ref[0] = jnp.broadcast_to(rows_new, (TILE, LANES)).T[0:1, :]


def update(slots, scalars, pieces, table, rows, cols, so_far):
    parts = len(pieces[0])
    block = pieces[0][0].shape[0]
    width = table.shape[1]
    steps = block // TILE
    place = lambda p, i, slots: (slots[p] * steps + i, 0)
    place3 = lambda p, i, slots: (slots[p] * steps + i, 0, 0)

    def own(part):
        return lambda p, i, slots: (jnp.where(p < part, 0, jnp.where(p > part, steps - 1, i)), 0)

    fixed = lambda p, i, slots: (0, 0)
    any_space = pl.BlockSpec(memory_space=pl.ANY)
    given = 5 + 4 * parts
    return pl.pallas_call(
        functools.partial(update_kernel, parts),
        grid_spec=pltpu.PrefetchScalarGridSpec(
            num_scalar_prefetch=1,
            grid=(4, steps),
            in_specs=[pl.BlockSpec(memory_space=pltpu.SMEM)]
            + [pl.BlockSpec((TILE, piece.shape[1]), own(part)) for part in range(4) for piece in pieces[part]]
            + [
                pl.BlockSpec((TILE, width), place),
                pl.BlockSpec((1, 1, TILE), place3),
                pl.BlockSpec((1, width), fixed),
                any_space,
                any_space,
                any_space,
            ],
            out_specs=[
                pl.BlockSpec((TILE, width), place),
                pl.BlockSpec((TILE, width), place),
                pl.BlockSpec((1, 1, TILE), place3),
            ],
        ),
        out_shape=[jax.ShapeDtypeStruct(part.shape, part.dtype) for part in so_far],
        input_output_aliases={given: 0, given + 1: 1, given + 2: 2},
        compiler_params=pltpu.CompilerParams(vmem_limit_bytes=vmem),
        cost_estimate=pl.CostEstimate(
            flops=40 * block * width, bytes_accessed=56 * block * width, transcendentals=4 * block * width
        ),
    )(slots, scalars, *[piece for four in pieces for piece in four], table, rows, cols, *so_far)


def stack_kernel(slots_ref, *refs):
    pieces, out_ref = refs[:-1], refs[-1]
    for place, piece in enumerate(pieces):

        @pl.when(pl.program_id(0) == place)
        def _(piece=piece):
            out_ref[0] = piece[...]


def lay_out(slots, pieces):
    shape = pieces[0].shape
    return pl.pallas_call(
        stack_kernel,
        grid_spec=pltpu.PrefetchScalarGridSpec(
            num_scalar_prefetch=1,
            grid=(len(pieces),),
            in_specs=[pl.BlockSpec(shape, lambda i, slots: (0, 0), pipeline_mode=pl.Buffered(1))] * len(pieces),
            out_specs=pl.BlockSpec((1,) + shape, lambda i, slots: (slots[i], 0, 0)),
        ),
        out_shape=jax.ShapeDtypeStruct((len(pieces),) + shape, pieces[0].dtype),
        compiler_params=pltpu.CompilerParams(vmem_limit_bytes=vmem),
        cost_estimate=pl.CostEstimate(flops=0, bytes_accessed=4 * len(pieces) * pieces[0].size, transcendentals=0),
    )(slots, *pieces)


def columns_kernel(members_ref, slots_ref, own_ref, *refs):
    pieces, out_ref = refs[:-1], refs[-1]
    rows = own_ref.shape[0]

    def at(offset):
        return pl.ds(pl.multiple_of(members_ref[offset] * rows, rows), rows)

    out_ref[at(0), :] = own_ref[...].astype(low_type)
    for place, piece in enumerate(pieces):

        @pl.when(pl.program_id(0) == place)
        def _(piece=piece):
            for offset in range(piece.shape[0]):
                out_ref[at(offset + 1), :] = piece[offset]


def lay_columns(members, slots, own, pieces):
    others, rows, columns = pieces[0].shape
    replicas = len(pieces)
    whole = jax.ShapeDtypeStruct(((others + 1) * rows, replicas * columns), low_type)
    return pl.pallas_call(
        columns_kernel,
        grid_spec=pltpu.PrefetchScalarGridSpec(
            num_scalar_prefetch=2,
            grid=(replicas,),
            in_specs=[pl.BlockSpec((rows, columns), lambda i, members, slots: (0, slots[i]))]
            + [pl.BlockSpec(pieces[0].shape, lambda i, *_: (0, 0, 0), pipeline_mode=pl.Buffered(1))] * replicas,
            out_specs=pl.BlockSpec(((others + 1) * rows, columns), lambda i, members, slots: (0, slots[i])),
        ),
        out_shape=whole,
        compiler_params=pltpu.CompilerParams(vmem_limit_bytes=vmem),
        cost_estimate=pl.CostEstimate(flops=0, bytes_accessed=4 * whole.size, transcendentals=0),
    )(members, slots, own, *pieces)


def rows_kernel(members_ref, slots_ref, own_ref, *refs):
    pieces, out_ref = refs[:-1], refs[-1]
    out_ref[members_ref[0], 0] = own_ref[0].astype(low_type)
    for place, piece in enumerate(pieces):

        @pl.when(pl.program_id(0) == place)
        def _(piece=piece):
            for offset in range(piece.shape[0]):
                out_ref[members_ref[offset + 1], 0] = piece[offset]


def lay_rows(members, slots, own, pieces):
    others, rows, columns = pieces[0].shape
    replicas = len(pieces)
    whole = jax.ShapeDtypeStruct((others + 1, replicas, rows, columns), low_type)
    return pl.pallas_call(
        rows_kernel,
        grid_spec=pltpu.PrefetchScalarGridSpec(
            num_scalar_prefetch=2,
            grid=(replicas,),
            in_specs=[pl.BlockSpec((1, rows, columns), lambda i, members, slots: (slots[i], 0, 0))]
            + [pl.BlockSpec(pieces[0].shape, lambda i, *_: (0, 0, 0), pipeline_mode=pl.Buffered(1))] * replicas,
            out_specs=pl.BlockSpec((others + 1, 1, rows, columns), lambda i, members, slots: (0, slots[i], 0, 0)),
        ),
        out_shape=whole,
        compiler_params=pltpu.CompilerParams(vmem_limit_bytes=vmem),
        cost_estimate=pl.CostEstimate(flops=0, bytes_accessed=4 * whole.size, transcendentals=0),
    )(members, slots, own.reshape(replicas, rows, columns), *pieces).reshape(-1, columns)


tie = lax.optimization_barrier


def flip(value, bit):
    size = lax.axis_size("rep")
    return lax.ppermute(value, "rep", [(i, i ^ bit) for i in range(size)])


def turn(value, offset):
    size = lax.axis_size("grp")
    return lax.ppermute(value, "grp", [(i, (i + offset) % size) for i in range(size)])


def spread(piece, order):
    have = {0: piece}
    for bit in order:
        have.update({place ^ bit: flip(part, bit) for place, part in have.items()})
    return have


def slots_of():
    return lax.axis_index("rep") ^ jnp.arange(lax.axis_size("rep"), dtype=jnp.int32)


def plane_gather(piece):
    if lax.axis_size("rep") != 8:
        return lax.all_gather(piece, "rep")
    have = spread(piece, [2, 4, 1])
    return lay_out(slots_of(), [have[place] for place in range(8)])


def halve(value, axis, bit):
    mine = (lax.axis_index("rep") // bit) % 2
    kept = lax.dynamic_index_in_dim(value, mine, axis, keepdims=False)
    sent = lax.dynamic_index_in_dim(value, 1 - mine, axis, keepdims=False)
    return kept, sent.astype(low_type)


class Fold:
    def __init__(self, axis, order):
        self.axis = axis
        self.order = order
        self.quick = lax.axis_size("rep") == 8
        self.value = None

    def cores(self, chunks):
        axis = self.axis
        if not self.quick:
            self.value = lax.psum_scatter(chunks, "rep", scatter_dimension=axis)
            return []
        shape = chunks.shape
        kept, sent = halve(chunks.reshape(shape[:axis] + (4, 2) + shape[axis + 1 :]), axis + 1, 1)
        return self.from_cores(kept, sent)

    def from_cores(self, kept, sent):
        self.kept, self.got = kept, flip(sent, 1)
        return [sent]

    def sum(self):
        if self.value is None:
            return self.kept + self.got.astype(jnp.float32)
        return self.value

    def plane(self, first):
        if not self.quick:
            return []
        value = self.sum()
        axis = self.axis
        bit = self.order[0 if first else 1]
        if first:
            shape = value.shape
            value = value.reshape(shape[:axis] + (2, 2) + shape[axis + 1 :])
            axis = axis + (1 if bit == 2 else 0)
        self.kept, sent = halve(value, axis, bit)
        self.value, self.got = None, flip(sent, bit)
        return [sent]

    def members(self):
        value = self.sum()
        member = lax.axis_index("grp")
        size = lax.axis_size("grp")
        self.own = lax.dynamic_index_in_dim(value, member, 0, keepdims=False)
        sent = [
            lax.dynamic_index_in_dim(value, (member + offset) % size, 0, keepdims=False).astype(low_type)
            for offset in range(1, size)
        ]
        self.came = [turn(part, offset + 1) for offset, part in enumerate(sent)]
        return sent

    def total(self):
        return sum((came.astype(jnp.float32) for came in self.came), self.own)


def gradient_chunks(gradient):
    groups = lax.axis_size("grp")
    replicas = lax.axis_size("rep")
    rows, columns = gradient.shape
    return gradient.reshape(groups, replicas, rows // (groups * replicas), columns)


def across_wide(chunks):
    member = lax.axis_index("grp")
    size = lax.axis_size("grp")
    total = lax.dynamic_index_in_dim(chunks, member, 0, keepdims=False)
    for offset in range(1, size):
        sent = lax.dynamic_index_in_dim(chunks, (member + offset) % size, 0, keepdims=False)
        total = total + turn(sent, offset)
    return total


def group_gather(value):
    member = lax.axis_index("grp")
    size = lax.axis_size("grp")
    result = jnp.zeros((size,) + value.shape, value.dtype)
    result = lax.dynamic_update_index_in_dim(result, value, member, 0)
    for offset in range(1, size):
        result = lax.dynamic_update_index_in_dim(
            result, turn(value, offset), (member + size - offset) % size, 0
        )
    return result


def plane_sum(value):
    for j in range(1, lax.axis_size("rep").bit_length() - 1):
        value = value + flip(value, 1 << j)
    return value


def rest_sum(value):
    value = value + flip(value, 1)
    size = lax.axis_size("grp")
    for j in range(size.bit_length() - 1):
        value = value + lax.ppermute(value, "grp", [(i, i ^ (1 << j)) for i in range(size)])
    return value


def fetch(own):
    return jnp.stack([turn(own, offset) for offset in range(1, lax.axis_size("grp"))])


def cut(value, axis):
    replicas = lax.axis_size("rep")
    size = value.shape[axis] // replicas
    return lax.dynamic_slice_in_dim(value, lax.axis_index("rep") * size, size, axis)


def members_of():
    groups = lax.axis_size("grp")
    return (lax.axis_index("grp") + groups - jnp.arange(groups, dtype=jnp.int32)) % groups


def contract(left, right, left_dim, right_dim):
    return lax.dot_general(
        left, right, (((left_dim,), (right_dim,)), ((), ())), preferred_element_type=jnp.float32
    )


def layer_norm(values, gain, shift):
    center = values - jnp.mean(values, axis=-1, keepdims=True)
    spread = jnp.mean(center * center, axis=-1, keepdims=True)
    return center * lax.rsqrt(spread + ln_eps) * gain + shift


def rope_tables(length):
    freqs = rope_base ** (-jnp.arange(HD // 2, dtype=jnp.float32) * 2.0 / HD)
    angles = jnp.arange(length, dtype=jnp.float32)[:, None] * freqs[None, :]
    cosine, sine = jnp.cos(angles), jnp.sin(angles)
    return (
        jnp.concatenate([cosine] * 4, axis=-1),
        jnp.concatenate([-sine, sine, -sine, sine], axis=-1),
    )


def swiglu(joined):
    middle = joined.shape[-1] // 2
    return jax.nn.silu(joined[:, :middle]) * joined[:, middle:]


def merge_stats(first_part, second_part):
    peak = jnp.maximum(first_part[0], second_part[0])
    spread = first_part[1] * jnp.exp(first_part[0] - peak) + second_part[1] * jnp.exp(
        second_part[0] - peak
    )
    return (peak, spread, first_part[2] + second_part[2])


def body(
    ids,
    lengths,
    picks,
    labels,
    loss_mask,
    table,
    w_qkv,
    w_out,
    w_gu,
    w_down,
    norms,
    table_rows,
    table_cols,
    qkv_rows,
    qkv_cols,
    out_rows,
    out_cols,
    gu_rows,
    gu_cols,
    down_rows,
    down_cols,
    norms_moment,
):
    member = lax.axis_index("grp")
    groups = lax.axis_size("grp")
    replica = lax.axis_index("rep")
    replicas = lax.axis_size("rep")
    seqs, length = ids.shape
    width = table.shape[1]
    vocab_rows = table.shape[0]
    own_rows = seqs * picks.shape[1]
    tokens = seqs * length
    block = -(-vocab_rows // (16 * replicas)) * 16
    padded = block * replicas

    packed = jnp.concatenate([ids.reshape(-1), labels.reshape(-1), loss_mask.reshape(-1)])
    group_packed = group_gather(packed)
    group_ids = group_packed[:, :tokens].reshape(-1)
    group_labels = group_packed[:, tokens : tokens + own_rows].reshape(-1)
    group_mask = group_packed[:, tokens + own_rows :].reshape(-1)
    shard_rows = w_qkv.shape[0]
    quick = replicas == 8
    near_shard = jnp.concatenate([w_qkv, w_out], axis=1)
    if quick:
        near_part = fetch(cut(near_shard, 1).astype(low_type))
        gu_part = fetch(cut(w_gu, 1).astype(low_type))

    local_ids = group_ids - member * vocab_rows
    owned = (local_ids >= 0) & (local_ids < vocab_rows)
    places, order = lax.sort(
        (jnp.where(owned, local_ids, padded), jnp.arange(local_ids.shape[0], dtype=jnp.int32)), num_keys=1
    )
    bounds = jnp.arange(replicas + 1, dtype=jnp.int32) * block
    starts = jnp.sum((places[None, :] < bounds[:, None]).astype(jnp.int32), axis=1)
    if quick:
        places, near_part = tie((places, near_part))
    again = jnp.concatenate([jnp.zeros((1,), jnp.int32), (places[1:] == places[:-1]).astype(jnp.int32)])
    codes = jnp.pad(places % block * 2 + again, (0, 8))
    padded_order = jnp.pad(order, (0, 8))
    found = lookup(starts, places, order, table)
    if quick:
        found, gu_part = tie((found, gu_part))
    embed = lax.psum_scatter(found, "grp", scatter_dimension=0, tiled=True)
    late_table, _ = lax.optimization_barrier((table, found))
    table_low = jnp.pad(late_table.astype(low_type), ((0, padded - vocab_rows), (0, 0)))

    if quick:
        members, slots = members_of(), slots_of()

        down_own, _ = tie((cut(w_down, 0), found))
        down_part = fetch(down_own.astype(low_type))

        def listed(have):
            return [have[place] for place in range(replicas)]

        near = lay_columns(members, slots, near_shard, listed(spread(near_part, [4, 2, 1])))
        w_down_low = lay_rows(members, slots, w_down, listed(spread(down_part, [4, 2, 1])))
        gu_have = spread(gu_part, [2, 4])
        gu_have, near, w_down_low, table_low = tie((gu_have, near, w_down_low, table_low))
        gu_have.update({place ^ 1: flip(part, 1) for place, part in gu_have.items()})
        w_gu_low = lay_columns(members, slots, w_gu, listed(gu_have))
        embed, near, w_gu_low, w_down_low, table_low = tie((embed, near, w_gu_low, w_down_low, table_low))
    else:
        near = lax.all_gather(near_shard.astype(low_type), "grp", tiled=True)
        w_gu_low = lax.all_gather(w_gu.astype(low_type), "grp", tiled=True)
        w_down_low = lax.all_gather(w_down.astype(low_type), "grp", tiled=True)
    w_out_low = near[:, 3 * width :]
    cosine, sine = rope_tables(length)
    first, first_low, queries, keys, values = project(embed, norms, cosine, sine, near)
    queries, group_mask = tie((queries, group_mask))
    loss_count = jnp.sum(group_mask).astype(jnp.float32)[None]
    for j in range(replicas.bit_length() - 1):
        loss_count = loss_count + flip(loss_count, 1 << j)
    loss_count = loss_count[0]
    mixed_low, log_sums = attend(lengths, queries, keys, values)
    first_sum = first + jnp.dot(mixed_low, w_out_low, preferred_element_type=jnp.float32)
    second = layer_norm(first_sum, norms[2], norms[3])
    second_low = second.astype(low_type)
    gate_up = jnp.dot(second_low, w_gu_low, preferred_element_type=jnp.float32)
    hidden_low = swiglu(gate_up).astype(low_type)
    second_sum = second + jnp.dot(hidden_low, w_down_low, preferred_element_type=jnp.float32)
    final = layer_norm(second_sum, norms[4], norms[5])

    flat_picks = (jnp.arange(seqs, dtype=jnp.int32)[:, None] * length + picks).reshape(-1)
    chosen = final[flat_picks].astype(low_type)
    group_chosen = group_gather(chosen).reshape(groups * own_rows, width)
    rows_at = jnp.arange(padded, dtype=jnp.int32)[:, None]
    logits = jnp.where(rows_at < vocab_rows, contract(table_low, group_chosen, 1, 1), neg_large)
    peak = jnp.max(logits, axis=0)
    spread_sum = jnp.sum(jnp.exp(logits - peak[None, :]), axis=0)
    local_labels = group_labels - member * vocab_rows
    inside = (local_labels >= 0) & (local_labels < vocab_rows)
    hits = (rows_at == local_labels[None, :]) & inside[None, :]
    target = jnp.sum(jnp.where(hits, logits, 0.0), axis=0)
    stats = group_gather(jnp.stack([peak, spread_sum, target]))
    so_far = (stats[0, 0], stats[0, 1], stats[0, 2])
    for place in range(1, groups):
        so_far = merge_stats(so_far, (stats[place, 0], stats[place, 1], stats[place, 2]))
    peak_all, spread_all, target_all = so_far
    log_total = peak_all + jnp.log(spread_all)
    counted = group_mask > 0
    terms = jnp.where(counted, log_total - target_all, 0.0)
    own_terms = lax.dynamic_slice_in_dim(terms, member * own_rows, own_rows)
    row_scale = jnp.where(counted, 1.0 / loss_count, 0.0)
    dlogits = (
        (jnp.exp(logits - log_total[None, :]) - hits.astype(jnp.float32)) * row_scale[None, :]
    ).astype(low_type)
    chosen_part = contract(dlogits, table_low, 0, 0)
    chosen_grad = across_wide(chosen_part.reshape(groups, own_rows, width))
    final_grad = jnp.zeros((tokens, width), jnp.float32).at[flat_picks].add(chosen_grad)

    _, pull = jax.vjp(layer_norm, second_sum, norms[4], norms[5])
    sum_grad, gain_three, shift_three = pull(final_grad)
    branch_low = sum_grad.astype(low_type)
    down = Fold(1, (2, 4))
    down.cores(gradient_chunks(contract(hidden_low, branch_low, 0, 0)))
    hidden_grad = contract(branch_low, w_down_low, 1, 1)
    _, pull = jax.vjp(swiglu, gate_up)
    gate_low = pull(hidden_grad)[0].astype(low_type)
    gate_low, _ = tie((gate_low, down.plane(True)))
    gate, up = Fold(1, (4, 2)), Fold(1, (2, 4))
    middle = gate_up.shape[1] // 2
    sent = gate.cores(gradient_chunks(contract(second_low, gate_low[:, :middle], 0, 0)))
    sent += up.cores(gradient_chunks(contract(second_low, gate_low[:, middle:], 0, 0)))
    gate_low, _ = tie((gate_low, sent))
    second_grad = sum_grad + contract(gate_low, w_gu_low, 1, 1)
    second_grad, _ = tie((second_grad, gate.plane(True) + up.plane(True) + down.plane(False)))
    _, pull = jax.vjp(layer_norm, first_sum, norms[2], norms[3])
    first_sum_grad, gain_two, shift_two = pull(second_grad)
    attn_low = first_sum_grad.astype(low_type)
    mixed_grad = contract(attn_low, w_out_low, 1, 1).astype(low_type)
    pairs = width // LANES
    third = pairs // 3
    sides = []
    for stage in range(3):
        if stage:
            sent = gate.plane(False) + up.plane(False) + down.members() if stage == 1 else gate.members() + up.members()
            mixed_grad, sides[-1], _ = tie((mixed_grad, sides[-1], sent))
        sides.append(
            attend_back(lengths, queries, keys, values, mixed_grad, log_sums, cosine, sine, stage * third, third)
        )
    joined_grad = jnp.concatenate([side for parts in zip(*sides) for side in parts], axis=1)
    first_grad = first_sum_grad + contract(joined_grad, near[:, : 3 * width], 1, 1)
    _, pull = jax.vjp(layer_norm, embed.astype(jnp.float32), norms[0], norms[1])
    embed_grad, gain_one, shift_one = pull(first_grad)
    norm_grad = jnp.stack([gain_one, shift_one, gain_two, shift_two, gain_three, shift_three])
    embed_low, joined_grad = tie((embed_grad.astype(low_type), joined_grad))
    group_embed = lax.all_gather(embed_low, "grp", axis=0, tiled=True)

    join = Fold(1, (2, 4))
    join.cores(
        gradient_chunks(
            jnp.concatenate(
                [contract(first_low, joined_grad, 0, 0), contract(mixed_low, attn_low, 0, 0)], axis=1
            )
        )
    )
    join.plane(True)
    join.plane(False)
    join.members()
    gu_share = jnp.concatenate([gate.total(), up.total()], axis=1)
    down_share, join_share = down.total(), join.total()
    part_rows = gu_share.shape[0]
    far_whole = plane_gather(
        jnp.concatenate(
            [gu_share.astype(low_type), down_share.astype(low_type).reshape(part_rows, -1)], axis=1
        )
    ).reshape(shard_rows, -1)
    near_whole = plane_gather(join_share.astype(low_type)).reshape(shard_rows, -1)
    shares = (join_share[:, : 3 * width], join_share[:, 3 * width :], gu_share, down_share)
    share_cols = [jnp.sum(gradient * gradient, axis=0) for gradient in shares]
    group_embed, near_whole, far_whole, share_cols = tie((group_embed, near_whole, far_whole, share_cols))

    core = replica % 2
    half_args = (starts, codes, padded_order, dlogits, group_chosen, group_embed, block)
    heads = [Fold(0, (2, 4)), Fold(0, (4, 2))]
    middle = width // 2
    if quick:
        sent = table_grad_half((1 - core)[None], *half_args, low_type)
        got = flip(sent, 1)
        value = table_grad_half(core[None], *half_args, jnp.float32) + got.astype(jnp.float32)
    else:
        both = [table_grad_half(jnp.full((1,), j, jnp.int32), *half_args, jnp.float32) for j in range(2)]
        value = jnp.stack(both, axis=1).reshape(replicas, block, width)
        value = lax.psum_scatter(value, "rep", scatter_dimension=0)
    for head, part in zip(heads, (value[..., :middle], value[..., middle:])):
        head.value = part
        head.plane(True)
    for head in heads:
        head.plane(False)
    table_parts = [head.sum() for head in heads]

    old_rows = (table_rows, qkv_rows, out_rows, gu_rows, down_rows)
    old_cols = (table_cols, qkv_cols, out_cols, gu_cols, down_cols)
    masters = (table, w_qkv, w_out, w_gu, w_down)
    col_parts = [
        jnp.concatenate([jnp.sum(gradient * gradient, axis=0) for gradient in table_parts])
    ] + share_cols
    row_old = jnp.stack([jnp.sum(rows) for rows in old_rows]) / replicas
    small = [norm_grad.reshape(-1)] + col_parts + [row_old, jnp.sum(own_terms)[None]]
    plane_totals = plane_sum(jnp.concatenate(small))
    table_lows = [part.astype(low_type) for part in table_parts]
    plane_totals, table_lows = tie((plane_totals, table_lows))
    totals = rest_sum(plane_totals)
    cuts = []
    start = 0
    for part in small:
        cuts.append(totals[start : start + part.shape[0]])
        start += part.shape[0]
    norm_sum = cuts[0].reshape(norm_grad.shape)
    col_totals = cuts[1:6]
    old_totals = cuts[6]
    loss_sum = cuts[7][0]
    squares = [jnp.sum(part) for part in col_totals]
    clip_norm = jnp.sqrt(sum(squares) + jnp.sum(norm_sum * norm_sum))
    factor = clip_limit / jnp.maximum(clip_norm, clip_limit)
    decay = 1.0 - float(STEP) ** (-0.8)

    wholes = [
        None,
        near_whole[:, : 3 * width],
        near_whole[:, 3 * width :],
        far_whole[:, : w_gu.shape[1]],
        far_whole[:, w_gu.shape[1] :].reshape(w_down.shape),
    ]

    outputs = []
    for place in range(5):
        rows, columns = masters[place].shape
        full_rows = rows * groups
        new_cols = (
            decay * old_cols[place] + (1.0 - decay) * (col_totals[place] * factor * factor) / full_rows
        )
        row_total = decay * old_totals[place] + (1.0 - decay) * (squares[place] * factor * factor) / columns
        row_mean = row_total / full_rows
        if place == 0 and quick:
            have = [
                spread(low, [2, 4, 1] if part % 2 else [4, 2, 1]) for part, low in enumerate(table_lows)
            ]
            tiles = padded // TILE
            row_tiles = jnp.pad(table_rows, (0, padded - vocab_rows), constant_values=1.0).reshape(tiles, 1, TILE)
            scalars = jnp.stack([factor, rate_matrix * factor * jnp.sqrt(row_mean)])
            so_far = (
                blank(table.shape, jnp.float32),
                blank(table.shape, jnp.float32),
                blank((tiles, 1, TILE), jnp.float32),
            )
            slots = slots_of()
            for four in ((0, 2, 4, 6), (1, 3, 5, 7)):
                so_far = update(
                    jnp.stack([slots[part] for part in four]),
                    scalars,
                    [[got[part] for got in have] for part in four],
                    table,
                    row_tiles,
                    lax.rsqrt(new_cols)[None, :],
                    so_far,
                )
            outputs.extend([so_far[0], so_far[2].reshape(-1)[:vocab_rows], new_cols, so_far[1]])
            continue
        if place == 0:
            whole = plane_gather(jnp.concatenate(table_lows, axis=1))
            gradient = whole.reshape(padded, width)[:vocab_rows].astype(jnp.float32)
        else:
            gradient = wholes[place].astype(jnp.float32)
        row_means = jnp.mean(gradient * gradient, axis=1)
        new_rows = decay * old_rows[place] + (1.0 - decay) * (row_means * factor * factor)
        clipped = gradient * factor
        scale = new_rows[:, None] * new_cols[None, :] / row_mean
        new_master = masters[place] - rate_matrix * clipped * lax.rsqrt(scale)
        outputs.extend([clipped, new_rows, new_cols, new_master])
    norm_clipped = norm_sum * factor
    moment_new = decay * norms_moment + (1.0 - decay) * norm_clipped * norm_clipped
    norms_new = norms - rate_norm * norm_clipped * lax.rsqrt(moment_new)
    return (
        (loss_sum, loss_count, clip_norm) + tuple(outputs) + (norm_clipped, moment_new, norms_new)
    )


def solution(mesh):
    in_specs = (
        P(("grp", "rep"), None),
        P(("grp", "rep")),
        P(("grp", "rep"), None),
        P(("grp", "rep"), None),
        P(("grp", "rep"), None),
        P("grp", None),
        P("grp", None),
        P("grp", None),
        P("grp", None),
        P("grp", None),
        P(),
        P("grp"),
        P(),
        P("grp"),
        P(),
        P("grp"),
        P(),
        P("grp"),
        P(),
        P("grp"),
        P(),
        P(),
    )
    out_specs = (
        P(),
        P(),
        P(),
        P("grp", None),
        P("grp"),
        P(),
        P("grp", None),
        P("grp", None),
        P("grp"),
        P(),
        P("grp", None),
        P("grp", None),
        P("grp"),
        P(),
        P("grp", None),
        P("grp", None),
        P("grp"),
        P(),
        P("grp", None),
        P("grp", None),
        P("grp"),
        P(),
        P("grp", None),
        P(),
        P(),
        P(),
    )
    return jax.shard_map(body, mesh=mesh, in_specs=in_specs, out_specs=out_specs, check_vma=False)
```

```python
import functools
import math

import jax
import jax.numpy as jnp
from jax import lax
from jax.experimental import pallas as pl
from jax.experimental.pallas import tpu as pltpu
from jax.sharding import PartitionSpec as P

HEADS = 12
HD = 64
STEP = 10
LANES = 128
ROWS = 256
CHUNK = 256
TILE = 480


ln_eps = 1e-05
rope_base = 10000.0
clip_limit = 0.01
rate_matrix = 0.03
rate_norm = 0.3
neg_large = -1e30
low_type = jnp.bfloat16
vmem = 56 * 1024 * 1024


def pair_lanes(shape):
    return lax.broadcasted_iota(jnp.int32, shape, len(shape) - 1)


def swap_halves(value):
    upper = (pair_lanes(value.shape) % HD) >= HD // 2
    return jnp.where(
        upper,
        pltpu.roll(value, HD // 2, axis=1),
        pltpu.roll(value, LANES - HD // 2, axis=1),
    )


def normalize(values, gain, shift):
    center = values - jnp.mean(values, axis=-1, keepdims=True)
    spread = jnp.mean(center * center, axis=-1, keepdims=True)
    return center * lax.rsqrt(spread + ln_eps) * gain + shift


def project_kernel(embed_ref, norms_ref, cosine_ref, sine_ref, w_ref, first_ref, low_ref, q_ref, k_ref, v_ref):
    first = normalize(embed_ref[...].astype(jnp.float32), norms_ref[0:1, :], norms_ref[1:2, :])
    first_ref[...] = first
    low = first.astype(low_type)
    low_ref[...] = low
    width = first.shape[1]
    cosine, sine = cosine_ref[...], sine_ref[...]
    for part, out_ref in enumerate((q_ref, k_ref)):
        joined = jnp.dot(low, w_ref[:, part * width : (part + 1) * width], preferred_element_type=jnp.float32)
        for start in range(0, width, LANES):
            piece = joined[:, start : start + LANES]
            out_ref[:, start : start + LANES] = (piece * cosine + swap_halves(piece) * sine).astype(low_type)
    v_ref[...] = jnp.dot(low, w_ref[:, 2 * width :], preferred_element_type=jnp.float32).astype(low_type)


def project(embed, norms, cosine, sine, weights):
    tokens, width = embed.shape
    row = lambda i: (i, 0)
    fixed = lambda i: (0, 0)
    low = jax.ShapeDtypeStruct((tokens, width), low_type)
    return pl.pallas_call(
        project_kernel,
        grid=(tokens // ROWS,),
        in_specs=[
            pl.BlockSpec((ROWS, width), row),
            pl.BlockSpec(norms.shape, fixed),
            pl.BlockSpec((ROWS, LANES), row),
            pl.BlockSpec((ROWS, LANES), row),
            pl.BlockSpec((width, 3 * width), fixed),
        ],
        out_specs=[pl.BlockSpec((ROWS, width), row)] * 5,
        out_shape=[jax.ShapeDtypeStruct((tokens, width), jnp.float32), low, low, low, low],
        compiler_params=pltpu.CompilerParams(vmem_limit_bytes=vmem),
        cost_estimate=pl.CostEstimate(flops=6 * tokens * width * width, bytes_accessed=20 * tokens * width, transcendentals=0),
    )(embed, norms, cosine, sine, weights)


def head_keys(k, bias, half):
    lanes = pair_lanes(k.shape)
    spare = HD - half * HD
    return jnp.where(lanes // HD == half, k, jnp.where(lanes == spare, bias, jnp.zeros_like(k)))


def head_queries(q, half, spare_value):
    lanes = pair_lanes(q.shape)
    spare = HD - half * HD
    scaled = q * jnp.asarray(1.0 / math.sqrt(HD), q.dtype)
    other = jnp.where(lanes == spare, jnp.full_like(q, spare_value), jnp.zeros_like(q))
    return jnp.where(lanes // HD == half, scaled, other)


def transposed_dot(left, right):
    return lax.dot_general(left, right, (((1,), (1,)), ((), ())), preferred_element_type=jnp.float32)


def key_bias(length_ref, tokens):
    place = lax.broadcasted_iota(jnp.int32, (tokens, LANES), 0)
    return jnp.where(place < length_ref[0], 0.0, neg_large).astype(low_type)


def attend_kernel(length_ref, q_ref, k_ref, v_ref, out_ref, log_ref, keys, turned):
    tokens = k_ref.shape[0]

    @pl.when(pl.program_id(1) == 0)
    def _():
        bias = key_bias(length_ref, tokens)
        for half in range(2):
            keys[half] = head_keys(k_ref[...], bias, half)
        turned[...] = v_ref[...].T

    parts = []
    for half in range(2):
        scores = transposed_dot(keys[half], head_queries(q_ref[...], half, 1.0))
        peak = jnp.max(scores, axis=0, keepdims=True)
        weights = jnp.exp(scores - peak)
        totals = jnp.sum(weights, axis=0, keepdims=True)
        probs = (weights * (1.0 / totals)).astype(low_type)
        parts.append(
            jnp.dot(turned[half * HD : (half + 1) * HD, :], probs, preferred_element_type=jnp.float32)
        )
        log_ref[0, half : half + 1, :] = peak + jnp.log(totals)
    out_ref[...] = jnp.concatenate(parts, axis=0).T.astype(low_type)


def attend(length, q, k, v):
    tokens, width = q.shape
    pairs = width // LANES
    own = lambda p, i, *_: (i, p)
    whole = lambda p, i, *_: (0, p)
    return pl.pallas_call(
        attend_kernel,
        grid_spec=pltpu.PrefetchScalarGridSpec(
            num_scalar_prefetch=1,
            grid=(pairs, tokens // ROWS),
            in_specs=[
                pl.BlockSpec((ROWS, LANES), own),
                pl.BlockSpec((tokens, LANES), whole),
                pl.BlockSpec((tokens, LANES), whole),
            ],
            out_specs=[
                pl.BlockSpec((ROWS, LANES), own),
                pl.BlockSpec((1, 2, ROWS), lambda p, i, *_: (p, 0, i)),
            ],
            scratch_shapes=[
                pltpu.VMEM((2, tokens, LANES), low_type),
                pltpu.VMEM((LANES, tokens), low_type),
            ],
        ),
        out_shape=[
            jax.ShapeDtypeStruct((tokens, width), low_type),
            jax.ShapeDtypeStruct((pairs, 2, tokens), jnp.float32),
        ],
        compiler_params=pltpu.CompilerParams(vmem_limit_bytes=vmem),
        cost_estimate=pl.CostEstimate(
            flops=16 * tokens * tokens * width, bytes_accessed=8 * tokens * width, transcendentals=tokens * tokens * width // HD
        ),
    )(length, q, k, v)


def rotate_back(grads, cosine, sine):
    return grads * cosine + swap_halves(grads * sine)


def attend_back_kernel(first_pair, length_ref, q_ref, k_ref, v_ref, d_ref, log_ref, cosq_ref, sinq_ref, cos_ref, sin_ref, *rest):
    dq_ref, dk_ref, dv_ref, keys, values, turned, dk_total, dv_total = rest[-8:]
    tokens = k_ref.shape[0]
    step = pl.program_id(1)

    @pl.when(step == 0)
    def _():
        bias = key_bias(length_ref, tokens)
        lanes = pair_lanes((tokens, LANES))
        for half in range(2):
            keys[half] = head_keys(k_ref[...], bias, half)
            values[half] = jnp.where(lanes // HD == half, v_ref[...], jnp.zeros_like(v_ref[...]))
        turned[...] = k_ref[...].T
        dk_total[...] = jnp.zeros_like(dk_total)
        dv_total[...] = jnp.zeros_like(dv_total)

    d = d_ref[...]
    lanes = pair_lanes(d.shape)
    parts = []
    dk = dv = None
    for half in range(2):
        scores = transposed_dot(keys[half], head_queries(q_ref[...], half, 1.0))
        probs = jnp.exp(scores - log_ref[0, half : half + 1, :])
        dprobs = transposed_dot(values[half], d)
        inner = jnp.sum(probs * dprobs, axis=0, keepdims=True)
        dscore = (probs * (dprobs - inner)).astype(low_type)
        parts.append(jnp.dot(turned[half * HD : (half + 1) * HD, :], dscore, preferred_element_type=jnp.float32))
        one_k = jnp.dot(dscore, head_queries(q_ref[...], half, 0.0), preferred_element_type=jnp.float32)
        one_v = jnp.dot(
            probs.astype(low_type), jnp.where(lanes // HD == half, d, jnp.zeros_like(d)), preferred_element_type=jnp.float32
        )
        dk = one_k if dk is None else dk + one_k
        dv = one_v if dv is None else dv + one_v
    dk_total[...] += dk
    dv_total[...] += dv
    dq = jnp.concatenate(parts, axis=0).T * (1.0 / math.sqrt(HD))
    dq_ref[...] = rotate_back(dq, cosq_ref[...], sinq_ref[...]).astype(low_type)

    @pl.when(step == pl.num_programs(1) - 1)
    def _():
        dk_ref[...] = rotate_back(dk_total[...], cos_ref[...], sin_ref[...]).astype(low_type)
        dv_ref[...] = dv_total[...].astype(low_type)


def attend_back(length, q, k, v, d, logs, cosine, sine, first_pair, pairs, after=()):
    tokens, width = q.shape
    own = lambda p, i, *_: (i, first_pair + p)
    whole = lambda p, i, *_: (0, first_pair + p)
    low = jax.ShapeDtypeStruct((tokens, pairs * LANES), low_type)
    fixed = pl.BlockSpec((tokens, LANES), lambda p, i, *_: (0, 0))
    row = pl.BlockSpec((ROWS, LANES), lambda p, i, *_: (i, 0))
    return pl.pallas_call(
        functools.partial(attend_back_kernel, first_pair),
        grid_spec=pltpu.PrefetchScalarGridSpec(
            num_scalar_prefetch=1,
            grid=(pairs, tokens // ROWS),
            in_specs=[
                pl.BlockSpec((ROWS, LANES), own),
                pl.BlockSpec((tokens, LANES), whole),
                pl.BlockSpec((tokens, LANES), whole),
                pl.BlockSpec((ROWS, LANES), own),
                pl.BlockSpec((1, 2, ROWS), lambda p, i, *_: (first_pair + p, 0, i)),
                row,
                row,
                fixed,
                fixed,
            ]
            + [pl.BlockSpec(memory_space=pl.ANY)] * len(after),
            out_specs=[
                pl.BlockSpec((ROWS, LANES), lambda p, i, *_: (i, p)),
                pl.BlockSpec((tokens, LANES), lambda p, i, *_: (0, p)),
                pl.BlockSpec((tokens, LANES), lambda p, i, *_: (0, p)),
            ],
            scratch_shapes=[
                pltpu.VMEM((2, tokens, LANES), low_type),
                pltpu.VMEM((2, tokens, LANES), low_type),
                pltpu.VMEM((LANES, tokens), low_type),
                pltpu.VMEM((tokens, LANES), jnp.float32),
                pltpu.VMEM((tokens, LANES), jnp.float32),
            ],
        ),
        out_shape=[low, low, low],
        compiler_params=pltpu.CompilerParams(vmem_limit_bytes=vmem),
        cost_estimate=pl.CostEstimate(
            flops=40 * tokens * tokens * pairs * LANES,
            bytes_accessed=16 * tokens * pairs * LANES,
            transcendentals=tokens * tokens * pairs * 2,
        ),
    )(length, q, k, v, d, logs, cosine, sine, cosine, sine, *after)


def blank(shape, dtype):
    return pl.pallas_call(
        lambda out_ref: None,
        out_shape=jax.ShapeDtypeStruct(shape, dtype),
        out_specs=pl.BlockSpec(memory_space=pl.ANY),
    )()


def lookup_kernel(starts_ref, places_ref, order_ref, table_ref, out_ref, rows):
    count = out_ref.shape[0]
    owned = starts_ref[starts_ref.shape[0] - 1]
    for start in range(0, count, CHUNK):
        rows[start : start + CHUNK, :] = jnp.zeros((CHUNK, rows.shape[1]), jnp.float32)

    def eight(step, carry):
        for j in range(8):
            i = step * 8 + j
            valid = i < owned
            source = jnp.where(valid, places_ref[i], 0)
            target = jnp.where(valid, order_ref[i], count)
            rows[pl.ds(target, 1), :] = table_ref[pl.ds(source, 1), :]
        return carry

    lax.fori_loop(0, (owned + 7) // 8, eight, 0)
    for start in range(0, count, CHUNK):
        out_ref[start : start + CHUNK, :] = rows[start : start + CHUNK, :].astype(low_type)


def lookup(starts, places, order, table):
    count = places.shape[0]
    width = table.shape[1]
    return pl.pallas_call(
        lookup_kernel,
        grid_spec=pltpu.PrefetchScalarGridSpec(
            num_scalar_prefetch=3,
            grid=(1,),
            in_specs=[pl.BlockSpec(table.shape, lambda i, *_: (0, 0), pipeline_mode=pl.Buffered(1))],
            out_specs=pl.BlockSpec((count, width), lambda i, *_: (0, 0), pipeline_mode=pl.Buffered(1)),
            scratch_shapes=[pltpu.VMEM((count + 8, width), jnp.float32)],
        ),
        out_shape=jax.ShapeDtypeStruct((count, width), low_type),
        compiler_params=pltpu.CompilerParams(vmem_limit_bytes=vmem),
        cost_estimate=pl.CostEstimate(flops=0, bytes_accessed=table.size * 12, transcendentals=0),
    )(starts, places, order, table)


def table_grad_kernel(chunks_ref, starts_ref, codes_ref, order_ref, dlogits_ref, chosen_ref, embed_ref, *refs):
    rows, sums = refs[-2:]
    step = pl.program_id(0)
    count, width = embed_ref.shape
    block = dlogits_ref.shape[0]

    @pl.when(step == 0)
    def _():
        for start in range(0, count, CHUNK):
            rows[start : start + CHUNK, :] = embed_ref[start : start + CHUNK, :].astype(jnp.float32)

    sums[...] = jnp.zeros_like(sums)
    chunk = chunks_ref[step]
    first, last = starts_ref[chunk], starts_ref[chunk + 1]

    def eight(turn, running):
        for j in range(8):
            i = first + turn * 8 + j
            code = codes_ref[i]
            place = jnp.where(i < last, code >> 1, block)
            running = jnp.where(code & 1, running, 0.0) + rows[pl.ds(order_ref[i], 1), :]
            sums[pl.ds(place, 1), :] = running
        return running

    lax.fori_loop(0, (last - first + 7) // 8, eight, jnp.zeros((1, width), jnp.float32))
    product = jnp.dot(dlogits_ref[...], chosen_ref[...], preferred_element_type=jnp.float32)
    result = product + sums[:block, :]
    if len(refs) == 3:
        refs[0][0] = result.astype(refs[0].dtype)
        return
    got_ref, sent_x, kept_x, sent_y, kept_y = refs[:-2]
    result = result + got_ref[0].astype(jnp.float32)
    left, right = result[:, : width // 2], result[:, width // 2 :]

    @pl.when(step % 2 == 0)
    def _():
        sent_x[0] = left.astype(sent_x.dtype)

    @pl.when(step % 2 == 1)
    def _():
        kept_x[0] = left

    @pl.when(step < 2)
    def _():
        sent_y[0] = right.astype(sent_y.dtype)

    @pl.when(step >= 2)
    def _():
        kept_y[0] = right


def table_grad_chunks(chunks, starts, codes, order, dlogits, chosen, embed, block, dtype, got=None):
    count, width = embed.shape
    picked = chosen.shape[0]
    steps = chunks.shape[0]
    fixed = lambda i, *_: (0, 0)
    in_specs = [
        pl.BlockSpec((block, picked), lambda i, chunks, *_: (chunks[i], 0)),
        pl.BlockSpec((picked, width), fixed),
        pl.BlockSpec((count, width), fixed, pipeline_mode=pl.Buffered(1)),
    ]
    whole = pl.BlockSpec((1, block, width), lambda i, *_: (i, 0, 0))
    if got is None:
        out_shape = jax.ShapeDtypeStruct((steps, block, width), dtype)
        out_specs = whole
    else:
        in_specs.append(whole)
        half = (1, block, width // 2)
        by_y = lambda i, *_: (i // 2, 0, 0)
        low = jax.ShapeDtypeStruct((2, block, width // 2), low_type)
        high = jax.ShapeDtypeStruct((2, block, width // 2), jnp.float32)
        out_shape = [low, high, low, high]
        out_specs = [
            pl.BlockSpec(half, by_y),
            pl.BlockSpec(half, by_y),
            pl.BlockSpec(half, lambda i, *_: (jnp.minimum(i, 1), 0, 0)),
            pl.BlockSpec(half, lambda i, *_: (jnp.maximum(i - 2, 0), 0, 0)),
        ]
    return pl.pallas_call(
        table_grad_kernel,
        grid_spec=pltpu.PrefetchScalarGridSpec(
            num_scalar_prefetch=4,
            grid=(steps,),
            in_specs=in_specs,
            out_specs=out_specs,
            scratch_shapes=[
                pltpu.VMEM((count, width), jnp.float32),
                pltpu.VMEM((block + 8, width), jnp.float32),
            ],
        ),
        out_shape=out_shape,
        compiler_params=pltpu.CompilerParams(vmem_limit_bytes=vmem),
        cost_estimate=pl.CostEstimate(
            flops=2 * steps * block * picked * width, bytes_accessed=8 * steps * block * width, transcendentals=0
        ),
    )(chunks, starts, codes, order, dlogits, chosen, embed, *(() if got is None else (got,)))


def update_kernel(places, parts, slots_ref, scalars_ref, *rest):
    given = len(places) * parts
    pieces = rest[:given]
    table_ref, rows_ref, cols_ref = rest[given : given + 3]
    grad_ref, new_ref, rows_new_ref = rest[-3:]
    factor, rate = scalars_ref[0], scalars_ref[1]
    decay = 1.0 - float(STEP) ** (-0.8)
    old = jnp.broadcast_to(rows_ref[0], (LANES, TILE)).T[:, 0:1]
    for part in range(len(places)):

        @pl.when(pl.program_id(0) == part)
        def _(part=part):
            own = pieces[part * parts : (part + 1) * parts]
            gradient = jnp.concatenate([piece[...] for piece in own], axis=1).astype(jnp.float32)
            means = jnp.mean(gradient * gradient, axis=1, keepdims=True)
            rows_new = decay * old + (1.0 - decay) * (means * factor * factor)
            grad_ref[...] = gradient * factor
            new_ref[...] = table_ref[...] - gradient * (rate * lax.rsqrt(rows_new)) * cols_ref[...]
            rows_new_ref[0] = jnp.broadcast_to(rows_new, (TILE, LANES)).T[0:1, :]


def update(places, slots, scalars, pieces, table, rows, cols, so_far):
    count = len(places)
    parts = len(pieces[0])
    block = pieces[0][0].shape[0]
    width = table.shape[1]
    steps = block // TILE

    def slot(p, slots):
        at = slots[places[0]]
        for j in range(1, count):
            at = jnp.where(p == j, slots[places[j]], at)
        return at

    place = lambda p, i, slots: (slot(p, slots) * steps + i, 0)
    place3 = lambda p, i, slots: (slot(p, slots) * steps + i, 0, 0)

    def own(part):
        return lambda p, i, slots: (jnp.where(p < part, 0, jnp.where(p > part, steps - 1, i)), 0)

    fixed = lambda p, i, slots: (0, 0)
    any_space = pl.BlockSpec(memory_space=pl.ANY)
    given = 5 + count * parts
    return pl.pallas_call(
        functools.partial(update_kernel, places, parts),
        grid_spec=pltpu.PrefetchScalarGridSpec(
            num_scalar_prefetch=1,
            grid=(count, steps),
            in_specs=[pl.BlockSpec(memory_space=pltpu.SMEM)]
            + [pl.BlockSpec((TILE, piece.shape[1]), own(part)) for part in range(count) for piece in pieces[part]]
            + [
                pl.BlockSpec((TILE, width), place),
                pl.BlockSpec((1, 1, TILE), place3),
                pl.BlockSpec((1, width), fixed),
                any_space,
                any_space,
                any_space,
            ],
            out_specs=[
                pl.BlockSpec((TILE, width), place),
                pl.BlockSpec((TILE, width), place),
                pl.BlockSpec((1, 1, TILE), place3),
            ],
        ),
        out_shape=[jax.ShapeDtypeStruct(part.shape, part.dtype) for part in so_far],
        input_output_aliases={given: 0, given + 1: 1, given + 2: 2},
        compiler_params=pltpu.CompilerParams(vmem_limit_bytes=vmem),
        cost_estimate=pl.CostEstimate(
            flops=10 * count * block * width, bytes_accessed=14 * count * block * width, transcendentals=0
        ),
    )(slots, scalars, *[piece for some in pieces for piece in some], table, rows, cols, *so_far)


def stack_kernel(slots_ref, *refs):
    pieces, out_ref = refs[:-1], refs[-1]
    for place, piece in enumerate(pieces):

        @pl.when(pl.program_id(0) == place)
        def _(piece=piece):
            out_ref[0] = piece[...]


def lay_out(slots, pieces):
    shape = pieces[0].shape
    return pl.pallas_call(
        stack_kernel,
        grid_spec=pltpu.PrefetchScalarGridSpec(
            num_scalar_prefetch=1,
            grid=(len(pieces),),
            in_specs=[pl.BlockSpec(shape, lambda i, slots: (0, 0), pipeline_mode=pl.Buffered(1))] * len(pieces),
            out_specs=pl.BlockSpec((1,) + shape, lambda i, slots: (slots[i], 0, 0)),
        ),
        out_shape=jax.ShapeDtypeStruct((len(pieces),) + shape, pieces[0].dtype),
        compiler_params=pltpu.CompilerParams(vmem_limit_bytes=vmem),
        cost_estimate=pl.CostEstimate(flops=0, bytes_accessed=4 * len(pieces) * pieces[0].size, transcendentals=0),
    )(slots, *pieces)


def columns_kernel(members_ref, slots_ref, own_ref, *refs):
    pieces, out_ref = refs[:-1], refs[-1]
    rows = own_ref.shape[0]

    def at(offset):
        return pl.ds(pl.multiple_of(members_ref[offset] * rows, rows), rows)

    out_ref[at(0), :] = own_ref[...].astype(low_type)
    for place, piece in enumerate(pieces):

        @pl.when(pl.program_id(0) == place)
        def _(piece=piece):
            for offset in range(piece.shape[0]):
                out_ref[at(offset + 1), :] = piece[offset]


def lay_columns(members, slots, own, pieces):
    others, rows, columns = pieces[0].shape
    replicas = len(pieces)
    whole = jax.ShapeDtypeStruct(((others + 1) * rows, replicas * columns), low_type)
    return pl.pallas_call(
        columns_kernel,
        grid_spec=pltpu.PrefetchScalarGridSpec(
            num_scalar_prefetch=2,
            grid=(replicas,),
            in_specs=[pl.BlockSpec((rows, columns), lambda i, members, slots: (0, slots[i]))]
            + [pl.BlockSpec(pieces[0].shape, lambda i, *_: (0, 0, 0), pipeline_mode=pl.Buffered(1))] * replicas,
            out_specs=pl.BlockSpec(((others + 1) * rows, columns), lambda i, members, slots: (0, slots[i])),
        ),
        out_shape=whole,
        compiler_params=pltpu.CompilerParams(vmem_limit_bytes=vmem),
        cost_estimate=pl.CostEstimate(flops=0, bytes_accessed=4 * whole.size, transcendentals=0),
    )(members, slots, own, *pieces)


def rows_kernel(members_ref, slots_ref, own_ref, *refs):
    pieces, out_ref = refs[:-1], refs[-1]
    out_ref[members_ref[0], 0] = own_ref[0].astype(low_type)
    for place, piece in enumerate(pieces):

        @pl.when(pl.program_id(0) == place)
        def _(piece=piece):
            for offset in range(piece.shape[0]):
                out_ref[members_ref[offset + 1], 0] = piece[offset]


def lay_rows(members, slots, own, pieces):
    others, rows, columns = pieces[0].shape
    replicas = len(pieces)
    whole = jax.ShapeDtypeStruct((others + 1, replicas, rows, columns), low_type)
    return pl.pallas_call(
        rows_kernel,
        grid_spec=pltpu.PrefetchScalarGridSpec(
            num_scalar_prefetch=2,
            grid=(replicas,),
            in_specs=[pl.BlockSpec((1, rows, columns), lambda i, members, slots: (slots[i], 0, 0))]
            + [pl.BlockSpec(pieces[0].shape, lambda i, *_: (0, 0, 0), pipeline_mode=pl.Buffered(1))] * replicas,
            out_specs=pl.BlockSpec((others + 1, 1, rows, columns), lambda i, members, slots: (0, slots[i], 0, 0)),
        ),
        out_shape=whole,
        compiler_params=pltpu.CompilerParams(vmem_limit_bytes=vmem),
        cost_estimate=pl.CostEstimate(flops=0, bytes_accessed=4 * whole.size, transcendentals=0),
    )(members, slots, own.reshape(replicas, rows, columns), *pieces).reshape(-1, columns)


tie = lax.optimization_barrier


def flip(value, bit):
    size = lax.axis_size("rep")
    return lax.ppermute(value, "rep", [(i, i ^ bit) for i in range(size)])


def turn(value, offset):
    size = lax.axis_size("grp")
    return lax.ppermute(value, "grp", [(i, (i + offset) % size) for i in range(size)])


def spread(piece, order):
    have = {0: piece}
    for bit in order:
        have.update({place ^ bit: flip(part, bit) for place, part in have.items()})
    return have


def slots_of():
    return lax.axis_index("rep") ^ jnp.arange(lax.axis_size("rep"), dtype=jnp.int32)


def plane_gather(piece):
    if lax.axis_size("rep") != 8:
        return lax.all_gather(piece, "rep")
    have = spread(piece, [2, 4, 1])
    return lay_out(slots_of(), [have[place] for place in range(8)])


def halve(value, axis, bit):
    mine = (lax.axis_index("rep") // bit) % 2
    kept = lax.dynamic_index_in_dim(value, mine, axis, keepdims=False)
    sent = lax.dynamic_index_in_dim(value, 1 - mine, axis, keepdims=False)
    return kept, sent.astype(low_type)


class Fold:
    def __init__(self, axis, order):
        self.axis = axis
        self.order = order
        self.quick = lax.axis_size("rep") == 8
        self.value = None

    def cores(self, chunks):
        axis = self.axis
        if not self.quick:
            self.value = lax.psum_scatter(chunks, "rep", scatter_dimension=axis)
            return []
        shape = chunks.shape
        kept, sent = halve(chunks.reshape(shape[:axis] + (4, 2) + shape[axis + 1 :]), axis + 1, 1)
        return self.from_cores(kept, sent)

    def from_cores(self, kept, sent):
        self.kept, self.got = kept, flip(sent, 1)
        return [sent]

    def sum(self):
        if self.value is None:
            return self.kept + self.got.astype(jnp.float32)
        return self.value

    def plane(self, first):
        if not self.quick:
            return []
        value = self.sum()
        axis = self.axis
        bit = self.order[0 if first else 1]
        if first:
            shape = value.shape
            value = value.reshape(shape[:axis] + (2, 2) + shape[axis + 1 :])
            axis = axis + (1 if bit == 2 else 0)
        self.kept, sent = halve(value, axis, bit)
        self.value, self.got = None, flip(sent, bit)
        return [sent]

    def members(self):
        value = self.sum()
        member = lax.axis_index("grp")
        size = lax.axis_size("grp")
        self.own = lax.dynamic_index_in_dim(value, member, 0, keepdims=False)
        sent = [
            lax.dynamic_index_in_dim(value, (member + offset) % size, 0, keepdims=False).astype(low_type)
            for offset in range(1, size)
        ]
        self.came = [turn(part, offset + 1) for offset, part in enumerate(sent)]
        return sent

    def total(self):
        return sum((came.astype(jnp.float32) for came in self.came), self.own)


def gradient_chunks(gradient):
    groups = lax.axis_size("grp")
    replicas = lax.axis_size("rep")
    rows, columns = gradient.shape
    return gradient.reshape(groups, replicas, rows // (groups * replicas), columns)


def across_wide(chunks):
    member = lax.axis_index("grp")
    size = lax.axis_size("grp")
    total = lax.dynamic_index_in_dim(chunks, member, 0, keepdims=False)
    for offset in range(1, size):
        sent = lax.dynamic_index_in_dim(chunks, (member + offset) % size, 0, keepdims=False)
        total = total + turn(sent, offset)
    return total


def group_gather(value):
    member = lax.axis_index("grp")
    size = lax.axis_size("grp")
    result = jnp.zeros((size,) + value.shape, value.dtype)
    result = lax.dynamic_update_index_in_dim(result, value, member, 0)
    for offset in range(1, size):
        result = lax.dynamic_update_index_in_dim(
            result, turn(value, offset), (member + size - offset) % size, 0
        )
    return result


def plane_sum(value):
    for j in range(1, lax.axis_size("rep").bit_length() - 1):
        value = value + flip(value, 1 << j)
    return value


def rest_sum(value):
    value = value + flip(value, 1)
    size = lax.axis_size("grp")
    for j in range(size.bit_length() - 1):
        value = value + lax.ppermute(value, "grp", [(i, i ^ (1 << j)) for i in range(size)])
    return value


def fetch(own):
    return jnp.stack([turn(own, offset) for offset in range(1, lax.axis_size("grp"))])


def cut(value, axis):
    replicas = lax.axis_size("rep")
    size = value.shape[axis] // replicas
    return lax.dynamic_slice_in_dim(value, lax.axis_index("rep") * size, size, axis)


def members_of():
    groups = lax.axis_size("grp")
    return (lax.axis_index("grp") + groups - jnp.arange(groups, dtype=jnp.int32)) % groups


def contract(left, right, left_dim, right_dim):
    return lax.dot_general(
        left, right, (((left_dim,), (right_dim,)), ((), ())), preferred_element_type=jnp.float32
    )


def layer_norm(values, gain, shift):
    center = values - jnp.mean(values, axis=-1, keepdims=True)
    spread = jnp.mean(center * center, axis=-1, keepdims=True)
    return center * lax.rsqrt(spread + ln_eps) * gain + shift


def rope_tables(length):
    freqs = rope_base ** (-jnp.arange(HD // 2, dtype=jnp.float32) * 2.0 / HD)
    angles = jnp.arange(length, dtype=jnp.float32)[:, None] * freqs[None, :]
    cosine, sine = jnp.cos(angles), jnp.sin(angles)
    return (
        jnp.concatenate([cosine] * 4, axis=-1),
        jnp.concatenate([-sine, sine, -sine, sine], axis=-1),
    )


def swiglu(joined):
    middle = joined.shape[-1] // 2
    return jax.nn.silu(joined[:, :middle]) * joined[:, middle:]


def merge_stats(first_part, second_part):
    peak = jnp.maximum(first_part[0], second_part[0])
    spread = first_part[1] * jnp.exp(first_part[0] - peak) + second_part[1] * jnp.exp(
        second_part[0] - peak
    )
    return (peak, spread, first_part[2] + second_part[2])


def body(
    ids,
    lengths,
    picks,
    labels,
    loss_mask,
    table,
    w_qkv,
    w_out,
    w_gu,
    w_down,
    norms,
    table_rows,
    table_cols,
    qkv_rows,
    qkv_cols,
    out_rows,
    out_cols,
    gu_rows,
    gu_cols,
    down_rows,
    down_cols,
    norms_moment,
):
    member = lax.axis_index("grp")
    groups = lax.axis_size("grp")
    replica = lax.axis_index("rep")
    replicas = lax.axis_size("rep")
    seqs, length = ids.shape
    width = table.shape[1]
    vocab_rows = table.shape[0]
    own_rows = seqs * picks.shape[1]
    tokens = seqs * length
    block = -(-vocab_rows // (16 * replicas)) * 16
    padded = block * replicas

    packed = jnp.concatenate([ids.reshape(-1), labels.reshape(-1), loss_mask.reshape(-1)])
    group_packed = group_gather(packed)
    group_ids = group_packed[:, :tokens].reshape(-1)
    group_labels = group_packed[:, tokens : tokens + own_rows].reshape(-1)
    group_mask = group_packed[:, tokens + own_rows :].reshape(-1)
    shard_rows = w_qkv.shape[0]
    quick = replicas == 8
    near_shard = jnp.concatenate([w_qkv, w_out], axis=1)
    if quick:
        near_part = fetch(cut(near_shard, 1).astype(low_type))
        gu_part = fetch(cut(w_gu, 1).astype(low_type))

    local_ids = group_ids - member * vocab_rows
    owned = (local_ids >= 0) & (local_ids < vocab_rows)
    places, order = lax.sort(
        (jnp.where(owned, local_ids, padded), jnp.arange(local_ids.shape[0], dtype=jnp.int32)), num_keys=1
    )
    bounds = jnp.arange(replicas + 1, dtype=jnp.int32) * block
    starts = jnp.sum((places[None, :] < bounds[:, None]).astype(jnp.int32), axis=1)
    if quick:
        places, near_part = tie((places, near_part))
    again = jnp.concatenate([jnp.zeros((1,), jnp.int32), (places[1:] == places[:-1]).astype(jnp.int32)])
    codes = jnp.pad(places % block * 2 + again, (0, 8))
    padded_order = jnp.pad(order, (0, 8))
    found = lookup(starts, places, order, table)
    if quick:
        found, gu_part = tie((found, gu_part))
    embed = lax.psum_scatter(found, "grp", scatter_dimension=0, tiled=True)
    late_table, _ = lax.optimization_barrier((table, found))
    table_low = jnp.pad(late_table.astype(low_type), ((0, padded - vocab_rows), (0, 0)))

    if quick:
        members, slots = members_of(), slots_of()

        down_own, _ = tie((cut(w_down, 0), found))
        down_part = fetch(down_own.astype(low_type))

        def listed(have):
            return [have[place] for place in range(replicas)]

        near = lay_columns(members, slots, near_shard, listed(spread(near_part, [4, 2, 1])))
        w_down_low = lay_rows(members, slots, w_down, listed(spread(down_part, [4, 2, 1])))
        gu_have = spread(gu_part, [2, 4])
        gu_have, near, w_down_low, table_low = tie((gu_have, near, w_down_low, table_low))
        gu_have.update({place ^ 1: flip(part, 1) for place, part in gu_have.items()})
        w_gu_low = lay_columns(members, slots, w_gu, listed(gu_have))
        embed, near, w_gu_low, w_down_low, table_low = tie((embed, near, w_gu_low, w_down_low, table_low))
    else:
        near = lax.all_gather(near_shard.astype(low_type), "grp", tiled=True)
        w_gu_low = lax.all_gather(w_gu.astype(low_type), "grp", tiled=True)
        w_down_low = lax.all_gather(w_down.astype(low_type), "grp", tiled=True)
    w_out_low = near[:, 3 * width :]
    cosine, sine = rope_tables(length)
    first, first_low, queries, keys, values = project(embed, norms, cosine, sine, near)
    queries, group_mask = tie((queries, group_mask))
    loss_count = jnp.sum(group_mask).astype(jnp.float32)[None]
    for j in range(replicas.bit_length() - 1):
        loss_count = loss_count + flip(loss_count, 1 << j)
    loss_count = loss_count[0]
    mixed_low, log_sums = attend(lengths, queries, keys, values)
    first_sum = first + jnp.dot(mixed_low, w_out_low, preferred_element_type=jnp.float32)
    second = layer_norm(first_sum, norms[2], norms[3])
    second_low = second.astype(low_type)
    gate_up = jnp.dot(second_low, w_gu_low, preferred_element_type=jnp.float32)
    hidden_low = swiglu(gate_up).astype(low_type)
    second_sum = second + jnp.dot(hidden_low, w_down_low, preferred_element_type=jnp.float32)
    final = layer_norm(second_sum, norms[4], norms[5])

    flat_picks = (jnp.arange(seqs, dtype=jnp.int32)[:, None] * length + picks).reshape(-1)
    chosen = final[flat_picks].astype(low_type)
    group_chosen = group_gather(chosen).reshape(groups * own_rows, width)
    rows_at = jnp.arange(padded, dtype=jnp.int32)[:, None]
    logits = jnp.where(rows_at < vocab_rows, contract(table_low, group_chosen, 1, 1), neg_large)
    peak = jnp.max(logits, axis=0)
    spread_sum = jnp.sum(jnp.exp(logits - peak[None, :]), axis=0)
    local_labels = group_labels - member * vocab_rows
    inside = (local_labels >= 0) & (local_labels < vocab_rows)
    hits = (rows_at == local_labels[None, :]) & inside[None, :]
    target = jnp.sum(jnp.where(hits, logits, 0.0), axis=0)
    stats = group_gather(jnp.stack([peak, spread_sum, target]))
    so_far = (stats[0, 0], stats[0, 1], stats[0, 2])
    for place in range(1, groups):
        so_far = merge_stats(so_far, (stats[place, 0], stats[place, 1], stats[place, 2]))
    peak_all, spread_all, target_all = so_far
    log_total = peak_all + jnp.log(spread_all)
    counted = group_mask > 0
    terms = jnp.where(counted, log_total - target_all, 0.0)
    own_terms = lax.dynamic_slice_in_dim(terms, member * own_rows, own_rows)
    row_scale = jnp.where(counted, 1.0 / loss_count, 0.0)
    dlogits = (
        (jnp.exp(logits - log_total[None, :]) - hits.astype(jnp.float32)) * row_scale[None, :]
    ).astype(low_type)
    chosen_part = contract(dlogits, table_low, 0, 0)
    chosen_grad = across_wide(chosen_part.reshape(groups, own_rows, width))
    final_grad = jnp.zeros((tokens, width), jnp.float32).at[flat_picks].add(chosen_grad)

    _, pull = jax.vjp(layer_norm, second_sum, norms[4], norms[5])
    sum_grad, gain_three, shift_three = pull(final_grad)
    branch_low = sum_grad.astype(low_type)
    down = Fold(1, (2, 4))
    down.cores(gradient_chunks(contract(hidden_low, branch_low, 0, 0)))
    hidden_grad = contract(branch_low, w_down_low, 1, 1)
    _, pull = jax.vjp(swiglu, gate_up)
    gate_low = pull(hidden_grad)[0].astype(low_type)
    gate_low, _ = tie((gate_low, down.plane(True)))
    gate, up = Fold(1, (4, 2)), Fold(1, (2, 4))
    middle = gate_up.shape[1] // 2
    sent = gate.cores(gradient_chunks(contract(second_low, gate_low[:, :middle], 0, 0)))
    sent += up.cores(gradient_chunks(contract(second_low, gate_low[:, middle:], 0, 0)))
    gate_low, _ = tie((gate_low, sent))
    second_grad = sum_grad + contract(gate_low, w_gu_low, 1, 1)
    second_grad, _ = tie((second_grad, gate.plane(True) + up.plane(True) + down.plane(False)))
    _, pull = jax.vjp(layer_norm, first_sum, norms[2], norms[3])
    first_sum_grad, gain_two, shift_two = pull(second_grad)
    attn_low = first_sum_grad.astype(low_type)
    mixed_grad = contract(attn_low, w_out_low, 1, 1).astype(low_type)
    pairs = width // LANES
    third = pairs // 3
    sides = []
    for stage in range(3):
        if stage:
            if stage == 1:
                sent = gate.plane(False) + up.plane(False) + down.members()
            else:
                sent = gate.members() + up.members()
            mixed_grad, sides[-1], _, down.came = tie((mixed_grad, sides[-1], sent, down.came))
        sides.append(
            attend_back(lengths, queries, keys, values, mixed_grad, log_sums, cosine, sine, stage * third, third)
        )
    sides, gate.came, up.came = tie((sides, gate.came, up.came))
    joined_grad = jnp.concatenate([side for parts in zip(*sides) for side in parts], axis=1)
    first_grad = first_sum_grad + contract(joined_grad, near[:, : 3 * width], 1, 1)
    _, pull = jax.vjp(layer_norm, embed.astype(jnp.float32), norms[0], norms[1])
    embed_grad, gain_one, shift_one = pull(first_grad)
    norm_grad = jnp.stack([gain_one, shift_one, gain_two, shift_two, gain_three, shift_three])
    embed_low, joined_grad = tie((embed_grad.astype(low_type), joined_grad))
    group_embed = lax.all_gather(embed_low, "grp", axis=0, tiled=True)

    join = Fold(1, (2, 4))
    join.cores(
        gradient_chunks(
            jnp.concatenate(
                [contract(first_low, joined_grad, 0, 0), contract(mixed_low, attn_low, 0, 0)], axis=1
            )
        )
    )
    join.plane(True)
    join.plane(False)
    join.members()
    gu_share = jnp.concatenate([gate.total(), up.total()], axis=1)
    down_share, join_share = down.total(), join.total()
    part_rows = gu_share.shape[0]
    far_whole = plane_gather(
        jnp.concatenate(
            [gu_share.astype(low_type), down_share.astype(low_type).reshape(part_rows, -1)], axis=1
        )
    ).reshape(shard_rows, -1)
    near_whole = plane_gather(join_share.astype(low_type)).reshape(shard_rows, -1)
    shares = (join_share[:, : 3 * width], join_share[:, 3 * width :], gu_share, down_share)
    share_cols = [jnp.sum(gradient * gradient, axis=0) for gradient in shares]
    group_embed, near_whole, far_whole, share_cols = tie((group_embed, near_whole, far_whole, share_cols))

    core = replica % 2
    middle = width // 2
    rest = (starts, codes, padded_order, dlogits, group_chosen, group_embed, block)
    if quick:
        chunks = ((replica // 2) ^ jnp.arange(3, -1, -1, dtype=jnp.int32)) * 2
        sent = table_grad_chunks(chunks + 1 - core, *rest, low_type)
        sent_x, kept_x, sent_y, kept_y = table_grad_chunks(chunks + core, *rest, low_type, flip(sent, 1))
        one = kept_x + flip(sent_x, 2).astype(jnp.float32)
        two = kept_y + flip(sent_y, 4).astype(jnp.float32)
        table_parts = [
            one[1] + flip(one[0].astype(low_type), 4).astype(jnp.float32),
            two[1] + flip(two[0].astype(low_type), 2).astype(jnp.float32),
        ]
    else:
        value = table_grad_chunks(jnp.arange(replicas, dtype=jnp.int32), *rest, jnp.float32)
        value = lax.psum_scatter(value, "rep", scatter_dimension=0)
        table_parts = [value[:, :middle], value[:, middle:]]

    old_rows = (table_rows, qkv_rows, out_rows, gu_rows, down_rows)
    old_cols = (table_cols, qkv_cols, out_cols, gu_cols, down_cols)
    masters = (table, w_qkv, w_out, w_gu, w_down)
    col_parts = [
        jnp.concatenate([jnp.sum(gradient * gradient, axis=0) for gradient in table_parts])
    ] + share_cols
    row_old = jnp.stack([jnp.sum(rows) for rows in old_rows]) / replicas
    small = [norm_grad.reshape(-1)] + col_parts + [row_old, jnp.sum(own_terms)[None]]
    plane_totals = plane_sum(jnp.concatenate(small))
    table_lows = [part.astype(low_type) for part in table_parts]
    plane_totals, table_lows = tie((plane_totals, table_lows))
    totals = rest_sum(plane_totals)
    cuts = []
    start = 0
    for part in small:
        cuts.append(totals[start : start + part.shape[0]])
        start += part.shape[0]
    norm_sum = cuts[0].reshape(norm_grad.shape)
    col_totals = cuts[1:6]
    old_totals = cuts[6]
    loss_sum = cuts[7][0]
    squares = [jnp.sum(part) for part in col_totals]
    clip_norm = jnp.sqrt(sum(squares) + jnp.sum(norm_sum * norm_sum))
    factor = clip_limit / jnp.maximum(clip_norm, clip_limit)
    decay = 1.0 - float(STEP) ** (-0.8)

    wholes = [
        None,
        near_whole[:, : 3 * width],
        near_whole[:, 3 * width :],
        far_whole[:, : w_gu.shape[1]],
        far_whole[:, w_gu.shape[1] :].reshape(w_down.shape),
    ]

    outputs = []
    for place in range(5):
        rows, columns = masters[place].shape
        full_rows = rows * groups
        new_cols = (
            decay * old_cols[place] + (1.0 - decay) * (col_totals[place] * factor * factor) / full_rows
        )
        row_total = decay * old_totals[place] + (1.0 - decay) * (squares[place] * factor * factor) / columns
        row_mean = row_total / full_rows
        if place == 0 and quick:
            have = [
                spread(low, [2, 4, 1] if part % 2 else [4, 2, 1]) for part, low in enumerate(table_lows)
            ]
            tiles = padded // TILE
            row_tiles = jnp.pad(table_rows, (0, padded - vocab_rows), constant_values=1.0).reshape(tiles, 1, TILE)
            scalars = jnp.stack([factor, rate_matrix * factor * jnp.sqrt(row_mean)])
            so_far = (
                blank(table.shape, jnp.float32),
                blank(table.shape, jnp.float32),
                blank((tiles, 1, TILE), jnp.float32),
            )
            for places in ((0,), (2, 4), (6,), (1, 3, 5, 7)):
                so_far = update(
                    places,
                    slots_of(),
                    scalars,
                    [[got[part] for got in have] for part in places],
                    table,
                    row_tiles,
                    lax.rsqrt(new_cols)[None, :],
                    so_far,
                )
            outputs.extend([so_far[0], so_far[2].reshape(-1)[:vocab_rows], new_cols, so_far[1]])
            continue
        if place == 0:
            whole = plane_gather(jnp.concatenate(table_lows, axis=1))
            gradient = whole.reshape(padded, width)[:vocab_rows].astype(jnp.float32)
        else:
            gradient = wholes[place].astype(jnp.float32)
        row_means = jnp.mean(gradient * gradient, axis=1)
        new_rows = decay * old_rows[place] + (1.0 - decay) * (row_means * factor * factor)
        clipped = gradient * factor
        scale = new_rows[:, None] * new_cols[None, :] / row_mean
        new_master = masters[place] - rate_matrix * clipped * lax.rsqrt(scale)
        outputs.extend([clipped, new_rows, new_cols, new_master])
    norm_clipped = norm_sum * factor
    moment_new = decay * norms_moment + (1.0 - decay) * norm_clipped * norm_clipped
    norms_new = norms - rate_norm * norm_clipped * lax.rsqrt(moment_new)
    return (
        (loss_sum, loss_count, clip_norm) + tuple(outputs) + (norm_clipped, moment_new, norms_new)
    )


def solution(mesh):
    in_specs = (
        P(("grp", "rep"), None),
        P(("grp", "rep")),
        P(("grp", "rep"), None),
        P(("grp", "rep"), None),
        P(("grp", "rep"), None),
        P("grp", None),
        P("grp", None),
        P("grp", None),
        P("grp", None),
        P("grp", None),
        P(),
        P("grp"),
        P(),
        P("grp"),
        P(),
        P("grp"),
        P(),
        P("grp"),
        P(),
        P("grp"),
        P(),
        P(),
    )
    out_specs = (
        P(),
        P(),
        P(),
        P("grp", None),
        P("grp"),
        P(),
        P("grp", None),
        P("grp", None),
        P("grp"),
        P(),
        P("grp", None),
        P("grp", None),
        P("grp"),
        P(),
        P("grp", None),
        P("grp", None),
        P("grp"),
        P(),
        P("grp", None),
        P("grp", None),
        P("grp"),
        P(),
        P("grp", None),
        P(),
        P(),
        P(),
    )
    return jax.shard_map(body, mesh=mesh, in_specs=in_specs, out_specs=out_specs, check_vma=False)
```

```python
import functools
import math

import jax
import jax.numpy as jnp
from jax import lax
from jax.experimental import pallas as pl
from jax.experimental.pallas import tpu as pltpu
from jax.sharding import PartitionSpec as P

HEADS = 12
HD = 64
STEP = 10
LANES = 128
ROWS = 256
CHUNK = 256
TILE = 480


ln_eps = 1e-05
rope_base = 10000.0
clip_limit = 0.01
rate_matrix = 0.03
rate_norm = 0.3
neg_large = -1e30
low_type = jnp.bfloat16
vmem = 56 * 1024 * 1024


def pair_lanes(shape):
    return lax.broadcasted_iota(jnp.int32, shape, len(shape) - 1)


def swap_halves(value):
    upper = (pair_lanes(value.shape) % HD) >= HD // 2
    return jnp.where(
        upper,
        pltpu.roll(value, HD // 2, axis=1),
        pltpu.roll(value, LANES - HD // 2, axis=1),
    )


def normalize(values, gain, shift):
    center = values - jnp.mean(values, axis=-1, keepdims=True)
    spread = jnp.mean(center * center, axis=-1, keepdims=True)
    return center * lax.rsqrt(spread + ln_eps) * gain + shift


def project_kernel(embed_ref, norms_ref, cosine_ref, sine_ref, w_ref, first_ref, low_ref, q_ref, k_ref, v_ref):
    first = normalize(embed_ref[...].astype(jnp.float32), norms_ref[0:1, :], norms_ref[1:2, :])
    first_ref[...] = first
    low = first.astype(low_type)
    low_ref[...] = low
    width = first.shape[1]
    cosine, sine = cosine_ref[...], sine_ref[...]
    for part, out_ref in enumerate((q_ref, k_ref)):
        joined = jnp.dot(low, w_ref[:, part * width : (part + 1) * width], preferred_element_type=jnp.float32)
        for start in range(0, width, LANES):
            piece = joined[:, start : start + LANES]
            out_ref[:, start : start + LANES] = (piece * cosine + swap_halves(piece) * sine).astype(low_type)
    v_ref[...] = jnp.dot(low, w_ref[:, 2 * width :], preferred_element_type=jnp.float32).astype(low_type)


def project(embed, norms, cosine, sine, weights):
    tokens, width = embed.shape
    row = lambda i: (i, 0)
    fixed = lambda i: (0, 0)
    low = jax.ShapeDtypeStruct((tokens, width), low_type)
    return pl.pallas_call(
        project_kernel,
        grid=(tokens // ROWS,),
        in_specs=[
            pl.BlockSpec((ROWS, width), row),
            pl.BlockSpec(norms.shape, fixed),
            pl.BlockSpec((ROWS, LANES), row),
            pl.BlockSpec((ROWS, LANES), row),
            pl.BlockSpec((width, 3 * width), fixed),
        ],
        out_specs=[pl.BlockSpec((ROWS, width), row)] * 5,
        out_shape=[jax.ShapeDtypeStruct((tokens, width), jnp.float32), low, low, low, low],
        compiler_params=pltpu.CompilerParams(vmem_limit_bytes=vmem),
        cost_estimate=pl.CostEstimate(flops=6 * tokens * width * width, bytes_accessed=20 * tokens * width, transcendentals=0),
    )(embed, norms, cosine, sine, weights)


def head_keys(k, bias, half):
    lanes = pair_lanes(k.shape)
    spare = HD - half * HD
    return jnp.where(lanes // HD == half, k, jnp.where(lanes == spare, bias, jnp.zeros_like(k)))


def head_queries(q, half, spare_value):
    lanes = pair_lanes(q.shape)
    spare = HD - half * HD
    scaled = q * jnp.asarray(1.0 / math.sqrt(HD), q.dtype)
    other = jnp.where(lanes == spare, jnp.full_like(q, spare_value), jnp.zeros_like(q))
    return jnp.where(lanes // HD == half, scaled, other)


def transposed_dot(left, right):
    return lax.dot_general(left, right, (((1,), (1,)), ((), ())), preferred_element_type=jnp.float32)


def key_bias(length_ref, tokens):
    place = lax.broadcasted_iota(jnp.int32, (tokens, LANES), 0)
    return jnp.where(place < length_ref[0], 0.0, neg_large).astype(low_type)


def attend_kernel(length_ref, q_ref, k_ref, v_ref, out_ref, log_ref, keys, turned):
    tokens = k_ref.shape[0]

    @pl.when(pl.program_id(1) == 0)
    def _():
        bias = key_bias(length_ref, tokens)
        for half in range(2):
            keys[half] = head_keys(k_ref[...], bias, half)
        turned[...] = v_ref[...].T

    parts = []
    for half in range(2):
        scores = transposed_dot(keys[half], head_queries(q_ref[...], half, 1.0))
        peak = jnp.max(scores, axis=0, keepdims=True)
        weights = jnp.exp(scores - peak)
        totals = jnp.sum(weights, axis=0, keepdims=True)
        probs = (weights * (1.0 / totals)).astype(low_type)
        parts.append(
            jnp.dot(turned[half * HD : (half + 1) * HD, :], probs, preferred_element_type=jnp.float32)
        )
        log_ref[0, half : half + 1, :] = peak + jnp.log(totals)
    out_ref[...] = jnp.concatenate(parts, axis=0).T.astype(low_type)


def attend(length, q, k, v):
    tokens, width = q.shape
    pairs = width // LANES
    own = lambda p, i, *_: (i, p)
    whole = lambda p, i, *_: (0, p)
    return pl.pallas_call(
        attend_kernel,
        grid_spec=pltpu.PrefetchScalarGridSpec(
            num_scalar_prefetch=1,
            grid=(pairs, tokens // ROWS),
            in_specs=[
                pl.BlockSpec((ROWS, LANES), own),
                pl.BlockSpec((tokens, LANES), whole),
                pl.BlockSpec((tokens, LANES), whole),
            ],
            out_specs=[
                pl.BlockSpec((ROWS, LANES), own),
                pl.BlockSpec((1, 2, ROWS), lambda p, i, *_: (p, 0, i)),
            ],
            scratch_shapes=[
                pltpu.VMEM((2, tokens, LANES), low_type),
                pltpu.VMEM((LANES, tokens), low_type),
            ],
        ),
        out_shape=[
            jax.ShapeDtypeStruct((tokens, width), low_type),
            jax.ShapeDtypeStruct((pairs, 2, tokens), jnp.float32),
        ],
        compiler_params=pltpu.CompilerParams(vmem_limit_bytes=vmem),
        cost_estimate=pl.CostEstimate(
            flops=16 * tokens * tokens * width, bytes_accessed=8 * tokens * width, transcendentals=tokens * tokens * width // HD
        ),
    )(length, q, k, v)


def rotate_back(grads, cosine, sine):
    return grads * cosine + swap_halves(grads * sine)


def attend_back_kernel(first_pair, length_ref, q_ref, k_ref, v_ref, d_ref, log_ref, cosq_ref, sinq_ref, cos_ref, sin_ref, *rest):
    dq_ref, dk_ref, dv_ref, keys, values, turned, dk_total, dv_total = rest[-8:]
    tokens = k_ref.shape[0]
    step = pl.program_id(1)

    @pl.when(step == 0)
    def _():
        bias = key_bias(length_ref, tokens)
        lanes = pair_lanes((tokens, LANES))
        for half in range(2):
            keys[half] = head_keys(k_ref[...], bias, half)
            values[half] = jnp.where(lanes // HD == half, v_ref[...], jnp.zeros_like(v_ref[...]))
        turned[...] = k_ref[...].T
        dk_total[...] = jnp.zeros_like(dk_total)
        dv_total[...] = jnp.zeros_like(dv_total)

    d = d_ref[...]
    lanes = pair_lanes(d.shape)
    parts = []
    dk = dv = None
    for half in range(2):
        scores = transposed_dot(keys[half], head_queries(q_ref[...], half, 1.0))
        probs = jnp.exp(scores - log_ref[0, half : half + 1, :])
        dprobs = transposed_dot(values[half], d)
        inner = jnp.sum(probs * dprobs, axis=0, keepdims=True)
        dscore = (probs * (dprobs - inner)).astype(low_type)
        parts.append(jnp.dot(turned[half * HD : (half + 1) * HD, :], dscore, preferred_element_type=jnp.float32))
        one_k = jnp.dot(dscore, head_queries(q_ref[...], half, 0.0), preferred_element_type=jnp.float32)
        one_v = jnp.dot(
            probs.astype(low_type), jnp.where(lanes // HD == half, d, jnp.zeros_like(d)), preferred_element_type=jnp.float32
        )
        dk = one_k if dk is None else dk + one_k
        dv = one_v if dv is None else dv + one_v
    dk_total[...] += dk
    dv_total[...] += dv
    dq = jnp.concatenate(parts, axis=0).T * (1.0 / math.sqrt(HD))
    dq_ref[...] = rotate_back(dq, cosq_ref[...], sinq_ref[...]).astype(low_type)

    @pl.when(step == pl.num_programs(1) - 1)
    def _():
        dk_ref[...] = rotate_back(dk_total[...], cos_ref[...], sin_ref[...]).astype(low_type)
        dv_ref[...] = dv_total[...].astype(low_type)


def attend_back(length, q, k, v, d, logs, cosine, sine, first_pair, pairs, after=()):
    tokens, width = q.shape
    own = lambda p, i, *_: (i, first_pair + p)
    whole = lambda p, i, *_: (0, first_pair + p)
    low = jax.ShapeDtypeStruct((tokens, pairs * LANES), low_type)
    fixed = pl.BlockSpec((tokens, LANES), lambda p, i, *_: (0, 0))
    row = pl.BlockSpec((ROWS, LANES), lambda p, i, *_: (i, 0))
    return pl.pallas_call(
        functools.partial(attend_back_kernel, first_pair),
        grid_spec=pltpu.PrefetchScalarGridSpec(
            num_scalar_prefetch=1,
            grid=(pairs, tokens // ROWS),
            in_specs=[
                pl.BlockSpec((ROWS, LANES), own),
                pl.BlockSpec((tokens, LANES), whole),
                pl.BlockSpec((tokens, LANES), whole),
                pl.BlockSpec((ROWS, LANES), own),
                pl.BlockSpec((1, 2, ROWS), lambda p, i, *_: (first_pair + p, 0, i)),
                row,
                row,
                fixed,
                fixed,
            ]
            + [pl.BlockSpec(memory_space=pl.ANY)] * len(after),
            out_specs=[
                pl.BlockSpec((ROWS, LANES), lambda p, i, *_: (i, p)),
                pl.BlockSpec((tokens, LANES), lambda p, i, *_: (0, p)),
                pl.BlockSpec((tokens, LANES), lambda p, i, *_: (0, p)),
            ],
            scratch_shapes=[
                pltpu.VMEM((2, tokens, LANES), low_type),
                pltpu.VMEM((2, tokens, LANES), low_type),
                pltpu.VMEM((LANES, tokens), low_type),
                pltpu.VMEM((tokens, LANES), jnp.float32),
                pltpu.VMEM((tokens, LANES), jnp.float32),
            ],
        ),
        out_shape=[low, low, low],
        compiler_params=pltpu.CompilerParams(vmem_limit_bytes=vmem),
        cost_estimate=pl.CostEstimate(
            flops=40 * tokens * tokens * pairs * LANES,
            bytes_accessed=16 * tokens * pairs * LANES,
            transcendentals=tokens * tokens * pairs * 2,
        ),
    )(length, q, k, v, d, logs, cosine, sine, cosine, sine, *after)


def forward_kernel(mixed_ref, first_ref, norms_ref, out_w_ref, gu_w_ref, down_w_ref, first_sum_ref, second_ref, gate_up_ref, hidden_ref, second_sum_ref, final_ref):
    width = first_ref.shape[1]
    middle = gu_w_ref.shape[1] // 2
    first_sum = first_ref[...] + jnp.dot(mixed_ref[...], out_w_ref[...], preferred_element_type=jnp.float32)
    first_sum_ref[...] = first_sum
    second = normalize(first_sum, norms_ref[2:3, :], norms_ref[3:4, :])
    low = second.astype(low_type)
    second_ref[...] = low
    total = second
    for start in range(0, middle, width):
        end = start + width
        gate = jnp.dot(low, gu_w_ref[:, start:end], preferred_element_type=jnp.float32)
        up = jnp.dot(low, gu_w_ref[:, middle + start : middle + end], preferred_element_type=jnp.float32)
        gate_up_ref[:, start:end] = gate
        gate_up_ref[:, middle + start : middle + end] = up
        hidden = (gate * (1.0 / (1.0 + jnp.exp(-gate))) * up).astype(low_type)
        hidden_ref[:, start:end] = hidden
        total = total + jnp.dot(hidden, down_w_ref[start:end, :], preferred_element_type=jnp.float32)
    second_sum_ref[...] = total
    final_ref[...] = normalize(total, norms_ref[4:5, :], norms_ref[5:6, :])


def feed_forward(mixed, first, norms, near, w_gu, w_down):
    tokens, width = first.shape
    middle = w_down.shape[0]
    row = lambda i: (i, 0)
    fixed = lambda i: (0, 0)
    once = pl.Buffered(1)
    narrow = pl.BlockSpec((ROWS, width), row)
    high = jax.ShapeDtypeStruct((tokens, width), jnp.float32)
    return pl.pallas_call(
        forward_kernel,
        grid=(tokens // ROWS,),
        in_specs=[
            narrow,
            narrow,
            pl.BlockSpec(norms.shape, fixed),
            pl.BlockSpec((width, width), lambda i: (0, 3), pipeline_mode=once),
            pl.BlockSpec(w_gu.shape, fixed, pipeline_mode=once),
            pl.BlockSpec(w_down.shape, fixed, pipeline_mode=once),
        ],
        out_specs=[
            narrow,
            narrow,
            pl.BlockSpec((ROWS, 2 * middle), row),
            pl.BlockSpec((ROWS, middle), row),
            narrow,
            narrow,
        ],
        out_shape=[
            high,
            jax.ShapeDtypeStruct((tokens, width), low_type),
            jax.ShapeDtypeStruct((tokens, 2 * middle), jnp.float32),
            jax.ShapeDtypeStruct((tokens, middle), low_type),
            high,
            high,
        ],
        compiler_params=pltpu.CompilerParams(vmem_limit_bytes=vmem),
        cost_estimate=pl.CostEstimate(
            flops=2 * tokens * width * (width + 3 * middle), bytes_accessed=14 * tokens * middle, transcendentals=tokens * middle
        ),
    )(mixed, first, norms, near, w_gu, w_down)


def normalize_back(values, gain, grads):
    center = values - jnp.mean(values, axis=-1, keepdims=True)
    inverse = lax.rsqrt(jnp.mean(center * center, axis=-1, keepdims=True) + ln_eps)
    unit = center * inverse
    scaled = grads * gain
    inner = jnp.mean(scaled * unit, axis=-1, keepdims=True)
    result = inverse * (scaled - jnp.mean(scaled, axis=-1, keepdims=True) - unit * inner)
    return result, jnp.sum(grads * unit, axis=0, keepdims=True), jnp.sum(grads, axis=0, keepdims=True)


def backward_kernel(grad_ref, second_sum_ref, first_sum_ref, gate_up_ref, norms_ref, out_w_ref, gu_w_ref, down_w_ref, branch_ref, gate_low_ref, first_sum_grad_ref, attn_ref, mixed_ref, norms_grad_ref):
    width = grad_ref.shape[1]
    middle = down_w_ref.shape[0]
    sum_grad, gain_three, shift_three = normalize_back(second_sum_ref[...], norms_ref[4:5, :], grad_ref[...])
    branch = sum_grad.astype(low_type)
    branch_ref[...] = branch
    total = sum_grad
    for start in range(0, middle, width):
        end = start + width
        hidden_grad = transposed_dot(branch, down_w_ref[start:end, :])
        gate = gate_up_ref[:, start:end]
        up = gate_up_ref[:, middle + start : middle + end]
        share = 1.0 / (1.0 + jnp.exp(-gate))
        gate_grad = (hidden_grad * up * (share * (1.0 + gate * (1.0 - share)))).astype(low_type)
        up_grad = (hidden_grad * (gate * share)).astype(low_type)
        gate_low_ref[:, start:end] = gate_grad
        gate_low_ref[:, middle + start : middle + end] = up_grad
        total = total + transposed_dot(gate_grad, gu_w_ref[:, start:end])
        total = total + transposed_dot(up_grad, gu_w_ref[:, middle + start : middle + end])
    first_sum_grad, gain_two, shift_two = normalize_back(first_sum_ref[...], norms_ref[2:3, :], total)
    first_sum_grad_ref[...] = first_sum_grad
    attn = first_sum_grad.astype(low_type)
    attn_ref[...] = attn
    mixed_ref[...] = transposed_dot(attn, out_w_ref[...]).astype(low_type)

    @pl.when(pl.program_id(0) == 0)
    def _():
        norms_grad_ref[...] = jnp.zeros_like(norms_grad_ref)

    norms_grad_ref[...] += jnp.concatenate([gain_two, shift_two, gain_three, shift_three], axis=0)


def feed_backward(grad, second_sum, first_sum, gate_up, norms, near, w_gu, w_down):
    tokens, width = grad.shape
    middle = w_down.shape[0]
    row = lambda i: (i, 0)
    fixed = lambda i: (0, 0)
    once = pl.Buffered(1)
    narrow = pl.BlockSpec((ROWS, width), row)
    wide = pl.BlockSpec((ROWS, 2 * middle), row)
    low = jax.ShapeDtypeStruct((tokens, width), low_type)
    return pl.pallas_call(
        backward_kernel,
        grid=(tokens // ROWS,),
        in_specs=[
            narrow,
            narrow,
            narrow,
            wide,
            pl.BlockSpec(norms.shape, fixed),
            pl.BlockSpec((width, width), lambda i: (0, 3), pipeline_mode=once),
            pl.BlockSpec(w_gu.shape, fixed, pipeline_mode=once),
            pl.BlockSpec(w_down.shape, fixed, pipeline_mode=once),
        ],
        out_specs=[narrow, wide, narrow, narrow, narrow, pl.BlockSpec((4, width), fixed)],
        out_shape=[
            low,
            jax.ShapeDtypeStruct((tokens, 2 * middle), low_type),
            jax.ShapeDtypeStruct((tokens, width), jnp.float32),
            low,
            low,
            jax.ShapeDtypeStruct((4, width), jnp.float32),
        ],
        compiler_params=pltpu.CompilerParams(vmem_limit_bytes=vmem),
        cost_estimate=pl.CostEstimate(
            flops=2 * tokens * width * (width + 3 * middle), bytes_accessed=14 * tokens * middle, transcendentals=tokens * middle
        ),
    )(grad, second_sum, first_sum, gate_up, norms, near, w_gu, w_down)


def blank(shape, dtype):
    return pl.pallas_call(
        lambda out_ref: None,
        out_shape=jax.ShapeDtypeStruct(shape, dtype),
        out_specs=pl.BlockSpec(memory_space=pl.ANY),
    )()


def lookup_kernel(starts_ref, places_ref, order_ref, table_ref, out_ref, rows):
    count = out_ref.shape[0]
    owned = starts_ref[starts_ref.shape[0] - 1]
    for start in range(0, count, CHUNK):
        rows[start : start + CHUNK, :] = jnp.zeros((CHUNK, rows.shape[1]), jnp.float32)

    def eight(step, carry):
        for j in range(8):
            i = step * 8 + j
            valid = i < owned
            source = jnp.where(valid, places_ref[i], 0)
            target = jnp.where(valid, order_ref[i], count)
            rows[pl.ds(target, 1), :] = table_ref[pl.ds(source, 1), :]
        return carry

    lax.fori_loop(0, (owned + 7) // 8, eight, 0)
    for start in range(0, count, CHUNK):
        out_ref[start : start + CHUNK, :] = rows[start : start + CHUNK, :].astype(low_type)


def lookup(starts, places, order, table):
    count = places.shape[0]
    width = table.shape[1]
    return pl.pallas_call(
        lookup_kernel,
        grid_spec=pltpu.PrefetchScalarGridSpec(
            num_scalar_prefetch=3,
            grid=(1,),
            in_specs=[pl.BlockSpec(table.shape, lambda i, *_: (0, 0), pipeline_mode=pl.Buffered(1))],
            out_specs=pl.BlockSpec((count, width), lambda i, *_: (0, 0), pipeline_mode=pl.Buffered(1)),
            scratch_shapes=[pltpu.VMEM((count + 8, width), jnp.float32)],
        ),
        out_shape=jax.ShapeDtypeStruct((count, width), low_type),
        compiler_params=pltpu.CompilerParams(vmem_limit_bytes=vmem),
        cost_estimate=pl.CostEstimate(flops=0, bytes_accessed=table.size * 12, transcendentals=0),
    )(starts, places, order, table)


def table_grad_kernel(chunks_ref, starts_ref, codes_ref, order_ref, dlogits_ref, chosen_ref, embed_ref, *refs):
    rows, sums = refs[-2:]
    step = pl.program_id(0)
    count, width = embed_ref.shape
    block = dlogits_ref.shape[0]

    @pl.when(step == 0)
    def _():
        for start in range(0, count, CHUNK):
            rows[start : start + CHUNK, :] = embed_ref[start : start + CHUNK, :].astype(jnp.float32)

    sums[...] = jnp.zeros_like(sums)
    chunk = chunks_ref[step]
    first, last = starts_ref[chunk], starts_ref[chunk + 1]

    def eight(turn, running):
        for j in range(8):
            i = first + turn * 8 + j
            code = codes_ref[i]
            place = jnp.where(i < last, code >> 1, block)
            running = jnp.where(code & 1, running, 0.0) + rows[pl.ds(order_ref[i], 1), :]
            sums[pl.ds(place, 1), :] = running
        return running

    lax.fori_loop(0, (last - first + 7) // 8, eight, jnp.zeros((1, width), jnp.float32))
    product = jnp.dot(dlogits_ref[...], chosen_ref[...], preferred_element_type=jnp.float32)
    result = product + sums[:block, :]
    if len(refs) == 3:
        refs[0][0] = result.astype(refs[0].dtype)
        return
    got_ref, sent_x, kept_x, sent_y, kept_y = refs[:-2]
    result = result + got_ref[0].astype(jnp.float32)
    left, right = result[:, : width // 2], result[:, width // 2 :]

    @pl.when(step % 2 == 0)
    def _():
        sent_x[0] = left.astype(sent_x.dtype)

    @pl.when(step % 2 == 1)
    def _():
        kept_x[0] = left

    @pl.when(step < 2)
    def _():
        sent_y[0] = right.astype(sent_y.dtype)

    @pl.when(step >= 2)
    def _():
        kept_y[0] = right


def table_grad_chunks(chunks, starts, codes, order, dlogits, chosen, embed, block, dtype, got=None):
    count, width = embed.shape
    picked = chosen.shape[0]
    steps = chunks.shape[0]
    fixed = lambda i, *_: (0, 0)
    in_specs = [
        pl.BlockSpec((block, picked), lambda i, chunks, *_: (chunks[i], 0)),
        pl.BlockSpec((picked, width), fixed),
        pl.BlockSpec((count, width), fixed, pipeline_mode=pl.Buffered(1)),
    ]
    whole = pl.BlockSpec((1, block, width), lambda i, *_: (i, 0, 0))
    if got is None:
        out_shape = jax.ShapeDtypeStruct((steps, block, width), dtype)
        out_specs = whole
    else:
        in_specs.append(whole)
        half = (1, block, width // 2)
        by_y = lambda i, *_: (i // 2, 0, 0)
        low = jax.ShapeDtypeStruct((2, block, width // 2), low_type)
        high = jax.ShapeDtypeStruct((2, block, width // 2), jnp.float32)
        out_shape = [low, high, low, high]
        out_specs = [
            pl.BlockSpec(half, by_y),
            pl.BlockSpec(half, by_y),
            pl.BlockSpec(half, lambda i, *_: (jnp.minimum(i, 1), 0, 0)),
            pl.BlockSpec(half, lambda i, *_: (jnp.maximum(i - 2, 0), 0, 0)),
        ]
    return pl.pallas_call(
        table_grad_kernel,
        grid_spec=pltpu.PrefetchScalarGridSpec(
            num_scalar_prefetch=4,
            grid=(steps,),
            in_specs=in_specs,
            out_specs=out_specs,
            scratch_shapes=[
                pltpu.VMEM((count, width), jnp.float32),
                pltpu.VMEM((block + 8, width), jnp.float32),
            ],
        ),
        out_shape=out_shape,
        compiler_params=pltpu.CompilerParams(vmem_limit_bytes=vmem),
        cost_estimate=pl.CostEstimate(
            flops=2 * steps * block * picked * width, bytes_accessed=8 * steps * block * width, transcendentals=0
        ),
    )(chunks, starts, codes, order, dlogits, chosen, embed, *(() if got is None else (got,)))


def update_kernel(places, parts, slots_ref, scalars_ref, *rest):
    given = len(places) * parts
    pieces = rest[:given]
    table_ref, rows_ref, cols_ref = rest[given : given + 3]
    grad_ref, new_ref, rows_new_ref = rest[-3:]
    factor, rate = scalars_ref[0], scalars_ref[1]
    decay = 1.0 - float(STEP) ** (-0.8)
    old = jnp.broadcast_to(rows_ref[0], (LANES, TILE)).T[:, 0:1]
    for part in range(len(places)):

        @pl.when(pl.program_id(0) == part)
        def _(part=part):
            own = pieces[part * parts : (part + 1) * parts]
            gradient = jnp.concatenate([piece[...] for piece in own], axis=1).astype(jnp.float32)
            means = jnp.mean(gradient * gradient, axis=1, keepdims=True)
            rows_new = decay * old + (1.0 - decay) * (means * factor * factor)
            grad_ref[...] = gradient * factor
            new_ref[...] = table_ref[...] - gradient * (rate * lax.rsqrt(rows_new)) * cols_ref[...]
            rows_new_ref[0] = jnp.broadcast_to(rows_new, (TILE, LANES)).T[0:1, :]


def update(places, slots, scalars, pieces, table, rows, cols, so_far):
    count = len(places)
    parts = len(pieces[0])
    block = pieces[0][0].shape[0]
    width = table.shape[1]
    steps = block // TILE

    def slot(p, slots):
        at = slots[places[0]]
        for j in range(1, count):
            at = jnp.where(p == j, slots[places[j]], at)
        return at

    place = lambda p, i, slots: (slot(p, slots) * steps + i, 0)
    place3 = lambda p, i, slots: (slot(p, slots) * steps + i, 0, 0)

    def own(part):
        return lambda p, i, slots: (jnp.where(p < part, 0, jnp.where(p > part, steps - 1, i)), 0)

    fixed = lambda p, i, slots: (0, 0)
    any_space = pl.BlockSpec(memory_space=pl.ANY)
    given = 5 + count * parts
    return pl.pallas_call(
        functools.partial(update_kernel, places, parts),
        grid_spec=pltpu.PrefetchScalarGridSpec(
            num_scalar_prefetch=1,
            grid=(count, steps),
            in_specs=[pl.BlockSpec(memory_space=pltpu.SMEM)]
            + [pl.BlockSpec((TILE, piece.shape[1]), own(part)) for part in range(count) for piece in pieces[part]]
            + [
                pl.BlockSpec((TILE, width), place),
                pl.BlockSpec((1, 1, TILE), place3),
                pl.BlockSpec((1, width), fixed),
                any_space,
                any_space,
                any_space,
            ],
            out_specs=[
                pl.BlockSpec((TILE, width), place),
                pl.BlockSpec((TILE, width), place),
                pl.BlockSpec((1, 1, TILE), place3),
            ],
        ),
        out_shape=[jax.ShapeDtypeStruct(part.shape, part.dtype) for part in so_far],
        input_output_aliases={given: 0, given + 1: 1, given + 2: 2},
        compiler_params=pltpu.CompilerParams(vmem_limit_bytes=vmem),
        cost_estimate=pl.CostEstimate(
            flops=10 * count * block * width, bytes_accessed=14 * count * block * width, transcendentals=0
        ),
    )(slots, scalars, *[piece for some in pieces for piece in some], table, rows, cols, *so_far)


def stack_kernel(slots_ref, *refs):
    pieces, out_ref = refs[:-1], refs[-1]
    for place, piece in enumerate(pieces):

        @pl.when(pl.program_id(0) == place)
        def _(piece=piece):
            out_ref[0] = piece[...]


def lay_out(slots, pieces):
    shape = pieces[0].shape
    return pl.pallas_call(
        stack_kernel,
        grid_spec=pltpu.PrefetchScalarGridSpec(
            num_scalar_prefetch=1,
            grid=(len(pieces),),
            in_specs=[pl.BlockSpec(shape, lambda i, slots: (0, 0), pipeline_mode=pl.Buffered(1))] * len(pieces),
            out_specs=pl.BlockSpec((1,) + shape, lambda i, slots: (slots[i], 0, 0)),
        ),
        out_shape=jax.ShapeDtypeStruct((len(pieces),) + shape, pieces[0].dtype),
        compiler_params=pltpu.CompilerParams(vmem_limit_bytes=vmem),
        cost_estimate=pl.CostEstimate(flops=0, bytes_accessed=4 * len(pieces) * pieces[0].size, transcendentals=0),
    )(slots, *pieces)


def columns_kernel(members_ref, slots_ref, own_ref, *refs):
    pieces, out_ref = refs[:-1], refs[-1]
    rows = own_ref.shape[0]

    def at(offset):
        return pl.ds(pl.multiple_of(members_ref[offset] * rows, rows), rows)

    out_ref[at(0), :] = own_ref[...].astype(low_type)
    for place, piece in enumerate(pieces):

        @pl.when(pl.program_id(0) == place)
        def _(piece=piece):
            for offset in range(piece.shape[0]):
                out_ref[at(offset + 1), :] = piece[offset]


def lay_columns(members, slots, own, pieces):
    others, rows, columns = pieces[0].shape
    replicas = len(pieces)
    whole = jax.ShapeDtypeStruct(((others + 1) * rows, replicas * columns), low_type)
    return pl.pallas_call(
        columns_kernel,
        grid_spec=pltpu.PrefetchScalarGridSpec(
            num_scalar_prefetch=2,
            grid=(replicas,),
            in_specs=[pl.BlockSpec((rows, columns), lambda i, members, slots: (0, slots[i]))]
            + [pl.BlockSpec(pieces[0].shape, lambda i, *_: (0, 0, 0), pipeline_mode=pl.Buffered(1))] * replicas,
            out_specs=pl.BlockSpec(((others + 1) * rows, columns), lambda i, members, slots: (0, slots[i])),
        ),
        out_shape=whole,
        compiler_params=pltpu.CompilerParams(vmem_limit_bytes=vmem),
        cost_estimate=pl.CostEstimate(flops=0, bytes_accessed=4 * whole.size, transcendentals=0),
    )(members, slots, own, *pieces)


def rows_kernel(members_ref, slots_ref, own_ref, *refs):
    pieces, out_ref = refs[:-1], refs[-1]
    out_ref[members_ref[0], 0] = own_ref[0].astype(low_type)
    for place, piece in enumerate(pieces):

        @pl.when(pl.program_id(0) == place)
        def _(piece=piece):
            for offset in range(piece.shape[0]):
                out_ref[members_ref[offset + 1], 0] = piece[offset]


def lay_rows(members, slots, own, pieces):
    others, rows, columns = pieces[0].shape
    replicas = len(pieces)
    whole = jax.ShapeDtypeStruct((others + 1, replicas, rows, columns), low_type)
    return pl.pallas_call(
        rows_kernel,
        grid_spec=pltpu.PrefetchScalarGridSpec(
            num_scalar_prefetch=2,
            grid=(replicas,),
            in_specs=[pl.BlockSpec((1, rows, columns), lambda i, members, slots: (slots[i], 0, 0))]
            + [pl.BlockSpec(pieces[0].shape, lambda i, *_: (0, 0, 0), pipeline_mode=pl.Buffered(1))] * replicas,
            out_specs=pl.BlockSpec((others + 1, 1, rows, columns), lambda i, members, slots: (0, slots[i], 0, 0)),
        ),
        out_shape=whole,
        compiler_params=pltpu.CompilerParams(vmem_limit_bytes=vmem),
        cost_estimate=pl.CostEstimate(flops=0, bytes_accessed=4 * whole.size, transcendentals=0),
    )(members, slots, own.reshape(replicas, rows, columns), *pieces).reshape(-1, columns)


tie = lax.optimization_barrier


def flip(value, bit):
    size = lax.axis_size("rep")
    return lax.ppermute(value, "rep", [(i, i ^ bit) for i in range(size)])


def turn(value, offset):
    size = lax.axis_size("grp")
    return lax.ppermute(value, "grp", [(i, (i + offset) % size) for i in range(size)])


def spread(piece, order):
    have = {0: piece}
    for bit in order:
        have.update({place ^ bit: flip(part, bit) for place, part in have.items()})
    return have


def slots_of():
    return lax.axis_index("rep") ^ jnp.arange(lax.axis_size("rep"), dtype=jnp.int32)


def plane_gather(piece):
    if lax.axis_size("rep") != 8:
        return lax.all_gather(piece, "rep")
    have = spread(piece, [2, 4, 1])
    return lay_out(slots_of(), [have[place] for place in range(8)])


def halve(value, axis, bit):
    mine = (lax.axis_index("rep") // bit) % 2
    kept = lax.dynamic_index_in_dim(value, mine, axis, keepdims=False)
    sent = lax.dynamic_index_in_dim(value, 1 - mine, axis, keepdims=False)
    return kept, sent.astype(low_type)


class Fold:
    def __init__(self, axis, order):
        self.axis = axis
        self.order = order
        self.quick = lax.axis_size("rep") == 8
        self.value = None

    def cores(self, chunks):
        axis = self.axis
        if not self.quick:
            self.value = lax.psum_scatter(chunks, "rep", scatter_dimension=axis)
            return []
        shape = chunks.shape
        kept, sent = halve(chunks.reshape(shape[:axis] + (4, 2) + shape[axis + 1 :]), axis + 1, 1)
        return self.from_cores(kept, sent)

    def from_cores(self, kept, sent):
        self.kept, self.got = kept, flip(sent, 1)
        return [sent]

    def sum(self):
        if self.value is None:
            return self.kept + self.got.astype(jnp.float32)
        return self.value

    def plane(self, first):
        if not self.quick:
            return []
        value = self.sum()
        axis = self.axis
        bit = self.order[0 if first else 1]
        if first:
            shape = value.shape
            value = value.reshape(shape[:axis] + (2, 2) + shape[axis + 1 :])
            axis = axis + (1 if bit == 2 else 0)
        self.kept, sent = halve(value, axis, bit)
        self.value, self.got = None, flip(sent, bit)
        return [sent]

    def members(self):
        value = self.sum()
        member = lax.axis_index("grp")
        size = lax.axis_size("grp")
        self.own = lax.dynamic_index_in_dim(value, member, 0, keepdims=False)
        sent = [
            lax.dynamic_index_in_dim(value, (member + offset) % size, 0, keepdims=False).astype(low_type)
            for offset in range(1, size)
        ]
        self.came = [turn(part, offset + 1) for offset, part in enumerate(sent)]
        return sent

    def total(self):
        return sum((came.astype(jnp.float32) for came in self.came), self.own)


def gradient_chunks(gradient):
    groups = lax.axis_size("grp")
    replicas = lax.axis_size("rep")
    rows, columns = gradient.shape
    return gradient.reshape(groups, replicas, rows // (groups * replicas), columns)


def across_wide(chunks):
    member = lax.axis_index("grp")
    size = lax.axis_size("grp")
    total = lax.dynamic_index_in_dim(chunks, member, 0, keepdims=False)
    for offset in range(1, size):
        sent = lax.dynamic_index_in_dim(chunks, (member + offset) % size, 0, keepdims=False)
        total = total + turn(sent, offset)
    return total


def group_gather(value):
    member = lax.axis_index("grp")
    size = lax.axis_size("grp")
    result = jnp.zeros((size,) + value.shape, value.dtype)
    result = lax.dynamic_update_index_in_dim(result, value, member, 0)
    for offset in range(1, size):
        result = lax.dynamic_update_index_in_dim(
            result, turn(value, offset), (member + size - offset) % size, 0
        )
    return result


def plane_sum(value):
    for j in range(1, lax.axis_size("rep").bit_length() - 1):
        value = value + flip(value, 1 << j)
    return value


def rest_sum(value):
    value = value + flip(value, 1)
    size = lax.axis_size("grp")
    for j in range(size.bit_length() - 1):
        value = value + lax.ppermute(value, "grp", [(i, i ^ (1 << j)) for i in range(size)])
    return value


def fetch(own):
    return jnp.stack([turn(own, offset) for offset in range(1, lax.axis_size("grp"))])


def cut(value, axis):
    replicas = lax.axis_size("rep")
    size = value.shape[axis] // replicas
    return lax.dynamic_slice_in_dim(value, lax.axis_index("rep") * size, size, axis)


def members_of():
    groups = lax.axis_size("grp")
    return (lax.axis_index("grp") + groups - jnp.arange(groups, dtype=jnp.int32)) % groups


def contract(left, right, left_dim, right_dim):
    return lax.dot_general(
        left, right, (((left_dim,), (right_dim,)), ((), ())), preferred_element_type=jnp.float32
    )


def layer_norm(values, gain, shift):
    center = values - jnp.mean(values, axis=-1, keepdims=True)
    spread = jnp.mean(center * center, axis=-1, keepdims=True)
    return center * lax.rsqrt(spread + ln_eps) * gain + shift


def rope_tables(length):
    freqs = rope_base ** (-jnp.arange(HD // 2, dtype=jnp.float32) * 2.0 / HD)
    angles = jnp.arange(length, dtype=jnp.float32)[:, None] * freqs[None, :]
    cosine, sine = jnp.cos(angles), jnp.sin(angles)
    return (
        jnp.concatenate([cosine] * 4, axis=-1),
        jnp.concatenate([-sine, sine, -sine, sine], axis=-1),
    )


def merge_stats(first_part, second_part):
    peak = jnp.maximum(first_part[0], second_part[0])
    spread = first_part[1] * jnp.exp(first_part[0] - peak) + second_part[1] * jnp.exp(
        second_part[0] - peak
    )
    return (peak, spread, first_part[2] + second_part[2])


def body(
    ids,
    lengths,
    picks,
    labels,
    loss_mask,
    table,
    w_qkv,
    w_out,
    w_gu,
    w_down,
    norms,
    table_rows,
    table_cols,
    qkv_rows,
    qkv_cols,
    out_rows,
    out_cols,
    gu_rows,
    gu_cols,
    down_rows,
    down_cols,
    norms_moment,
):
    member = lax.axis_index("grp")
    groups = lax.axis_size("grp")
    replica = lax.axis_index("rep")
    replicas = lax.axis_size("rep")
    seqs, length = ids.shape
    width = table.shape[1]
    vocab_rows = table.shape[0]
    own_rows = seqs * picks.shape[1]
    tokens = seqs * length
    block = -(-vocab_rows // (16 * replicas)) * 16
    padded = block * replicas

    packed = jnp.concatenate([ids.reshape(-1), labels.reshape(-1), loss_mask.reshape(-1)])
    group_packed = group_gather(packed)
    group_ids = group_packed[:, :tokens].reshape(-1)
    group_labels = group_packed[:, tokens : tokens + own_rows].reshape(-1)
    group_mask = group_packed[:, tokens + own_rows :].reshape(-1)
    shard_rows = w_qkv.shape[0]
    quick = replicas == 8
    near_shard = jnp.concatenate([w_qkv, w_out], axis=1)
    if quick:
        near_part = fetch(cut(near_shard, 1).astype(low_type))
        gu_part = fetch(cut(w_gu, 1).astype(low_type))

    local_ids = group_ids - member * vocab_rows
    owned = (local_ids >= 0) & (local_ids < vocab_rows)
    places, order = lax.sort(
        (jnp.where(owned, local_ids, padded), jnp.arange(local_ids.shape[0], dtype=jnp.int32)), num_keys=1
    )
    bounds = jnp.arange(replicas + 1, dtype=jnp.int32) * block
    starts = jnp.sum((places[None, :] < bounds[:, None]).astype(jnp.int32), axis=1)
    if quick:
        places, near_part = tie((places, near_part))
    again = jnp.concatenate([jnp.zeros((1,), jnp.int32), (places[1:] == places[:-1]).astype(jnp.int32)])
    codes = jnp.pad(places % block * 2 + again, (0, 8))
    padded_order = jnp.pad(order, (0, 8))
    found = lookup(starts, places, order, table)
    if quick:
        found, gu_part = tie((found, gu_part))
    embed = lax.psum_scatter(found, "grp", scatter_dimension=0, tiled=True)
    late_table, _ = lax.optimization_barrier((table, found))
    table_low = jnp.pad(late_table.astype(low_type), ((0, padded - vocab_rows), (0, 0)))

    if quick:
        members, slots = members_of(), slots_of()

        down_own, _ = tie((cut(w_down, 0), found))
        down_part = fetch(down_own.astype(low_type))

        def listed(have):
            return [have[place] for place in range(replicas)]

        near = lay_columns(members, slots, near_shard, listed(spread(near_part, [4, 2, 1])))
        w_down_low = lay_rows(members, slots, w_down, listed(spread(down_part, [4, 2, 1])))
        gu_have = spread(gu_part, [2, 4])
        gu_have, near, w_down_low, table_low = tie((gu_have, near, w_down_low, table_low))
        gu_have.update({place ^ 1: flip(part, 1) for place, part in gu_have.items()})
        w_gu_low = lay_columns(members, slots, w_gu, listed(gu_have))
        embed, near, w_gu_low, w_down_low, table_low = tie((embed, near, w_gu_low, w_down_low, table_low))
    else:
        near = lax.all_gather(near_shard.astype(low_type), "grp", tiled=True)
        w_gu_low = lax.all_gather(w_gu.astype(low_type), "grp", tiled=True)
        w_down_low = lax.all_gather(w_down.astype(low_type), "grp", tiled=True)
    cosine, sine = rope_tables(length)
    first, first_low, queries, keys, values = project(embed, norms, cosine, sine, near)
    queries, group_mask = tie((queries, group_mask))
    loss_count = jnp.sum(group_mask).astype(jnp.float32)[None]
    for j in range(replicas.bit_length() - 1):
        loss_count = loss_count + flip(loss_count, 1 << j)
    loss_count = loss_count[0]
    mixed_low, log_sums = attend(lengths, queries, keys, values)
    first_sum, second_low, gate_up, hidden_low, second_sum, final = feed_forward(
        mixed_low, first, norms, near, w_gu_low, w_down_low
    )

    flat_picks = (jnp.arange(seqs, dtype=jnp.int32)[:, None] * length + picks).reshape(-1)
    chosen = final[flat_picks].astype(low_type)
    group_chosen = group_gather(chosen).reshape(groups * own_rows, width)
    rows_at = jnp.arange(padded, dtype=jnp.int32)[:, None]
    logits = jnp.where(rows_at < vocab_rows, contract(table_low, group_chosen, 1, 1), neg_large)
    peak = jnp.max(logits, axis=0)
    spread_sum = jnp.sum(jnp.exp(logits - peak[None, :]), axis=0)
    local_labels = group_labels - member * vocab_rows
    inside = (local_labels >= 0) & (local_labels < vocab_rows)
    hits = (rows_at == local_labels[None, :]) & inside[None, :]
    target = jnp.sum(jnp.where(hits, logits, 0.0), axis=0)
    stats = group_gather(jnp.stack([peak, spread_sum, target]))
    so_far = (stats[0, 0], stats[0, 1], stats[0, 2])
    for place in range(1, groups):
        so_far = merge_stats(so_far, (stats[place, 0], stats[place, 1], stats[place, 2]))
    peak_all, spread_all, target_all = so_far
    log_total = peak_all + jnp.log(spread_all)
    counted = group_mask > 0
    terms = jnp.where(counted, log_total - target_all, 0.0)
    own_terms = lax.dynamic_slice_in_dim(terms, member * own_rows, own_rows)
    row_scale = jnp.where(counted, 1.0 / loss_count, 0.0)
    dlogits = (
        (jnp.exp(logits - log_total[None, :]) - hits.astype(jnp.float32)) * row_scale[None, :]
    ).astype(low_type)
    chosen_part = contract(dlogits, table_low, 0, 0)
    chosen_grad = across_wide(chosen_part.reshape(groups, own_rows, width))
    final_grad = jnp.zeros((tokens, width), jnp.float32).at[flat_picks].add(chosen_grad)

    branch_low, gate_low, first_sum_grad, attn_low, mixed_grad, late_norms = feed_backward(
        final_grad, second_sum, first_sum, gate_up, norms, near, w_gu_low, w_down_low
    )
    down, gate, up = Fold(1, (4, 2)), Fold(1, (2, 4)), Fold(1, (4, 2))
    middle = gate_up.shape[1] // 2
    sent = down.cores(gradient_chunks(contract(hidden_low, branch_low, 0, 0)))
    gate_low, _ = tie((gate_low, sent))
    sent = gate.cores(gradient_chunks(contract(second_low, gate_low[:, :middle], 0, 0)))
    gate_low, _ = tie((gate_low, sent))
    up.cores(gradient_chunks(contract(second_low, gate_low[:, middle:], 0, 0)))
    pairs = width // LANES
    third = pairs // 3
    sides = []
    for stage in range(3):
        if stage == 0:
            sent = down.plane(True) + gate.plane(True) + up.plane(True)
        elif stage == 1:
            sent = down.plane(False) + gate.plane(False)
        else:
            sent = down.members() + gate.members() + up.plane(False)
        mixed_grad, sides, _ = tie((mixed_grad, sides, sent))
        sides = list(sides) + [
            attend_back(lengths, queries, keys, values, mixed_grad, log_sums, cosine, sine, stage * third, third)
        ]
    sent = up.members()
    sides, down.came, gate.came, _ = tie((sides, down.came, gate.came, sent))
    joined_grad = jnp.concatenate([side for parts in zip(*sides) for side in parts], axis=1)
    first_grad = first_sum_grad + contract(joined_grad, near[:, : 3 * width], 1, 1)
    _, pull = jax.vjp(layer_norm, embed.astype(jnp.float32), norms[0], norms[1])
    embed_grad, gain_one, shift_one = pull(first_grad)
    norm_grad = jnp.concatenate([gain_one[None], shift_one[None], late_norms])
    embed_low, joined_grad = tie((embed_grad.astype(low_type), joined_grad))
    group_embed = lax.all_gather(embed_low, "grp", axis=0, tiled=True)

    join = Fold(1, (2, 4))
    join.cores(
        gradient_chunks(
            jnp.concatenate(
                [contract(first_low, joined_grad, 0, 0), contract(mixed_low, attn_low, 0, 0)], axis=1
            )
        )
    )
    join.plane(True)
    join.plane(False)
    join.members()
    gu_share = jnp.concatenate([gate.total(), up.total()], axis=1)
    down_share, join_share = down.total(), join.total()
    part_rows = gu_share.shape[0]
    far_whole = plane_gather(
        jnp.concatenate(
            [gu_share.astype(low_type), down_share.astype(low_type).reshape(part_rows, -1)], axis=1
        )
    ).reshape(shard_rows, -1)
    near_whole = plane_gather(join_share.astype(low_type)).reshape(shard_rows, -1)
    shares = (join_share[:, : 3 * width], join_share[:, 3 * width :], gu_share, down_share)
    share_cols = [jnp.sum(gradient * gradient, axis=0) for gradient in shares]
    group_embed, near_whole, far_whole, share_cols = tie((group_embed, near_whole, far_whole, share_cols))

    core = replica % 2
    middle = width // 2
    rest = (starts, codes, padded_order, dlogits, group_chosen, group_embed, block)
    if quick:
        chunks = ((replica // 2) ^ jnp.arange(3, -1, -1, dtype=jnp.int32)) * 2
        sent = table_grad_chunks(chunks + 1 - core, *rest, low_type)
        sent_x, kept_x, sent_y, kept_y = table_grad_chunks(chunks + core, *rest, low_type, flip(sent, 1))
        one = kept_x + flip(sent_x, 2).astype(jnp.float32)
        two = kept_y + flip(sent_y, 4).astype(jnp.float32)
        table_parts = [
            one[1] + flip(one[0].astype(low_type), 4).astype(jnp.float32),
            two[1] + flip(two[0].astype(low_type), 2).astype(jnp.float32),
        ]
    else:
        value = table_grad_chunks(jnp.arange(replicas, dtype=jnp.int32), *rest, jnp.float32)
        value = lax.psum_scatter(value, "rep", scatter_dimension=0)
        table_parts = [value[:, :middle], value[:, middle:]]

    old_rows = (table_rows, qkv_rows, out_rows, gu_rows, down_rows)
    old_cols = (table_cols, qkv_cols, out_cols, gu_cols, down_cols)
    masters = (table, w_qkv, w_out, w_gu, w_down)
    col_parts = [
        jnp.concatenate([jnp.sum(gradient * gradient, axis=0) for gradient in table_parts])
    ] + share_cols
    row_old = jnp.stack([jnp.sum(rows) for rows in old_rows]) / replicas
    small = [norm_grad.reshape(-1)] + col_parts + [row_old, jnp.sum(own_terms)[None]]
    plane_totals = plane_sum(jnp.concatenate(small))
    table_lows = [part.astype(low_type) for part in table_parts]
    plane_totals, table_lows = tie((plane_totals, table_lows))
    totals = rest_sum(plane_totals)
    cuts = []
    start = 0
    for part in small:
        cuts.append(totals[start : start + part.shape[0]])
        start += part.shape[0]
    norm_sum = cuts[0].reshape(norm_grad.shape)
    col_totals = cuts[1:6]
    old_totals = cuts[6]
    loss_sum = cuts[7][0]
    squares = [jnp.sum(part) for part in col_totals]
    clip_norm = jnp.sqrt(sum(squares) + jnp.sum(norm_sum * norm_sum))
    factor = clip_limit / jnp.maximum(clip_norm, clip_limit)
    decay = 1.0 - float(STEP) ** (-0.8)

    wholes = [
        None,
        near_whole[:, : 3 * width],
        near_whole[:, 3 * width :],
        far_whole[:, : w_gu.shape[1]],
        far_whole[:, w_gu.shape[1] :].reshape(w_down.shape),
    ]

    outputs = []
    for place in range(5):
        rows, columns = masters[place].shape
        full_rows = rows * groups
        new_cols = (
            decay * old_cols[place] + (1.0 - decay) * (col_totals[place] * factor * factor) / full_rows
        )
        row_total = decay * old_totals[place] + (1.0 - decay) * (squares[place] * factor * factor) / columns
        row_mean = row_total / full_rows
        if place == 0 and quick:
            have = [
                spread(low, [2, 4, 1] if part % 2 else [4, 2, 1]) for part, low in enumerate(table_lows)
            ]
            tiles = padded // TILE
            row_tiles = jnp.pad(table_rows, (0, padded - vocab_rows), constant_values=1.0).reshape(tiles, 1, TILE)
            scalars = jnp.stack([factor, rate_matrix * factor * jnp.sqrt(row_mean)])
            so_far = (
                blank(table.shape, jnp.float32),
                blank(table.shape, jnp.float32),
                blank((tiles, 1, TILE), jnp.float32),
            )
            for places in ((0,), (2, 4), (6,), (1, 3, 5, 7)):
                so_far = update(
                    places,
                    slots_of(),
                    scalars,
                    [[got[part] for got in have] for part in places],
                    table,
                    row_tiles,
                    lax.rsqrt(new_cols)[None, :],
                    so_far,
                )
            outputs.extend([so_far[0], so_far[2].reshape(-1)[:vocab_rows], new_cols, so_far[1]])
            continue
        if place == 0:
            whole = plane_gather(jnp.concatenate(table_lows, axis=1))
            gradient = whole.reshape(padded, width)[:vocab_rows].astype(jnp.float32)
        else:
            gradient = wholes[place].astype(jnp.float32)
        row_means = jnp.mean(gradient * gradient, axis=1)
        new_rows = decay * old_rows[place] + (1.0 - decay) * (row_means * factor * factor)
        clipped = gradient * factor
        scale = new_rows[:, None] * new_cols[None, :] / row_mean
        new_master = masters[place] - rate_matrix * clipped * lax.rsqrt(scale)
        outputs.extend([clipped, new_rows, new_cols, new_master])
    norm_clipped = norm_sum * factor
    moment_new = decay * norms_moment + (1.0 - decay) * norm_clipped * norm_clipped
    norms_new = norms - rate_norm * norm_clipped * lax.rsqrt(moment_new)
    return (
        (loss_sum, loss_count, clip_norm) + tuple(outputs) + (norm_clipped, moment_new, norms_new)
    )


def solution(mesh):
    in_specs = (
        P(("grp", "rep"), None),
        P(("grp", "rep")),
        P(("grp", "rep"), None),
        P(("grp", "rep"), None),
        P(("grp", "rep"), None),
        P("grp", None),
        P("grp", None),
        P("grp", None),
        P("grp", None),
        P("grp", None),
        P(),
        P("grp"),
        P(),
        P("grp"),
        P(),
        P("grp"),
        P(),
        P("grp"),
        P(),
        P("grp"),
        P(),
        P(),
    )
    out_specs = (
        P(),
        P(),
        P(),
        P("grp", None),
        P("grp"),
        P(),
        P("grp", None),
        P("grp", None),
        P("grp"),
        P(),
        P("grp", None),
        P("grp", None),
        P("grp"),
        P(),
        P("grp", None),
        P("grp", None),
        P("grp"),
        P(),
        P("grp", None),
        P("grp", None),
        P("grp"),
        P(),
        P("grp", None),
        P(),
        P(),
        P(),
    )
    return jax.shard_map(body, mesh=mesh, in_specs=in_specs, out_specs=out_specs, check_vma=False)
```

```python
import functools
import math

import jax
import jax.numpy as jnp
from jax import lax
from jax.experimental import pallas as pl
from jax.experimental.pallas import tpu as pltpu
from jax.sharding import PartitionSpec as P

HEADS = 12
HD = 64
STEP = 10
LANES = 128
ROWS = 256
CHUNK = 256
TILE = 480


ln_eps = 1e-05
rope_base = 10000.0
clip_limit = 0.01
rate_matrix = 0.03
rate_norm = 0.3
neg_large = -1e30
low_type = jnp.bfloat16
vmem = 56 * 1024 * 1024


def pair_lanes(shape):
    return lax.broadcasted_iota(jnp.int32, shape, len(shape) - 1)


def swap_halves(value):
    upper = (pair_lanes(value.shape) % HD) >= HD // 2
    return jnp.where(
        upper,
        pltpu.roll(value, HD // 2, axis=1),
        pltpu.roll(value, LANES - HD // 2, axis=1),
    )


def normalize(values, gain, shift):
    center = values - jnp.mean(values, axis=-1, keepdims=True)
    spread = jnp.mean(center * center, axis=-1, keepdims=True)
    return center * lax.rsqrt(spread + ln_eps) * gain + shift


def project_kernel(embed_ref, norms_ref, cosine_ref, sine_ref, w_ref, first_ref, low_ref, q_ref, k_ref, v_ref):
    first = normalize(embed_ref[...].astype(jnp.float32), norms_ref[0:1, :], norms_ref[1:2, :])
    first_ref[...] = first
    low = first.astype(low_type)
    low_ref[...] = low
    width = first.shape[1]
    cosine, sine = cosine_ref[...], sine_ref[...]
    for part, out_ref in enumerate((q_ref, k_ref)):
        joined = jnp.dot(low, w_ref[:, part * width : (part + 1) * width], preferred_element_type=jnp.float32)
        for start in range(0, width, LANES):
            piece = joined[:, start : start + LANES]
            out_ref[:, start : start + LANES] = (piece * cosine + swap_halves(piece) * sine).astype(low_type)
    v_ref[...] = jnp.dot(low, w_ref[:, 2 * width :], preferred_element_type=jnp.float32).astype(low_type)


def project(embed, norms, cosine, sine, weights):
    tokens, width = embed.shape
    row = lambda i: (i, 0)
    fixed = lambda i: (0, 0)
    low = jax.ShapeDtypeStruct((tokens, width), low_type)
    return pl.pallas_call(
        project_kernel,
        grid=(tokens // ROWS,),
        in_specs=[
            pl.BlockSpec((ROWS, width), row),
            pl.BlockSpec(norms.shape, fixed),
            pl.BlockSpec((ROWS, LANES), row),
            pl.BlockSpec((ROWS, LANES), row),
            pl.BlockSpec((width, 3 * width), fixed),
        ],
        out_specs=[pl.BlockSpec((ROWS, width), row)] * 5,
        out_shape=[jax.ShapeDtypeStruct((tokens, width), jnp.float32), low, low, low, low],
        compiler_params=pltpu.CompilerParams(vmem_limit_bytes=vmem),
        cost_estimate=pl.CostEstimate(flops=6 * tokens * width * width, bytes_accessed=20 * tokens * width, transcendentals=0),
    )(embed, norms, cosine, sine, weights)


def head_keys(k, bias, half):
    lanes = pair_lanes(k.shape)
    spare = HD - half * HD
    return jnp.where(lanes // HD == half, k, jnp.where(lanes == spare, bias, jnp.zeros_like(k)))


def head_queries(q, half, spare_value):
    lanes = pair_lanes(q.shape)
    spare = HD - half * HD
    scaled = q * jnp.asarray(1.0 / math.sqrt(HD), q.dtype)
    other = jnp.where(lanes == spare, jnp.full_like(q, spare_value), jnp.zeros_like(q))
    return jnp.where(lanes // HD == half, scaled, other)


def transposed_dot(left, right):
    return lax.dot_general(left, right, (((1,), (1,)), ((), ())), preferred_element_type=jnp.float32)


def key_bias(length_ref, tokens):
    place = lax.broadcasted_iota(jnp.int32, (tokens, LANES), 0)
    return jnp.where(place < length_ref[0], 0.0, neg_large).astype(low_type)


def attend_kernel(length_ref, q_ref, k_ref, v_ref, out_ref, log_ref, keys, turned):
    tokens = k_ref.shape[0]

    @pl.when(pl.program_id(1) == 0)
    def _():
        bias = key_bias(length_ref, tokens)
        for half in range(2):
            keys[half] = head_keys(k_ref[...], bias, half)
        turned[...] = v_ref[...].T

    parts = []
    for half in range(2):
        scores = transposed_dot(keys[half], head_queries(q_ref[...], half, 1.0))
        peak = jnp.max(scores, axis=0, keepdims=True)
        weights = jnp.exp(scores - peak)
        totals = jnp.sum(weights, axis=0, keepdims=True)
        probs = (weights * (1.0 / totals)).astype(low_type)
        parts.append(
            jnp.dot(turned[half * HD : (half + 1) * HD, :], probs, preferred_element_type=jnp.float32)
        )
        log_ref[0, half : half + 1, :] = peak + jnp.log(totals)
    out_ref[...] = jnp.concatenate(parts, axis=0).T.astype(low_type)


def attend(length, q, k, v):
    tokens, width = q.shape
    pairs = width // LANES
    own = lambda p, i, *_: (i, p)
    whole = lambda p, i, *_: (0, p)
    return pl.pallas_call(
        attend_kernel,
        grid_spec=pltpu.PrefetchScalarGridSpec(
            num_scalar_prefetch=1,
            grid=(pairs, tokens // ROWS),
            in_specs=[
                pl.BlockSpec((ROWS, LANES), own),
                pl.BlockSpec((tokens, LANES), whole),
                pl.BlockSpec((tokens, LANES), whole),
            ],
            out_specs=[
                pl.BlockSpec((ROWS, LANES), own),
                pl.BlockSpec((1, 2, ROWS), lambda p, i, *_: (p, 0, i)),
            ],
            scratch_shapes=[
                pltpu.VMEM((2, tokens, LANES), low_type),
                pltpu.VMEM((LANES, tokens), low_type),
            ],
        ),
        out_shape=[
            jax.ShapeDtypeStruct((tokens, width), low_type),
            jax.ShapeDtypeStruct((pairs, 2, tokens), jnp.float32),
        ],
        compiler_params=pltpu.CompilerParams(vmem_limit_bytes=vmem),
        cost_estimate=pl.CostEstimate(
            flops=16 * tokens * tokens * width, bytes_accessed=8 * tokens * width, transcendentals=tokens * tokens * width // HD
        ),
    )(length, q, k, v)


def rotate_back(grads, cosine, sine):
    return grads * cosine + swap_halves(grads * sine)


def attend_back_kernel(first_pair, length_ref, q_ref, k_ref, v_ref, d_ref, log_ref, cosq_ref, sinq_ref, cos_ref, sin_ref, *rest):
    dq_ref, dk_ref, dv_ref, keys, values, turned, dk_total, dv_total = rest[-8:]
    tokens = k_ref.shape[0]
    step = pl.program_id(1)

    @pl.when(step == 0)
    def _():
        bias = key_bias(length_ref, tokens)
        lanes = pair_lanes((tokens, LANES))
        for half in range(2):
            keys[half] = head_keys(k_ref[...], bias, half)
            values[half] = jnp.where(lanes // HD == half, v_ref[...], jnp.zeros_like(v_ref[...]))
        turned[...] = k_ref[...].T
        dk_total[...] = jnp.zeros_like(dk_total)
        dv_total[...] = jnp.zeros_like(dv_total)

    d = d_ref[...]
    lanes = pair_lanes(d.shape)
    parts = []
    dk = dv = None
    for half in range(2):
        scores = transposed_dot(keys[half], head_queries(q_ref[...], half, 1.0))
        probs = jnp.exp(scores - log_ref[0, half : half + 1, :])
        dprobs = transposed_dot(values[half], d)
        inner = jnp.sum(probs * dprobs, axis=0, keepdims=True)
        dscore = (probs * (dprobs - inner)).astype(low_type)
        parts.append(jnp.dot(turned[half * HD : (half + 1) * HD, :], dscore, preferred_element_type=jnp.float32))
        one_k = jnp.dot(dscore, head_queries(q_ref[...], half, 0.0), preferred_element_type=jnp.float32)
        one_v = jnp.dot(
            probs.astype(low_type), jnp.where(lanes // HD == half, d, jnp.zeros_like(d)), preferred_element_type=jnp.float32
        )
        dk = one_k if dk is None else dk + one_k
        dv = one_v if dv is None else dv + one_v
    dk_total[...] += dk
    dv_total[...] += dv
    dq = jnp.concatenate(parts, axis=0).T * (1.0 / math.sqrt(HD))
    dq_ref[...] = rotate_back(dq, cosq_ref[...], sinq_ref[...]).astype(low_type)

    @pl.when(step == pl.num_programs(1) - 1)
    def _():
        dk_ref[...] = rotate_back(dk_total[...], cos_ref[...], sin_ref[...]).astype(low_type)
        dv_ref[...] = dv_total[...].astype(low_type)


def attend_back(length, q, k, v, d, logs, cosine, sine, first_pair, pairs, after=()):
    tokens, width = q.shape
    own = lambda p, i, *_: (i, first_pair + p)
    whole = lambda p, i, *_: (0, first_pair + p)
    low = jax.ShapeDtypeStruct((tokens, pairs * LANES), low_type)
    fixed = pl.BlockSpec((tokens, LANES), lambda p, i, *_: (0, 0))
    row = pl.BlockSpec((ROWS, LANES), lambda p, i, *_: (i, 0))
    return pl.pallas_call(
        functools.partial(attend_back_kernel, first_pair),
        grid_spec=pltpu.PrefetchScalarGridSpec(
            num_scalar_prefetch=1,
            grid=(pairs, tokens // ROWS),
            in_specs=[
                pl.BlockSpec((ROWS, LANES), own),
                pl.BlockSpec((tokens, LANES), whole),
                pl.BlockSpec((tokens, LANES), whole),
                pl.BlockSpec((ROWS, LANES), own),
                pl.BlockSpec((1, 2, ROWS), lambda p, i, *_: (first_pair + p, 0, i)),
                row,
                row,
                fixed,
                fixed,
            ]
            + [pl.BlockSpec(memory_space=pl.ANY)] * len(after),
            out_specs=[
                pl.BlockSpec((ROWS, LANES), lambda p, i, *_: (i, p)),
                pl.BlockSpec((tokens, LANES), lambda p, i, *_: (0, p)),
                pl.BlockSpec((tokens, LANES), lambda p, i, *_: (0, p)),
            ],
            scratch_shapes=[
                pltpu.VMEM((2, tokens, LANES), low_type),
                pltpu.VMEM((2, tokens, LANES), low_type),
                pltpu.VMEM((LANES, tokens), low_type),
                pltpu.VMEM((tokens, LANES), jnp.float32),
                pltpu.VMEM((tokens, LANES), jnp.float32),
            ],
        ),
        out_shape=[low, low, low],
        compiler_params=pltpu.CompilerParams(vmem_limit_bytes=vmem),
        cost_estimate=pl.CostEstimate(
            flops=40 * tokens * tokens * pairs * LANES,
            bytes_accessed=16 * tokens * pairs * LANES,
            transcendentals=tokens * tokens * pairs * 2,
        ),
    )(length, q, k, v, d, logs, cosine, sine, cosine, sine, *after)


def forward_kernel(mixed_ref, first_ref, norms_ref, out_w_ref, gu_w_ref, down_w_ref, first_sum_ref, second_ref, gate_up_ref, hidden_ref, second_sum_ref, final_ref):
    width = first_ref.shape[1]
    middle = gu_w_ref.shape[1] // 2
    first_sum = first_ref[...] + jnp.dot(mixed_ref[...], out_w_ref[...], preferred_element_type=jnp.float32)
    first_sum_ref[...] = first_sum
    second = normalize(first_sum, norms_ref[2:3, :], norms_ref[3:4, :])
    low = second.astype(low_type)
    second_ref[...] = low
    total = second
    for start in range(0, middle, width):
        end = start + width
        gate = jnp.dot(low, gu_w_ref[:, start:end], preferred_element_type=jnp.float32)
        up = jnp.dot(low, gu_w_ref[:, middle + start : middle + end], preferred_element_type=jnp.float32)
        gate_up_ref[:, start:end] = gate
        gate_up_ref[:, middle + start : middle + end] = up
        hidden = (gate * (1.0 / (1.0 + jnp.exp(-gate))) * up).astype(low_type)
        hidden_ref[:, start:end] = hidden
        total = total + jnp.dot(hidden, down_w_ref[start:end, :], preferred_element_type=jnp.float32)
    second_sum_ref[...] = total
    final_ref[...] = normalize(total, norms_ref[4:5, :], norms_ref[5:6, :])


def feed_forward(mixed, first, norms, near, w_gu, w_down):
    tokens, width = first.shape
    middle = w_down.shape[0]
    row = lambda i: (i, 0)
    fixed = lambda i: (0, 0)
    once = pl.Buffered(1)
    narrow = pl.BlockSpec((ROWS, width), row)
    high = jax.ShapeDtypeStruct((tokens, width), jnp.float32)
    return pl.pallas_call(
        forward_kernel,
        grid=(tokens // ROWS,),
        in_specs=[
            narrow,
            narrow,
            pl.BlockSpec(norms.shape, fixed),
            pl.BlockSpec((width, width), lambda i: (0, 3), pipeline_mode=once),
            pl.BlockSpec(w_gu.shape, fixed, pipeline_mode=once),
            pl.BlockSpec(w_down.shape, fixed, pipeline_mode=once),
        ],
        out_specs=[
            narrow,
            narrow,
            pl.BlockSpec((ROWS, 2 * middle), row),
            pl.BlockSpec((ROWS, middle), row),
            narrow,
            narrow,
        ],
        out_shape=[
            high,
            jax.ShapeDtypeStruct((tokens, width), low_type),
            jax.ShapeDtypeStruct((tokens, 2 * middle), jnp.float32),
            jax.ShapeDtypeStruct((tokens, middle), low_type),
            high,
            high,
        ],
        compiler_params=pltpu.CompilerParams(vmem_limit_bytes=vmem),
        cost_estimate=pl.CostEstimate(
            flops=2 * tokens * width * (width + 3 * middle), bytes_accessed=14 * tokens * middle, transcendentals=tokens * middle
        ),
    )(mixed, first, norms, near, w_gu, w_down)


def normalize_back(values, gain, grads):
    center = values - jnp.mean(values, axis=-1, keepdims=True)
    inverse = lax.rsqrt(jnp.mean(center * center, axis=-1, keepdims=True) + ln_eps)
    unit = center * inverse
    scaled = grads * gain
    inner = jnp.mean(scaled * unit, axis=-1, keepdims=True)
    result = inverse * (scaled - jnp.mean(scaled, axis=-1, keepdims=True) - unit * inner)
    return result, jnp.sum(grads * unit, axis=0, keepdims=True), jnp.sum(grads, axis=0, keepdims=True)


def backward_kernel(grad_ref, second_sum_ref, first_sum_ref, gate_up_ref, norms_ref, out_w_ref, gu_w_ref, down_w_ref, branch_ref, gate_low_ref, first_sum_grad_ref, attn_ref, mixed_ref, norms_grad_ref):
    width = grad_ref.shape[1]
    middle = down_w_ref.shape[0]
    sum_grad, gain_three, shift_three = normalize_back(second_sum_ref[...], norms_ref[4:5, :], grad_ref[...])
    branch = sum_grad.astype(low_type)
    branch_ref[...] = branch
    total = sum_grad
    for start in range(0, middle, width):
        end = start + width
        hidden_grad = transposed_dot(branch, down_w_ref[start:end, :])
        gate = gate_up_ref[:, start:end]
        up = gate_up_ref[:, middle + start : middle + end]
        share = 1.0 / (1.0 + jnp.exp(-gate))
        gate_grad = (hidden_grad * up * (share * (1.0 + gate * (1.0 - share)))).astype(low_type)
        up_grad = (hidden_grad * (gate * share)).astype(low_type)
        gate_low_ref[:, start:end] = gate_grad
        gate_low_ref[:, middle + start : middle + end] = up_grad
        total = total + transposed_dot(gate_grad, gu_w_ref[:, start:end])
        total = total + transposed_dot(up_grad, gu_w_ref[:, middle + start : middle + end])
    first_sum_grad, gain_two, shift_two = normalize_back(first_sum_ref[...], norms_ref[2:3, :], total)
    first_sum_grad_ref[...] = first_sum_grad
    attn = first_sum_grad.astype(low_type)
    attn_ref[...] = attn
    mixed_ref[...] = transposed_dot(attn, out_w_ref[...]).astype(low_type)

    @pl.when(pl.program_id(0) == 0)
    def _():
        norms_grad_ref[...] = jnp.zeros_like(norms_grad_ref)

    norms_grad_ref[...] += jnp.concatenate([gain_two, shift_two, gain_three, shift_three], axis=0)


def feed_backward(grad, second_sum, first_sum, gate_up, norms, near, w_gu, w_down):
    tokens, width = grad.shape
    middle = w_down.shape[0]
    row = lambda i: (i, 0)
    fixed = lambda i: (0, 0)
    once = pl.Buffered(1)
    narrow = pl.BlockSpec((ROWS, width), row)
    wide = pl.BlockSpec((ROWS, 2 * middle), row)
    low = jax.ShapeDtypeStruct((tokens, width), low_type)
    return pl.pallas_call(
        backward_kernel,
        grid=(tokens // ROWS,),
        in_specs=[
            narrow,
            narrow,
            narrow,
            wide,
            pl.BlockSpec(norms.shape, fixed),
            pl.BlockSpec((width, width), lambda i: (0, 3), pipeline_mode=once),
            pl.BlockSpec(w_gu.shape, fixed, pipeline_mode=once),
            pl.BlockSpec(w_down.shape, fixed, pipeline_mode=once),
        ],
        out_specs=[narrow, wide, narrow, narrow, narrow, pl.BlockSpec((4, width), fixed)],
        out_shape=[
            low,
            jax.ShapeDtypeStruct((tokens, 2 * middle), low_type),
            jax.ShapeDtypeStruct((tokens, width), jnp.float32),
            low,
            low,
            jax.ShapeDtypeStruct((4, width), jnp.float32),
        ],
        compiler_params=pltpu.CompilerParams(vmem_limit_bytes=vmem),
        cost_estimate=pl.CostEstimate(
            flops=2 * tokens * width * (width + 3 * middle), bytes_accessed=14 * tokens * middle, transcendentals=tokens * middle
        ),
    )(grad, second_sum, first_sum, gate_up, norms, near, w_gu, w_down)


def blank(shape, dtype):
    return pl.pallas_call(
        lambda out_ref: None,
        out_shape=jax.ShapeDtypeStruct(shape, dtype),
        out_specs=pl.BlockSpec(memory_space=pl.ANY),
    )()


def lookup_kernel(starts_ref, places_ref, order_ref, table_ref, out_ref, rows):
    count = out_ref.shape[0]
    owned = starts_ref[starts_ref.shape[0] - 1]
    for start in range(0, count, CHUNK):
        rows[start : start + CHUNK, :] = jnp.zeros((CHUNK, rows.shape[1]), jnp.float32)

    def eight(step, carry):
        for j in range(8):
            i = step * 8 + j
            valid = i < owned
            source = jnp.where(valid, places_ref[i], 0)
            target = jnp.where(valid, order_ref[i], count)
            rows[pl.ds(target, 1), :] = table_ref[pl.ds(source, 1), :]
        return carry

    lax.fori_loop(0, (owned + 7) // 8, eight, 0)
    for start in range(0, count, CHUNK):
        out_ref[start : start + CHUNK, :] = rows[start : start + CHUNK, :].astype(low_type)


def lookup(starts, places, order, table, count):
    width = table.shape[1]
    return pl.pallas_call(
        lookup_kernel,
        grid_spec=pltpu.PrefetchScalarGridSpec(
            num_scalar_prefetch=3,
            grid=(1,),
            in_specs=[pl.BlockSpec(table.shape, lambda i, *_: (0, 0), pipeline_mode=pl.Buffered(1))],
            out_specs=pl.BlockSpec((count, width), lambda i, *_: (0, 0), pipeline_mode=pl.Buffered(1)),
            scratch_shapes=[pltpu.VMEM((count + 8, width), jnp.float32)],
        ),
        out_shape=jax.ShapeDtypeStruct((count, width), low_type),
        compiler_params=pltpu.CompilerParams(vmem_limit_bytes=vmem),
        cost_estimate=pl.CostEstimate(flops=0, bytes_accessed=table.size * 12, transcendentals=0),
    )(starts, places, order, table)


def table_grad_kernel(chunks_ref, starts_ref, codes_ref, order_ref, dlogits_ref, chosen_ref, embed_ref, *refs):
    rows, sums = refs[-2:]
    step = pl.program_id(0)
    count, width = embed_ref.shape
    block = dlogits_ref.shape[0]

    @pl.when(step == 0)
    def _():
        for start in range(0, count, CHUNK):
            rows[start : start + CHUNK, :] = embed_ref[start : start + CHUNK, :].astype(jnp.float32)

    sums[...] = jnp.zeros_like(sums)
    chunk = chunks_ref[step]
    first, last = starts_ref[chunk], starts_ref[chunk + 1]

    def eight(turn, running):
        for j in range(8):
            i = first + turn * 8 + j
            code = codes_ref[i]
            place = jnp.where(i < last, code >> 1, block)
            running = jnp.where(code & 1, running, 0.0) + rows[pl.ds(order_ref[i], 1), :]
            sums[pl.ds(place, 1), :] = running
        return running

    lax.fori_loop(0, (last - first + 7) // 8, eight, jnp.zeros((1, width), jnp.float32))
    product = jnp.dot(dlogits_ref[...], chosen_ref[...], preferred_element_type=jnp.float32)
    result = product + sums[:block, :]
    if len(refs) == 3:
        refs[0][0] = result.astype(refs[0].dtype)
        return
    got_ref, sent_x, kept_x, sent_y, kept_y = refs[:-2]
    result = result + got_ref[0].astype(jnp.float32)
    left, right = result[:, : width // 2], result[:, width // 2 :]

    @pl.when(step % 2 == 0)
    def _():
        sent_x[0] = left.astype(sent_x.dtype)

    @pl.when(step % 2 == 1)
    def _():
        kept_x[0] = left

    @pl.when(step < 2)
    def _():
        sent_y[0] = right.astype(sent_y.dtype)

    @pl.when(step >= 2)
    def _():
        kept_y[0] = right


def table_grad_chunks(chunks, starts, codes, order, dlogits, chosen, embed, block, dtype, got=None):
    count, width = embed.shape
    picked = chosen.shape[0]
    steps = chunks.shape[0]
    fixed = lambda i, *_: (0, 0)
    in_specs = [
        pl.BlockSpec((block, picked), lambda i, chunks, *_: (chunks[i], 0)),
        pl.BlockSpec((picked, width), fixed),
        pl.BlockSpec((count, width), fixed, pipeline_mode=pl.Buffered(1)),
    ]
    whole = pl.BlockSpec((1, block, width), lambda i, *_: (i, 0, 0))
    if got is None:
        out_shape = jax.ShapeDtypeStruct((steps, block, width), dtype)
        out_specs = whole
    else:
        in_specs.append(whole)
        half = (1, block, width // 2)
        by_y = lambda i, *_: (i // 2, 0, 0)
        low = jax.ShapeDtypeStruct((2, block, width // 2), low_type)
        high = jax.ShapeDtypeStruct((2, block, width // 2), jnp.float32)
        out_shape = [low, high, low, high]
        out_specs = [
            pl.BlockSpec(half, by_y),
            pl.BlockSpec(half, by_y),
            pl.BlockSpec(half, lambda i, *_: (jnp.minimum(i, 1), 0, 0)),
            pl.BlockSpec(half, lambda i, *_: (jnp.maximum(i - 2, 0), 0, 0)),
        ]
    return pl.pallas_call(
        table_grad_kernel,
        grid_spec=pltpu.PrefetchScalarGridSpec(
            num_scalar_prefetch=4,
            grid=(steps,),
            in_specs=in_specs,
            out_specs=out_specs,
            scratch_shapes=[
                pltpu.VMEM((count, width), jnp.float32),
                pltpu.VMEM((block + 8, width), jnp.float32),
            ],
        ),
        out_shape=out_shape,
        compiler_params=pltpu.CompilerParams(vmem_limit_bytes=vmem),
        cost_estimate=pl.CostEstimate(
            flops=2 * steps * block * picked * width, bytes_accessed=8 * steps * block * width, transcendentals=0
        ),
    )(chunks, starts, codes, order, dlogits, chosen, embed, *(() if got is None else (got,)))


def update_kernel(places, parts, slots_ref, scalars_ref, *rest):
    given = len(places) * parts
    pieces = rest[:given]
    table_ref, rows_ref, cols_ref = rest[given : given + 3]
    grad_ref, new_ref, rows_new_ref = rest[-3:]
    factor, rate = scalars_ref[0], scalars_ref[1]
    decay = 1.0 - float(STEP) ** (-0.8)
    old = jnp.broadcast_to(rows_ref[0], (LANES, TILE)).T[:, 0:1]
    for part in range(len(places)):

        @pl.when(pl.program_id(0) == part)
        def _(part=part):
            own = pieces[part * parts : (part + 1) * parts]
            gradient = jnp.concatenate([piece[...] for piece in own], axis=1).astype(jnp.float32)
            means = jnp.mean(gradient * gradient, axis=1, keepdims=True)
            rows_new = decay * old + (1.0 - decay) * (means * factor * factor)
            grad_ref[...] = gradient * factor
            new_ref[...] = table_ref[...] - gradient * (rate * lax.rsqrt(rows_new)) * cols_ref[...]
            rows_new_ref[0] = jnp.broadcast_to(rows_new, (TILE, LANES)).T[0:1, :]


def update(places, slots, scalars, pieces, table, rows, cols, so_far):
    count = len(places)
    parts = len(pieces[0])
    block = pieces[0][0].shape[0]
    width = table.shape[1]
    steps = block // TILE

    def slot(p, slots):
        at = slots[places[0]]
        for j in range(1, count):
            at = jnp.where(p == j, slots[places[j]], at)
        return at

    place = lambda p, i, slots: (slot(p, slots) * steps + i, 0)
    place3 = lambda p, i, slots: (slot(p, slots) * steps + i, 0, 0)

    def own(part):
        return lambda p, i, slots: (jnp.where(p < part, 0, jnp.where(p > part, steps - 1, i)), 0)

    fixed = lambda p, i, slots: (0, 0)
    any_space = pl.BlockSpec(memory_space=pl.ANY)
    given = 5 + count * parts
    return pl.pallas_call(
        functools.partial(update_kernel, places, parts),
        grid_spec=pltpu.PrefetchScalarGridSpec(
            num_scalar_prefetch=1,
            grid=(count, steps),
            in_specs=[pl.BlockSpec(memory_space=pltpu.SMEM)]
            + [pl.BlockSpec((TILE, piece.shape[1]), own(part)) for part in range(count) for piece in pieces[part]]
            + [
                pl.BlockSpec((TILE, width), place),
                pl.BlockSpec((1, 1, TILE), place3),
                pl.BlockSpec((1, width), fixed),
                any_space,
                any_space,
                any_space,
            ],
            out_specs=[
                pl.BlockSpec((TILE, width), place),
                pl.BlockSpec((TILE, width), place),
                pl.BlockSpec((1, 1, TILE), place3),
            ],
        ),
        out_shape=[jax.ShapeDtypeStruct(part.shape, part.dtype) for part in so_far],
        input_output_aliases={given: 0, given + 1: 1, given + 2: 2},
        compiler_params=pltpu.CompilerParams(vmem_limit_bytes=vmem),
        cost_estimate=pl.CostEstimate(
            flops=10 * count * block * width, bytes_accessed=14 * count * block * width, transcendentals=0
        ),
    )(slots, scalars, *[piece for some in pieces for piece in some], table, rows, cols, *so_far)


def stack_kernel(slots_ref, *refs):
    pieces, out_ref = refs[:-1], refs[-1]
    for place, piece in enumerate(pieces):

        @pl.when(pl.program_id(0) == place)
        def _(piece=piece):
            out_ref[0] = piece[...]


def lay_out(slots, pieces):
    shape = pieces[0].shape
    return pl.pallas_call(
        stack_kernel,
        grid_spec=pltpu.PrefetchScalarGridSpec(
            num_scalar_prefetch=1,
            grid=(len(pieces),),
            in_specs=[pl.BlockSpec(shape, lambda i, slots: (0, 0), pipeline_mode=pl.Buffered(1))] * len(pieces),
            out_specs=pl.BlockSpec((1,) + shape, lambda i, slots: (slots[i], 0, 0)),
        ),
        out_shape=jax.ShapeDtypeStruct((len(pieces),) + shape, pieces[0].dtype),
        compiler_params=pltpu.CompilerParams(vmem_limit_bytes=vmem),
        cost_estimate=pl.CostEstimate(flops=0, bytes_accessed=4 * len(pieces) * pieces[0].size, transcendentals=0),
    )(slots, *pieces)


def columns_kernel(members_ref, slots_ref, own_ref, *refs):
    pieces, out_ref = refs[:-1], refs[-1]
    rows = own_ref.shape[0]

    def at(offset):
        return pl.ds(pl.multiple_of(members_ref[offset] * rows, rows), rows)

    out_ref[at(0), :] = own_ref[...].astype(low_type)
    for place, piece in enumerate(pieces):

        @pl.when(pl.program_id(0) == place)
        def _(piece=piece):
            for offset in range(piece.shape[0]):
                out_ref[at(offset + 1), :] = piece[offset]


def lay_columns(members, slots, own, pieces):
    others, rows, columns = pieces[0].shape
    replicas = len(pieces)
    whole = jax.ShapeDtypeStruct(((others + 1) * rows, replicas * columns), low_type)
    return pl.pallas_call(
        columns_kernel,
        grid_spec=pltpu.PrefetchScalarGridSpec(
            num_scalar_prefetch=2,
            grid=(replicas,),
            in_specs=[pl.BlockSpec((rows, columns), lambda i, members, slots: (0, slots[i]))]
            + [pl.BlockSpec(pieces[0].shape, lambda i, *_: (0, 0, 0), pipeline_mode=pl.Buffered(1))] * replicas,
            out_specs=pl.BlockSpec(((others + 1) * rows, columns), lambda i, members, slots: (0, slots[i])),
        ),
        out_shape=whole,
        compiler_params=pltpu.CompilerParams(vmem_limit_bytes=vmem),
        cost_estimate=pl.CostEstimate(flops=0, bytes_accessed=4 * whole.size, transcendentals=0),
    )(members, slots, own, *pieces)


def rows_kernel(members_ref, slots_ref, own_ref, *refs):
    pieces, out_ref = refs[:-1], refs[-1]
    out_ref[members_ref[0], 0] = own_ref[0].astype(low_type)
    for place, piece in enumerate(pieces):

        @pl.when(pl.program_id(0) == place)
        def _(piece=piece):
            for offset in range(piece.shape[0]):
                out_ref[members_ref[offset + 1], 0] = piece[offset]


def lay_rows(members, slots, own, pieces):
    others, rows, columns = pieces[0].shape
    replicas = len(pieces)
    whole = jax.ShapeDtypeStruct((others + 1, replicas, rows, columns), low_type)
    return pl.pallas_call(
        rows_kernel,
        grid_spec=pltpu.PrefetchScalarGridSpec(
            num_scalar_prefetch=2,
            grid=(replicas,),
            in_specs=[pl.BlockSpec((1, rows, columns), lambda i, members, slots: (slots[i], 0, 0))]
            + [pl.BlockSpec(pieces[0].shape, lambda i, *_: (0, 0, 0), pipeline_mode=pl.Buffered(1))] * replicas,
            out_specs=pl.BlockSpec((others + 1, 1, rows, columns), lambda i, members, slots: (0, slots[i], 0, 0)),
        ),
        out_shape=whole,
        compiler_params=pltpu.CompilerParams(vmem_limit_bytes=vmem),
        cost_estimate=pl.CostEstimate(flops=0, bytes_accessed=4 * whole.size, transcendentals=0),
    )(members, slots, own.reshape(replicas, rows, columns), *pieces).reshape(-1, columns)


tie = lax.optimization_barrier


def flip(value, bit):
    size = lax.axis_size("rep")
    return lax.ppermute(value, "rep", [(i, i ^ bit) for i in range(size)])


def turn(value, offset):
    size = lax.axis_size("grp")
    return lax.ppermute(value, "grp", [(i, (i + offset) % size) for i in range(size)])


def wave(have, bit):
    return have | {place ^ bit: flip(part, bit) for place, part in have.items()}


def spread(piece, order):
    have = {0: piece}
    for bit in order:
        have = wave(have, bit)
    return have


def slots_of():
    return lax.axis_index("rep") ^ jnp.arange(lax.axis_size("rep"), dtype=jnp.int32)


def plane_gather(piece):
    if lax.axis_size("rep") != 8:
        return lax.all_gather(piece, "rep")
    have = spread(piece, [2, 4, 1])
    return lay_out(slots_of(), [have[place] for place in range(8)])


def halve(value, axis, bit):
    mine = (lax.axis_index("rep") // bit) % 2
    kept = lax.dynamic_index_in_dim(value, mine, axis, keepdims=False)
    sent = lax.dynamic_index_in_dim(value, 1 - mine, axis, keepdims=False)
    return kept, sent.astype(low_type)


class Fold:
    def __init__(self, axis, order):
        self.axis = axis
        self.order = order
        self.quick = lax.axis_size("rep") == 8
        self.value = None

    def cores(self, chunks):
        axis = self.axis
        if not self.quick:
            self.value = lax.psum_scatter(chunks, "rep", scatter_dimension=axis)
            return []
        shape = chunks.shape
        kept, sent = halve(chunks.reshape(shape[:axis] + (4, 2) + shape[axis + 1 :]), axis + 1, 1)
        return self.from_cores(kept, sent)

    def from_cores(self, kept, sent):
        self.kept, self.got = kept, flip(sent, 1)
        return [sent]

    def sum(self):
        if self.value is None:
            return self.kept + self.got.astype(jnp.float32)
        return self.value

    def plane(self, first):
        if not self.quick:
            return []
        value = self.sum()
        axis = self.axis
        bit = self.order[0 if first else 1]
        if first:
            shape = value.shape
            value = value.reshape(shape[:axis] + (2, 2) + shape[axis + 1 :])
            axis = axis + (1 if bit == 2 else 0)
        self.kept, sent = halve(value, axis, bit)
        self.value, self.got = None, flip(sent, bit)
        return [sent]

    def members(self):
        value = self.sum()
        member = lax.axis_index("grp")
        size = lax.axis_size("grp")
        self.own = lax.dynamic_index_in_dim(value, member, 0, keepdims=False)
        sent = [
            lax.dynamic_index_in_dim(value, (member + offset) % size, 0, keepdims=False).astype(low_type)
            for offset in range(1, size)
        ]
        self.came = [turn(part, offset + 1) for offset, part in enumerate(sent)]
        return sent

    def total(self):
        return sum((came.astype(jnp.float32) for came in self.came), self.own)


def gradient_chunks(gradient):
    groups = lax.axis_size("grp")
    replicas = lax.axis_size("rep")
    rows, columns = gradient.shape
    return gradient.reshape(groups, replicas, rows // (groups * replicas), columns)


def across_wide(chunks):
    member = lax.axis_index("grp")
    size = lax.axis_size("grp")
    total = lax.dynamic_index_in_dim(chunks, member, 0, keepdims=False)
    for offset in range(1, size):
        sent = lax.dynamic_index_in_dim(chunks, (member + offset) % size, 0, keepdims=False)
        total = total + turn(sent, offset)
    return total


def group_gather(value):
    member = lax.axis_index("grp")
    size = lax.axis_size("grp")
    result = jnp.zeros((size,) + value.shape, value.dtype)
    result = lax.dynamic_update_index_in_dim(result, value, member, 0)
    for offset in range(1, size):
        result = lax.dynamic_update_index_in_dim(
            result, turn(value, offset), (member + size - offset) % size, 0
        )
    return result


def plane_sum(value):
    for j in range(1, lax.axis_size("rep").bit_length() - 1):
        value = value + flip(value, 1 << j)
    return value


def rest_sum(value):
    value = value + flip(value, 1)
    size = lax.axis_size("grp")
    for j in range(size.bit_length() - 1):
        value = value + lax.ppermute(value, "grp", [(i, i ^ (1 << j)) for i in range(size)])
    return value


def fetch(own):
    return jnp.stack([turn(own, offset) for offset in range(1, lax.axis_size("grp"))])


def cut(value, axis):
    replicas = lax.axis_size("rep")
    size = value.shape[axis] // replicas
    return lax.dynamic_slice_in_dim(value, lax.axis_index("rep") * size, size, axis)


def members_of():
    groups = lax.axis_size("grp")
    return (lax.axis_index("grp") + groups - jnp.arange(groups, dtype=jnp.int32)) % groups


def contract(left, right, left_dim, right_dim):
    return lax.dot_general(
        left, right, (((left_dim,), (right_dim,)), ((), ())), preferred_element_type=jnp.float32
    )


def layer_norm(values, gain, shift):
    center = values - jnp.mean(values, axis=-1, keepdims=True)
    spread = jnp.mean(center * center, axis=-1, keepdims=True)
    return center * lax.rsqrt(spread + ln_eps) * gain + shift


def rope_tables(length):
    freqs = rope_base ** (-jnp.arange(HD // 2, dtype=jnp.float32) * 2.0 / HD)
    angles = jnp.arange(length, dtype=jnp.float32)[:, None] * freqs[None, :]
    cosine, sine = jnp.cos(angles), jnp.sin(angles)
    return (
        jnp.concatenate([cosine] * 4, axis=-1),
        jnp.concatenate([-sine, sine, -sine, sine], axis=-1),
    )


def merge_stats(first_part, second_part):
    peak = jnp.maximum(first_part[0], second_part[0])
    spread = first_part[1] * jnp.exp(first_part[0] - peak) + second_part[1] * jnp.exp(
        second_part[0] - peak
    )
    return (peak, spread, first_part[2] + second_part[2])


def body(
    ids,
    lengths,
    picks,
    labels,
    loss_mask,
    table,
    w_qkv,
    w_out,
    w_gu,
    w_down,
    norms,
    table_rows,
    table_cols,
    qkv_rows,
    qkv_cols,
    out_rows,
    out_cols,
    gu_rows,
    gu_cols,
    down_rows,
    down_cols,
    norms_moment,
):
    member = lax.axis_index("grp")
    groups = lax.axis_size("grp")
    replica = lax.axis_index("rep")
    replicas = lax.axis_size("rep")
    seqs, length = ids.shape
    width = table.shape[1]
    vocab_rows = table.shape[0]
    own_rows = seqs * picks.shape[1]
    tokens = seqs * length
    block = -(-vocab_rows // (16 * replicas)) * 16
    padded = block * replicas

    packed = jnp.concatenate([ids.reshape(-1), labels.reshape(-1), loss_mask.reshape(-1)])
    group_packed = group_gather(packed)
    group_ids = group_packed[:, :tokens].reshape(-1)
    group_labels = group_packed[:, tokens : tokens + own_rows].reshape(-1)
    group_mask = group_packed[:, tokens + own_rows :].reshape(-1)
    shard_rows = w_qkv.shape[0]
    quick = replicas == 8
    near_shard = jnp.concatenate([w_qkv, w_out], axis=1)
    if quick:
        near_part = fetch(cut(near_shard, 1).astype(low_type))
        gu_part = fetch(cut(w_gu, 1).astype(low_type))

    local_ids = group_ids - member * vocab_rows
    owned = (local_ids >= 0) & (local_ids < vocab_rows)
    keys = jnp.where(owned, local_ids, padded)
    tokens_at = jnp.arange(local_ids.shape[0], dtype=jnp.int32)
    if quick:
        slot_rows = tokens // 2
        owners = group_ids.reshape(groups, tokens) // vocab_rows
        own_ids = ids.reshape(1, tokens) // vocab_rows
        asked = jnp.concatenate([owners == member, own_ids == jnp.arange(groups, dtype=jnp.int32)[:, None]])
        below = jnp.arange(tokens)[:, None] <= jnp.arange(tokens)[None, :]
        ranks = jnp.dot(asked.astype(low_type), below.astype(low_type), preferred_element_type=jnp.float32)
        ranks = ranks.astype(jnp.int32) - 1
        slot_of = (jnp.arange(groups, dtype=jnp.int32) - member + groups) % groups
        slots_at = slot_of[:, None] * slot_rows + ranks[:groups]
        slots_at = jnp.where(ranks[:groups] < slot_rows, slots_at, groups * slot_rows).reshape(-1)
        own_ranks = jnp.sum(jnp.where(asked[groups:], ranks[groups:], 0), axis=0)
        source = (member - own_ids[0] + groups) % groups * slot_rows + own_ranks
        asks = jnp.sum((owners[:, None, :] == jnp.arange(groups)[None, :, None]).astype(jnp.int32), axis=-1)
        uneven = jnp.max((asks > slot_rows).astype(jnp.int32))[None]
        for j in range(replicas.bit_length() - 1):
            uneven = jnp.maximum(uneven, flip(uneven, 1 << j))
        places, order, slots_at = lax.sort((keys, tokens_at, slots_at), num_keys=1)
    else:
        places, order = lax.sort((keys, tokens_at), num_keys=1)
    bounds = jnp.arange(replicas + 1, dtype=jnp.int32) * block
    starts = jnp.sum((places[None, :] < bounds[:, None]).astype(jnp.int32), axis=1)
    again = jnp.concatenate([jnp.zeros((1,), jnp.int32), (places[1:] == places[:-1]).astype(jnp.int32)])
    codes = jnp.pad(places % block * 2 + again, (0, 8))
    padded_order = jnp.pad(order, (0, 8))
    count = local_ids.shape[0]
    if quick:
        places, near_part = tie((places, near_part))
        found = lookup(starts, places, slots_at, table, groups * slot_rows)
        found, gu_part = tie((found, gu_part))
        packs = found.reshape(groups, slot_rows, width)
        turned = [turn(packs[offset], offset) for offset in range(1, groups)]

        def compact(came):
            pick = source[:, None] == jnp.arange(groups * slot_rows, dtype=jnp.int32)[None, :]
            return jnp.dot(pick.astype(low_type), came, preferred_element_type=jnp.float32).astype(low_type)

        def general(came):
            rows = lookup(starts, places, order, table, count)
            return lax.psum_scatter(rows, "grp", scatter_dimension=0, tiled=True)

    else:
        found = lookup(starts, places, order, table, count)
        embed = lax.psum_scatter(found, "grp", scatter_dimension=0, tiled=True)
    late_table, _ = lax.optimization_barrier((table, found))
    table_low = jnp.pad(late_table.astype(low_type), ((0, padded - vocab_rows), (0, 0)))

    if quick:
        members, slots = members_of(), slots_of()


        def listed(have):
            return [have[place] for place in range(replicas)]

        near_have, gu_have = wave({0: near_part}, 4), wave({0: gu_part}, 2)
        near_have, turned[0], turned[-1] = tie((near_have, turned[0], turned[-1]))
        near_have = wave(near_have, 2)
        gu_have = wave(gu_have, 4)
        near = lay_columns(members, slots, near_shard, listed(wave(near_have, 1)))
        gu_have, near, table_low, turned[1:-1] = tie((gu_have, near, table_low, turned[1:-1]))
        w_gu_low = lay_columns(members, slots, w_gu, listed(wave(gu_have, 1)))
        down_own, _ = tie((cut(w_down, 0), turned))
        down_have = listed(spread(fetch(down_own.astype(low_type)), [4, 2, 1]))
        came = jnp.concatenate([packs[0]] + turned)
        came, near, w_gu_low, table_low = tie((came, near, w_gu_low, table_low))
        embed = lax.cond(uneven[0] > 0, general, compact, came)
    else:
        near = lax.all_gather(near_shard.astype(low_type), "grp", tiled=True)
        w_gu_low = lax.all_gather(w_gu.astype(low_type), "grp", tiled=True)
        w_down_low = lax.all_gather(w_down.astype(low_type), "grp", tiled=True)
    cosine, sine = rope_tables(length)
    first, first_low, queries, keys, values = project(embed, norms, cosine, sine, near)
    queries, group_mask = tie((queries, group_mask))
    loss_count = jnp.sum(group_mask).astype(jnp.float32)[None]
    for j in range(replicas.bit_length() - 1):
        loss_count = loss_count + flip(loss_count, 1 << j)
    loss_count = loss_count[0]
    mixed_low, log_sums = attend(lengths, queries, keys, values)
    if quick:
        mixed_low, down_have = tie((mixed_low, down_have))
        w_down_low = lay_rows(members, slots, w_down, down_have)
    first_sum, second_low, gate_up, hidden_low, second_sum, final = feed_forward(
        mixed_low, first, norms, near, w_gu_low, w_down_low
    )

    flat_picks = (jnp.arange(seqs, dtype=jnp.int32)[:, None] * length + picks).reshape(-1)
    chosen = final[flat_picks].astype(low_type)
    group_chosen = group_gather(chosen).reshape(groups * own_rows, width)
    rows_at = jnp.arange(padded, dtype=jnp.int32)[:, None]
    logits = jnp.where(rows_at < vocab_rows, contract(table_low, group_chosen, 1, 1), neg_large)
    peak = jnp.max(logits, axis=0)
    spread_sum = jnp.sum(jnp.exp(logits - peak[None, :]), axis=0)
    local_labels = group_labels - member * vocab_rows
    inside = (local_labels >= 0) & (local_labels < vocab_rows)
    hits = (rows_at == local_labels[None, :]) & inside[None, :]
    target = jnp.sum(jnp.where(hits, logits, 0.0), axis=0)
    stats = group_gather(jnp.stack([peak, spread_sum, target]))
    so_far = (stats[0, 0], stats[0, 1], stats[0, 2])
    for place in range(1, groups):
        so_far = merge_stats(so_far, (stats[place, 0], stats[place, 1], stats[place, 2]))
    peak_all, spread_all, target_all = so_far
    log_total = peak_all + jnp.log(spread_all)
    counted = group_mask > 0
    terms = jnp.where(counted, log_total - target_all, 0.0)
    own_terms = lax.dynamic_slice_in_dim(terms, member * own_rows, own_rows)
    row_scale = jnp.where(counted, 1.0 / loss_count, 0.0)
    dlogits = (
        (jnp.exp(logits - log_total[None, :]) - hits.astype(jnp.float32)) * row_scale[None, :]
    ).astype(low_type)
    chosen_part = contract(dlogits, table_low, 0, 0)
    chosen_grad = across_wide(chosen_part.reshape(groups, own_rows, width))
    final_grad = jnp.zeros((tokens, width), jnp.float32).at[flat_picks].add(chosen_grad)

    branch_low, gate_low, first_sum_grad, attn_low, mixed_grad, late_norms = feed_backward(
        final_grad, second_sum, first_sum, gate_up, norms, near, w_gu_low, w_down_low
    )
    down, gate, up = Fold(1, (4, 2)), Fold(1, (2, 4)), Fold(1, (4, 2))
    middle = gate_up.shape[1] // 2
    sent = down.cores(gradient_chunks(contract(hidden_low, branch_low, 0, 0)))
    gate_low, _ = tie((gate_low, sent))
    sent = gate.cores(gradient_chunks(contract(second_low, gate_low[:, :middle], 0, 0)))
    gate_low, _ = tie((gate_low, sent))
    up.cores(gradient_chunks(contract(second_low, gate_low[:, middle:], 0, 0)))
    pairs = width // LANES
    third = pairs // 3
    sides = []
    for stage in range(3):
        if stage == 0:
            sent = down.plane(True) + gate.plane(True) + up.plane(True)
        elif stage == 1:
            sent = down.plane(False) + gate.plane(False)
        else:
            sent = down.members() + gate.members() + up.plane(False)
        mixed_grad, sides, _ = tie((mixed_grad, sides, sent))
        sides = list(sides) + [
            attend_back(lengths, queries, keys, values, mixed_grad, log_sums, cosine, sine, stage * third, third)
        ]
    sent = up.members()
    sides, down.came, gate.came, _ = tie((sides, down.came, gate.came, sent))
    joined_grad = jnp.concatenate([side for parts in zip(*sides) for side in parts], axis=1)
    first_grad = first_sum_grad + contract(joined_grad, near[:, : 3 * width], 1, 1)
    _, pull = jax.vjp(layer_norm, embed.astype(jnp.float32), norms[0], norms[1])
    embed_grad, gain_one, shift_one = pull(first_grad)
    norm_grad = jnp.concatenate([gain_one[None], shift_one[None], late_norms])
    embed_low, joined_grad = tie((embed_grad.astype(low_type), joined_grad))
    group_embed = lax.all_gather(embed_low, "grp", axis=0, tiled=True)

    join = Fold(1, (2, 4))
    join.cores(
        gradient_chunks(
            jnp.concatenate(
                [contract(first_low, joined_grad, 0, 0), contract(mixed_low, attn_low, 0, 0)], axis=1
            )
        )
    )
    join.plane(True)
    join.plane(False)
    join.members()
    gu_share = jnp.concatenate([gate.total(), up.total()], axis=1)
    down_share, join_share = down.total(), join.total()
    part_rows = gu_share.shape[0]
    far_whole = plane_gather(
        jnp.concatenate(
            [gu_share.astype(low_type), down_share.astype(low_type).reshape(part_rows, -1)], axis=1
        )
    ).reshape(shard_rows, -1)
    near_whole = plane_gather(join_share.astype(low_type)).reshape(shard_rows, -1)
    shares = (join_share[:, : 3 * width], join_share[:, 3 * width :], gu_share, down_share)
    share_cols = [jnp.sum(gradient * gradient, axis=0) for gradient in shares]
    group_embed, near_whole, far_whole, share_cols = tie((group_embed, near_whole, far_whole, share_cols))

    core = replica % 2
    middle = width // 2
    rest = (starts, codes, padded_order, dlogits, group_chosen, group_embed, block)
    if quick:
        chunks = ((replica // 2) ^ jnp.arange(3, -1, -1, dtype=jnp.int32)) * 2
        sent = table_grad_chunks(chunks + 1 - core, *rest, low_type)
        sent_x, kept_x, sent_y, kept_y = table_grad_chunks(chunks + core, *rest, low_type, flip(sent, 1))
        one = kept_x + flip(sent_x, 2).astype(jnp.float32)
        two = kept_y + flip(sent_y, 4).astype(jnp.float32)
        table_parts = [
            one[1] + flip(one[0].astype(low_type), 4).astype(jnp.float32),
            two[1] + flip(two[0].astype(low_type), 2).astype(jnp.float32),
        ]
    else:
        value = table_grad_chunks(jnp.arange(replicas, dtype=jnp.int32), *rest, jnp.float32)
        value = lax.psum_scatter(value, "rep", scatter_dimension=0)
        table_parts = [value[:, :middle], value[:, middle:]]

    old_rows = (table_rows, qkv_rows, out_rows, gu_rows, down_rows)
    old_cols = (table_cols, qkv_cols, out_cols, gu_cols, down_cols)
    masters = (table, w_qkv, w_out, w_gu, w_down)
    col_parts = [
        jnp.concatenate([jnp.sum(gradient * gradient, axis=0) for gradient in table_parts])
    ] + share_cols
    row_old = jnp.stack([jnp.sum(rows) for rows in old_rows]) / replicas
    small = [norm_grad.reshape(-1)] + col_parts + [row_old, jnp.sum(own_terms)[None]]
    plane_totals = plane_sum(jnp.concatenate(small))
    table_lows = [part.astype(low_type) for part in table_parts]
    plane_totals, table_lows = tie((plane_totals, table_lows))
    totals = rest_sum(plane_totals)
    cuts = []
    start = 0
    for part in small:
        cuts.append(totals[start : start + part.shape[0]])
        start += part.shape[0]
    norm_sum = cuts[0].reshape(norm_grad.shape)
    col_totals = cuts[1:6]
    old_totals = cuts[6]
    loss_sum = cuts[7][0]
    squares = [jnp.sum(part) for part in col_totals]
    clip_norm = jnp.sqrt(sum(squares) + jnp.sum(norm_sum * norm_sum))
    factor = clip_limit / jnp.maximum(clip_norm, clip_limit)
    decay = 1.0 - float(STEP) ** (-0.8)

    wholes = [
        None,
        near_whole[:, : 3 * width],
        near_whole[:, 3 * width :],
        far_whole[:, : w_gu.shape[1]],
        far_whole[:, w_gu.shape[1] :].reshape(w_down.shape),
    ]

    outputs = []
    for place in range(5):
        rows, columns = masters[place].shape
        full_rows = rows * groups
        new_cols = (
            decay * old_cols[place] + (1.0 - decay) * (col_totals[place] * factor * factor) / full_rows
        )
        row_total = decay * old_totals[place] + (1.0 - decay) * (squares[place] * factor * factor) / columns
        row_mean = row_total / full_rows
        if place == 0 and quick:
            have = [
                spread(low, [2, 4, 1] if part % 2 else [4, 2, 1]) for part, low in enumerate(table_lows)
            ]
            tiles = padded // TILE
            row_tiles = jnp.pad(table_rows, (0, padded - vocab_rows), constant_values=1.0).reshape(tiles, 1, TILE)
            scalars = jnp.stack([factor, rate_matrix * factor * jnp.sqrt(row_mean)])
            so_far = (
                blank(table.shape, jnp.float32),
                blank(table.shape, jnp.float32),
                blank((tiles, 1, TILE), jnp.float32),
            )
            for places in ((0,), (2, 4), (6,), (1, 3, 5, 7)):
                so_far = update(
                    places,
                    slots_of(),
                    scalars,
                    [[got[part] for got in have] for part in places],
                    table,
                    row_tiles,
                    lax.rsqrt(new_cols)[None, :],
                    so_far,
                )
            outputs.extend([so_far[0], so_far[2].reshape(-1)[:vocab_rows], new_cols, so_far[1]])
            continue
        if place == 0:
            whole = plane_gather(jnp.concatenate(table_lows, axis=1))
            gradient = whole.reshape(padded, width)[:vocab_rows].astype(jnp.float32)
        else:
            gradient = wholes[place].astype(jnp.float32)
        row_means = jnp.mean(gradient * gradient, axis=1)
        new_rows = decay * old_rows[place] + (1.0 - decay) * (row_means * factor * factor)
        clipped = gradient * factor
        scale = new_rows[:, None] * new_cols[None, :] / row_mean
        new_master = masters[place] - rate_matrix * clipped * lax.rsqrt(scale)
        outputs.extend([clipped, new_rows, new_cols, new_master])
    norm_clipped = norm_sum * factor
    moment_new = decay * norms_moment + (1.0 - decay) * norm_clipped * norm_clipped
    norms_new = norms - rate_norm * norm_clipped * lax.rsqrt(moment_new)
    return (
        (loss_sum, loss_count, clip_norm) + tuple(outputs) + (norm_clipped, moment_new, norms_new)
    )


def solution(mesh):
    in_specs = (
        P(("grp", "rep"), None),
        P(("grp", "rep")),
        P(("grp", "rep"), None),
        P(("grp", "rep"), None),
        P(("grp", "rep"), None),
        P("grp", None),
        P("grp", None),
        P("grp", None),
        P("grp", None),
        P("grp", None),
        P(),
        P("grp"),
        P(),
        P("grp"),
        P(),
        P("grp"),
        P(),
        P("grp"),
        P(),
        P("grp"),
        P(),
        P(),
    )
    out_specs = (
        P(),
        P(),
        P(),
        P("grp", None),
        P("grp"),
        P(),
        P("grp", None),
        P("grp", None),
        P("grp"),
        P(),
        P("grp", None),
        P("grp", None),
        P("grp"),
        P(),
        P("grp", None),
        P("grp", None),
        P("grp"),
        P(),
        P("grp", None),
        P("grp", None),
        P("grp"),
        P(),
        P("grp", None),
        P(),
        P(),
        P(),
    )
    return jax.shard_map(body, mesh=mesh, in_specs=in_specs, out_specs=out_specs, check_vma=False)
```

```python
import functools
import math

import jax
import jax.numpy as jnp
from jax import lax
from jax.experimental import pallas as pl
from jax.experimental.pallas import tpu as pltpu
from jax.sharding import PartitionSpec as P

HEADS = 12
HD = 64
STEP = 10
LANES = 128
ROWS = 256
CHUNK = 256
TILE = 480


ln_eps = 1e-05
rope_base = 10000.0
clip_limit = 0.01
rate_matrix = 0.03
rate_norm = 0.3
neg_large = -1e30
low_type = jnp.bfloat16
vmem = 56 * 1024 * 1024


def pair_lanes(shape):
    return lax.broadcasted_iota(jnp.int32, shape, len(shape) - 1)


def swap_halves(value):
    upper = (pair_lanes(value.shape) % HD) >= HD // 2
    return jnp.where(
        upper,
        pltpu.roll(value, HD // 2, axis=1),
        pltpu.roll(value, LANES - HD // 2, axis=1),
    )


def normalize(values, gain, shift):
    center = values - jnp.mean(values, axis=-1, keepdims=True)
    spread = jnp.mean(center * center, axis=-1, keepdims=True)
    return center * lax.rsqrt(spread + ln_eps) * gain + shift


def project_kernel(embed_ref, norms_ref, cosine_ref, sine_ref, w_ref, first_ref, low_ref, q_ref, k_ref, v_ref):
    first = normalize(embed_ref[...].astype(jnp.float32), norms_ref[0:1, :], norms_ref[1:2, :])
    first_ref[...] = first
    low = first.astype(low_type)
    low_ref[...] = low
    width = first.shape[1]
    cosine, sine = cosine_ref[...], sine_ref[...]
    for part, out_ref in enumerate((q_ref, k_ref)):
        joined = jnp.dot(low, w_ref[:, part * width : (part + 1) * width], preferred_element_type=jnp.float32)
        for start in range(0, width, LANES):
            piece = joined[:, start : start + LANES]
            out_ref[:, start : start + LANES] = (piece * cosine + swap_halves(piece) * sine).astype(low_type)
    v_ref[...] = jnp.dot(low, w_ref[:, 2 * width :], preferred_element_type=jnp.float32).astype(low_type)


def project(embed, norms, cosine, sine, weights):
    tokens, width = embed.shape
    row = lambda i: (i, 0)
    fixed = lambda i: (0, 0)
    low = jax.ShapeDtypeStruct((tokens, width), low_type)
    return pl.pallas_call(
        project_kernel,
        grid=(tokens // ROWS,),
        in_specs=[
            pl.BlockSpec((ROWS, width), row),
            pl.BlockSpec(norms.shape, fixed),
            pl.BlockSpec((ROWS, LANES), row),
            pl.BlockSpec((ROWS, LANES), row),
            pl.BlockSpec((width, 3 * width), fixed),
        ],
        out_specs=[pl.BlockSpec((ROWS, width), row)] * 5,
        out_shape=[jax.ShapeDtypeStruct((tokens, width), jnp.float32), low, low, low, low],
        compiler_params=pltpu.CompilerParams(vmem_limit_bytes=vmem),
        cost_estimate=pl.CostEstimate(flops=6 * tokens * width * width, bytes_accessed=20 * tokens * width, transcendentals=0),
    )(embed, norms, cosine, sine, weights)


def head_keys(k, bias, half):
    lanes = pair_lanes(k.shape)
    spare = HD - half * HD
    return jnp.where(lanes // HD == half, k, jnp.where(lanes == spare, bias, jnp.zeros_like(k)))


def head_queries(q, half, spare_value):
    lanes = pair_lanes(q.shape)
    spare = HD - half * HD
    scaled = q * jnp.asarray(1.0 / math.sqrt(HD), q.dtype)
    other = jnp.where(lanes == spare, jnp.full_like(q, spare_value), jnp.zeros_like(q))
    return jnp.where(lanes // HD == half, scaled, other)


def transposed_dot(left, right):
    return lax.dot_general(left, right, (((1,), (1,)), ((), ())), preferred_element_type=jnp.float32)


def key_bias(length_ref, tokens):
    place = lax.broadcasted_iota(jnp.int32, (tokens, LANES), 0)
    return jnp.where(place < length_ref[0], 0.0, neg_large).astype(low_type)


def attend_kernel(length_ref, q_ref, k_ref, v_ref, out_ref, log_ref, keys, turned):
    tokens = k_ref.shape[0]

    @pl.when(pl.program_id(1) == 0)
    def _():
        bias = key_bias(length_ref, tokens)
        for half in range(2):
            keys[half] = head_keys(k_ref[...], bias, half)
        turned[...] = v_ref[...].T

    parts = []
    for half in range(2):
        scores = transposed_dot(keys[half], head_queries(q_ref[...], half, 1.0))
        peak = jnp.max(scores, axis=0, keepdims=True)
        weights = jnp.exp(scores - peak)
        totals = jnp.sum(weights, axis=0, keepdims=True)
        probs = (weights * (1.0 / totals)).astype(low_type)
        parts.append(
            jnp.dot(turned[half * HD : (half + 1) * HD, :], probs, preferred_element_type=jnp.float32)
        )
        log_ref[0, half : half + 1, :] = peak + jnp.log(totals)
    out_ref[...] = jnp.concatenate(parts, axis=0).T.astype(low_type)


def attend(length, q, k, v):
    tokens, width = q.shape
    pairs = width // LANES
    own = lambda p, i, *_: (i, p)
    whole = lambda p, i, *_: (0, p)
    return pl.pallas_call(
        attend_kernel,
        grid_spec=pltpu.PrefetchScalarGridSpec(
            num_scalar_prefetch=1,
            grid=(pairs, tokens // ROWS),
            in_specs=[
                pl.BlockSpec((ROWS, LANES), own),
                pl.BlockSpec((tokens, LANES), whole),
                pl.BlockSpec((tokens, LANES), whole),
            ],
            out_specs=[
                pl.BlockSpec((ROWS, LANES), own),
                pl.BlockSpec((1, 2, ROWS), lambda p, i, *_: (p, 0, i)),
            ],
            scratch_shapes=[
                pltpu.VMEM((2, tokens, LANES), low_type),
                pltpu.VMEM((LANES, tokens), low_type),
            ],
        ),
        out_shape=[
            jax.ShapeDtypeStruct((tokens, width), low_type),
            jax.ShapeDtypeStruct((pairs, 2, tokens), jnp.float32),
        ],
        compiler_params=pltpu.CompilerParams(vmem_limit_bytes=vmem),
        cost_estimate=pl.CostEstimate(
            flops=16 * tokens * tokens * width, bytes_accessed=8 * tokens * width, transcendentals=tokens * tokens * width // HD
        ),
    )(length, q, k, v)


def rotate_back(grads, cosine, sine):
    return grads * cosine + swap_halves(grads * sine)


def attend_back_kernel(first_pair, length_ref, q_ref, k_ref, v_ref, d_ref, log_ref, cosq_ref, sinq_ref, cos_ref, sin_ref, *rest):
    dq_ref, dk_ref, dv_ref, keys, values, turned, dk_total, dv_total = rest[-8:]
    tokens = k_ref.shape[0]
    step = pl.program_id(1)

    @pl.when(step == 0)
    def _():
        bias = key_bias(length_ref, tokens)
        lanes = pair_lanes((tokens, LANES))
        for half in range(2):
            keys[half] = head_keys(k_ref[...], bias, half)
            values[half] = jnp.where(lanes // HD == half, v_ref[...], jnp.zeros_like(v_ref[...]))
        turned[...] = k_ref[...].T
        dk_total[...] = jnp.zeros_like(dk_total)
        dv_total[...] = jnp.zeros_like(dv_total)

    d = d_ref[...]
    lanes = pair_lanes(d.shape)
    parts = []
    dk = dv = None
    for half in range(2):
        scores = transposed_dot(keys[half], head_queries(q_ref[...], half, 1.0))
        probs = jnp.exp(scores - log_ref[0, half : half + 1, :])
        dprobs = transposed_dot(values[half], d)
        inner = jnp.sum(probs * dprobs, axis=0, keepdims=True)
        dscore = (probs * (dprobs - inner)).astype(low_type)
        parts.append(jnp.dot(turned[half * HD : (half + 1) * HD, :], dscore, preferred_element_type=jnp.float32))
        one_k = jnp.dot(dscore, head_queries(q_ref[...], half, 0.0), preferred_element_type=jnp.float32)
        one_v = jnp.dot(
            probs.astype(low_type), jnp.where(lanes // HD == half, d, jnp.zeros_like(d)), preferred_element_type=jnp.float32
        )
        dk = one_k if dk is None else dk + one_k
        dv = one_v if dv is None else dv + one_v
    dk_total[...] += dk
    dv_total[...] += dv
    dq = jnp.concatenate(parts, axis=0).T * (1.0 / math.sqrt(HD))
    dq_ref[...] = rotate_back(dq, cosq_ref[...], sinq_ref[...]).astype(low_type)

    @pl.when(step == pl.num_programs(1) - 1)
    def _():
        dk_ref[...] = rotate_back(dk_total[...], cos_ref[...], sin_ref[...]).astype(low_type)
        dv_ref[...] = dv_total[...].astype(low_type)


def attend_back(length, q, k, v, d, logs, cosine, sine, first_pair, pairs, after=()):
    tokens, width = q.shape
    own = lambda p, i, *_: (i, first_pair + p)
    whole = lambda p, i, *_: (0, first_pair + p)
    low = jax.ShapeDtypeStruct((tokens, pairs * LANES), low_type)
    fixed = pl.BlockSpec((tokens, LANES), lambda p, i, *_: (0, 0))
    row = pl.BlockSpec((ROWS, LANES), lambda p, i, *_: (i, 0))
    return pl.pallas_call(
        functools.partial(attend_back_kernel, first_pair),
        grid_spec=pltpu.PrefetchScalarGridSpec(
            num_scalar_prefetch=1,
            grid=(pairs, tokens // ROWS),
            in_specs=[
                pl.BlockSpec((ROWS, LANES), own),
                pl.BlockSpec((tokens, LANES), whole),
                pl.BlockSpec((tokens, LANES), whole),
                pl.BlockSpec((ROWS, LANES), own),
                pl.BlockSpec((1, 2, ROWS), lambda p, i, *_: (first_pair + p, 0, i)),
                row,
                row,
                fixed,
                fixed,
            ]
            + [pl.BlockSpec(memory_space=pl.ANY)] * len(after),
            out_specs=[
                pl.BlockSpec((ROWS, LANES), lambda p, i, *_: (i, p)),
                pl.BlockSpec((tokens, LANES), lambda p, i, *_: (0, p)),
                pl.BlockSpec((tokens, LANES), lambda p, i, *_: (0, p)),
            ],
            scratch_shapes=[
                pltpu.VMEM((2, tokens, LANES), low_type),
                pltpu.VMEM((2, tokens, LANES), low_type),
                pltpu.VMEM((LANES, tokens), low_type),
                pltpu.VMEM((tokens, LANES), jnp.float32),
                pltpu.VMEM((tokens, LANES), jnp.float32),
            ],
        ),
        out_shape=[low, low, low],
        compiler_params=pltpu.CompilerParams(vmem_limit_bytes=vmem),
        cost_estimate=pl.CostEstimate(
            flops=40 * tokens * tokens * pairs * LANES,
            bytes_accessed=16 * tokens * pairs * LANES,
            transcendentals=tokens * tokens * pairs * 2,
        ),
    )(length, q, k, v, d, logs, cosine, sine, cosine, sine, *after)


def forward_kernel(mixed_ref, first_ref, norms_ref, out_w_ref, gu_w_ref, down_w_ref, first_sum_ref, second_ref, gate_up_ref, hidden_ref, second_sum_ref, final_ref):
    width = first_ref.shape[1]
    middle = gu_w_ref.shape[1] // 2
    first_sum = first_ref[...] + jnp.dot(mixed_ref[...], out_w_ref[...], preferred_element_type=jnp.float32)
    first_sum_ref[...] = first_sum
    second = normalize(first_sum, norms_ref[2:3, :], norms_ref[3:4, :])
    low = second.astype(low_type)
    second_ref[...] = low
    total = second
    for start in range(0, middle, width):
        end = start + width
        gate = jnp.dot(low, gu_w_ref[:, start:end], preferred_element_type=jnp.float32)
        up = jnp.dot(low, gu_w_ref[:, middle + start : middle + end], preferred_element_type=jnp.float32)
        gate_up_ref[:, start:end] = gate
        gate_up_ref[:, middle + start : middle + end] = up
        hidden = (gate * (1.0 / (1.0 + jnp.exp(-gate))) * up).astype(low_type)
        hidden_ref[:, start:end] = hidden
        total = total + jnp.dot(hidden, down_w_ref[start:end, :], preferred_element_type=jnp.float32)
    second_sum_ref[...] = total
    final_ref[...] = normalize(total, norms_ref[4:5, :], norms_ref[5:6, :])


def feed_forward(mixed, first, norms, near, w_gu, w_down):
    tokens, width = first.shape
    middle = w_down.shape[0]
    row = lambda i: (i, 0)
    fixed = lambda i: (0, 0)
    once = pl.Buffered(1)
    narrow = pl.BlockSpec((ROWS, width), row)
    high = jax.ShapeDtypeStruct((tokens, width), jnp.float32)
    return pl.pallas_call(
        forward_kernel,
        grid=(tokens // ROWS,),
        in_specs=[
            narrow,
            narrow,
            pl.BlockSpec(norms.shape, fixed),
            pl.BlockSpec((width, width), lambda i: (0, 3), pipeline_mode=once),
            pl.BlockSpec(w_gu.shape, fixed, pipeline_mode=once),
            pl.BlockSpec(w_down.shape, fixed, pipeline_mode=once),
        ],
        out_specs=[
            narrow,
            narrow,
            pl.BlockSpec((ROWS, 2 * middle), row),
            pl.BlockSpec((ROWS, middle), row),
            narrow,
            narrow,
        ],
        out_shape=[
            high,
            jax.ShapeDtypeStruct((tokens, width), low_type),
            jax.ShapeDtypeStruct((tokens, 2 * middle), jnp.float32),
            jax.ShapeDtypeStruct((tokens, middle), low_type),
            high,
            high,
        ],
        compiler_params=pltpu.CompilerParams(vmem_limit_bytes=vmem),
        cost_estimate=pl.CostEstimate(
            flops=2 * tokens * width * (width + 3 * middle), bytes_accessed=14 * tokens * middle, transcendentals=tokens * middle
        ),
    )(mixed, first, norms, near, w_gu, w_down)


def normalize_back(values, gain, grads):
    center = values - jnp.mean(values, axis=-1, keepdims=True)
    inverse = lax.rsqrt(jnp.mean(center * center, axis=-1, keepdims=True) + ln_eps)
    unit = center * inverse
    scaled = grads * gain
    inner = jnp.mean(scaled * unit, axis=-1, keepdims=True)
    result = inverse * (scaled - jnp.mean(scaled, axis=-1, keepdims=True) - unit * inner)
    return result, jnp.sum(grads * unit, axis=0, keepdims=True), jnp.sum(grads, axis=0, keepdims=True)


def backward_kernel(grad_ref, second_sum_ref, first_sum_ref, gate_up_ref, norms_ref, out_w_ref, gu_w_ref, down_w_ref, branch_ref, gate_low_ref, first_sum_grad_ref, attn_ref, mixed_ref, norms_grad_ref):
    width = grad_ref.shape[1]
    middle = down_w_ref.shape[0]
    sum_grad, gain_three, shift_three = normalize_back(second_sum_ref[...], norms_ref[4:5, :], grad_ref[...])
    branch = sum_grad.astype(low_type)
    branch_ref[...] = branch
    total = sum_grad
    for start in range(0, middle, width):
        end = start + width
        hidden_grad = transposed_dot(branch, down_w_ref[start:end, :])
        gate = gate_up_ref[:, start:end]
        up = gate_up_ref[:, middle + start : middle + end]
        share = 1.0 / (1.0 + jnp.exp(-gate))
        gate_grad = (hidden_grad * up * (share * (1.0 + gate * (1.0 - share)))).astype(low_type)
        up_grad = (hidden_grad * (gate * share)).astype(low_type)
        gate_low_ref[:, start:end] = gate_grad
        gate_low_ref[:, middle + start : middle + end] = up_grad
        total = total + transposed_dot(gate_grad, gu_w_ref[:, start:end])
        total = total + transposed_dot(up_grad, gu_w_ref[:, middle + start : middle + end])
    first_sum_grad, gain_two, shift_two = normalize_back(first_sum_ref[...], norms_ref[2:3, :], total)
    first_sum_grad_ref[...] = first_sum_grad
    attn = first_sum_grad.astype(low_type)
    attn_ref[...] = attn
    mixed_ref[...] = transposed_dot(attn, out_w_ref[...]).astype(low_type)

    @pl.when(pl.program_id(0) == 0)
    def _():
        norms_grad_ref[...] = jnp.zeros_like(norms_grad_ref)

    norms_grad_ref[...] += jnp.concatenate([gain_two, shift_two, gain_three, shift_three], axis=0)


def feed_backward(grad, second_sum, first_sum, gate_up, norms, near, w_gu, w_down):
    tokens, width = grad.shape
    middle = w_down.shape[0]
    row = lambda i: (i, 0)
    fixed = lambda i: (0, 0)
    once = pl.Buffered(1)
    narrow = pl.BlockSpec((ROWS, width), row)
    wide = pl.BlockSpec((ROWS, 2 * middle), row)
    low = jax.ShapeDtypeStruct((tokens, width), low_type)
    return pl.pallas_call(
        backward_kernel,
        grid=(tokens // ROWS,),
        in_specs=[
            narrow,
            narrow,
            narrow,
            wide,
            pl.BlockSpec(norms.shape, fixed),
            pl.BlockSpec((width, width), lambda i: (0, 3), pipeline_mode=once),
            pl.BlockSpec(w_gu.shape, fixed, pipeline_mode=once),
            pl.BlockSpec(w_down.shape, fixed, pipeline_mode=once),
        ],
        out_specs=[narrow, wide, narrow, narrow, narrow, pl.BlockSpec((4, width), fixed)],
        out_shape=[
            low,
            jax.ShapeDtypeStruct((tokens, 2 * middle), low_type),
            jax.ShapeDtypeStruct((tokens, width), jnp.float32),
            low,
            low,
            jax.ShapeDtypeStruct((4, width), jnp.float32),
        ],
        compiler_params=pltpu.CompilerParams(vmem_limit_bytes=vmem),
        cost_estimate=pl.CostEstimate(
            flops=2 * tokens * width * (width + 3 * middle), bytes_accessed=14 * tokens * middle, transcendentals=tokens * middle
        ),
    )(grad, second_sum, first_sum, gate_up, norms, near, w_gu, w_down)


def blank(shape, dtype):
    return pl.pallas_call(
        lambda out_ref: None,
        out_shape=jax.ShapeDtypeStruct(shape, dtype),
        out_specs=pl.BlockSpec(memory_space=pl.ANY),
    )()


def lookup_kernel(starts_ref, places_ref, order_ref, table_ref, out_ref, rows):
    count = out_ref.shape[0]
    owned = starts_ref[starts_ref.shape[0] - 1]
    for start in range(0, count, CHUNK):
        rows[start : start + CHUNK, :] = jnp.zeros((CHUNK, rows.shape[1]), jnp.float32)

    def eight(step, carry):
        for j in range(8):
            i = step * 8 + j
            valid = i < owned
            source = jnp.where(valid, places_ref[i], 0)
            target = jnp.where(valid, order_ref[i], count)
            rows[pl.ds(target, 1), :] = table_ref[pl.ds(source, 1), :]
        return carry

    lax.fori_loop(0, (owned + 7) // 8, eight, 0)
    for start in range(0, count, CHUNK):
        out_ref[start : start + CHUNK, :] = rows[start : start + CHUNK, :].astype(low_type)


def lookup(starts, places, order, table):
    count = places.shape[0]
    width = table.shape[1]
    return pl.pallas_call(
        lookup_kernel,
        grid_spec=pltpu.PrefetchScalarGridSpec(
            num_scalar_prefetch=3,
            grid=(1,),
            in_specs=[pl.BlockSpec(table.shape, lambda i, *_: (0, 0), pipeline_mode=pl.Buffered(1))],
            out_specs=pl.BlockSpec((count, width), lambda i, *_: (0, 0), pipeline_mode=pl.Buffered(1)),
            scratch_shapes=[pltpu.VMEM((count + 8, width), jnp.float32)],
        ),
        out_shape=jax.ShapeDtypeStruct((count, width), low_type),
        compiler_params=pltpu.CompilerParams(vmem_limit_bytes=vmem),
        cost_estimate=pl.CostEstimate(flops=0, bytes_accessed=table.size * 12, transcendentals=0),
    )(starts, places, order, table)


def table_grad_kernel(chunks_ref, starts_ref, codes_ref, order_ref, dlogits_ref, chosen_ref, embed_ref, *refs):
    rows, sums = refs[-2:]
    step = pl.program_id(0)
    count, width = embed_ref.shape
    block = dlogits_ref.shape[0]

    @pl.when(step == 0)
    def _():
        for start in range(0, count, CHUNK):
            rows[start : start + CHUNK, :] = embed_ref[start : start + CHUNK, :].astype(jnp.float32)

    sums[...] = jnp.zeros_like(sums)
    chunk = chunks_ref[step]
    first, last = starts_ref[chunk], starts_ref[chunk + 1]

    def eight(turn, running):
        for j in range(8):
            i = first + turn * 8 + j
            code = codes_ref[i]
            place = jnp.where(i < last, code >> 1, block)
            running = jnp.where(code & 1, running, 0.0) + rows[pl.ds(order_ref[i], 1), :]
            sums[pl.ds(place, 1), :] = running
        return running

    lax.fori_loop(0, (last - first + 7) // 8, eight, jnp.zeros((1, width), jnp.float32))
    product = jnp.dot(dlogits_ref[...], chosen_ref[...], preferred_element_type=jnp.float32)
    result = product + sums[:block, :]
    if len(refs) == 3:
        refs[0][0] = result.astype(refs[0].dtype)
        return
    got_ref, sent_x, kept_x, sent_y, kept_y = refs[:-2]
    result = result + got_ref[0].astype(jnp.float32)
    left, right = result[:, : width // 2], result[:, width // 2 :]

    @pl.when(step % 2 == 0)
    def _():
        sent_x[0] = left.astype(sent_x.dtype)

    @pl.when(step % 2 == 1)
    def _():
        kept_x[0] = left

    @pl.when(step < 2)
    def _():
        sent_y[0] = right.astype(sent_y.dtype)

    @pl.when(step >= 2)
    def _():
        kept_y[0] = right


def table_grad_chunks(chunks, starts, codes, order, dlogits, chosen, embed, block, dtype, got=None):
    count, width = embed.shape
    picked = chosen.shape[0]
    steps = chunks.shape[0]
    fixed = lambda i, *_: (0, 0)
    in_specs = [
        pl.BlockSpec((block, picked), lambda i, chunks, *_: (chunks[i], 0)),
        pl.BlockSpec((picked, width), fixed),
        pl.BlockSpec((count, width), fixed, pipeline_mode=pl.Buffered(1)),
    ]
    whole = pl.BlockSpec((1, block, width), lambda i, *_: (i, 0, 0))
    if got is None:
        out_shape = jax.ShapeDtypeStruct((steps, block, width), dtype)
        out_specs = whole
    else:
        in_specs.append(whole)
        half = (1, block, width // 2)
        by_y = lambda i, *_: (i // 2, 0, 0)
        low = jax.ShapeDtypeStruct((2, block, width // 2), low_type)
        high = jax.ShapeDtypeStruct((2, block, width // 2), jnp.float32)
        out_shape = [low, high, low, high]
        out_specs = [
            pl.BlockSpec(half, by_y),
            pl.BlockSpec(half, by_y),
            pl.BlockSpec(half, lambda i, *_: (jnp.minimum(i, 1), 0, 0)),
            pl.BlockSpec(half, lambda i, *_: (jnp.maximum(i - 2, 0), 0, 0)),
        ]
    return pl.pallas_call(
        table_grad_kernel,
        grid_spec=pltpu.PrefetchScalarGridSpec(
            num_scalar_prefetch=4,
            grid=(steps,),
            in_specs=in_specs,
            out_specs=out_specs,
            scratch_shapes=[
                pltpu.VMEM((count, width), jnp.float32),
                pltpu.VMEM((block + 8, width), jnp.float32),
            ],
        ),
        out_shape=out_shape,
        compiler_params=pltpu.CompilerParams(vmem_limit_bytes=vmem),
        cost_estimate=pl.CostEstimate(
            flops=2 * steps * block * picked * width, bytes_accessed=8 * steps * block * width, transcendentals=0
        ),
    )(chunks, starts, codes, order, dlogits, chosen, embed, *(() if got is None else (got,)))


def update_kernel(places, parts, slots_ref, scalars_ref, *rest):
    given = len(places) * parts
    pieces = rest[:given]
    table_ref, rows_ref, cols_ref = rest[given : given + 3]
    grad_ref, new_ref, rows_new_ref = rest[-3:]
    factor, rate = scalars_ref[0], scalars_ref[1]
    decay = 1.0 - float(STEP) ** (-0.8)
    old = jnp.broadcast_to(rows_ref[0], (LANES, TILE)).T[:, 0:1]
    for part in range(len(places)):

        @pl.when(pl.program_id(0) == part)
        def _(part=part):
            own = pieces[part * parts : (part + 1) * parts]
            gradient = jnp.concatenate([piece[...] for piece in own], axis=1).astype(jnp.float32)
            means = jnp.mean(gradient * gradient, axis=1, keepdims=True)
            rows_new = decay * old + (1.0 - decay) * (means * factor * factor)
            grad_ref[...] = gradient * factor
            new_ref[...] = table_ref[...] - gradient * (rate * lax.rsqrt(rows_new)) * cols_ref[...]
            rows_new_ref[0] = jnp.broadcast_to(rows_new, (TILE, LANES)).T[0:1, :]


def update(places, slots, scalars, pieces, table, rows, cols, so_far):
    count = len(places)
    parts = len(pieces[0])
    block = pieces[0][0].shape[0]
    width = table.shape[1]
    steps = block // TILE

    def slot(p, slots):
        at = slots[places[0]]
        for j in range(1, count):
            at = jnp.where(p == j, slots[places[j]], at)
        return at

    place = lambda p, i, slots: (slot(p, slots) * steps + i, 0)
    place3 = lambda p, i, slots: (slot(p, slots) * steps + i, 0, 0)

    def own(part):
        return lambda p, i, slots: (jnp.where(p < part, 0, jnp.where(p > part, steps - 1, i)), 0)

    fixed = lambda p, i, slots: (0, 0)
    any_space = pl.BlockSpec(memory_space=pl.ANY)
    given = 5 + count * parts
    return pl.pallas_call(
        functools.partial(update_kernel, places, parts),
        grid_spec=pltpu.PrefetchScalarGridSpec(
            num_scalar_prefetch=1,
            grid=(count, steps),
            in_specs=[pl.BlockSpec(memory_space=pltpu.SMEM)]
            + [pl.BlockSpec((TILE, piece.shape[1]), own(part)) for part in range(count) for piece in pieces[part]]
            + [
                pl.BlockSpec((TILE, width), place),
                pl.BlockSpec((1, 1, TILE), place3),
                pl.BlockSpec((1, width), fixed),
                any_space,
                any_space,
                any_space,
            ],
            out_specs=[
                pl.BlockSpec((TILE, width), place),
                pl.BlockSpec((TILE, width), place),
                pl.BlockSpec((1, 1, TILE), place3),
            ],
        ),
        out_shape=[jax.ShapeDtypeStruct(part.shape, part.dtype) for part in so_far],
        input_output_aliases={given: 0, given + 1: 1, given + 2: 2},
        compiler_params=pltpu.CompilerParams(vmem_limit_bytes=vmem),
        cost_estimate=pl.CostEstimate(
            flops=10 * count * block * width, bytes_accessed=14 * count * block * width, transcendentals=0
        ),
    )(slots, scalars, *[piece for some in pieces for piece in some], table, rows, cols, *so_far)


def stack_kernel(slots_ref, *refs):
    pieces, out_ref = refs[:-1], refs[-1]
    for place, piece in enumerate(pieces):

        @pl.when(pl.program_id(0) == place)
        def _(piece=piece):
            out_ref[0] = piece[...]


def lay_out(slots, pieces):
    shape = pieces[0].shape
    return pl.pallas_call(
        stack_kernel,
        grid_spec=pltpu.PrefetchScalarGridSpec(
            num_scalar_prefetch=1,
            grid=(len(pieces),),
            in_specs=[pl.BlockSpec(shape, lambda i, slots: (0, 0), pipeline_mode=pl.Buffered(1))] * len(pieces),
            out_specs=pl.BlockSpec((1,) + shape, lambda i, slots: (slots[i], 0, 0)),
        ),
        out_shape=jax.ShapeDtypeStruct((len(pieces),) + shape, pieces[0].dtype),
        compiler_params=pltpu.CompilerParams(vmem_limit_bytes=vmem),
        cost_estimate=pl.CostEstimate(flops=0, bytes_accessed=4 * len(pieces) * pieces[0].size, transcendentals=0),
    )(slots, *pieces)


def columns_kernel(members_ref, slots_ref, own_ref, *refs):
    pieces, out_ref = refs[:-1], refs[-1]
    rows = own_ref.shape[0]

    def at(offset):
        return pl.ds(pl.multiple_of(members_ref[offset] * rows, rows), rows)

    out_ref[at(0), :] = own_ref[...].astype(low_type)
    for place, piece in enumerate(pieces):

        @pl.when(pl.program_id(0) == place)
        def _(piece=piece):
            for offset in range(piece.shape[0]):
                out_ref[at(offset + 1), :] = piece[offset]


def lay_columns(members, slots, own, pieces):
    others, rows, columns = pieces[0].shape
    replicas = len(pieces)
    whole = jax.ShapeDtypeStruct(((others + 1) * rows, replicas * columns), low_type)
    return pl.pallas_call(
        columns_kernel,
        grid_spec=pltpu.PrefetchScalarGridSpec(
            num_scalar_prefetch=2,
            grid=(replicas,),
            in_specs=[pl.BlockSpec((rows, columns), lambda i, members, slots: (0, slots[i]))]
            + [pl.BlockSpec(pieces[0].shape, lambda i, *_: (0, 0, 0), pipeline_mode=pl.Buffered(1))] * replicas,
            out_specs=pl.BlockSpec(((others + 1) * rows, columns), lambda i, members, slots: (0, slots[i])),
        ),
        out_shape=whole,
        compiler_params=pltpu.CompilerParams(vmem_limit_bytes=vmem),
        cost_estimate=pl.CostEstimate(flops=0, bytes_accessed=4 * whole.size, transcendentals=0),
    )(members, slots, own, *pieces)


def rows_kernel(members_ref, slots_ref, own_ref, *refs):
    pieces, out_ref = refs[:-1], refs[-1]
    out_ref[members_ref[0], 0] = own_ref[0].astype(low_type)
    for place, piece in enumerate(pieces):

        @pl.when(pl.program_id(0) == place)
        def _(piece=piece):
            for offset in range(piece.shape[0]):
                out_ref[members_ref[offset + 1], 0] = piece[offset]


def lay_rows(members, slots, own, pieces):
    others, rows, columns = pieces[0].shape
    replicas = len(pieces)
    whole = jax.ShapeDtypeStruct((others + 1, replicas, rows, columns), low_type)
    return pl.pallas_call(
        rows_kernel,
        grid_spec=pltpu.PrefetchScalarGridSpec(
            num_scalar_prefetch=2,
            grid=(replicas,),
            in_specs=[pl.BlockSpec((1, rows, columns), lambda i, members, slots: (slots[i], 0, 0))]
            + [pl.BlockSpec(pieces[0].shape, lambda i, *_: (0, 0, 0), pipeline_mode=pl.Buffered(1))] * replicas,
            out_specs=pl.BlockSpec((others + 1, 1, rows, columns), lambda i, members, slots: (0, slots[i], 0, 0)),
        ),
        out_shape=whole,
        compiler_params=pltpu.CompilerParams(vmem_limit_bytes=vmem),
        cost_estimate=pl.CostEstimate(flops=0, bytes_accessed=4 * whole.size, transcendentals=0),
    )(members, slots, own.reshape(replicas, rows, columns), *pieces).reshape(-1, columns)


tie = lax.optimization_barrier


def flip(value, bit):
    size = lax.axis_size("rep")
    return lax.ppermute(value, "rep", [(i, i ^ bit) for i in range(size)])


def turn(value, offset):
    size = lax.axis_size("grp")
    return lax.ppermute(value, "grp", [(i, (i + offset) % size) for i in range(size)])


def wave(have, bit):
    return have | {place ^ bit: flip(part, bit) for place, part in have.items()}


def spread(piece, order):
    have = {0: piece}
    for bit in order:
        have = wave(have, bit)
    return have


def slots_of():
    return lax.axis_index("rep") ^ jnp.arange(lax.axis_size("rep"), dtype=jnp.int32)


def plane_gather(piece):
    if lax.axis_size("rep") != 8:
        return lax.all_gather(piece, "rep")
    have = spread(piece, [2, 4, 1])
    return lay_out(slots_of(), [have[place] for place in range(8)])


def halve(value, axis, bit):
    mine = (lax.axis_index("rep") // bit) % 2
    kept = lax.dynamic_index_in_dim(value, mine, axis, keepdims=False)
    sent = lax.dynamic_index_in_dim(value, 1 - mine, axis, keepdims=False)
    return kept, sent.astype(low_type)


class Fold:
    def __init__(self, axis, order):
        self.axis = axis
        self.order = order
        self.quick = lax.axis_size("rep") == 8
        self.value = None

    def cores(self, chunks):
        axis = self.axis
        if not self.quick:
            self.value = lax.psum_scatter(chunks, "rep", scatter_dimension=axis)
            return []
        shape = chunks.shape
        kept, sent = halve(chunks.reshape(shape[:axis] + (4, 2) + shape[axis + 1 :]), axis + 1, 1)
        return self.from_cores(kept, sent)

    def from_cores(self, kept, sent):
        self.kept, self.got = kept, flip(sent, 1)
        return [sent]

    def sum(self):
        if self.value is None:
            return self.kept + self.got.astype(jnp.float32)
        return self.value

    def plane(self, first):
        if not self.quick:
            return []
        value = self.sum()
        axis = self.axis
        bit = self.order[0 if first else 1]
        if first:
            shape = value.shape
            value = value.reshape(shape[:axis] + (2, 2) + shape[axis + 1 :])
            axis = axis + (1 if bit == 2 else 0)
        self.kept, sent = halve(value, axis, bit)
        self.value, self.got = None, flip(sent, bit)
        return [sent]

    def members(self):
        value = self.sum()
        member = lax.axis_index("grp")
        size = lax.axis_size("grp")
        self.own = lax.dynamic_index_in_dim(value, member, 0, keepdims=False)
        sent = [
            lax.dynamic_index_in_dim(value, (member + offset) % size, 0, keepdims=False).astype(low_type)
            for offset in range(1, size)
        ]
        self.came = [turn(part, offset + 1) for offset, part in enumerate(sent)]
        return sent

    def total(self):
        return sum((came.astype(jnp.float32) for came in self.came), self.own)


def gradient_chunks(gradient):
    groups = lax.axis_size("grp")
    replicas = lax.axis_size("rep")
    rows, columns = gradient.shape
    return gradient.reshape(groups, replicas, rows // (groups * replicas), columns)


def across(chunks):
    member = lax.axis_index("grp")
    size = lax.axis_size("grp")
    total = lax.dynamic_index_in_dim(chunks, member, 0, keepdims=False)
    for offset in range(1, size):
        sent = lax.dynamic_index_in_dim(chunks, (member + offset) % size, 0, keepdims=False)
        total = total + turn(sent.astype(low_type), offset).astype(jnp.float32)
    return total


def group_gather(value):
    member = lax.axis_index("grp")
    size = lax.axis_size("grp")
    result = jnp.zeros((size,) + value.shape, value.dtype)
    result = lax.dynamic_update_index_in_dim(result, value, member, 0)
    for offset in range(1, size):
        result = lax.dynamic_update_index_in_dim(
            result, turn(value, offset), (member + size - offset) % size, 0
        )
    return result


def plane_sum(value):
    for j in range(1, lax.axis_size("rep").bit_length() - 1):
        value = value + flip(value, 1 << j)
    return value


def rest_sum(value):
    value = value + flip(value, 1)
    size = lax.axis_size("grp")
    for j in range(size.bit_length() - 1):
        value = value + lax.ppermute(value, "grp", [(i, i ^ (1 << j)) for i in range(size)])
    return value


def fetch(own):
    return jnp.stack([turn(own, offset) for offset in range(1, lax.axis_size("grp"))])


def cut(value, axis):
    replicas = lax.axis_size("rep")
    size = value.shape[axis] // replicas
    return lax.dynamic_slice_in_dim(value, lax.axis_index("rep") * size, size, axis)


def members_of():
    groups = lax.axis_size("grp")
    return (lax.axis_index("grp") + groups - jnp.arange(groups, dtype=jnp.int32)) % groups


def contract(left, right, left_dim, right_dim):
    return lax.dot_general(
        left, right, (((left_dim,), (right_dim,)), ((), ())), preferred_element_type=jnp.float32
    )


def layer_norm(values, gain, shift):
    center = values - jnp.mean(values, axis=-1, keepdims=True)
    spread = jnp.mean(center * center, axis=-1, keepdims=True)
    return center * lax.rsqrt(spread + ln_eps) * gain + shift


def rope_tables(length):
    freqs = rope_base ** (-jnp.arange(HD // 2, dtype=jnp.float32) * 2.0 / HD)
    angles = jnp.arange(length, dtype=jnp.float32)[:, None] * freqs[None, :]
    cosine, sine = jnp.cos(angles), jnp.sin(angles)
    return (
        jnp.concatenate([cosine] * 4, axis=-1),
        jnp.concatenate([-sine, sine, -sine, sine], axis=-1),
    )


def merge_stats(first_part, second_part):
    peak = jnp.maximum(first_part[0], second_part[0])
    spread = first_part[1] * jnp.exp(first_part[0] - peak) + second_part[1] * jnp.exp(
        second_part[0] - peak
    )
    return (peak, spread, first_part[2] + second_part[2])


def body(
    ids,
    lengths,
    picks,
    labels,
    loss_mask,
    table,
    w_qkv,
    w_out,
    w_gu,
    w_down,
    norms,
    table_rows,
    table_cols,
    qkv_rows,
    qkv_cols,
    out_rows,
    out_cols,
    gu_rows,
    gu_cols,
    down_rows,
    down_cols,
    norms_moment,
):
    member = lax.axis_index("grp")
    groups = lax.axis_size("grp")
    replica = lax.axis_index("rep")
    replicas = lax.axis_size("rep")
    seqs, length = ids.shape
    width = table.shape[1]
    vocab_rows = table.shape[0]
    own_rows = seqs * picks.shape[1]
    tokens = seqs * length
    block = -(-vocab_rows // (16 * replicas)) * 16
    padded = block * replicas

    packed = jnp.concatenate([ids.reshape(-1), labels.reshape(-1), loss_mask.reshape(-1)])
    group_packed = group_gather(packed)
    group_ids = group_packed[:, :tokens].reshape(-1)
    group_labels = group_packed[:, tokens : tokens + own_rows].reshape(-1)
    group_mask = group_packed[:, tokens + own_rows :].reshape(-1)
    shard_rows = w_qkv.shape[0]
    quick = replicas == 8
    near_shard = jnp.concatenate([w_qkv, w_out], axis=1)
    if quick:
        near_part = fetch(cut(near_shard, 1).astype(low_type))
        gu_part = fetch(cut(w_gu, 1).astype(low_type))

    local_ids = group_ids - member * vocab_rows
    owned = (local_ids >= 0) & (local_ids < vocab_rows)
    places, order = lax.sort(
        (jnp.where(owned, local_ids, padded), jnp.arange(local_ids.shape[0], dtype=jnp.int32)), num_keys=1
    )
    bounds = jnp.arange(replicas + 1, dtype=jnp.int32) * block
    starts = jnp.sum((places[None, :] < bounds[:, None]).astype(jnp.int32), axis=1)
    if quick:
        places, near_part = tie((places, near_part))
    again = jnp.concatenate([jnp.zeros((1,), jnp.int32), (places[1:] == places[:-1]).astype(jnp.int32)])
    codes = jnp.pad(places % block * 2 + again, (0, 8))
    padded_order = jnp.pad(order, (0, 8))
    found = lookup(starts, places, order, table)
    if quick:
        found, gu_part = tie((found, gu_part))
    embed = lax.psum_scatter(found, "grp", scatter_dimension=0, tiled=True)
    late_table, _ = lax.optimization_barrier((table, found))
    table_low = jnp.pad(late_table.astype(low_type), ((0, padded - vocab_rows), (0, 0)))

    if quick:
        members, slots = members_of(), slots_of()

        down_own, _ = tie((cut(w_down, 0), found))
        down_part = fetch(down_own.astype(low_type))

        def listed(have):
            return [have[place] for place in range(replicas)]

        near = lay_columns(members, slots, near_shard, listed(spread(near_part, [4, 2, 1])))
        w_down_low = lay_rows(members, slots, w_down, listed(spread(down_part, [4, 2, 1])))
        gu_have = spread(gu_part, [2, 4])
        gu_have, near, w_down_low, table_low = tie((gu_have, near, w_down_low, table_low))
        gu_have.update({place ^ 1: flip(part, 1) for place, part in gu_have.items()})
        w_gu_low = lay_columns(members, slots, w_gu, listed(gu_have))
        embed, near, w_gu_low, w_down_low, table_low = tie((embed, near, w_gu_low, w_down_low, table_low))
    else:
        near = lax.all_gather(near_shard.astype(low_type), "grp", tiled=True)
        w_gu_low = lax.all_gather(w_gu.astype(low_type), "grp", tiled=True)
        w_down_low = lax.all_gather(w_down.astype(low_type), "grp", tiled=True)
    cosine, sine = rope_tables(length)
    first, first_low, queries, keys, values = project(embed, norms, cosine, sine, near)
    queries, group_mask = tie((queries, group_mask))
    loss_count = jnp.sum(group_mask).astype(jnp.float32)[None]
    for j in range(replicas.bit_length() - 1):
        loss_count = loss_count + flip(loss_count, 1 << j)
    loss_count = loss_count[0]
    mixed_low, log_sums = attend(lengths, queries, keys, values)
    first_sum, second_low, gate_up, hidden_low, second_sum, final = feed_forward(
        mixed_low, first, norms, near, w_gu_low, w_down_low
    )

    flat_picks = (jnp.arange(seqs, dtype=jnp.int32)[:, None] * length + picks).reshape(-1)
    chosen = final[flat_picks].astype(low_type)
    group_chosen = group_gather(chosen).reshape(groups * own_rows, width)
    rows_at = jnp.arange(padded, dtype=jnp.int32)[:, None]
    logits = jnp.where(rows_at < vocab_rows, contract(table_low, group_chosen, 1, 1), neg_large)
    peak = jnp.max(logits, axis=0)
    spread_sum = jnp.sum(jnp.exp(logits - peak[None, :]), axis=0)
    local_labels = group_labels - member * vocab_rows
    inside = (local_labels >= 0) & (local_labels < vocab_rows)
    hits = (rows_at == local_labels[None, :]) & inside[None, :]
    target = jnp.sum(jnp.where(hits, logits, 0.0), axis=0)
    stats = group_gather(jnp.stack([peak, spread_sum, target]))
    so_far = (stats[0, 0], stats[0, 1], stats[0, 2])
    for place in range(1, groups):
        so_far = merge_stats(so_far, (stats[place, 0], stats[place, 1], stats[place, 2]))
    peak_all, spread_all, target_all = so_far
    log_total = peak_all + jnp.log(spread_all)
    counted = group_mask > 0
    terms = jnp.where(counted, log_total - target_all, 0.0)
    own_terms = lax.dynamic_slice_in_dim(terms, member * own_rows, own_rows)
    row_scale = jnp.where(counted, 1.0 / loss_count, 0.0)
    dlogits = (
        (jnp.exp(logits - log_total[None, :]) - hits.astype(jnp.float32)) * row_scale[None, :]
    ).astype(low_type)
    chosen_part = contract(dlogits, table_low, 0, 0)
    chosen_grad = across(chosen_part.reshape(groups, own_rows, width))
    final_grad = jnp.zeros((tokens, width), jnp.float32).at[flat_picks].add(chosen_grad)

    branch_low, gate_low, first_sum_grad, attn_low, mixed_grad, late_norms = feed_backward(
        final_grad, second_sum, first_sum, gate_up, norms, near, w_gu_low, w_down_low
    )
    down, gate, up = Fold(1, (4, 2)), Fold(1, (2, 4)), Fold(1, (4, 2))
    middle = gate_up.shape[1] // 2
    sent = down.cores(gradient_chunks(contract(hidden_low, branch_low, 0, 0)))
    gate_low, _ = tie((gate_low, sent))
    sent = gate.cores(gradient_chunks(contract(second_low, gate_low[:, :middle], 0, 0)))
    gate_low, _ = tie((gate_low, sent))
    up.cores(gradient_chunks(contract(second_low, gate_low[:, middle:], 0, 0)))
    pairs = width // LANES
    third = pairs // 3
    sides = []
    for stage in range(3):
        if stage == 0:
            sent = down.plane(True) + gate.plane(True) + up.plane(True)
        elif stage == 1:
            sent = down.plane(False) + gate.plane(False)
        else:
            sent = down.members() + gate.members() + up.plane(False)
        mixed_grad, sides, _ = tie((mixed_grad, sides, sent))
        sides = list(sides) + [
            attend_back(lengths, queries, keys, values, mixed_grad, log_sums, cosine, sine, stage * third, third)
        ]
    sent = up.members()
    sides, down.came, gate.came, _ = tie((sides, down.came, gate.came, sent))
    joined_grad = jnp.concatenate([side for parts in zip(*sides) for side in parts], axis=1)
    first_grad = first_sum_grad + contract(joined_grad, near[:, : 3 * width], 1, 1)
    _, pull = jax.vjp(layer_norm, embed.astype(jnp.float32), norms[0], norms[1])
    embed_grad, gain_one, shift_one = pull(first_grad)
    norm_grad = jnp.concatenate([gain_one[None], shift_one[None], late_norms])
    embed_low, joined_grad = tie((embed_grad.astype(low_type), joined_grad))
    group_embed = lax.all_gather(embed_low, "grp", axis=0, tiled=True)

    join = Fold(1, (2, 4))
    join.cores(
        gradient_chunks(
            jnp.concatenate(
                [contract(first_low, joined_grad, 0, 0), contract(mixed_low, attn_low, 0, 0)], axis=1
            )
        )
    )
    join.plane(True)
    join.plane(False)
    join.members()
    gu_share = jnp.concatenate([gate.total(), up.total()], axis=1)
    down_share, join_share = down.total(), join.total()
    part_rows = gu_share.shape[0]
    far_whole = plane_gather(
        jnp.concatenate(
            [gu_share.astype(low_type), down_share.astype(low_type).reshape(part_rows, -1)], axis=1
        )
    ).reshape(shard_rows, -1)
    near_whole = plane_gather(join_share.astype(low_type)).reshape(shard_rows, -1)
    shares = (join_share[:, : 3 * width], join_share[:, 3 * width :], gu_share, down_share)
    share_cols = [jnp.sum(gradient * gradient, axis=0) for gradient in shares]
    group_embed, near_whole, far_whole, share_cols = tie((group_embed, near_whole, far_whole, share_cols))

    core = replica % 2
    middle = width // 2
    rest = (starts, codes, padded_order, dlogits, group_chosen, group_embed, block)
    if quick:
        chunks = ((replica // 2) ^ jnp.arange(3, -1, -1, dtype=jnp.int32)) * 2
        sent = table_grad_chunks(chunks + 1 - core, *rest, low_type)
        sent_x, kept_x, sent_y, kept_y = table_grad_chunks(chunks + core, *rest, low_type, flip(sent, 1))
        one = kept_x + flip(sent_x, 2).astype(jnp.float32)
        two = kept_y + flip(sent_y, 4).astype(jnp.float32)
        table_parts = [
            one[1] + flip(one[0].astype(low_type), 4).astype(jnp.float32),
            two[1] + flip(two[0].astype(low_type), 2).astype(jnp.float32),
        ]
    else:
        value = table_grad_chunks(jnp.arange(replicas, dtype=jnp.int32), *rest, jnp.float32)
        value = lax.psum_scatter(value, "rep", scatter_dimension=0)
        table_parts = [value[:, :middle], value[:, middle:]]

    old_rows = (table_rows, qkv_rows, out_rows, gu_rows, down_rows)
    old_cols = (table_cols, qkv_cols, out_cols, gu_cols, down_cols)
    masters = (table, w_qkv, w_out, w_gu, w_down)
    col_parts = [
        jnp.concatenate([jnp.sum(gradient * gradient, axis=0) for gradient in table_parts])
    ] + share_cols
    row_old = jnp.stack([jnp.sum(rows) for rows in old_rows]) / replicas
    small = [norm_grad.reshape(-1)] + col_parts + [row_old, jnp.sum(own_terms)[None]]
    plane_totals = plane_sum(jnp.concatenate(small))
    table_lows = [part.astype(low_type) for part in table_parts]
    plane_totals, table_lows = tie((plane_totals, table_lows))
    if quick:
        have = [spread(low, bits) for low, bits in zip(table_lows, ((4, 2), (2, 4)))]
        plane_totals, have = tie((plane_totals, have))
    totals = rest_sum(plane_totals)
    cuts = []
    start = 0
    for part in small:
        cuts.append(totals[start : start + part.shape[0]])
        start += part.shape[0]
    norm_sum = cuts[0].reshape(norm_grad.shape)
    col_totals = cuts[1:6]
    old_totals = cuts[6]
    loss_sum = cuts[7][0]
    squares = [jnp.sum(part) for part in col_totals]
    clip_norm = jnp.sqrt(sum(squares) + jnp.sum(norm_sum * norm_sum))
    factor = clip_limit / jnp.maximum(clip_norm, clip_limit)
    decay = 1.0 - float(STEP) ** (-0.8)

    wholes = [
        None,
        near_whole[:, : 3 * width],
        near_whole[:, 3 * width :],
        far_whole[:, : w_gu.shape[1]],
        far_whole[:, w_gu.shape[1] :].reshape(w_down.shape),
    ]

    outputs = []
    for place in range(5):
        rows, columns = masters[place].shape
        full_rows = rows * groups
        new_cols = (
            decay * old_cols[place] + (1.0 - decay) * (col_totals[place] * factor * factor) / full_rows
        )
        row_total = decay * old_totals[place] + (1.0 - decay) * (squares[place] * factor * factor) / columns
        row_mean = row_total / full_rows
        if place == 0 and quick:
            have = [wave(got, 1) for got in have]
            tiles = padded // TILE
            row_tiles = jnp.pad(table_rows, (0, padded - vocab_rows), constant_values=1.0).reshape(tiles, 1, TILE)
            scalars = jnp.stack([factor, rate_matrix * factor * jnp.sqrt(row_mean)])
            so_far = (
                blank(table.shape, jnp.float32),
                blank(table.shape, jnp.float32),
                blank((tiles, 1, TILE), jnp.float32),
            )
            for places in ((0,), (2, 4), (6,), (1, 3, 5, 7)):
                so_far = update(
                    places,
                    slots_of(),
                    scalars,
                    [[got[part] for got in have] for part in places],
                    table,
                    row_tiles,
                    lax.rsqrt(new_cols)[None, :],
                    so_far,
                )
            outputs.extend([so_far[0], so_far[2].reshape(-1)[:vocab_rows], new_cols, so_far[1]])
            continue
        if place == 0:
            whole = plane_gather(jnp.concatenate(table_lows, axis=1))
            gradient = whole.reshape(padded, width)[:vocab_rows].astype(jnp.float32)
        else:
            gradient = wholes[place].astype(jnp.float32)
        row_means = jnp.mean(gradient * gradient, axis=1)
        new_rows = decay * old_rows[place] + (1.0 - decay) * (row_means * factor * factor)
        clipped = gradient * factor
        scale = new_rows[:, None] * new_cols[None, :] / row_mean
        new_master = masters[place] - rate_matrix * clipped * lax.rsqrt(scale)
        outputs.extend([clipped, new_rows, new_cols, new_master])
    norm_clipped = norm_sum * factor
    moment_new = decay * norms_moment + (1.0 - decay) * norm_clipped * norm_clipped
    norms_new = norms - rate_norm * norm_clipped * lax.rsqrt(moment_new)
    return (
        (loss_sum, loss_count, clip_norm) + tuple(outputs) + (norm_clipped, moment_new, norms_new)
    )


def solution(mesh):
    in_specs = (
        P(("grp", "rep"), None),
        P(("grp", "rep")),
        P(("grp", "rep"), None),
        P(("grp", "rep"), None),
        P(("grp", "rep"), None),
        P("grp", None),
        P("grp", None),
        P("grp", None),
        P("grp", None),
        P("grp", None),
        P(),
        P("grp"),
        P(),
        P("grp"),
        P(),
        P("grp"),
        P(),
        P("grp"),
        P(),
        P("grp"),
        P(),
        P(),
    )
    out_specs = (
        P(),
        P(),
        P(),
        P("grp", None),
        P("grp"),
        P(),
        P("grp", None),
        P("grp", None),
        P("grp"),
        P(),
        P("grp", None),
        P("grp", None),
        P("grp"),
        P(),
        P("grp", None),
        P("grp", None),
        P("grp"),
        P(),
        P("grp", None),
        P("grp", None),
        P("grp"),
        P(),
        P("grp", None),
        P(),
        P(),
        P(),
    )
    return jax.shard_map(body, mesh=mesh, in_specs=in_specs, out_specs=out_specs, check_vma=False)
```
